32 devices in a mesh: rep: 2 (over x), fsdp: 16 (over z, y, core).
Axes of the slice: x: 2, y: 2, z: 4, core: 2. Of those that a mesh axis runs over, the one named last changes fastest.
Arguments:
- tokens: bfloat16 [32, 1024, 768], P(('rep', 'fsdp')), may hold values from -6 to 6
- cotangent: bfloat16 [32, 1024, 768], P(('rep', 'fsdp')), may hold values from -6 to 6
- image_counts: int32 [32, 3], P(('rep', 'fsdp')), may hold values from 0 to 576, as said below
- patch_rows: int32 [32, 1024], P(('rep', 'fsdp')), may hold values from 0 to 23, as said below
- patch_cols: int32 [32, 1024], P(('rep', 'fsdp')), may hold values from 0 to 23, as said below
- ln1_gain: bfloat16 [768], P('fsdp'), may hold values from 0.099609375 to 1.8984375
- ln1_bias: bfloat16 [768], P('fsdp'), may hold values from -1.5 to 1.5
- qkv_weight: bfloat16 [768, 2304], P('fsdp'), may hold values from -0.21875 to 0.21875
- qkv_bias: bfloat16 [2304], P('fsdp'), may hold values from -1.5 to 1.5
- rope_freqs: bfloat16 [768], P('fsdp'), may hold values from -1 to 1
- out_weight: bfloat16 [768, 768], P('fsdp'), may hold values from -0.875 to 0.875
- out_bias: bfloat16 [768], P('fsdp'), may hold values from -1.5 to 1.5
- ln2_gain: bfloat16 [768], P('fsdp'), may hold values from 0.099609375 to 1.8984375
- ln2_bias: bfloat16 [768], P('fsdp'), may hold values from -1.5 to 1.5
- fc1_weight: bfloat16 [768, 3072], P('fsdp'), may hold values from -0.21875 to 0.21875
- fc1_bias: bfloat16 [3072], P('fsdp'), may hold values from -1.5 to 1.5
- fc2_weight: bfloat16 [3072, 768], P('fsdp'), may hold values from -0.109375 to 0.109375
- fc2_bias: bfloat16 [768], P('fsdp'), may hold values from -1.5 to 1.5
Outputs:
- output_tokens: bfloat16 [32, 1024, 768], P(('rep', 'fsdp'))
- input_grad: bfloat16 [32, 1024, 768], P(('rep', 'fsdp'))
- grad_ln1_gain: float32 [768], P('fsdp')
- grad_ln1_bias: float32 [768], P('fsdp')
- grad_qkv_weight: float32 [768, 2304], P('fsdp')
- grad_qkv_bias: float32 [2304], P('fsdp')
- grad_rope_freqs: float32 [768], P('fsdp')
- grad_out_weight: float32 [768, 768], P('fsdp')
- grad_out_bias: float32 [768], P('fsdp')
- grad_ln2_gain: float32 [768], P('fsdp')
- grad_ln2_bias: float32 [768], P('fsdp')
- grad_fc1_weight: float32 [768, 3072], P('fsdp')
- grad_fc1_bias: float32 [3072], P('fsdp')
- grad_fc2_weight: float32 [3072, 768], P('fsdp')
- grad_fc2_bias: float32 [768], P('fsdp')
The draws below stay inside these ranges and needn't reach their ends.
Inputs may be any that keep to these rules, and one draw needn't show every extreme that they name: `image_counts`: each row packs whole images from its first slot on; counts are 196, 400 or 576, the first of every row is 576, zeros follow the last image, and a row's counts sum to at most 1024. `patch_rows`: an image's slots run row by row over its square of patches; padding slots hold 0. `patch_cols`: the column within that row; padding slots hold 0.
All inputs are finite; a program needn't handle non-finite values.
Results may differ from the reference program's by a relative error of at most 0.015.
Values may be sent and summed in bfloat16 or wider, within the bound.
No kernel may reach another device: no remote copies, remote signals or barrier semaphores. Data moves between devices by JAX's collectives and lax.ppermute only.
A program may use at most 256 MiB of HBM per device.

```python
import jax
import jax.numpy as jnp
from jax import lax

D = 768
HEADS = 12
HEAD_DIM = 64
FF = 3072
SLOTS = 1024
SIDE_S = 14
SIDE_M = 20
SIDE_L = 24
IMGS = 3
ROWS = 32


def packed_images(key):
    kinds = jax.random.randint(key, (ROWS, IMGS), 0, 3)
    place_img = jnp.arange(IMGS, dtype=jnp.int32)
    row_ids = jnp.arange(ROWS, dtype=jnp.int32)
    kinds = jnp.where(row_ids[:, None] == 0, 0, kinds)
    kinds = jnp.where(place_img[None, :] == 0, 2, kinds)
    sides = jnp.where(kinds == 0, SIDE_S, jnp.where(kinds == 1, SIDE_M, SIDE_L)).astype(jnp.int32)
    counts = sides * sides
    ends = jnp.cumsum(counts, axis=1)
    keep = ends <= SLOTS
    counts = jnp.where(keep, counts, 0).astype(jnp.int32)
    sides = jnp.where(keep, sides, 1).astype(jnp.int32)
    return (counts, sides)


def patch_places(key):
    counts, sides = packed_images(key)
    ends = jnp.cumsum(counts, axis=1)
    starts = ends - counts
    slot_ids = jnp.arange(SLOTS, dtype=jnp.int32)
    owner = jnp.sum((slot_ids[None, :, None] >= ends[:, None, :]).astype(jnp.int32), axis=2)
    live = slot_ids[None, :] < ends[:, -1:]
    owner_safe = jnp.minimum(owner, IMGS - 1)
    start_at = jnp.take_along_axis(starts, owner_safe, axis=1)
    side_at = jnp.take_along_axis(sides, owner_safe, axis=1)
    local = slot_ids[None, :] - start_at
    row_at = jnp.where(live, local // side_at, 0).astype(jnp.int32)
    col_at = jnp.where(live, local % side_at, 0).astype(jnp.int32)
    return (row_at, col_at)


def draw_image_counts(key, part):
    counts, sides = packed_images(key)
    return counts


def draw_patch_rows(key, part):
    row_at, col_at = patch_places(key)
    return row_at


def draw_patch_cols(key, part):
    row_at, col_at = patch_places(key)
    return col_at


def with_spikes(drawn, own_key, source, target, blocks, factor):
    def block_of(position):
        return (jnp.arange(drawn.shape[position]) // (drawn.shape[position] // blocks)).reshape((-1,) + (1,) * (drawn.ndim - 1 - position))

    one_side = jax.random.permutation(own_key, blocks)[block_of(target)]
    far = (block_of(target) + blocks // 2) % blocks
    return jnp.where((block_of(source) == one_side) | (block_of(source) == far), factor * drawn, drawn)


def level_of(rng, extent, cuts, smallest, high):
    gain, own = 1.0, jax.random.fold_in(rng, 6)
    for dim, shards_of in cuts:
        heights = jnp.exp(jax.random.uniform(jax.random.fold_in(own, dim), (shards_of,), jnp.float32, smallest / len(cuts), high / len(cuts)))
        gain = gain * jnp.repeat(heights, extent[dim] // shards_of).reshape([-1 if axis == dim else 1 for axis in range(len(extent))])
    return gain


def scatter_about(stream_key, dims, scale, reach, cuts=(), kind=jnp.bfloat16):
    gain = level_of(stream_key, dims, cuts, -0.22, 0.18) if cuts else 1.0
    values = jax.random.normal(stream_key, dims, jnp.float32) * scale * gain
    return jnp.minimum(jnp.maximum(values, -reach), reach).astype(kind)


def gaussian_with(own_key, shape, scale, bound, pieces, heavy, kind=jnp.bfloat16):
    drawn = scale * jax.random.normal(own_key, shape, jnp.float32)
    if pieces:
        drawn = drawn * level_of(own_key, shape, pieces, -0.22, 0.18)
    return jnp.clip(with_spikes(drawn, jax.random.fold_in(own_key, 3), *heavy), -bound, bound).astype(kind)


def setup_inputs(seed: int = 0) -> dict:
    arg_keys = jax.random.split(jax.random.key(seed), 19)
    tokens = gaussian_with(arg_keys[0], (ROWS, SLOTS, D), 1.0, 6.0, ((0, 32),), (0, 2, 32, 2.75))
    cotangent = scatter_about(arg_keys[1], (ROWS, SLOTS, D), 1.0, 6.0, ((0, 32),))
    image_counts = draw_image_counts(jax.random.fold_in(arg_keys[18], 71), 0)
    patch_rows = draw_patch_rows(jax.random.fold_in(arg_keys[18], 71), 0)
    patch_cols = draw_patch_cols(jax.random.fold_in(arg_keys[18], 71), 0)
    ln1_gain = jnp.clip(1.0 + 0.18 * jax.random.normal(arg_keys[5], (D,), jnp.float32), 0.099609375, 1.8984375).astype(jnp.bfloat16)
    ln1_bias = scatter_about(arg_keys[6], (D,), 0.3, 1.5, ((0, 16),))
    qkv_weight = scatter_about(arg_keys[7], (D, 3 * D), D ** -0.5, 0.21875, ((0, 16),))
    qkv_bias = scatter_about(arg_keys[8], (3 * D,), 0.3, 1.5, ((0, 16),))
    rope_freqs = jnp.clip(jax.random.uniform(arg_keys[9], (D,), jnp.float32, -1.0, 1.0) * level_of(arg_keys[9], (D,), ((0, 16),), -0.4, 0.0), -1.0, 1.0).astype(jnp.bfloat16)
    out_weight = scatter_about(arg_keys[10], (D, D), (D // 16) ** -0.5, 0.875, ((0, 16),))
    out_bias = scatter_about(arg_keys[11], (D,), 0.3, 1.5, ((0, 16),))
    ln2_gain = jnp.clip(1.0 + 0.18 * jax.random.normal(arg_keys[12], (D,), jnp.float32), 0.099609375, 1.8984375).astype(jnp.bfloat16)
    ln2_bias = scatter_about(arg_keys[13], (D,), 0.3, 1.5, ((0, 16),))
    fc1_weight = scatter_about(arg_keys[14], (D, FF), D ** -0.5, 0.21875, ((0, 16),))
    fc1_bias = scatter_about(arg_keys[15], (FF,), 0.3, 1.5, ((0, 16),))
    fc2_weight = scatter_about(arg_keys[16], (FF, D), FF ** -0.5, 0.109375, ((0, 16),))
    fc2_bias = scatter_about(arg_keys[17], (D,), 0.3, 1.5, ((0, 16),))
    return dict(tokens=tokens, cotangent=cotangent, image_counts=image_counts, patch_rows=patch_rows, patch_cols=patch_cols, ln1_gain=ln1_gain, ln1_bias=ln1_bias, qkv_weight=qkv_weight, qkv_bias=qkv_bias, rope_freqs=rope_freqs, out_weight=out_weight, out_bias=out_bias, ln2_gain=ln2_gain, ln2_bias=ln2_bias, fc1_weight=fc1_weight, fc1_bias=fc1_bias, fc2_weight=fc2_weight, fc2_bias=fc2_bias)


@jax.custom_vjp
def low(v):
    return lax.optimization_barrier(v.astype(jnp.bfloat16)).astype(jnp.float32)

@jax.custom_vjp
def low_back(v):
    return v

def low_keep(v):
    return (low(v), None)

def low_pass(kept, grad):
    return (grad,)

def back_keep(v):
    return (v, None)

def back_low(kept, grad):
    return (low(grad),)
low.defvjp(low_keep, low_pass)
low_back.defvjp(back_keep, back_low)

def layer_norm(vector, gain_vec, shift_vec):
    center = lax.optimization_barrier(jnp.mean(vector, axis=-1, keepdims=True))
    deviation = vector - center
    spread = lax.optimization_barrier(jnp.mean(deviation * deviation, axis=-1, keepdims=True))
    return deviation * lax.rsqrt(spread + 1e-06) * gain_vec + shift_vec

def segment_ids(counts, slots):
    ends = jnp.cumsum(counts)
    place = jnp.arange(slots, dtype=jnp.int32)
    inside = lax.optimization_barrier(jnp.sum((place[:, None] >= ends[None, :]).astype(jnp.int32), axis=1))
    return jnp.where(place < ends[-1], inside, -1).astype(jnp.int32)

def rotate(rows_f, cols_f, queries, key_in, freqs):
    heads = queries.shape[1]
    half = queries.shape[2] // 2
    col_freq = freqs[:heads * half].reshape(heads, half)
    row_freq = freqs[heads * half:].reshape(heads, half)
    angle = cols_f[:, None, None] * col_freq[None] + rows_f[:, None, None] * row_freq[None]
    cosine = jnp.cos(angle)
    sine = jnp.sin(angle)

    def turn(values):
        first = values[..., :half]
        second = values[..., half:]
        return jnp.concatenate([first * cosine - second * sine, first * sine + second * cosine], axis=-1)
    return (turn(queries), turn(key_in))

def attend(query_b, key_b, value_b, seg):
    slots = query_b.shape[0]
    block = min(512, slots)
    scale = query_b.shape[2] ** (-0.5)
    place = jnp.arange(slots, dtype=jnp.int32)

    def one_block(block_at):
        start = (block_at * block).astype(jnp.int32)
        query_blk = lax.dynamic_slice_in_dim(query_b, start, block, 0)
        seg_blk = lax.dynamic_slice_in_dim(seg, start, block, 0)
        place_blk = start + jnp.arange(block, dtype=jnp.int32)
        raw = low_back(jnp.einsum('qhd,khd->hqk', query_blk, key_b, precision=lax.Precision.HIGHEST) * scale)
        allowed = (seg_blk[:, None] == seg[None, :]) & (seg_blk[:, None] >= 0) | (place_blk[:, None] == place[None, :])
        masked = jnp.where(allowed[None], raw, -1e+30)
        peak = lax.optimization_barrier(jnp.max(masked, axis=-1, keepdims=True))
        weights = jnp.exp(masked - peak)
        prob = weights / lax.optimization_barrier(jnp.sum(weights, axis=-1, keepdims=True))
        return jnp.einsum('hqk,khd->qhd', low(prob), value_b, precision=lax.Precision.HIGHEST)
    blocks_out = lax.map(jax.checkpoint(one_block), jnp.arange(slots // block, dtype=jnp.int32))
    return blocks_out.reshape(slots, query_b.shape[1] * query_b.shape[2])

def forward(inputs, rows_f, cols_f, seg, params):
    gain_one, shift_one, w_qkv, b_qkv, freqs, w_out, b_out, gain_two, shift_two, w_up, b_up, w_down, b_down = params
    width = HEADS * HEAD_DIM
    hp = lax.Precision.HIGHEST
    normed = low(layer_norm(inputs, gain_one, shift_one))
    qkv = low_back(jnp.dot(normed, w_qkv, precision=hp) + b_qkv)
    queries = qkv[:, :width].reshape(-1, HEADS, HEAD_DIM)
    key_in = qkv[:, width:2 * width].reshape(-1, HEADS, HEAD_DIM)
    value_in = qkv[:, 2 * width:].reshape(-1, HEADS, HEAD_DIM)
    query_rot, key_rot = rotate(rows_f, cols_f, queries, key_in, freqs)
    mixed = attend(low(query_rot), low(key_rot), low(value_in), seg)
    mixed_b = low(low_back(mixed))
    hidden_one = inputs + (low_back(jnp.dot(mixed_b, w_out, precision=hp)) + b_out)
    normed_two = low(layer_norm(hidden_one, gain_two, shift_two))
    pre_act = low_back(jnp.dot(normed_two, w_up, precision=hp) + b_up)
    act_b = low(jax.nn.gelu(pre_act))
    return hidden_one + (low_back(jnp.dot(act_b, w_down, precision=hp)) + b_down)

def reference(tokens, cotangent, image_counts, patch_rows, patch_cols, ln1_gain, ln1_bias, qkv_weight, qkv_bias, rope_freqs, out_weight, out_bias, ln2_gain, ln2_bias, fc1_weight, fc1_bias, fc2_weight, fc2_bias):
    params = tuple((w.astype(jnp.float32) for w in (ln1_gain, ln1_bias, qkv_weight, qkv_bias, rope_freqs, out_weight, out_bias, ln2_gain, ln2_bias, fc1_weight, fc1_bias, fc2_weight, fc2_bias)))

    def one_row(total, row):
        x_row, dy_row, counts, rows_i, cols_i = row
        seg = segment_ids(counts, SLOTS)
        rows_f = rows_i.astype(jnp.float32)
        cols_f = cols_i.astype(jnp.float32)
        result, back_fn = jax.vjp(lambda xv, pv: forward(xv, rows_f, cols_f, seg, pv), x_row.astype(jnp.float32), params)
        dx_row, dparams = back_fn(dy_row.astype(jnp.float32))
        total = jax.tree.map(jnp.add, total, dparams)
        return (total, (result.astype(jnp.bfloat16), dx_row.astype(jnp.bfloat16)))
    zeros = jax.tree.map(jnp.zeros_like, params)
    total, (outputs, input_grads) = lax.scan(one_row, zeros, (tokens, cotangent, image_counts, patch_rows, patch_cols))
    return (outputs, input_grads, total[0], total[1], total[2], total[3], total[4], total[5], total[6], total[7], total[8], total[9], total[10], total[11], total[12])
```

```python
from functools import partial

import jax
import jax.numpy as jnp
from jax import lax
from jax.experimental import pallas as pl
from jax.experimental.pallas import tpu as pltpu
from jax.sharding import PartitionSpec as P

HEADS = 12
HEAD_DIM = 64
HALF = HEAD_DIM // 2
FIRST = 576
CUT = 512
WIDE = 640
NEG = -1e30
EPS = 1e-6
BF = jnp.bfloat16
F32 = jnp.float32
VMEM_LIMIT = 56 * 1024 * 1024
GELU_C = 0.7978845608028654
GELU_A = 0.044715


def nn(a, b):
    return lax.dot_general(a, b, (((1,), (0,)), ((), ())), preferred_element_type=F32)


def nt(a, b):
    return lax.dot_general(a, b, (((1,), (1,)), ((), ())), preferred_element_type=F32)


def tn(a, b):
    return lax.dot_general(a, b, (((0,), (0,)), ((), ())), preferred_element_type=F32)


def params(**kw):
    return pltpu.CompilerParams(vmem_limit_bytes=VMEM_LIMIT, **kw)


def norm_parts(v):
    mean = jnp.mean(v, axis=-1, keepdims=True)
    dev = v - mean
    var = jnp.mean(dev * dev, axis=-1, keepdims=True)
    inv = lax.rsqrt(var + EPS)
    return dev * inv, inv


def lane_partial(v):
    total = v[:, :128]
    for i in range(1, v.shape[1] // 128):
        total = total + v[:, i * 128 : (i + 1) * 128]
    return total


def norm1_kernel(x_ref, gain_ref, shift_ref, a_ref, at_ref):
    xhat, _ = norm_parts(x_ref[...].astype(F32))
    a = (xhat * gain_ref[...] + shift_ref[...]).astype(BF)
    a_ref[...] = a
    at_ref[...] = a.T


def norm1(x, gain, shift):
    slots, width = x.shape
    blk = 256
    return pl.pallas_call(
        norm1_kernel,
        grid=(slots // blk,),
        in_specs=[
            pl.BlockSpec((blk, width), lambda i: (i, 0)),
            pl.BlockSpec((1, width), lambda i: (0, 0)),
            pl.BlockSpec((1, width), lambda i: (0, 0)),
        ],
        out_specs=[
            pl.BlockSpec((blk, width), lambda i: (i, 0)),
            pl.BlockSpec((width, blk), lambda i: (0, i)),
        ],
        out_shape=[
            jax.ShapeDtypeStruct((slots, width), BF),
            jax.ShapeDtypeStruct((width, slots), BF),
        ],
        compiler_params=params(),
        name="norm1",
    )(x, gain, shift)


def qkv_kernel(a_ref, wq_ref, wk_ref, wv_ref, bq_ref, bk_ref, bv_ref, cos_ref, sin_ref, q_ref, k_ref, v_ref):
    heads = wq_ref.shape[1] // HEAD_DIM
    a = a_ref[...]
    cos = cos_ref[...]
    sin = sin_ref[...]
    for w_ref, b_ref, out_ref, scale in ((wq_ref, bq_ref, q_ref, HEAD_DIM**-0.5), (wk_ref, bk_ref, k_ref, 1.0)):
        u = nt(w_ref[...].T, a) + b_ref[...]
        for h in range(heads):
            u1 = u[h * HEAD_DIM : h * HEAD_DIM + HALF]
            u2 = u[h * HEAD_DIM + HALF : (h + 1) * HEAD_DIM]
            c = cos[h * HALF : (h + 1) * HALF]
            s = sin[h * HALF : (h + 1) * HALF]
            out_ref[h * HEAD_DIM : h * HEAD_DIM + HALF, :] = ((u1 * c - u2 * s) * scale).astype(BF)
            out_ref[h * HEAD_DIM + HALF : (h + 1) * HEAD_DIM, :] = ((u1 * s + u2 * c) * scale).astype(BF)
    v_ref[...] = (nt(wv_ref[...].T, a) + bv_ref[...]).astype(BF)


def project(a, w, bias, cos, sin):
    slots, width = a.shape
    cols = 256
    groups = width // cols
    wspec = lambda part: pl.BlockSpec((width, cols), lambda g: (0, part * groups + g))
    bspec = lambda part: pl.BlockSpec((cols, 1), lambda g: (part * groups + g, 0))
    out = pl.BlockSpec((cols, slots), lambda g: (g, 0))
    return pl.pallas_call(
        qkv_kernel,
        grid=(groups,),
        in_specs=[pl.BlockSpec((slots, width), lambda g: (0, 0))]
        + [wspec(i) for i in range(3)]
        + [bspec(i) for i in range(3)]
        + [pl.BlockSpec((cols // 2, slots), lambda g: (g, 0))] * 2,
        out_specs=[out] * 3,
        out_shape=[jax.ShapeDtypeStruct((width, slots), BF)] * 3,
        compiler_params=params(),
        name="qkv",
    )(a, w, w, w, bias, bias, bias, cos, sin)


def second_bias(counts_ref, slots):
    shape = (slots - FIRST, slots - CUT)
    key = lax.broadcasted_iota(jnp.int32, shape, 0) + FIRST
    query = lax.broadcasted_iota(jnp.int32, shape, 1) + CUT
    end0 = counts_ref[0]
    end1 = end0 + counts_ref[1]
    end2 = end1 + counts_ref[2]

    def seg(place):
        return (place >= end0).astype(jnp.int32) + (place >= end1).astype(jnp.int32)

    allowed = ((seg(key) == seg(query)) & (key < end2) & (query < end2)) | (key == query)
    return jnp.where(allowed, 0.0, NEG)


def attend_kernel(counts_ref, q_ref, k_ref, v_ref, o_ref, lse_ref, bias_ref):
    slots = q_ref.shape[1]

    @pl.when(pl.program_id(0) == 0)
    def _():
        bias_ref[...] = second_bias(counts_ref, slots)

    k = k_ref[...].T
    q = q_ref[...]
    v = v_ref[...]

    def part(scores, first, values):
        peak = jnp.max(scores, axis=0, keepdims=True)
        weights = jnp.exp(scores - peak)
        total = jnp.sum(weights, axis=0, keepdims=True)
        wb = weights.astype(BF)
        gap = jnp.zeros((values.shape[1] - wb.shape[0], wb.shape[1]), BF)
        wb = jnp.concatenate([wb, gap] if first else [gap, wb], axis=0)
        mixed = nn(values, wb) * (1.0 / total)
        return mixed, peak + jnp.log(total)

    mixed1, lse1 = part(nn(k[:FIRST], q[:, :WIDE]), True, v[:, :WIDE])
    mixed2, lse2 = part(nn(k[FIRST:], q[:, CUT:]) + bias_ref[...], False, v[:, CUT:])
    edge = lax.broadcasted_iota(jnp.int32, (1, WIDE - CUT), 1) < FIRST - CUT
    for out, one, two in ((o_ref, mixed1, mixed2), (lse_ref.at[0], lse1, lse2)):
        out[:, :CUT] = one[:, :CUT].astype(out.dtype)
        out[:, CUT:WIDE] = jnp.where(edge, one[:, CUT:], two[:, : WIDE - CUT]).astype(out.dtype)
        out[:, WIDE:] = two[:, WIDE - CUT :].astype(out.dtype)


def attend(counts, q, k, v):
    width, slots = q.shape
    head = pl.BlockSpec((HEAD_DIM, slots), lambda h: (h, 0))
    return pl.pallas_call(
        attend_kernel,
        grid=(width // HEAD_DIM,),
        in_specs=[pl.BlockSpec(memory_space=pltpu.SMEM)] + [head] * 3,
        out_specs=[head, pl.BlockSpec((1, 1, slots), lambda h: (h, 0, 0))],
        out_shape=[
            jax.ShapeDtypeStruct((width, slots), BF),
            jax.ShapeDtypeStruct((width // HEAD_DIM, 1, slots), F32),
        ],
        scratch_shapes=[pltpu.VMEM((slots - FIRST, slots - CUT), F32)],
        compiler_params=params(),
        name="attend",
    )(counts, q, k, v)


def attend_back_kernel(
    counts_ref, q_ref, k_ref, v_ref, o_ref, do_ref, lse_ref, cos_ref, sin_ref, place_ref,
    dq_ref, dk_ref, dv_ref, bq_ref, bk_ref, bv_ref, fc_ref, fr_ref, bias_ref,
):
    slots = q_ref.shape[1]

    @pl.when(pl.program_id(0) == 0)
    def _():
        bias_ref[...] = second_bias(counts_ref, slots)

    kt = k_ref[...]
    k = kt.T
    v = v_ref[...].T
    q = q_ref[...]
    do = do_ref[...]
    lse = lse_ref[0]
    delta = jnp.sum(do.astype(F32) * o_ref[...].astype(F32), axis=0, keepdims=True)
    lane1 = lax.broadcasted_iota(jnp.int32, (1, WIDE), 1)
    lane2 = lax.broadcasted_iota(jnp.int32, (1, slots - CUT), 1)
    lse1 = jnp.where(lane1 < FIRST, lse[:, :WIDE], -NEG)
    lse2 = jnp.where(lane2 >= FIRST - CUT, lse[:, CUT:], -NEG)

    def part(scores, grads, queries, outs, keys, delta_row, first):
        prob = jnp.exp(scores)
        ds = (prob * (grads - delta_row)).astype(BF)
        pb = prob.astype(BF)
        gap = jnp.zeros((keys.shape[1] - pb.shape[0], pb.shape[1]), BF)
        pb = jnp.concatenate([pb, gap] if first else [gap, pb], axis=0)
        ds = jnp.concatenate([ds, gap] if first else [gap, ds], axis=0)
        return nn(keys, ds), nt(queries, ds), nt(outs, pb)

    grads1 = part(
        nn(k[:FIRST], q[:, :WIDE]) - lse1, nn(v[:FIRST], do[:, :WIDE]),
        q[:, :WIDE], do[:, :WIDE], kt[:, :WIDE], delta[:, :WIDE], True,
    )
    grads2 = part(
        nn(k[FIRST:], q[:, CUT:]) + bias_ref[...] - lse2, nn(v[FIRST:], do[:, CUT:]),
        q[:, CUT:], do[:, CUT:], kt[:, CUT:], delta[:, CUT:], False,
    )
    dq, dk, dv = (
        jnp.concatenate([one[:, :CUT], one[:, CUT:] + two[:, : WIDE - CUT], two[:, WIDE - CUT :]], axis=1)
        for one, two in zip(grads1, grads2)
    )
    scale = HEAD_DIM**-0.5
    cos = cos_ref[...]
    sin = sin_ref[...]
    dangle = None
    for r, rot, out, bias_out in ((dq * scale, q.astype(F32) * (1.0 / scale), dq_ref, bq_ref), (dk, kt.astype(F32), dk_ref, bk_ref)):
        r1, r2 = r[:HALF], r[HALF:]
        term = r2 * rot[:HALF] - r1 * rot[HALF:]
        dangle = term if dangle is None else dangle + term
        g1 = (r1 * cos + r2 * sin).astype(BF)
        g2 = (r2 * cos - r1 * sin).astype(BF)
        out[:HALF, :] = g1
        out[HALF:, :] = g2
        bias_out[:HALF, :] = lane_partial(g1.astype(F32))
        bias_out[HALF:, :] = lane_partial(g2.astype(F32))
    dvb = dv.astype(BF)
    dv_ref[...] = dvb
    bv_ref[...] = lane_partial(dvb.astype(F32))
    fc_ref[...] = lane_partial(dangle * place_ref[0:1, :])
    fr_ref[...] = lane_partial(dangle * place_ref[1:2, :])


def attend_back(counts, q, k, v, o, do, lse, cos, sin, places):
    width, slots = q.shape
    heads = width // HEAD_DIM
    head = pl.BlockSpec((HEAD_DIM, slots), lambda h: (h, 0))
    half = pl.BlockSpec((HALF, slots), lambda h: (h, 0))
    return pl.pallas_call(
        attend_back_kernel,
        grid=(heads,),
        in_specs=[pl.BlockSpec(memory_space=pltpu.SMEM)]
        + [head] * 5
        + [pl.BlockSpec((1, 1, slots), lambda h: (h, 0, 0)), half, half]
        + [pl.BlockSpec((2, slots), lambda h: (0, 0))],
        out_specs=[head] * 3
        + [pl.BlockSpec((HEAD_DIM, 128), lambda h: (h, 0))] * 3
        + [pl.BlockSpec((HALF, 128), lambda h: (h, 0))] * 2,
        out_shape=[jax.ShapeDtypeStruct((width, slots), BF)] * 3
        + [jax.ShapeDtypeStruct((width, 128), F32)] * 3
        + [jax.ShapeDtypeStruct((width // 2, 128), F32)] * 2,
        scratch_shapes=[pltpu.VMEM((slots - FIRST, slots - CUT), F32)],
        compiler_params=params(),
        name="attend_back",
    )(counts, q, k, v, o, do, lse, cos, sin, places)


def out_kernel(o_ref, x_ref, w_ref, b_ref, gain_ref, shift_ref, h_ref, c_ref, ct_ref):
    h = x_ref[...].astype(F32) + (nn(o_ref[...].T, w_ref[...]) + b_ref[...])
    h_ref[...] = h
    xhat, _ = norm_parts(h)
    c = (xhat * gain_ref[...] + shift_ref[...]).astype(BF)
    c_ref[...] = c
    ct_ref[...] = c.T


def out_project(o, x, w, b, gain, shift):
    slots, width = x.shape
    blk = 256
    row = pl.BlockSpec((1, width), lambda i: (0, 0))
    rows = pl.BlockSpec((blk, width), lambda i: (i, 0))
    cols = pl.BlockSpec((width, blk), lambda i: (0, i))
    return pl.pallas_call(
        out_kernel,
        grid=(slots // blk,),
        in_specs=[cols, rows, pl.BlockSpec((width, width), lambda i: (0, 0)), row, row, row],
        out_specs=[rows, rows, cols],
        out_shape=[
            jax.ShapeDtypeStruct((slots, width), F32),
            jax.ShapeDtypeStruct((slots, width), BF),
            jax.ShapeDtypeStruct((width, slots), BF),
        ],
        compiler_params=params(),
        name="out_project",
    )(o, x, w, b, gain, shift)


def mlp_kernel(c_ref, ct_ref, dy_ref, h_ref, w1_ref, b1_ref, w2_ref, b2_ref, y_ref, dc_ref, g1_ref, g2_ref, gb1_ref, y_acc, hb_scr, dp_scr):
    slots = c_ref.shape[0]
    tile = 256

    @pl.when(pl.program_id(0) == 0)
    def _():
        y_acc[...] = h_ref[...] + b2_ref[...]
        dc_ref[...] = jnp.zeros_like(dc_ref)

    gb1_ref[...] = jnp.zeros_like(gb1_ref)

    def step(i, _):
        rows = pl.ds(pl.multiple_of(i * tile, tile), tile)
        pre = nn(c_ref[rows, :], w1_ref[...]) + b1_ref[...]
        square = pre * pre
        th = jnp.tanh(GELU_C * (pre + GELU_A * (pre * square)))
        cdf = 0.5 * (1.0 + th)
        hb = (pre * cdf).astype(BF)
        slope = cdf + 0.5 * pre * (1.0 - th * th) * (GELU_C * (1.0 + (3.0 * GELU_A) * square))
        hb_scr[rows, :] = hb
        y_acc[rows, :] += nn(hb, w2_ref[...])
        dpre = (nt(dy_ref[rows, :], w2_ref[...]) * slope).astype(BF)
        dp_scr[rows, :] = dpre
        dc_ref[rows, :] += nt(dpre, w1_ref[...])
        gb1_ref[...] += jnp.sum(dpre.astype(F32), axis=0, keepdims=True)
        return 0

    lax.fori_loop(0, slots // tile, step, 0)
    g1_ref[...] = nn(ct_ref[...], dp_scr[...]).astype(g1_ref.dtype)
    g2_ref[...] = tn(hb_scr[...], dy_ref[...]).astype(g2_ref.dtype)

    @pl.when(pl.program_id(0) == pl.num_programs(0) - 1)
    def _():
        y_ref[...] = y_acc[...].astype(BF)


def mlp(c, ct, dy, h, w1, b1, w2, b2):
    slots, width = c.shape
    hidden = w1.shape[1]
    blk = 512
    whole = lambda r, k: pl.BlockSpec((r, k), lambda j: (0, 0))
    return pl.pallas_call(
        mlp_kernel,
        grid=(hidden // blk,),
        in_specs=[
            whole(slots, width),
            whole(width, slots),
            whole(slots, width),
            whole(slots, width),
            pl.BlockSpec((width, blk), lambda j: (0, j)),
            pl.BlockSpec((1, blk), lambda j: (0, j)),
            pl.BlockSpec((blk, width), lambda j: (j, 0)),
            whole(1, width),
        ],
        out_specs=[
            whole(slots, width),
            whole(slots, width),
            pl.BlockSpec((width, blk), lambda j: (0, j)),
            pl.BlockSpec((blk, width), lambda j: (j, 0)),
            pl.BlockSpec((1, blk), lambda j: (0, j)),
        ],
        out_shape=[
            jax.ShapeDtypeStruct((slots, width), BF),
            jax.ShapeDtypeStruct((slots, width), F32),
            jax.ShapeDtypeStruct((width, hidden), BF),
            jax.ShapeDtypeStruct((hidden, width), BF),
            jax.ShapeDtypeStruct((1, hidden), F32),
        ],
        scratch_shapes=[
            pltpu.VMEM((slots, width), F32),
            pltpu.VMEM((slots, blk), BF),
            pltpu.VMEM((slots, blk), BF),
        ],
        compiler_params=params(),
        name="mlp",
    )(c, ct, dy, h, w1, b1, w2, b2)


def norm_back(grad, v, gain):
    xhat, inv = norm_parts(v)
    g = grad * gain
    lead = jnp.mean(g, axis=-1, keepdims=True)
    slope = jnp.mean(g * xhat, axis=-1, keepdims=True)
    return (g - lead - xhat * slope) * inv, jnp.sum(grad * xhat, axis=0, keepdims=True), jnp.sum(grad, axis=0, keepdims=True)


def out_back_kernel(dc_ref, h_ref, dy_ref, o_ref, w_ref, gain_ref, dh_ref, do_ref, gw_ref, sums_ref, acc_ref):
    i = pl.program_id(0)

    @pl.when(i == 0)
    def _():
        acc_ref[...] = jnp.zeros_like(acc_ref)
        sums_ref[...] = jnp.zeros_like(sums_ref)

    dy = dy_ref[...].astype(F32)
    part, dgain, dshift = norm_back(dc_ref[...], h_ref[...], gain_ref[...])
    dh = dy + part
    dh_ref[...] = dh
    dhb = dh.astype(BF)
    do_ref[...] = nt(w_ref[...], dhb).astype(BF)
    acc_ref[...] += nn(o_ref[...], dhb)
    sums_ref[0:1, :] += dgain
    sums_ref[1:2, :] += dshift
    sums_ref[2:3, :] += jnp.sum(dh, axis=0, keepdims=True)
    sums_ref[3:4, :] += jnp.sum(dy, axis=0, keepdims=True)

    @pl.when(i == pl.num_programs(0) - 1)
    def _():
        gw_ref[...] = acc_ref[...].astype(gw_ref.dtype)


def out_back(dc, h, dy, o, w, gain):
    slots, width = h.shape
    blk = 256
    rows = pl.BlockSpec((blk, width), lambda i: (i, 0))
    cols = pl.BlockSpec((width, blk), lambda i: (0, i))
    whole = lambda r, k: pl.BlockSpec((r, k), lambda i: (0, 0))
    return pl.pallas_call(
        out_back_kernel,
        grid=(slots // blk,),
        in_specs=[rows, rows, rows, cols, whole(width, width), whole(1, width)],
        out_specs=[rows, cols, whole(width, width), whole(8, width)],
        out_shape=[
            jax.ShapeDtypeStruct((slots, width), F32),
            jax.ShapeDtypeStruct((width, slots), BF),
            jax.ShapeDtypeStruct((width, width), BF),
            jax.ShapeDtypeStruct((8, width), F32),
        ],
        scratch_shapes=[pltpu.VMEM((width, width), F32)],
        compiler_params=params(),
        name="out_back",
    )(dc, h, dy, o, w, gain)


def qkv_back_kernel(at_ref, dqkv_ref, w_ref, x_ref, dh_ref, gain_ref, gw_ref, dx_ref, sums_ref, acc_ref):
    j = pl.program_id(0)

    @pl.when(j == 0)
    def _():
        acc_ref[...] = jnp.zeros_like(acc_ref)

    d = dqkv_ref[...]
    gw_ref[...] = nt(at_ref[...], d).astype(gw_ref.dtype)
    acc_ref[...] += nn(w_ref[...], d)

    @pl.when(j == pl.num_programs(0) - 1)
    def _():
        sums_ref[...] = jnp.zeros_like(sums_ref)
        tile = 256
        for i in range(x_ref.shape[0] // tile):
            rows = slice(i * tile, (i + 1) * tile)
            da = acc_ref[:, rows].T
            part, dgain, dshift = norm_back(da, x_ref[rows, :].astype(F32), gain_ref[...])
            dx_ref[rows, :] = (dh_ref[rows, :] + part).astype(BF)
            sums_ref[0:1, :] += dgain
            sums_ref[1:2, :] += dshift


def qkv_back(at, dqkv, w, x, dh, gain):
    slots, width = x.shape
    outs = w.shape[1]
    blk = 768
    whole = lambda r, k: pl.BlockSpec((r, k), lambda j: (0, 0))
    return pl.pallas_call(
        qkv_back_kernel,
        grid=(outs // blk,),
        in_specs=[
            whole(width, slots),
            pl.BlockSpec((blk, slots), lambda j: (j, 0)),
            pl.BlockSpec((width, blk), lambda j: (0, j)),
            whole(slots, width),
            whole(slots, width),
            whole(1, width),
        ],
        out_specs=[pl.BlockSpec((width, blk), lambda j: (0, j)), whole(slots, width), whole(8, width)],
        out_shape=[
            jax.ShapeDtypeStruct((width, outs), BF),
            jax.ShapeDtypeStruct((slots, width), BF),
            jax.ShapeDtypeStruct((8, width), F32),
        ],
        scratch_shapes=[pltpu.VMEM((width, slots), F32)],
        compiler_params=params(),
        name="qkv_back",
    )(at, dqkv, w, x, dh, gain)


def body(
    tokens, cotangent, image_counts, patch_rows, patch_cols, ln1_gain, ln1_bias, qkv_weight, qkv_bias, rope_freqs,
    out_weight, out_bias, ln2_gain, ln2_bias, fc1_weight, fc1_bias, fc2_weight, fc2_bias,
):
    x = tokens[0]
    dy = cotangent[0]
    counts = image_counts[0]
    width = x.shape[1]
    small = (ln1_gain, ln1_bias, qkv_bias, rope_freqs, out_bias, ln2_gain, ln2_bias, fc1_bias, fc2_bias)
    sizes = [s.shape[0] for s in small]
    gather = partial(lax.all_gather, axis_name="fsdp", axis=0, tiled=True)
    packed = lax.all_gather(jnp.concatenate(small), "fsdp", axis=0)
    vectors = []
    at = 0
    for size in sizes:
        vectors.append(packed[:, at : at + size].reshape(-1).astype(F32))
        at += size
    gain1, shift1, b_qkv, freqs, b_out, gain2, shift2, b1, b2 = vectors
    w_qkv = gather(qkv_weight)
    w_out = gather(out_weight)
    w1 = gather(fc1_weight)
    w2 = gather(fc2_weight)

    row = lambda v: v[None, :]
    a, a_t = norm1(x, row(gain1), row(shift1))
    places = jnp.concatenate([patch_cols, patch_rows], axis=0).astype(F32)
    half = freqs.shape[0] // 2
    angle = freqs[:half, None] * places[0:1] + freqs[half:, None] * places[1:2]
    cos = jnp.cos(angle)
    sin = jnp.sin(angle)
    q, k, v = project(a, w_qkv, b_qkv[:, None], cos, sin)
    o, lse = attend(counts, q, k, v)
    h, c, c_t = out_project(o, x, w_out, row(b_out), row(gain2), row(shift2))
    y, dc, g_w1, g_w2, g_b1 = mlp(c, c_t, dy, h, w1, row(b1), w2, row(b2))
    dh, do, g_wout, sums2 = out_back(dc, h, dy, o, w_out, row(gain2))
    dq, dk, dv, s_bq, s_bk, s_bv, s_fc, s_fr = attend_back(counts, q, k, v, o, do, lse, cos, sin, places)
    dqkv = jnp.concatenate([dq, dk, dv], axis=0)
    g_wqkv, dx, sums1 = qkv_back(a_t, dqkv, w_qkv, x, dh, row(gain1))

    scatter = partial(lax.psum_scatter, axis_name="fsdp", scatter_dimension=0, tiled=True)
    both = lambda g: lax.psum(scatter(g), "rep").astype(F32)
    g_bqkv = jnp.sum(jnp.concatenate([s_bq, s_bk, s_bv], axis=0), axis=1)
    g_freq = jnp.sum(jnp.concatenate([s_fc, s_fr], axis=0), axis=1)
    small_grads = (sums1[0], sums1[1], g_bqkv, g_freq, sums2[2], sums2[0], sums2[1], g_b1[0], sums2[3])
    shards = mesh_size = packed.shape[0]
    block = jnp.concatenate([g.reshape(shards, -1) for g in small_grads], axis=1)
    total = lax.psum(block, ("rep", "fsdp"))
    mine = lax.dynamic_index_in_dim(total, lax.axis_index("fsdp"), 0, keepdims=False)
    outs = []
    at = 0
    for size in sizes:
        outs.append(mine[at : at + size])
        at += size
    s_gain1, s_shift1, s_bqkv, s_freq, s_bout, s_gain2, s_shift2, s_b1, s_b2 = outs
    return (
        y[None], dx[None], s_gain1, s_shift1, both(g_wqkv), s_bqkv, s_freq, both(g_wout), s_bout,
        s_gain2, s_shift2, both(g_w1), s_b1, both(g_w2), s_b2,
    )


def solution(mesh):
    row = P(("rep", "fsdp"), None)
    rows = P(("rep", "fsdp"), None, None)
    vec = P("fsdp")
    mat = P("fsdp", None)
    in_specs = (rows, rows, row, row, row, vec, vec, mat, vec, vec, mat, vec, vec, vec, mat, vec, mat, vec)
    out_specs = (rows, rows, vec, vec, mat, vec, vec, mat, vec, vec, vec, mat, vec, mat, vec)
    return jax.shard_map(body, mesh=mesh, in_specs=in_specs, out_specs=out_specs, check_vma=False)
```

```python
from functools import partial

import jax
import jax.numpy as jnp
from jax import lax
from jax.experimental import pallas as pl
from jax.experimental.pallas import tpu as pltpu
from jax.sharding import PartitionSpec as P

HEADS = 12
HEAD_DIM = 64
HALF = HEAD_DIM // 2
FIRST = 576
CUT = 512
WIDE = 640
NEG = -1e30
EPS = 1e-6
BF = jnp.bfloat16
F32 = jnp.float32
GELU_C = 0.7978845608028654
GELU_A = 0.044715


def nn(a, b):
    return lax.dot_general(a, b, (((1,), (0,)), ((), ())), preferred_element_type=F32)


def nt(a, b):
    return lax.dot_general(a, b, (((1,), (1,)), ((), ())), preferred_element_type=F32)


def tn(a, b):
    return lax.dot_general(a, b, (((0,), (0,)), ((), ())), preferred_element_type=F32)


def params(mib=56):
    return pltpu.CompilerParams(vmem_limit_bytes=mib << 20)


def cost(us):
    return pl.CostEstimate(flops=int(us * 1.1e9), bytes_accessed=1 << 16, transcendentals=0)


def norm_parts(v):
    mean = jnp.mean(v, axis=-1, keepdims=True)
    dev = v - mean
    var = jnp.mean(dev * dev, axis=-1, keepdims=True)
    inv = lax.rsqrt(var + EPS)
    return dev * inv, inv


def lane_partial(v):
    total = v[:, :128]
    for i in range(1, v.shape[1] // 128):
        total = total + v[:, i * 128 : (i + 1) * 128]
    return total


def norm1_kernel(x_ref, gain_ref, shift_ref, a_ref, at_ref):
    xhat, _ = norm_parts(x_ref[...].astype(F32))
    a = (xhat * gain_ref[...] + shift_ref[...]).astype(BF)
    a_ref[...] = a
    at_ref[...] = a.T


def norm1(x, gain, shift):
    slots, width = x.shape
    blk = 256
    return pl.pallas_call(
        norm1_kernel,
        grid=(slots // blk,),
        in_specs=[
            pl.BlockSpec((blk, width), lambda i: (i, 0)),
            pl.BlockSpec((1, width), lambda i: (0, 0)),
            pl.BlockSpec((1, width), lambda i: (0, 0)),
        ],
        out_specs=[
            pl.BlockSpec((blk, width), lambda i: (i, 0)),
            pl.BlockSpec((width, blk), lambda i: (0, i)),
        ],
        out_shape=[
            jax.ShapeDtypeStruct((slots, width), BF),
            jax.ShapeDtypeStruct((width, slots), BF),
        ],
        compiler_params=params(),
        cost_estimate=cost(5),
        name="norm1",
    )(x, gain, shift)


def qkv_kernel(a_ref, wq_ref, wk_ref, wv_ref, bq_ref, bk_ref, bv_ref, cos_ref, sin_ref, q_ref, k_ref, v_ref):
    heads = wq_ref.shape[1] // HEAD_DIM
    a = a_ref[...]
    cos = cos_ref[...]
    sin = sin_ref[...]
    for w_ref, b_ref, out_ref, scale in ((wq_ref, bq_ref, q_ref, HEAD_DIM**-0.5), (wk_ref, bk_ref, k_ref, 1.0)):
        u = nt(w_ref[...].T, a) + b_ref[...]
        for h in range(heads):
            u1 = u[h * HEAD_DIM : h * HEAD_DIM + HALF]
            u2 = u[h * HEAD_DIM + HALF : (h + 1) * HEAD_DIM]
            c = cos[h * HALF : (h + 1) * HALF]
            s = sin[h * HALF : (h + 1) * HALF]
            out_ref[h * HEAD_DIM : h * HEAD_DIM + HALF, :] = ((u1 * c - u2 * s) * scale).astype(BF)
            out_ref[h * HEAD_DIM + HALF : (h + 1) * HEAD_DIM, :] = ((u1 * s + u2 * c) * scale).astype(BF)
    v_ref[...] = (nt(wv_ref[...].T, a) + bv_ref[...]).astype(BF)


def project(a, w, bias, cos, sin):
    slots, width = a.shape
    cols = 256
    groups = width // cols
    wspec = lambda part: pl.BlockSpec((width, cols), lambda g: (0, part * groups + g))
    bspec = lambda part: pl.BlockSpec((cols, 1), lambda g: (part * groups + g, 0))
    out = pl.BlockSpec((cols, slots), lambda g: (g, 0))
    return pl.pallas_call(
        qkv_kernel,
        grid=(groups,),
        in_specs=[pl.BlockSpec((slots, width), lambda g: (0, 0))]
        + [wspec(i) for i in range(3)]
        + [bspec(i) for i in range(3)]
        + [pl.BlockSpec((cols // 2, slots), lambda g: (g, 0))] * 2,
        out_specs=[out] * 3,
        out_shape=[jax.ShapeDtypeStruct((width, slots), BF)] * 3,
        compiler_params=params(),
        name="qkv",
    )(a, w, w, w, bias, bias, bias, cos, sin)


def second_bias(counts_ref, slots):
    shape = (slots - FIRST, slots - CUT)
    key = lax.broadcasted_iota(jnp.int32, shape, 0) + FIRST
    query = lax.broadcasted_iota(jnp.int32, shape, 1) + CUT
    end0 = counts_ref[0]
    end1 = end0 + counts_ref[1]
    end2 = end1 + counts_ref[2]

    def seg(place):
        return (place >= end0).astype(jnp.int32) + (place >= end1).astype(jnp.int32)

    allowed = ((seg(key) == seg(query)) & (key < end2) & (query < end2)) | (key == query)
    return jnp.where(allowed, 0.0, NEG)


def attend_kernel(counts_ref, q_ref, k_ref, v_ref, o_ref, lse_ref, bias_ref):
    slots = q_ref.shape[1]

    @pl.when(pl.program_id(0) == 0)
    def _():
        bias_ref[...] = second_bias(counts_ref, slots)

    k = k_ref[...].T
    q = q_ref[...]
    v = v_ref[...]

    def part(scores, first, values):
        peak = jnp.max(scores, axis=0, keepdims=True)
        weights = jnp.exp(scores - peak)
        total = jnp.sum(weights, axis=0, keepdims=True)
        wb = weights.astype(BF)
        gap = jnp.zeros((values.shape[1] - wb.shape[0], wb.shape[1]), BF)
        wb = jnp.concatenate([wb, gap] if first else [gap, wb], axis=0)
        mixed = nn(values, wb) * (1.0 / total)
        return mixed, peak + jnp.log(total)

    mixed1, lse1 = part(nn(k[:FIRST], q[:, :WIDE]), True, v[:, :WIDE])
    mixed2, lse2 = part(nn(k[FIRST:], q[:, CUT:]) + bias_ref[...], False, v[:, CUT:])
    edge = lax.broadcasted_iota(jnp.int32, (1, WIDE - CUT), 1) < FIRST - CUT
    for out, one, two in ((o_ref, mixed1, mixed2), (lse_ref.at[0], lse1, lse2)):
        out[:, :CUT] = one[:, :CUT].astype(out.dtype)
        out[:, CUT:WIDE] = jnp.where(edge, one[:, CUT:], two[:, : WIDE - CUT]).astype(out.dtype)
        out[:, WIDE:] = two[:, WIDE - CUT :].astype(out.dtype)


def attend(counts, q, k, v):
    width, slots = q.shape
    head = pl.BlockSpec((HEAD_DIM, slots), lambda h: (h, 0))
    return pl.pallas_call(
        attend_kernel,
        grid=(width // HEAD_DIM,),
        in_specs=[pl.BlockSpec(memory_space=pltpu.SMEM)] + [head] * 3,
        out_specs=[head, pl.BlockSpec((1, 1, slots), lambda h: (h, 0, 0))],
        out_shape=[
            jax.ShapeDtypeStruct((width, slots), BF),
            jax.ShapeDtypeStruct((width // HEAD_DIM, 1, slots), F32),
        ],
        scratch_shapes=[pltpu.VMEM((slots - FIRST, slots - CUT), F32)],
        compiler_params=params(),
        cost_estimate=cost(9),
        name="attend",
    )(counts, q, k, v)


def attend_back_kernel(
    counts_ref, q_ref, k_ref, v_ref, o_ref, do_ref, lse_ref, cos_ref, sin_ref, place_ref,
    dq_ref, dk_ref, dv_ref, bq_ref, bk_ref, bv_ref, fc_ref, fr_ref, bias_ref,
):
    slots = q_ref.shape[1]

    @pl.when(pl.program_id(0) == 0)
    def _():
        bias_ref[...] = second_bias(counts_ref, slots)

    kt = k_ref[...]
    k = kt.T
    v = v_ref[...].T
    q = q_ref[...]
    do = do_ref[...]
    lse = lse_ref[0]
    delta = jnp.sum(do.astype(F32) * o_ref[...].astype(F32), axis=0, keepdims=True)
    lane1 = lax.broadcasted_iota(jnp.int32, (1, WIDE), 1)
    lane2 = lax.broadcasted_iota(jnp.int32, (1, slots - CUT), 1)
    lse1 = jnp.where(lane1 < FIRST, lse[:, :WIDE], -NEG)
    lse2 = jnp.where(lane2 >= FIRST - CUT, lse[:, CUT:], -NEG)

    def part(scores, grads, queries, outs, keys, delta_row, first):
        prob = jnp.exp(scores)
        ds = (prob * (grads - delta_row)).astype(BF)
        pb = prob.astype(BF)
        gap = jnp.zeros((keys.shape[1] - pb.shape[0], pb.shape[1]), BF)
        pb = jnp.concatenate([pb, gap] if first else [gap, pb], axis=0)
        ds = jnp.concatenate([ds, gap] if first else [gap, ds], axis=0)
        return nn(keys, ds), nt(queries, ds), nt(outs, pb)

    grads1 = part(
        nn(k[:FIRST], q[:, :WIDE]) - lse1, nn(v[:FIRST], do[:, :WIDE]),
        q[:, :WIDE], do[:, :WIDE], kt[:, :WIDE], delta[:, :WIDE], True,
    )
    grads2 = part(
        nn(k[FIRST:], q[:, CUT:]) + bias_ref[...] - lse2, nn(v[FIRST:], do[:, CUT:]),
        q[:, CUT:], do[:, CUT:], kt[:, CUT:], delta[:, CUT:], False,
    )
    dq, dk, dv = (
        jnp.concatenate([one[:, :CUT], one[:, CUT:] + two[:, : WIDE - CUT], two[:, WIDE - CUT :]], axis=1)
        for one, two in zip(grads1, grads2)
    )
    scale = HEAD_DIM**-0.5
    cos = cos_ref[...]
    sin = sin_ref[...]
    dangle = None
    for r, rot, out, bias_out in ((dq * scale, q.astype(F32) * (1.0 / scale), dq_ref, bq_ref), (dk, kt.astype(F32), dk_ref, bk_ref)):
        r1, r2 = r[:HALF], r[HALF:]
        term = r2 * rot[:HALF] - r1 * rot[HALF:]
        dangle = term if dangle is None else dangle + term
        g1 = (r1 * cos + r2 * sin).astype(BF)
        g2 = (r2 * cos - r1 * sin).astype(BF)
        out[:HALF, :] = g1
        out[HALF:, :] = g2
        bias_out[:HALF, :] = lane_partial(g1.astype(F32))
        bias_out[HALF:, :] = lane_partial(g2.astype(F32))
    dvb = dv.astype(BF)
    dv_ref[...] = dvb
    bv_ref[...] = lane_partial(dvb.astype(F32))
    fc_ref[...] = lane_partial(dangle * place_ref[0:1, :])
    fr_ref[...] = lane_partial(dangle * place_ref[1:2, :])


def attend_back(counts, q, k, v, o, do, lse, cos, sin, places):
    width, slots = q.shape
    heads = width // HEAD_DIM
    head = pl.BlockSpec((HEAD_DIM, slots), lambda h: (h, 0))
    half = pl.BlockSpec((HALF, slots), lambda h: (h, 0))
    return pl.pallas_call(
        attend_back_kernel,
        grid=(heads,),
        in_specs=[pl.BlockSpec(memory_space=pltpu.SMEM)]
        + [head] * 5
        + [pl.BlockSpec((1, 1, slots), lambda h: (h, 0, 0)), half, half]
        + [pl.BlockSpec((2, slots), lambda h: (0, 0))],
        out_specs=[head] * 3
        + [pl.BlockSpec((HEAD_DIM, 128), lambda h: (h, 0))] * 3
        + [pl.BlockSpec((HALF, 128), lambda h: (h, 0))] * 2,
        out_shape=[jax.ShapeDtypeStruct((width, slots), BF)] * 3
        + [jax.ShapeDtypeStruct((width, 128), F32)] * 3
        + [jax.ShapeDtypeStruct((width // 2, 128), F32)] * 2,
        scratch_shapes=[pltpu.VMEM((slots - FIRST, slots - CUT), F32)],
        compiler_params=params(),
        cost_estimate=cost(14),
        name="attend_back",
    )(counts, q, k, v, o, do, lse, cos, sin, places)


def out_kernel(o_ref, x_ref, w_ref, b_ref, gain_ref, shift_ref, h_ref, c_ref, ct_ref):
    h = x_ref[...].astype(F32) + (nn(o_ref[...].T, w_ref[...]) + b_ref[...])
    h_ref[...] = h
    xhat, _ = norm_parts(h)
    c = (xhat * gain_ref[...] + shift_ref[...]).astype(BF)
    c_ref[...] = c
    ct_ref[...] = c.T


def out_project(o, x, w, b, gain, shift):
    slots, width = x.shape
    blk = 256
    row = pl.BlockSpec((1, width), lambda i: (0, 0))
    rows = pl.BlockSpec((blk, width), lambda i: (i, 0))
    cols = pl.BlockSpec((width, blk), lambda i: (0, i))
    return pl.pallas_call(
        out_kernel,
        grid=(slots // blk,),
        in_specs=[cols, rows, pl.BlockSpec((width, width), lambda i: (0, 0)), row, row, row],
        out_specs=[rows, rows, cols],
        out_shape=[
            jax.ShapeDtypeStruct((slots, width), F32),
            jax.ShapeDtypeStruct((slots, width), BF),
            jax.ShapeDtypeStruct((width, slots), BF),
        ],
        compiler_params=params(),
        name="out_project",
    )(o, x, w, b, gain, shift)


def mlp_kernel(c_ref, ct_ref, dy_ref, h_ref, w1_ref, b1_ref, w2_ref, b2_ref, y_ref, dc_ref, g1_ref, g2_ref, gb1_ref, y_acc, hb_scr, dp_scr):
    slots = c_ref.shape[0]
    tile = 256

    @pl.when(pl.program_id(0) == 0)
    def _():
        y_acc[...] = h_ref[...] + b2_ref[...]
        dc_ref[...] = jnp.zeros_like(dc_ref)

    gb1_ref[...] = jnp.zeros_like(gb1_ref)

    def step(i, _):
        rows = pl.ds(pl.multiple_of(i * tile, tile), tile)
        pre = nn(c_ref[rows, :], w1_ref[...]) + b1_ref[...]
        square = pre * pre
        th = jnp.tanh(GELU_C * (pre + GELU_A * (pre * square)))
        cdf = 0.5 * (1.0 + th)
        hb = (pre * cdf).astype(BF)
        slope = cdf + 0.5 * pre * (1.0 - th * th) * (GELU_C * (1.0 + (3.0 * GELU_A) * square))
        hb_scr[rows, :] = hb
        y_acc[rows, :] += nn(hb, w2_ref[...])
        dpre = (nt(dy_ref[rows, :], w2_ref[...]) * slope).astype(BF)
        dp_scr[rows, :] = dpre
        dc_ref[rows, :] += nt(dpre, w1_ref[...])
        gb1_ref[...] += jnp.sum(dpre.astype(F32), axis=0, keepdims=True)
        return 0

    lax.fori_loop(0, slots // tile, step, 0)
    g1_ref[...] = nn(ct_ref[...], dp_scr[...]).astype(g1_ref.dtype)
    g2_ref[...] = tn(hb_scr[...], dy_ref[...]).astype(g2_ref.dtype)

    @pl.when(pl.program_id(0) == pl.num_programs(0) - 1)
    def _():
        y_ref[...] = y_acc[...].astype(BF)


def mlp(c, ct, dy, h, w1, b1, w2, b2):
    slots, width = c.shape
    hidden = w1.shape[1]
    blk = 512
    whole = lambda r, k: pl.BlockSpec((r, k), lambda j: (0, 0))
    return pl.pallas_call(
        mlp_kernel,
        grid=(hidden // blk,),
        in_specs=[
            whole(slots, width),
            whole(width, slots),
            whole(slots, width),
            whole(slots, width),
            pl.BlockSpec((width, blk), lambda j: (0, j)),
            pl.BlockSpec((1, blk), lambda j: (0, j)),
            pl.BlockSpec((blk, width), lambda j: (j, 0)),
            whole(1, width),
        ],
        out_specs=[
            whole(slots, width),
            whole(slots, width),
            pl.BlockSpec((width, blk), lambda j: (0, j)),
            pl.BlockSpec((blk, width), lambda j: (j, 0)),
            pl.BlockSpec((1, blk), lambda j: (0, j)),
        ],
        out_shape=[
            jax.ShapeDtypeStruct((slots, width), BF),
            jax.ShapeDtypeStruct((slots, width), F32),
            jax.ShapeDtypeStruct((width, hidden), BF),
            jax.ShapeDtypeStruct((hidden, width), BF),
            jax.ShapeDtypeStruct((1, hidden), F32),
        ],
        scratch_shapes=[
            pltpu.VMEM((slots, width), F32),
            pltpu.VMEM((slots, blk), BF),
            pltpu.VMEM((slots, blk), BF),
        ],
        compiler_params=params(),
        name="mlp",
    )(c, ct, dy, h, w1, b1, w2, b2)


def norm_back(grad, v, gain):
    xhat, inv = norm_parts(v)
    g = grad * gain
    lead = jnp.mean(g, axis=-1, keepdims=True)
    slope = jnp.mean(g * xhat, axis=-1, keepdims=True)
    return (g - lead - xhat * slope) * inv, jnp.sum(grad * xhat, axis=0, keepdims=True), jnp.sum(grad, axis=0, keepdims=True)


def out_back_kernel(dc_ref, h_ref, dy_ref, o_ref, w_ref, gain_ref, dh_ref, do_ref, gw_ref, sums_ref, acc_ref):
    i = pl.program_id(0)

    @pl.when(i == 0)
    def _():
        acc_ref[...] = jnp.zeros_like(acc_ref)
        sums_ref[...] = jnp.zeros_like(sums_ref)

    dy = dy_ref[...].astype(F32)
    part, dgain, dshift = norm_back(dc_ref[...], h_ref[...], gain_ref[...])
    dh = dy + part
    dh_ref[...] = dh
    dhb = dh.astype(BF)
    do_ref[...] = nt(w_ref[...], dhb).astype(BF)
    acc_ref[...] += nn(o_ref[...], dhb)
    sums_ref[0:1, :] += dgain
    sums_ref[1:2, :] += dshift
    sums_ref[2:3, :] += jnp.sum(dh, axis=0, keepdims=True)
    sums_ref[3:4, :] += jnp.sum(dy, axis=0, keepdims=True)

    @pl.when(i == pl.num_programs(0) - 1)
    def _():
        gw_ref[...] = acc_ref[...].astype(gw_ref.dtype)


def out_back(dc, h, dy, o, w, gain):
    slots, width = h.shape
    blk = 256
    rows = pl.BlockSpec((blk, width), lambda i: (i, 0))
    cols = pl.BlockSpec((width, blk), lambda i: (0, i))
    whole = lambda r, k: pl.BlockSpec((r, k), lambda i: (0, 0))
    return pl.pallas_call(
        out_back_kernel,
        grid=(slots // blk,),
        in_specs=[rows, rows, rows, cols, whole(width, width), whole(1, width)],
        out_specs=[rows, cols, whole(width, width), whole(8, width)],
        out_shape=[
            jax.ShapeDtypeStruct((slots, width), F32),
            jax.ShapeDtypeStruct((width, slots), BF),
            jax.ShapeDtypeStruct((width, width), BF),
            jax.ShapeDtypeStruct((8, width), F32),
        ],
        scratch_shapes=[pltpu.VMEM((width, width), F32)],
        compiler_params=params(),
        name="out_back",
    )(dc, h, dy, o, w, gain)


def qkv_back_kernel(at_ref, dqkv_ref, w_ref, x_ref, dh_ref, gain_ref, gw_ref, dx_ref, sums_ref, acc_ref):
    j = pl.program_id(0)

    @pl.when(j == 0)
    def _():
        acc_ref[...] = jnp.zeros_like(acc_ref)

    d = dqkv_ref[...]
    gw_ref[...] = nt(at_ref[...], d).astype(gw_ref.dtype)
    acc_ref[...] += nn(w_ref[...], d)

    @pl.when(j == pl.num_programs(0) - 1)
    def _():
        sums_ref[...] = jnp.zeros_like(sums_ref)
        tile = 256
        for i in range(x_ref.shape[0] // tile):
            rows = slice(i * tile, (i + 1) * tile)
            da = acc_ref[:, rows].T
            part, dgain, dshift = norm_back(da, x_ref[rows, :].astype(F32), gain_ref[...])
            dx_ref[rows, :] = (dh_ref[rows, :] + part).astype(BF)
            sums_ref[0:1, :] += dgain
            sums_ref[1:2, :] += dshift


def qkv_back(at, dqkv, w, x, dh, gain):
    slots, width = x.shape
    outs = w.shape[1]
    blk = 768
    whole = lambda r, k: pl.BlockSpec((r, k), lambda j: (0, 0))
    return pl.pallas_call(
        qkv_back_kernel,
        grid=(outs // blk,),
        in_specs=[
            whole(width, slots),
            pl.BlockSpec((blk, slots), lambda j: (j, 0)),
            pl.BlockSpec((width, blk), lambda j: (0, j)),
            whole(slots, width),
            whole(slots, width),
            whole(1, width),
        ],
        out_specs=[pl.BlockSpec((width, blk), lambda j: (0, j)), whole(slots, width), whole(8, width)],
        out_shape=[
            jax.ShapeDtypeStruct((width, outs), BF),
            jax.ShapeDtypeStruct((slots, width), BF),
            jax.ShapeDtypeStruct((8, width), F32),
        ],
        scratch_shapes=[pltpu.VMEM((width, slots), F32)],
        compiler_params=params(),
        name="qkv_back",
    )(at, dqkv, w, x, dh, gain)


def body_any(
    tokens, cotangent, image_counts, patch_rows, patch_cols, ln1_gain, ln1_bias, qkv_weight, qkv_bias, rope_freqs,
    out_weight, out_bias, ln2_gain, ln2_bias, fc1_weight, fc1_bias, fc2_weight, fc2_bias,
):
    x = tokens[0]
    dy = cotangent[0]
    counts = image_counts[0]
    width = x.shape[1]
    small = (ln1_gain, ln1_bias, qkv_bias, rope_freqs, out_bias, ln2_gain, ln2_bias, fc1_bias, fc2_bias)
    sizes = [s.shape[0] for s in small]
    gather = partial(lax.all_gather, axis_name="fsdp", axis=0, tiled=True)
    packed = lax.all_gather(jnp.concatenate(small), "fsdp", axis=0)
    vectors = []
    at = 0
    for size in sizes:
        vectors.append(packed[:, at : at + size].reshape(-1).astype(F32))
        at += size
    gain1, shift1, b_qkv, freqs, b_out, gain2, shift2, b1, b2 = vectors
    w_qkv = gather(qkv_weight)
    w_out = gather(out_weight)
    w1 = gather(fc1_weight)
    w2 = gather(fc2_weight)

    row = lambda v: v[None, :]
    a, a_t = norm1(x, row(gain1), row(shift1))
    places = jnp.concatenate([patch_cols, patch_rows], axis=0).astype(F32)
    half = freqs.shape[0] // 2
    angle = freqs[:half, None] * places[0:1] + freqs[half:, None] * places[1:2]
    cos = jnp.cos(angle)
    sin = jnp.sin(angle)
    q, k, v = project(a, w_qkv, b_qkv[:, None], cos, sin)
    o, lse = attend(counts, q, k, v)
    h, c, c_t = out_project(o, x, w_out, row(b_out), row(gain2), row(shift2))
    y, dc, g_w1, g_w2, g_b1 = mlp(c, c_t, dy, h, w1, row(b1), w2, row(b2))
    dh, do, g_wout, sums2 = out_back(dc, h, dy, o, w_out, row(gain2))
    dq, dk, dv, s_bq, s_bk, s_bv, s_fc, s_fr = attend_back(counts, q, k, v, o, do, lse, cos, sin, places)
    dqkv = jnp.concatenate([dq, dk, dv], axis=0)
    g_wqkv, dx, sums1 = qkv_back(a_t, dqkv, w_qkv, x, dh, row(gain1))

    scatter = partial(lax.psum_scatter, axis_name="fsdp", scatter_dimension=0, tiled=True)
    both = lambda g: lax.psum(scatter(g), "rep").astype(F32)
    g_bqkv = jnp.sum(jnp.concatenate([s_bq, s_bk, s_bv], axis=0), axis=1)
    g_freq = jnp.sum(jnp.concatenate([s_fc, s_fr], axis=0), axis=1)
    small_grads = (sums1[0], sums1[1], g_bqkv, g_freq, sums2[2], sums2[0], sums2[1], g_b1[0], sums2[3])
    shards = mesh_size = packed.shape[0]
    block = jnp.concatenate([g.reshape(shards, -1) for g in small_grads], axis=1)
    total = lax.psum(block, ("rep", "fsdp"))
    mine = lax.dynamic_index_in_dim(total, lax.axis_index("fsdp"), 0, keepdims=False)
    outs = []
    at = 0
    for size in sizes:
        outs.append(mine[at : at + size])
        at += size
    s_gain1, s_shift1, s_bqkv, s_freq, s_bout, s_gain2, s_shift2, s_b1, s_b2 = outs
    return (
        y[None], dx[None], s_gain1, s_shift1, both(g_wqkv), s_bqkv, s_freq, both(g_wout), s_bout,
        s_gain2, s_shift2, both(g_w1), s_b1, both(g_w2), s_b2,
    )


SHARDS = 16
GROUPS = 2
LEAVING = (0, 8, 4, 12, 2, 10, 6, 14)


def swap(v, mask):
    return lax.ppermute(v, "fsdp", [(i, i ^ mask) for i in range(SHARDS)])


def tie(v, *after):
    return lax.optimization_barrier((v,) + after)[0]


class Gather:
    def __init__(self, mine):
        self.piece = {0: mine}

    def send(self, source, mask, after):
        v = self.piece[source]
        self.piece[source ^ mask] = swap(tie(v, *after) if after else v, mask)

    def stage1(self, *after):
        for mask in (8, 4, 2):
            self.send(0, mask, after)

    def stage2(self, *after):
        self.send(8, 4, after)
        self.send(4, 2, after)
        self.send(8, 2, after)

    def stage3(self, *after):
        self.send(12, 2, after)

    def cores(self, *after):
        for p in (0, 8, 4, 2, 6, 10, 12, 14):
            self.send(p, 1, after)
        return [self.piece[p] for p in range(SHARDS)]


class Scatter:
    def __init__(self, near, far):
        self.got = [near, swap(far, 1)]
        self.size = 4

    def total(self, lo, hi):
        out = self.got[0][lo:hi].astype(F32)
        for g in self.got[1:]:
            out = out + g[lo:hi].astype(F32)
        return out.astype(BF)

    def step(self):
        lo = self.size
        sent = self.total(lo, 2 * lo)
        self.got.append(swap(sent, {4: 2, 2: 4, 1: 8}[lo]))
        self.size = lo // 2
        return sent

    def finish(self):
        mine = self.total(0, 1)[0]
        return mine, lax.ppermute(mine, "rep", [(0, 1), (1, 0)])


def start_all(copies):
    for copy in copies:
        copy.start()


def wait_all(copies):
    for copy in copies:
        copy.wait()


def fetch(refs, order_ref, moves, sem):
    copies = []
    for p, ref in enumerate(refs):
        for rows, place in moves:
            copies.append(pltpu.make_async_copy(ref.at[rows], place(order_ref[p]), sem.at[len(copies)]))
    return copies


ANY = pl.BlockSpec(memory_space=pl.ANY)
SMEM = pl.BlockSpec(memory_space=pltpu.SMEM)
VMEM = pl.BlockSpec(memory_space=pltpu.VMEM)


def group_piece_kernel(w_ref, o_ref, a_ref, b_ref):
    rows, cols = w_ref.shape[0], a_ref.shape[1]
    for i in range(3):
        for g, out in enumerate((a_ref, b_ref)):
            out[i * rows : (i + 1) * rows, :] = w_ref[:, (i * GROUPS + g) * cols : (i * GROUPS + g + 1) * cols]
    for i in range(2):
        b_ref[(3 + i) * rows : (4 + i) * rows, :] = o_ref[:, i * cols : (i + 1) * cols]


def group_pieces(w, w_out):
    rows, cols = w.shape[0], w_out.shape[1] // 2
    return pl.pallas_call(
        group_piece_kernel,
        in_specs=[VMEM, VMEM],
        out_specs=[VMEM, VMEM],
        out_shape=[jax.ShapeDtypeStruct((3 * rows, cols), BF), jax.ShapeDtypeStruct((5 * rows, cols), BF)],
        compiler_params=params(),
        cost_estimate=cost(2),
        name="group_pieces",
    )(w, w_out)


def mlp_piece_kernel(w1_ref, w2_ref, *outs):
    rows1 = w1_ref.shape[0]
    own = w2_ref.shape[0] // 2
    per = SHARDS // 2
    w1 = w1_ref[...].astype(F32)
    for i, out in enumerate(outs):
        for b in range(2):
            runs = [w1[:, (2 * (b * per + j) + i) * own :][:, :own] for j in range(per)]
            out[b * rows1 : (b + 1) * rows1, :] = jnp.concatenate(runs, axis=1).astype(BF)
        out[2 * rows1 :, :] = w2_ref[i * own : (i + 1) * own, :]


def mlp_pieces(w1, w2):
    rows = 2 * w1.shape[0] + w2.shape[0] // 2
    return pl.pallas_call(
        mlp_piece_kernel,
        in_specs=[VMEM, VMEM],
        out_specs=[VMEM, VMEM],
        out_shape=[jax.ShapeDtypeStruct((rows, w2.shape[1]), BF)] * 2,
        compiler_params=params(),
        cost_estimate=cost(2),
        name="mlp_pieces",
    )(w1, w2)


def mlp_join_kernel(*refs):
    ins, (w1_ref, w2_ref) = refs[:4], refs[4:]
    rows1 = w1_ref.shape[0]
    own = w2_ref.shape[0] // 2
    per = SHARDS // 2
    sums = [ins[2 * i][...].astype(F32) + ins[2 * i + 1][...].astype(F32) for i in range(2)]
    runs = []
    for b in range(2):
        for j in range(per):
            runs += [m[b * rows1 : (b + 1) * rows1, j * own : (j + 1) * own] for m in sums]
    w1_ref[...] = jnp.concatenate(runs, axis=1)
    for i in range(2):
        w2_ref[i * own : (i + 1) * own, :] = sums[i][2 * rows1 :]


def mlp_join(rows1, parts):
    own = parts[0].shape[0] - 2 * rows1
    return pl.pallas_call(
        mlp_join_kernel,
        in_specs=[VMEM] * 4,
        out_specs=[VMEM] * 2,
        out_shape=[
            jax.ShapeDtypeStruct((rows1, 2 * own * SHARDS), F32),
            jax.ShapeDtypeStruct((2 * own, parts[0].shape[1]), F32),
        ],
        compiler_params=params(),
        cost_estimate=cost(3),
        name="mlp_join",
    )(*parts)


def spread(packed, lo, size):
    return jnp.concatenate([packed[j : j + 1, lo : lo + size] for j in range(packed.shape[0])], axis=1)


def column(v):
    return jnp.broadcast_to(v, (8, v.shape[1])).T[:, 0:1]


def look_up(table, places):
    top = table.astype(BF)
    rest = table - top.astype(F32)
    middle = rest.astype(BF)
    low = (rest - middle.astype(F32)).astype(BF)
    return nn(top, places) + nn(middle, places) + nn(low, places)


def prepare_kernel(sizes, packed_ref, x_ref, cols_ref, rows_ref, a_ref, at_ref, cos_ref, sin_ref, vec_ref, b1_ref, bias_ref, sel_ref):
    packed = packed_ref[...].astype(F32)
    starts = [sum(sizes[:i]) for i in range(len(sizes))]
    gain1, shift1, b_qkv, freqs, b_out, gain2, shift2 = (spread(packed, starts[i], sizes[i]) for i in range(7))
    b2 = spread(packed, starts[8], sizes[8])
    for i, v in enumerate((b_out, gain1, gain2, shift2, b2)):
        vec_ref[i : i + 1, :] = v
    own = sizes[7] // 2
    for i in range(2):
        b1_ref[i : i + 1, :] = spread(packed, starts[7] + i * own, own)
    bias_ref[...] = column(b_qkv)
    tile = 256
    for i in range(x_ref.shape[0] // tile):
        rows = slice(i * tile, (i + 1) * tile)
        xhat, _ = norm_parts(x_ref[rows, :].astype(F32))
        a = (xhat * gain1 + shift1).astype(BF)
        a_ref[rows, :] = a
        at_ref[:, rows] = a.T
    freq = column(freqs)
    half = freq.shape[0] // 2
    slots = x_ref.shape[0]
    spots = lax.broadcasted_iota(jnp.int32, (1, 128), 1).astype(F32)
    found = []
    for f, at in ((freq[:half], cols_ref[...]), (freq[half:], rows_ref[...])):
        angle = f * spots
        one_hot = jnp.where(lax.broadcasted_iota(jnp.int32, (128, slots), 0) == at, 1.0, 0.0).astype(BF)
        found.append((look_up(jnp.cos(angle), one_hot), look_up(jnp.sin(angle), one_hot)))
    (cos_c, sin_c), (cos_r, sin_r) = found
    cos_ref[...] = cos_c * cos_r - sin_c * sin_r
    sin_ref[...] = sin_c * cos_r + cos_c * sin_r
    line = lax.broadcasted_iota(jnp.int32, sel_ref.shape, 0)
    sel = jnp.where(line == 0, cols_ref[...].astype(F32), rows_ref[...].astype(F32))
    sel_ref[...] = jnp.where(line < 2, sel, jnp.where(line == 2, 1.0, 0.0)).astype(BF)


def prepare(sizes, packed, x, patch_cols, patch_rows):
    slots, width = x.shape
    own = sizes[7] // 2
    shape = jax.ShapeDtypeStruct
    return pl.pallas_call(
        partial(prepare_kernel, sizes),
        in_specs=[VMEM] * 4,
        out_specs=[VMEM] * 8,
        out_shape=[
            shape((slots, width), BF),
            shape((width, slots), BF),
            shape((width // 2, slots), F32),
            shape((width // 2, slots), F32),
            shape((8, width), F32),
            shape((2, own * SHARDS), F32),
            shape((3 * width, 1), F32),
            shape((16, slots), BF),
        ],
        compiler_params=params(40),
        cost_estimate=cost(9),
        name="prepare",
    )(packed, x, patch_cols, patch_rows)


def pack_kernel(sums1_ref, sums2_ref, b1a_ref, b1b_ref, *rest):
    heads, out_ref = rest[:-1], rest[-1]
    bias = [r[2:3, :] for r in heads[:GROUPS]]
    freq = [r[...] for r in heads[GROUPS:]]
    cols = bias[0].shape[1] // 3
    b_qkv = jnp.concatenate([b[:, i * cols : (i + 1) * cols] for i in range(3) for b in bias], axis=1)
    g_freq = jnp.concatenate([f[i : i + 1] for i in range(2) for f in freq], axis=1)
    vectors = (
        sums1_ref[0:1, :], sums1_ref[1:2, :], b_qkv, g_freq, sums2_ref[2:3, :], sums2_ref[0:1, :], sums2_ref[1:2, :],
        b1a_ref[...], b1b_ref[...], sums2_ref[3:4, :],
    )
    lines = []
    for j in range(SHARDS):
        runs = []
        for v in vectors:
            n = v.shape[1] // SHARDS
            runs.append(v[:, j * n : (j + 1) * n])
        lines.append(jnp.concatenate(runs, axis=1))
    out_ref[...] = jnp.concatenate(lines, axis=0)


def pack(size, *sums):
    return pl.pallas_call(
        pack_kernel,
        in_specs=[VMEM] * len(sums),
        out_specs=VMEM,
        out_shape=jax.ShapeDtypeStruct((SHARDS, size), F32),
        compiler_params=params(16),
        cost_estimate=cost(3),
        name="pack",
    )(*sums)


def group_kernel(group, order_ref, a_ref, bias_ref, cos_ref, sin_ref, *rest):
    pieces, (q_ref, k_ref, v_ref, w_scr, sem) = rest[:SHARDS], rest[SHARDS:]
    cols = q_ref.shape[0]
    part = w_scr.shape[1] // 3
    copies = fetch(pieces, order_ref, [(slice(0, 3 * part), lambda d: w_scr.at[d])], sem)
    start_all(copies)
    a = a_ref[...]
    turn = slice(group * cols // 2, (group + 1) * cols // 2)
    cos = cos_ref[turn, :]
    sin = sin_ref[turn, :]
    wait_all(copies)

    def weight(i):
        return w_scr[:, i * part : (i + 1) * part, :].reshape(a.shape[1], cols).T

    def bias(i):
        at = i * a.shape[1] + group * cols
        return bias_ref[at : at + cols, :]

    for i, out_ref, scale in ((0, q_ref, HEAD_DIM**-0.5), (1, k_ref, 1.0)):
        u = nt(weight(i), a) + bias(i)
        for h in range(cols // HEAD_DIM):
            u1 = u[h * HEAD_DIM : h * HEAD_DIM + HALF]
            u2 = u[h * HEAD_DIM + HALF : (h + 1) * HEAD_DIM]
            c = cos[h * HALF : (h + 1) * HALF]
            s = sin[h * HALF : (h + 1) * HALF]
            out_ref[h * HEAD_DIM : h * HEAD_DIM + HALF, :] = ((u1 * c - u2 * s) * scale).astype(BF)
            out_ref[h * HEAD_DIM + HALF : (h + 1) * HEAD_DIM, :] = ((u1 * s + u2 * c) * scale).astype(BF)
    v_ref[...] = (nt(weight(2), a) + bias(2)).astype(BF)


def project_group(group, order, a, bias, cos, sin, pieces):
    slots, width = a.shape
    cols = pieces[0].shape[1]
    return pl.pallas_call(
        partial(group_kernel, group),
        in_specs=[SMEM] + [VMEM] * 4 + [ANY] * SHARDS,
        out_specs=[VMEM] * 3,
        out_shape=[jax.ShapeDtypeStruct((cols, slots), BF)] * 3,
        scratch_shapes=[pltpu.VMEM((SHARDS, 3 * width // SHARDS, cols), BF), pltpu.SemaphoreType.DMA((SHARDS,))],
        compiler_params=params(),
        cost_estimate=cost(7),
        name="qkv_group",
    )(order, a, bias, cos, sin, *pieces)


def out_moves(w_scr, start):
    rows = w_scr.shape[1]
    half = w_scr.shape[2] // 2
    return [
        (slice(start + i * rows, start + (i + 1) * rows), lambda d, i=i: w_scr.at[d, :, pl.ds(i * half, half)])
        for i in range(2)
    ]


def out_group_kernel(start, order_ref, vec_ref, *rest):
    o_refs, x_ref, pieces = rest[:GROUPS], rest[GROUPS], rest[GROUPS + 1 : GROUPS + 1 + SHARDS]
    h_ref, c_ref, ct_ref, w_scr, sem = rest[GROUPS + 1 + SHARDS :]

    @pl.when(pl.program_id(0) == 0)
    def _():
        copies = fetch(pieces, order_ref, out_moves(w_scr, start), sem)
        start_all(copies)
        wait_all(copies)

    width = x_ref.shape[1]
    o = jnp.concatenate([r[...].T for r in o_refs], axis=1)
    h = x_ref[...].astype(F32) + (nn(o, w_scr[...].reshape(width, width)) + vec_ref[0:1, :])
    h_ref[...] = h
    xhat, _ = norm_parts(h)
    c = (xhat * vec_ref[2:3, :] + vec_ref[3:4, :]).astype(BF)
    c_ref[...] = c
    ct_ref[...] = c.T


def out_project_fast(order, o, x, vec, pieces, start):
    slots, width = x.shape
    blk = 256
    rows = pl.BlockSpec((blk, width), lambda i: (i, 0))
    cols = pl.BlockSpec((width, blk), lambda i: (0, i))
    return pl.pallas_call(
        partial(out_group_kernel, start),
        grid=(slots // blk,),
        in_specs=[SMEM, VMEM] + [pl.BlockSpec((width // GROUPS, blk), lambda i: (0, i))] * GROUPS + [rows] + [ANY] * SHARDS,
        out_specs=[rows, rows, cols],
        out_shape=[
            jax.ShapeDtypeStruct((slots, width), F32),
            jax.ShapeDtypeStruct((slots, width), BF),
            jax.ShapeDtypeStruct((width, slots), BF),
        ],
        scratch_shapes=[pltpu.VMEM((SHARDS, width // SHARDS, width), BF), pltpu.SemaphoreType.DMA((2 * SHARDS,))],
        compiler_params=params(),
        cost_estimate=cost(8),
        name="out_project",
    )(order, vec, *o, x, *pieces)


def mlp_half_kernel(part, first, split, n_in, order_ref, c_ref, ct_ref, dy_ref, b1_ref, vec_ref, *rest):
    acc_in, rest = (rest[:1], rest[1:]) if first else (rest[:2], rest[2:])
    pieces, rest = rest[:n_in], rest[n_in:]
    n_g = 2 if split else 1
    y_ref, dc_ref = rest[:2]
    g_refs = rest[2 : 2 + n_g]
    gb1_ref, w1_scr, w2_scr, g1_scr, g2_scr, hb_scr, dp_scr, y_acc, dc_acc, sem, load_sem = rest[2 + n_g : 13 + n_g]
    y_out = y_acc if first else rest[13 + n_g]
    slots, width = c_ref.shape
    rows1 = w1_scr.shape[2]
    rows2 = w2_scr.shape[1]
    blk = w1_scr.shape[3]
    steps = w1_scr.shape[0]
    per = blk // rows2
    tile = 512
    refs = [pieces[0].at[p] for p in range(SHARDS)] if n_in == 1 else pieces
    places = range(SHARDS) if n_in == 1 else order_ref
    loads = [
        fetch(refs, places, [(slice(j * rows1, (j + 1) * rows1), lambda d, j=j: w1_scr.at[j, d])], sem.at[j])
        for j in range(steps)
    ]
    loads.insert(1, fetch(refs, places, [(slice(steps * rows1, steps * rows1 + rows2), lambda d: w2_scr.at[d])], sem.at[steps]))
    sums = [pltpu.make_async_copy(src, dst, load_sem.at[i]) for i, (src, dst) in enumerate(zip(acc_in, (y_acc, dc_acc)))]
    for copies in loads[:2] + [sums] + loads[2:]:
        start_all(copies)
    sends = []
    for j in range(steps):
        cols = slice(j * blk, (j + 1) * blk)
        wait_all(loads[0] if j == 0 else loads[1 + j])
        w1 = w1_scr[j].reshape(width, blk)
        if j == 0:
            wait_all(loads[1] + sums)
        w2 = w2_scr[j * per : (j + 1) * per].reshape(blk, width)
        total = None
        for i in range(slots // tile):
            rows = slice(i * tile, (i + 1) * tile)
            pre = nn(c_ref[rows, :], w1) + b1_ref[part : part + 1, cols]
            square = pre * pre
            th = jnp.tanh(GELU_C * (pre + GELU_A * (pre * square)))
            cdf = 0.5 * (1.0 + th)
            hb = (pre * cdf).astype(BF)
            slope = cdf + 0.5 * pre * (1.0 - th * th) * (GELU_C * (1.0 + (3.0 * GELU_A) * square))
            hb_scr[rows, :] = hb
            y = y_acc[rows, :] + nn(hb, w2)
            if first and j == 0:
                y = y + vec_ref[4:5, :]
            dpre = (nt(dy_ref[rows, :], w2) * slope).astype(BF)
            dp_scr[rows, :] = dpre
            term = jnp.sum(dpre.astype(F32), axis=0, keepdims=True)
            total = term if total is None else total + term
            dc = nt(dpre, w1)
            if not (first and j == 0):
                dc = dc + dc_acc[rows, :]
            dc_acc[rows, :] = dc
            if j == steps - 1:
                y_out[rows, :] = y.astype(y_out.dtype)
                sends += [
                    pltpu.make_async_copy(y_out.at[rows], y_ref.at[rows], load_sem.at[2 + 2 * i]),
                    pltpu.make_async_copy(dc_acc.at[rows], dc_ref.at[rows], load_sem.at[3 + 2 * i]),
                ]
                start_all(sends[-2:])
            else:
                y_acc[rows, :] = y
        gb1_ref[:, cols] = total
        g1_scr[j] = nn(ct_ref[...], dp_scr[...]).astype(BF).reshape(SHARDS, rows1, blk)
        if split:
            dests = [(g_refs[b].at[i], order_ref[p + b]) for b in range(2) for i, p in enumerate(LEAVING)]
        else:
            dests = [(g_refs[0].at[p], p) for p in range(SHARDS)]
        copies = [
            pltpu.make_async_copy(g1_scr.at[j, d], dst.at[slice(j * rows1, (j + 1) * rows1)], sem.at[j, n])
            for n, (dst, d) in enumerate(dests)
        ]
        start_all(copies)
        sends += copies
        g2_scr[j * per : (j + 1) * per] = tn(hb_scr[...], dy_ref[...]).astype(BF).reshape(per, rows2, width)
    copies = [
        pltpu.make_async_copy(g2_scr.at[d], dst.at[slice(steps * rows1, steps * rows1 + rows2)], sem.at[steps, n])
        for n, (dst, d) in enumerate(dests)
    ]
    start_all(copies)
    wait_all(sends + copies)


def mlp_half(part, order, c, ct, dy, b1, vec, sums, pieces, split):
    slots, width = c.shape
    rows1 = width // SHARDS
    rows2 = pieces[0].shape[-2] - 2 * rows1
    hidden = rows2 * SHARDS
    steps = 2
    blk = hidden // steps
    first = len(sums) == 1
    block = jax.ShapeDtypeStruct((SHARDS // 2 if split else SHARDS, 2 * rows1 + rows2, width), BF)
    return pl.pallas_call(
        partial(mlp_half_kernel, part, first, split, len(pieces)),
        in_specs=[SMEM] + [VMEM] * 5 + [ANY] * (len(sums) + len(pieces)),
        out_specs=[ANY, ANY] + [ANY] * (2 if split else 1) + [VMEM],
        out_shape=[jax.ShapeDtypeStruct((slots, width), F32 if first else BF), jax.ShapeDtypeStruct((slots, width), F32)]
        + [block] * (2 if split else 1)
        + [jax.ShapeDtypeStruct((1, hidden), F32)],
        scratch_shapes=[
            pltpu.VMEM((steps, SHARDS, rows1, blk), BF),
            pltpu.VMEM((SHARDS, rows2, width), BF),
            pltpu.VMEM((steps, SHARDS, rows1, blk), BF),
            pltpu.VMEM((SHARDS, rows2, width), BF),
            pltpu.VMEM((slots, blk), BF),
            pltpu.VMEM((slots, blk), BF),
            pltpu.VMEM((slots, width), F32),
            pltpu.VMEM((slots, width), F32),
            pltpu.SemaphoreType.DMA((steps + 1, SHARDS)),
            pltpu.SemaphoreType.DMA((8,)),
        ]
        + ([] if first else [pltpu.VMEM((slots, width), BF)]),
        compiler_params=params(56),
        cost_estimate=cost(23),
        name="mlp_half",
    )(order, c, ct, dy, b1, vec, *sums, *pieces)


def out_back_fast_kernel(start, order_ref, dc_ref, h_ref, dy_ref, vec_ref, *rest):
    o_refs, pieces = rest[:GROUPS], rest[GROUPS : GROUPS + SHARDS]
    dh_ref, do_ref, near_ref, far_ref, sums_ref, acc_ref, g_scr, w_scr, sem = rest[GROUPS + SHARDS :]
    i = pl.program_id(0)
    width = h_ref.shape[1]
    each = width // SHARDS
    half = width // 2

    @pl.when(i == 0)
    def _():
        copies = fetch(pieces, order_ref, out_moves(w_scr, start), sem)
        start_all(copies)
        acc_ref[...] = jnp.zeros_like(acc_ref)
        sums_ref[...] = jnp.zeros_like(sums_ref)
        wait_all(copies)

    dy = dy_ref[...].astype(F32)
    part, dgain, dshift = norm_back(dc_ref[...], h_ref[...], vec_ref[2:3, :])
    dh = dy + part
    dh_ref[...] = dh
    dhb = dh.astype(BF)
    do_ref[...] = nt(w_scr[...].reshape(width, width), dhb).astype(BF)
    rows = width // GROUPS
    for g in range(GROUPS):
        acc_ref[g * rows : (g + 1) * rows, :] += nn(o_refs[g][...], dhb)
    sums_ref[0:1, :] += dgain
    sums_ref[1:2, :] += dshift
    sums_ref[2:3, :] += jnp.sum(dh, axis=0, keepdims=True)
    sums_ref[3:4, :] += jnp.sum(dy, axis=0, keepdims=True)

    @pl.when(i == pl.num_programs(0) - 1)
    def _():
        g_scr[...] = acc_ref[...].astype(BF).reshape(g_scr.shape)
        copies = []
        for b, out in enumerate((near_ref, far_ref)):
            for n, p in enumerate(LEAVING):
                for k in range(2):
                    src = g_scr.at[order_ref[p + b], :, pl.ds(k * half, half)]
                    dst = out.at[n, pl.ds(k * each, each)]
                    copies.append(pltpu.make_async_copy(src, dst, sem.at[len(copies)]))
        start_all(copies)
        wait_all(copies)


def out_back_fast(order, dc, h, dy, vec, o, pieces, start):
    slots, width = h.shape
    blk = 256
    rows = pl.BlockSpec((blk, width), lambda i: (i, 0))
    cols = pl.BlockSpec((width, blk), lambda i: (0, i))
    whole = lambda r, k: pl.BlockSpec((r, k), lambda i: (0, 0))
    block = jax.ShapeDtypeStruct((SHARDS // 2, 2 * width // SHARDS, width // 2), BF)
    return pl.pallas_call(
        partial(out_back_fast_kernel, start),
        grid=(slots // blk,),
        in_specs=[SMEM, rows, rows, rows, VMEM]
        + [pl.BlockSpec((width // GROUPS, blk), lambda i: (0, i))] * GROUPS
        + [ANY] * SHARDS,
        out_specs=[rows, cols, ANY, ANY, whole(8, width)],
        out_shape=[
            jax.ShapeDtypeStruct((slots, width), F32),
            jax.ShapeDtypeStruct((width, slots), BF),
            block,
            block,
            jax.ShapeDtypeStruct((8, width), F32),
        ],
        scratch_shapes=[
            pltpu.VMEM((width, width), F32),
            pltpu.VMEM((SHARDS, width // SHARDS, width), BF),
            pltpu.VMEM((SHARDS, width // SHARDS, width), BF),
            pltpu.SemaphoreType.DMA((2 * SHARDS,)),
        ],
        compiler_params=params(),
        cost_estimate=cost(12),
        name="out_back",
    )(order, dc, h, dy, vec, *o, *pieces)


def heads_back_kernel(
    counts_ref, q_ref, k_ref, v_ref, o_ref, do_ref, lse_ref, cos_ref, sin_ref,
    dq_ref, dk_ref, dv_ref, dangle_ref, bias_ref,
):
    slots = q_ref.shape[1]

    @pl.when(pl.program_id(0) == 0)
    def _():
        bias_ref[...] = second_bias(counts_ref, slots)

    kt = k_ref[...]
    k = kt.T
    v = v_ref[...].T
    q = q_ref[...]
    do = do_ref[...]
    lse = lse_ref[0]
    delta = jnp.sum(do.astype(F32) * o_ref[...].astype(F32), axis=0, keepdims=True)
    lane1 = lax.broadcasted_iota(jnp.int32, (1, WIDE), 1)
    lane2 = lax.broadcasted_iota(jnp.int32, (1, slots - CUT), 1)
    lse1 = jnp.where(lane1 < FIRST, lse[:, :WIDE], -NEG)
    lse2 = jnp.where(lane2 >= FIRST - CUT, lse[:, CUT:], -NEG)

    def part(scores, grads, queries, outs, keys, delta_row, first):
        prob = jnp.exp(scores)
        ds = (prob * (grads - delta_row)).astype(BF)
        pb = prob.astype(BF)
        gap = jnp.zeros((keys.shape[1] - pb.shape[0], pb.shape[1]), BF)
        pb = jnp.concatenate([pb, gap] if first else [gap, pb], axis=0)
        ds = jnp.concatenate([ds, gap] if first else [gap, ds], axis=0)
        return nn(keys, ds), nt(queries, ds), nt(outs, pb)

    grads1 = part(
        nn(k[:FIRST], q[:, :WIDE]) - lse1, nn(v[:FIRST], do[:, :WIDE]),
        q[:, :WIDE], do[:, :WIDE], kt[:, :WIDE], delta[:, :WIDE], True,
    )
    grads2 = part(
        nn(k[FIRST:], q[:, CUT:]) + bias_ref[...] - lse2, nn(v[FIRST:], do[:, CUT:]),
        q[:, CUT:], do[:, CUT:], kt[:, CUT:], delta[:, CUT:], False,
    )
    dq, dk, dv = (
        jnp.concatenate([one[:, :CUT], one[:, CUT:] + two[:, : WIDE - CUT], two[:, WIDE - CUT :]], axis=1)
        for one, two in zip(grads1, grads2)
    )
    scale = HEAD_DIM**-0.5
    cos = cos_ref[...]
    sin = sin_ref[...]
    dangle = None
    for r, rot, out in ((dq * scale, q.astype(F32) * (1.0 / scale), dq_ref), (dk, kt.astype(F32), dk_ref)):
        r1, r2 = r[:HALF], r[HALF:]
        term = r2 * rot[:HALF] - r1 * rot[HALF:]
        dangle = term if dangle is None else dangle + term
        g1 = (r1 * cos + r2 * sin).astype(BF)
        g2 = (r2 * cos - r1 * sin).astype(BF)
        out[:HALF, :] = g1
        out[HALF:, :] = g2
    dv_ref[...] = dv.astype(BF)
    dangle_ref[...] = dangle.astype(BF)


def heads_back(group, counts, q, k, v, o, do, lse, cos, sin):
    width, slots = q.shape
    heads = width // HEAD_DIM
    head = pl.BlockSpec((HEAD_DIM, slots), lambda h: (h, 0))
    half = pl.BlockSpec((HALF, slots), lambda h: (h, 0))
    turn = pl.BlockSpec((HALF, slots), lambda h: (group * heads + h, 0))
    late = pl.BlockSpec((HEAD_DIM, slots), lambda h: (group * heads + h, 0))
    return pl.pallas_call(
        heads_back_kernel,
        grid=(heads,),
        in_specs=[pl.BlockSpec(memory_space=pltpu.SMEM)]
        + [head] * 4
        + [late, pl.BlockSpec((1, 1, slots), lambda h: (h, 0, 0)), turn, turn],
        out_specs=[head] * 3 + [half],
        out_shape=[jax.ShapeDtypeStruct((width, slots), BF)] * 3 + [jax.ShapeDtypeStruct((width // 2, slots), BF)],
        scratch_shapes=[pltpu.VMEM((slots - FIRST, slots - CUT), F32)],
        compiler_params=params(),
        cost_estimate=cost(14),
        name="heads_back",
    )(counts, q, k, v, o, do, lse, cos, sin)


def qkv_grad_kernel(order_ref, at_ref, sel_ref, dangle_ref, dq_ref, dk_ref, dv_ref, *rest):
    more, (near_ref, far_ref, bias_ref, freq_ref, g_scr, sem, more_sem) = rest[:-7], rest[-7:]
    part = g_scr.shape[1] // 3
    outs = (near_ref, far_ref)
    extra = [
        pltpu.make_async_copy(ref.at[n], out.at[n, pl.ds(3 * part, ref.shape[1])], more_sem.at[b, n])
        for b, (ref, out) in enumerate(zip(more, outs))
        for n in range(SHARDS // 2)
    ]
    start_all(extra)
    at = at_ref[...]
    for i, ref in enumerate((dq_ref, dk_ref, dv_ref)):
        g = nt(at, ref[...]).astype(BF)
        g_scr[:, i * part : (i + 1) * part, :] = g.reshape(SHARDS, part, g.shape[1])
        bias_ref[:, i * g.shape[1] : (i + 1) * g.shape[1]] = nt(sel_ref[...], ref[...])
    freq_ref[...] = nt(sel_ref[...], dangle_ref[...])
    copies = []
    for b, out in enumerate(outs):
        for n, p in enumerate(LEAVING):
            dst = out.at[n, pl.ds(0, 3 * part)]
            copies.append(pltpu.make_async_copy(g_scr.at[order_ref[p + b]], dst, sem.at[len(copies)]))
    start_all(copies)
    wait_all(copies + extra)


def qkv_grad(order, at, sel, dangle, dq, dk, dv, *more):
    width, slots = at.shape
    cols = dq.shape[0]
    rows = 3 * width // SHARDS
    total = rows + (more[0].shape[1] if more else 0)
    return pl.pallas_call(
        qkv_grad_kernel,
        in_specs=[SMEM] + [VMEM] * (6 + len(more)),
        out_specs=[ANY, ANY, VMEM, VMEM],
        out_shape=[jax.ShapeDtypeStruct((SHARDS // 2, total, cols), BF)] * 2
        + [jax.ShapeDtypeStruct((sel.shape[0], 3 * cols), F32), jax.ShapeDtypeStruct((sel.shape[0], cols // 2), F32)],
        scratch_shapes=[
            pltpu.VMEM((SHARDS, rows, cols), BF),
            pltpu.SemaphoreType.DMA((SHARDS,)),
            pltpu.SemaphoreType.DMA((2, SHARDS // 2)),
        ],
        compiler_params=params(),
        cost_estimate=cost(6),
        name="qkv_grad",
    )(order, at, sel, dangle, dq, dk, dv, *more)


def input_kernel(order_ref, x_ref, dh_ref, vec_ref, *rest):
    grads = rest[: 3 * GROUPS]
    pieces = [rest[3 * GROUPS + g * SHARDS : 3 * GROUPS + (g + 1) * SHARDS] for g in range(GROUPS)]
    dx_ref, sums_ref, w_scr, sem = rest[3 * GROUPS + GROUPS * SHARDS :]
    width, blk = x_ref.shape[1], x_ref.shape[0]
    i = pl.program_id(0)
    part = width // SHARDS

    @pl.when(i == 0)
    def _():
        copies = []
        for g in range(GROUPS):
            copies += fetch(pieces[g], order_ref, [(slice(0, 3 * part), lambda d: w_scr.at[g, d])], sem.at[g])
        start_all(copies)
        sums_ref[...] = jnp.zeros_like(sums_ref)
        wait_all(copies)

    da = None
    for g in range(GROUPS):
        for n in range(3):
            w = w_scr[g, :, n * part : (n + 1) * part, :].reshape(width, width // GROUPS)
            term = nn(w, grads[3 * g + n][...])
            da = term if da is None else da + term
    out, dgain, dshift = norm_back(da.T, x_ref[...].astype(F32), vec_ref[1:2, :])
    dx_ref[...] = (dh_ref[...] + out).astype(BF)
    sums_ref[0:1, :] += dgain
    sums_ref[1:2, :] += dshift


def input_back(order, x, dh, vec, grads, pieces):
    slots, width = x.shape
    blk = 256
    rows = pl.BlockSpec((blk, width), lambda i: (i, 0))
    whole = lambda r, k: pl.BlockSpec((r, k), lambda i: (0, 0))
    return pl.pallas_call(
        input_kernel,
        grid=(slots // blk,),
        in_specs=[SMEM, rows, rows, VMEM]
        + [pl.BlockSpec((width // GROUPS, blk), lambda i: (0, i))] * (3 * GROUPS)
        + [ANY] * (GROUPS * SHARDS),
        out_specs=[rows, whole(8, width)],
        out_shape=[jax.ShapeDtypeStruct((slots, width), BF), jax.ShapeDtypeStruct((8, width), F32)],
        scratch_shapes=[
            pltpu.VMEM((GROUPS, SHARDS, 3 * width // SHARDS, width // GROUPS), BF),
            pltpu.SemaphoreType.DMA((GROUPS, SHARDS)),
        ],
        compiler_params=params(),
        cost_estimate=cost(12),
        name="input_back",
    )(order, x, dh, vec, *grads, *[p for group in pieces for p in group])


def body_fast(
    tokens, cotangent, image_counts, patch_rows, patch_cols, ln1_gain, ln1_bias, qkv_weight, qkv_bias, rope_freqs,
    out_weight, out_bias, ln2_gain, ln2_bias, fc1_weight, fc1_bias, fc2_weight, fc2_bias,
):
    x = tokens[0]
    dy = cotangent[0]
    counts = image_counts[0]
    slots, width = x.shape
    cols = width // GROUPS
    half = width // 2
    order = lax.axis_index("fsdp") ^ jnp.arange(SHARDS, dtype=jnp.int32)

    own = fc2_weight.shape[0] // 2
    piece_a, piece_b = group_pieces(qkv_weight, out_weight)
    gather_a = Gather(piece_a)
    gather_a.stage1()
    piece_c, piece_d = mlp_pieces(tie(fc1_weight, piece_a), fc2_weight)

    small = (ln1_gain, ln1_bias, qkv_bias, rope_freqs, out_bias, ln2_gain, ln2_bias, fc1_bias, fc2_bias)
    sizes = [s.shape[0] for s in small]
    mine = jnp.concatenate(small)
    packed = lax.all_to_all(jnp.broadcast_to(mine[None], (SHARDS, mine.shape[0])), "fsdp", 0, 0, tiled=True)
    gather_a.stage2(packed)
    a, a_t, cos, sin, vec, b1, bias, sel = prepare(sizes, packed, tie(x, gather_a.piece[12]), patch_cols, patch_rows)
    gather_a.stage3()
    gather_b = Gather(piece_b)
    gather_b.stage1(gather_a.piece[12])
    gather_b.stage2(a)
    gather_b.stage3()
    gather_c = Gather(piece_c)
    gather_c.stage1(a)
    pieces_a = gather_a.cores()
    q, k, v = project_group(0, order, a, bias, cos, sin, pieces_a)
    pieces_d = [lax.all_gather(tie(piece_d, gather_b.piece[12]), "fsdp", axis=0)]
    heads = [(q, k, v) + tuple(attend(counts, q, k, v))]
    gather_c.stage2(q)
    pieces_b = gather_b.cores()
    q, k, v = project_group(1, order, a, bias, cos, sin, pieces_b)
    gather_c.stage3(q)
    heads.append((q, k, v) + tuple(attend(counts, q, k, v)))
    pieces_c = gather_c.cores()
    pieces_all = (pieces_a, pieces_b)
    o = [t[3] for t in heads]
    at_out = piece_a.shape[0]
    h, c, c_t = out_project_fast(order, o, x, vec, pieces_b, at_out)
    y, dc, g_c, g_b1a = mlp_half(0, order, c, c_t, dy, b1, vec, (h,), pieces_c, False)
    mlp_c = lax.psum_scatter(tie(g_c, *pieces_d), "fsdp", scatter_dimension=0, tiled=True)[0]
    y, dc, near_d, far_d, g_b1b = mlp_half(1, order, c, c_t, dy, b1, vec, (y, dc), pieces_d, True)
    scatter_d = Scatter(near_d, far_d)
    dh, do, near_o, far_o, sums2 = out_back_fast(order, dc, h, dy, vec, o, pieces_b, at_out)

    def back(g, do):
        q, k, v, og, lse = heads[g]
        *three, dangle = heads_back(g, counts, q, k, v, og, do, lse, cos, sin)
        return three, dangle

    sent = scatter_d.step()
    grads_b, dangle_b = back(1, tie(do, sent))
    near_b, far_b, bias_b, freq_b = qkv_grad(order, a_t, sel, dangle_b, *grads_b, near_o, far_o)
    scatter_b = Scatter(near_b, far_b)
    grads_a, dangle_a = back(0, tie(do, near_b))
    sent = (scatter_b.step(), scatter_d.step())
    near_a, far_a, bias_a, freq_a = qkv_grad(order, a_t, sel, tie(dangle_a, *sent), *grads_a)
    scatter_a = Scatter(near_a, far_a)
    sent = (scatter_a.step(), scatter_d.step(), scatter_b.step())
    dx, sums1 = input_back(order, x, tie(dh, *sent), vec, grads_a + grads_b, pieces_all)
    for _ in range(2):
        scatter_a.step()
    scatter_b.step()
    mlp_d = scatter_d.finish()
    mine_b = scatter_b.finish()
    mine_a = scatter_a.finish()
    other_c = lax.ppermute(mlp_c, "rep", [(0, 1), (1, 0)])
    s_a = mine_a[0].astype(F32) + mine_a[1].astype(F32)
    s_b = mine_b[0].astype(F32) + mine_b[1].astype(F32)
    rows1 = width // SHARDS
    s_w1, s_w2 = mlp_join(rows1, (mlp_c, other_c) + mlp_d)
    s_wqkv = jnp.concatenate([s[i * rows1 : (i + 1) * rows1] for i in range(3) for s in (s_a, s_b)], axis=1)
    s_wout = jnp.concatenate([s_b[3 * rows1 : 4 * rows1], s_b[4 * rows1 :]], axis=1)

    block = pack(sum(sizes), sums1, sums2, g_b1a, g_b1b, bias_a, bias_b, freq_a, freq_b)
    mine = jnp.sum(lax.all_to_all(block, "fsdp", 0, 0, tiled=True), axis=0)
    mine = mine + lax.ppermute(mine, "rep", [(0, 1), (1, 0)])
    outs = []
    at = 0
    for size in sizes:
        outs.append(mine[at : at + size])
        at += size
    s_gain1, s_shift1, s_bqkv, s_freq, s_bout, s_gain2, s_shift2, s_b1, s_b2 = outs
    return (
        y[None], dx[None], s_gain1, s_shift1, s_wqkv, s_bqkv, s_freq, s_wout, s_bout,
        s_gain2, s_shift2, s_w1, s_b1, s_w2, s_b2,
    )


def solution(mesh):
    row = P(("rep", "fsdp"), None)
    rows = P(("rep", "fsdp"), None, None)
    vec = P("fsdp")
    mat = P("fsdp", None)
    in_specs = (rows, rows, row, row, row, vec, vec, mat, vec, vec, mat, vec, vec, vec, mat, vec, mat, vec)
    out_specs = (rows, rows, vec, vec, mat, vec, vec, mat, vec, vec, vec, mat, vec, mat, vec)
    fast = mesh.shape["fsdp"] == SHARDS and mesh.shape["rep"] == 2
    return jax.shard_map(
        body_fast if fast else body_any, mesh=mesh, in_specs=in_specs, out_specs=out_specs, check_vma=False
    )
```

```python
from functools import partial

import jax
import jax.numpy as jnp
from jax import lax
from jax.experimental import pallas as pl
from jax.experimental.pallas import tpu as pltpu
from jax.sharding import PartitionSpec as P

HEADS = 12
HEAD_DIM = 64
HALF = HEAD_DIM // 2
FIRST = 576
CUT = 512
WIDE = 640
NEG = -1e30
EPS = 1e-6
BF = jnp.bfloat16
F32 = jnp.float32
GELU_C = 0.7978845608028654
GELU_A = 0.044715


def nn(a, b):
    return lax.dot_general(a, b, (((1,), (0,)), ((), ())), preferred_element_type=F32)


def nt(a, b):
    return lax.dot_general(a, b, (((1,), (1,)), ((), ())), preferred_element_type=F32)


def tn(a, b):
    return lax.dot_general(a, b, (((0,), (0,)), ((), ())), preferred_element_type=F32)


def params(mib=56):
    return pltpu.CompilerParams(vmem_limit_bytes=mib << 20)


def cost(us):
    return pl.CostEstimate(flops=int(us * 1.1e9), bytes_accessed=1 << 16, transcendentals=0)


def norm_parts(v):
    mean = jnp.mean(v, axis=-1, keepdims=True)
    dev = v - mean
    var = jnp.mean(dev * dev, axis=-1, keepdims=True)
    inv = lax.rsqrt(var + EPS)
    return dev * inv, inv


def lane_partial(v):
    total = v[:, :128]
    for i in range(1, v.shape[1] // 128):
        total = total + v[:, i * 128 : (i + 1) * 128]
    return total


def norm1_kernel(x_ref, gain_ref, shift_ref, a_ref, at_ref):
    xhat, _ = norm_parts(x_ref[...].astype(F32))
    a = (xhat * gain_ref[...] + shift_ref[...]).astype(BF)
    a_ref[...] = a
    at_ref[...] = a.T


def norm1(x, gain, shift):
    slots, width = x.shape
    blk = 256
    return pl.pallas_call(
        norm1_kernel,
        grid=(slots // blk,),
        in_specs=[
            pl.BlockSpec((blk, width), lambda i: (i, 0)),
            pl.BlockSpec((1, width), lambda i: (0, 0)),
            pl.BlockSpec((1, width), lambda i: (0, 0)),
        ],
        out_specs=[
            pl.BlockSpec((blk, width), lambda i: (i, 0)),
            pl.BlockSpec((width, blk), lambda i: (0, i)),
        ],
        out_shape=[
            jax.ShapeDtypeStruct((slots, width), BF),
            jax.ShapeDtypeStruct((width, slots), BF),
        ],
        compiler_params=params(),
        cost_estimate=cost(5),
        name="norm1",
    )(x, gain, shift)


def qkv_kernel(a_ref, wq_ref, wk_ref, wv_ref, bq_ref, bk_ref, bv_ref, cos_ref, sin_ref, q_ref, k_ref, v_ref):
    heads = wq_ref.shape[1] // HEAD_DIM
    a = a_ref[...]
    cos = cos_ref[...]
    sin = sin_ref[...]
    for w_ref, b_ref, out_ref, scale in ((wq_ref, bq_ref, q_ref, HEAD_DIM**-0.5), (wk_ref, bk_ref, k_ref, 1.0)):
        u = nt(w_ref[...].T, a) + b_ref[...]
        for h in range(heads):
            u1 = u[h * HEAD_DIM : h * HEAD_DIM + HALF]
            u2 = u[h * HEAD_DIM + HALF : (h + 1) * HEAD_DIM]
            c = cos[h * HALF : (h + 1) * HALF]
            s = sin[h * HALF : (h + 1) * HALF]
            out_ref[h * HEAD_DIM : h * HEAD_DIM + HALF, :] = ((u1 * c - u2 * s) * scale).astype(BF)
            out_ref[h * HEAD_DIM + HALF : (h + 1) * HEAD_DIM, :] = ((u1 * s + u2 * c) * scale).astype(BF)
    v_ref[...] = (nt(wv_ref[...].T, a) + bv_ref[...]).astype(BF)


def project(a, w, bias, cos, sin):
    slots, width = a.shape
    cols = 256
    groups = width // cols
    wspec = lambda part: pl.BlockSpec((width, cols), lambda g: (0, part * groups + g))
    bspec = lambda part: pl.BlockSpec((cols, 1), lambda g: (part * groups + g, 0))
    out = pl.BlockSpec((cols, slots), lambda g: (g, 0))
    return pl.pallas_call(
        qkv_kernel,
        grid=(groups,),
        in_specs=[pl.BlockSpec((slots, width), lambda g: (0, 0))]
        + [wspec(i) for i in range(3)]
        + [bspec(i) for i in range(3)]
        + [pl.BlockSpec((cols // 2, slots), lambda g: (g, 0))] * 2,
        out_specs=[out] * 3,
        out_shape=[jax.ShapeDtypeStruct((width, slots), BF)] * 3,
        compiler_params=params(),
        name="qkv",
    )(a, w, w, w, bias, bias, bias, cos, sin)


def second_bias(counts_ref, slots):
    shape = (slots - FIRST, slots - CUT)
    key = lax.broadcasted_iota(jnp.int32, shape, 0) + FIRST
    query = lax.broadcasted_iota(jnp.int32, shape, 1) + CUT
    end0 = counts_ref[0]
    end1 = end0 + counts_ref[1]
    end2 = end1 + counts_ref[2]

    def seg(place):
        return (place >= end0).astype(jnp.int32) + (place >= end1).astype(jnp.int32)

    allowed = ((seg(key) == seg(query)) & (key < end2) & (query < end2)) | (key == query)
    return jnp.where(allowed, 0.0, NEG)


def attend_kernel(counts_ref, q_ref, k_ref, v_ref, o_ref, lse_ref, bias_ref):
    slots = q_ref.shape[1]

    @pl.when(pl.program_id(0) == 0)
    def _():
        bias_ref[...] = second_bias(counts_ref, slots)

    def part(scores, first, values):
        peak = jnp.max(scores, axis=0, keepdims=True)
        weights = jnp.exp(scores - peak)
        total = jnp.sum(weights, axis=0, keepdims=True)
        wb = weights.astype(BF)
        gap = jnp.zeros((values.shape[1] - wb.shape[0], wb.shape[1]), BF)
        wb = jnp.concatenate([wb, gap] if first else [gap, wb], axis=0)
        mixed = nn(values, wb) * (1.0 / total)
        return mixed, peak + jnp.log(total)

    edge = lax.broadcasted_iota(jnp.int32, (1, WIDE - CUT), 1) < FIRST - CUT
    for h in range(q_ref.shape[0] // HEAD_DIM):
        rows = slice(h * HEAD_DIM, (h + 1) * HEAD_DIM)
        k = k_ref[rows, :].T
        q = q_ref[rows, :]
        v = v_ref[rows, :]
        mixed1, lse1 = part(nn(k[:FIRST], q[:, :WIDE]), True, v[:, :WIDE])
        mixed2, lse2 = part(nn(k[FIRST:], q[:, CUT:]) + bias_ref[...], False, v[:, CUT:])
        for out, one, two in ((o_ref.at[rows], mixed1, mixed2), (lse_ref.at[h], lse1, lse2)):
            out[:, :CUT] = one[:, :CUT].astype(out.dtype)
            out[:, CUT:WIDE] = jnp.where(edge, one[:, CUT:], two[:, : WIDE - CUT]).astype(out.dtype)
            out[:, WIDE:] = two[:, WIDE - CUT :].astype(out.dtype)


def attend(counts, q, k, v):
    width, slots = q.shape
    heads = width // HEAD_DIM
    each = 2
    head = pl.BlockSpec((each * HEAD_DIM, slots), lambda h: (h, 0))
    return pl.pallas_call(
        attend_kernel,
        grid=(heads // each,),
        in_specs=[pl.BlockSpec(memory_space=pltpu.SMEM)] + [head] * 3,
        out_specs=[head, pl.BlockSpec((each, 1, slots), lambda h: (h, 0, 0))],
        out_shape=[jax.ShapeDtypeStruct((width, slots), BF), jax.ShapeDtypeStruct((heads, 1, slots), F32)],
        scratch_shapes=[pltpu.VMEM((slots - FIRST, slots - CUT), F32)],
        compiler_params=params(),
        cost_estimate=cost(8),
        name="attend",
    )(counts, q, k, v)


def attend_back_kernel(
    counts_ref, q_ref, k_ref, v_ref, o_ref, do_ref, lse_ref, cos_ref, sin_ref, place_ref,
    dq_ref, dk_ref, dv_ref, bq_ref, bk_ref, bv_ref, fc_ref, fr_ref, bias_ref,
):
    slots = q_ref.shape[1]

    @pl.when(pl.program_id(0) == 0)
    def _():
        bias_ref[...] = second_bias(counts_ref, slots)

    kt = k_ref[...]
    k = kt.T
    v = v_ref[...].T
    q = q_ref[...]
    do = do_ref[...]
    lse = lse_ref[0]
    delta = jnp.sum(do.astype(F32) * o_ref[...].astype(F32), axis=0, keepdims=True)
    lane1 = lax.broadcasted_iota(jnp.int32, (1, WIDE), 1)
    lane2 = lax.broadcasted_iota(jnp.int32, (1, slots - CUT), 1)
    lse1 = jnp.where(lane1 < FIRST, lse[:, :WIDE], -NEG)
    lse2 = jnp.where(lane2 >= FIRST - CUT, lse[:, CUT:], -NEG)

    def part(scores, grads, queries, outs, keys, delta_row, first):
        prob = jnp.exp(scores)
        ds = (prob * (grads - delta_row)).astype(BF)
        pb = prob.astype(BF)
        gap = jnp.zeros((keys.shape[1] - pb.shape[0], pb.shape[1]), BF)
        pb = jnp.concatenate([pb, gap] if first else [gap, pb], axis=0)
        ds = jnp.concatenate([ds, gap] if first else [gap, ds], axis=0)
        return nn(keys, ds), nt(queries, ds), nt(outs, pb)

    grads1 = part(
        nn(k[:FIRST], q[:, :WIDE]) - lse1, nn(v[:FIRST], do[:, :WIDE]),
        q[:, :WIDE], do[:, :WIDE], kt[:, :WIDE], delta[:, :WIDE], True,
    )
    grads2 = part(
        nn(k[FIRST:], q[:, CUT:]) + bias_ref[...] - lse2, nn(v[FIRST:], do[:, CUT:]),
        q[:, CUT:], do[:, CUT:], kt[:, CUT:], delta[:, CUT:], False,
    )
    dq, dk, dv = (
        jnp.concatenate([one[:, :CUT], one[:, CUT:] + two[:, : WIDE - CUT], two[:, WIDE - CUT :]], axis=1)
        for one, two in zip(grads1, grads2)
    )
    scale = HEAD_DIM**-0.5
    cos = cos_ref[...]
    sin = sin_ref[...]
    dangle = None
    for r, rot, out, bias_out in ((dq * scale, q.astype(F32) * (1.0 / scale), dq_ref, bq_ref), (dk, kt.astype(F32), dk_ref, bk_ref)):
        r1, r2 = r[:HALF], r[HALF:]
        term = r2 * rot[:HALF] - r1 * rot[HALF:]
        dangle = term if dangle is None else dangle + term
        g1 = (r1 * cos + r2 * sin).astype(BF)
        g2 = (r2 * cos - r1 * sin).astype(BF)
        out[:HALF, :] = g1
        out[HALF:, :] = g2
        bias_out[:HALF, :] = lane_partial(g1.astype(F32))
        bias_out[HALF:, :] = lane_partial(g2.astype(F32))
    dvb = dv.astype(BF)
    dv_ref[...] = dvb
    bv_ref[...] = lane_partial(dvb.astype(F32))
    fc_ref[...] = lane_partial(dangle * place_ref[0:1, :])
    fr_ref[...] = lane_partial(dangle * place_ref[1:2, :])


def attend_back(counts, q, k, v, o, do, lse, cos, sin, places):
    width, slots = q.shape
    heads = width // HEAD_DIM
    head = pl.BlockSpec((HEAD_DIM, slots), lambda h: (h, 0))
    half = pl.BlockSpec((HALF, slots), lambda h: (h, 0))
    return pl.pallas_call(
        attend_back_kernel,
        grid=(heads,),
        in_specs=[pl.BlockSpec(memory_space=pltpu.SMEM)]
        + [head] * 5
        + [pl.BlockSpec((1, 1, slots), lambda h: (h, 0, 0)), half, half]
        + [pl.BlockSpec((2, slots), lambda h: (0, 0))],
        out_specs=[head] * 3
        + [pl.BlockSpec((HEAD_DIM, 128), lambda h: (h, 0))] * 3
        + [pl.BlockSpec((HALF, 128), lambda h: (h, 0))] * 2,
        out_shape=[jax.ShapeDtypeStruct((width, slots), BF)] * 3
        + [jax.ShapeDtypeStruct((width, 128), F32)] * 3
        + [jax.ShapeDtypeStruct((width // 2, 128), F32)] * 2,
        scratch_shapes=[pltpu.VMEM((slots - FIRST, slots - CUT), F32)],
        compiler_params=params(),
        cost_estimate=cost(14),
        name="attend_back",
    )(counts, q, k, v, o, do, lse, cos, sin, places)


def out_kernel(o_ref, x_ref, w_ref, b_ref, gain_ref, shift_ref, h_ref, c_ref, ct_ref):
    h = x_ref[...].astype(F32) + (nn(o_ref[...].T, w_ref[...]) + b_ref[...])
    h_ref[...] = h
    xhat, _ = norm_parts(h)
    c = (xhat * gain_ref[...] + shift_ref[...]).astype(BF)
    c_ref[...] = c
    ct_ref[...] = c.T


def out_project(o, x, w, b, gain, shift):
    slots, width = x.shape
    blk = 256
    row = pl.BlockSpec((1, width), lambda i: (0, 0))
    rows = pl.BlockSpec((blk, width), lambda i: (i, 0))
    cols = pl.BlockSpec((width, blk), lambda i: (0, i))
    return pl.pallas_call(
        out_kernel,
        grid=(slots // blk,),
        in_specs=[cols, rows, pl.BlockSpec((width, width), lambda i: (0, 0)), row, row, row],
        out_specs=[rows, rows, cols],
        out_shape=[
            jax.ShapeDtypeStruct((slots, width), F32),
            jax.ShapeDtypeStruct((slots, width), BF),
            jax.ShapeDtypeStruct((width, slots), BF),
        ],
        compiler_params=params(),
        name="out_project",
    )(o, x, w, b, gain, shift)


def mlp_kernel(c_ref, ct_ref, dy_ref, h_ref, w1_ref, b1_ref, w2_ref, b2_ref, y_ref, dc_ref, g1_ref, g2_ref, gb1_ref, y_acc, hb_scr, dp_scr):
    slots = c_ref.shape[0]
    tile = 256

    @pl.when(pl.program_id(0) == 0)
    def _():
        y_acc[...] = h_ref[...] + b2_ref[...]
        dc_ref[...] = jnp.zeros_like(dc_ref)

    gb1_ref[...] = jnp.zeros_like(gb1_ref)

    def step(i, _):
        rows = pl.ds(pl.multiple_of(i * tile, tile), tile)
        pre = nn(c_ref[rows, :], w1_ref[...]) + b1_ref[...]
        square = pre * pre
        th = jnp.tanh(GELU_C * (pre + GELU_A * (pre * square)))
        cdf = 0.5 * (1.0 + th)
        hb = (pre * cdf).astype(BF)
        slope = cdf + 0.5 * pre * (1.0 - th * th) * (GELU_C * (1.0 + (3.0 * GELU_A) * square))
        hb_scr[rows, :] = hb
        y_acc[rows, :] += nn(hb, w2_ref[...])
        dpre = (nt(dy_ref[rows, :], w2_ref[...]) * slope).astype(BF)
        dp_scr[rows, :] = dpre
        dc_ref[rows, :] += nt(dpre, w1_ref[...])
        gb1_ref[...] += jnp.sum(dpre.astype(F32), axis=0, keepdims=True)
        return 0

    lax.fori_loop(0, slots // tile, step, 0)
    g1_ref[...] = nn(ct_ref[...], dp_scr[...]).astype(g1_ref.dtype)
    g2_ref[...] = tn(hb_scr[...], dy_ref[...]).astype(g2_ref.dtype)

    @pl.when(pl.program_id(0) == pl.num_programs(0) - 1)
    def _():
        y_ref[...] = y_acc[...].astype(BF)


def mlp(c, ct, dy, h, w1, b1, w2, b2):
    slots, width = c.shape
    hidden = w1.shape[1]
    blk = 512
    whole = lambda r, k: pl.BlockSpec((r, k), lambda j: (0, 0))
    return pl.pallas_call(
        mlp_kernel,
        grid=(hidden // blk,),
        in_specs=[
            whole(slots, width),
            whole(width, slots),
            whole(slots, width),
            whole(slots, width),
            pl.BlockSpec((width, blk), lambda j: (0, j)),
            pl.BlockSpec((1, blk), lambda j: (0, j)),
            pl.BlockSpec((blk, width), lambda j: (j, 0)),
            whole(1, width),
        ],
        out_specs=[
            whole(slots, width),
            whole(slots, width),
            pl.BlockSpec((width, blk), lambda j: (0, j)),
            pl.BlockSpec((blk, width), lambda j: (j, 0)),
            pl.BlockSpec((1, blk), lambda j: (0, j)),
        ],
        out_shape=[
            jax.ShapeDtypeStruct((slots, width), BF),
            jax.ShapeDtypeStruct((slots, width), F32),
            jax.ShapeDtypeStruct((width, hidden), BF),
            jax.ShapeDtypeStruct((hidden, width), BF),
            jax.ShapeDtypeStruct((1, hidden), F32),
        ],
        scratch_shapes=[
            pltpu.VMEM((slots, width), F32),
            pltpu.VMEM((slots, blk), BF),
            pltpu.VMEM((slots, blk), BF),
        ],
        compiler_params=params(),
        name="mlp",
    )(c, ct, dy, h, w1, b1, w2, b2)


def norm_back(grad, v, gain):
    xhat, inv = norm_parts(v)
    g = grad * gain
    lead = jnp.mean(g, axis=-1, keepdims=True)
    slope = jnp.mean(g * xhat, axis=-1, keepdims=True)
    return (g - lead - xhat * slope) * inv, jnp.sum(grad * xhat, axis=0, keepdims=True), jnp.sum(grad, axis=0, keepdims=True)


def out_back_kernel(dc_ref, h_ref, dy_ref, o_ref, w_ref, gain_ref, dh_ref, do_ref, gw_ref, sums_ref, acc_ref):
    i = pl.program_id(0)

    @pl.when(i == 0)
    def _():
        acc_ref[...] = jnp.zeros_like(acc_ref)
        sums_ref[...] = jnp.zeros_like(sums_ref)

    dy = dy_ref[...].astype(F32)
    part, dgain, dshift = norm_back(dc_ref[...], h_ref[...], gain_ref[...])
    dh = dy + part
    dh_ref[...] = dh
    dhb = dh.astype(BF)
    do_ref[...] = nt(w_ref[...], dhb).astype(BF)
    acc_ref[...] += nn(o_ref[...], dhb)
    sums_ref[0:1, :] += dgain
    sums_ref[1:2, :] += dshift
    sums_ref[2:3, :] += jnp.sum(dh, axis=0, keepdims=True)
    sums_ref[3:4, :] += jnp.sum(dy, axis=0, keepdims=True)

    @pl.when(i == pl.num_programs(0) - 1)
    def _():
        gw_ref[...] = acc_ref[...].astype(gw_ref.dtype)


def out_back(dc, h, dy, o, w, gain):
    slots, width = h.shape
    blk = 256
    rows = pl.BlockSpec((blk, width), lambda i: (i, 0))
    cols = pl.BlockSpec((width, blk), lambda i: (0, i))
    whole = lambda r, k: pl.BlockSpec((r, k), lambda i: (0, 0))
    return pl.pallas_call(
        out_back_kernel,
        grid=(slots // blk,),
        in_specs=[rows, rows, rows, cols, whole(width, width), whole(1, width)],
        out_specs=[rows, cols, whole(width, width), whole(8, width)],
        out_shape=[
            jax.ShapeDtypeStruct((slots, width), F32),
            jax.ShapeDtypeStruct((width, slots), BF),
            jax.ShapeDtypeStruct((width, width), BF),
            jax.ShapeDtypeStruct((8, width), F32),
        ],
        scratch_shapes=[pltpu.VMEM((width, width), F32)],
        compiler_params=params(),
        name="out_back",
    )(dc, h, dy, o, w, gain)


def qkv_back_kernel(at_ref, dqkv_ref, w_ref, x_ref, dh_ref, gain_ref, gw_ref, dx_ref, sums_ref, acc_ref):
    j = pl.program_id(0)

    @pl.when(j == 0)
    def _():
        acc_ref[...] = jnp.zeros_like(acc_ref)

    d = dqkv_ref[...]
    gw_ref[...] = nt(at_ref[...], d).astype(gw_ref.dtype)
    acc_ref[...] += nn(w_ref[...], d)

    @pl.when(j == pl.num_programs(0) - 1)
    def _():
        sums_ref[...] = jnp.zeros_like(sums_ref)
        tile = 256
        for i in range(x_ref.shape[0] // tile):
            rows = slice(i * tile, (i + 1) * tile)
            da = acc_ref[:, rows].T
            part, dgain, dshift = norm_back(da, x_ref[rows, :].astype(F32), gain_ref[...])
            dx_ref[rows, :] = (dh_ref[rows, :] + part).astype(BF)
            sums_ref[0:1, :] += dgain
            sums_ref[1:2, :] += dshift


def qkv_back(at, dqkv, w, x, dh, gain):
    slots, width = x.shape
    outs = w.shape[1]
    blk = 768
    whole = lambda r, k: pl.BlockSpec((r, k), lambda j: (0, 0))
    return pl.pallas_call(
        qkv_back_kernel,
        grid=(outs // blk,),
        in_specs=[
            whole(width, slots),
            pl.BlockSpec((blk, slots), lambda j: (j, 0)),
            pl.BlockSpec((width, blk), lambda j: (0, j)),
            whole(slots, width),
            whole(slots, width),
            whole(1, width),
        ],
        out_specs=[pl.BlockSpec((width, blk), lambda j: (0, j)), whole(slots, width), whole(8, width)],
        out_shape=[
            jax.ShapeDtypeStruct((width, outs), BF),
            jax.ShapeDtypeStruct((slots, width), BF),
            jax.ShapeDtypeStruct((8, width), F32),
        ],
        scratch_shapes=[pltpu.VMEM((width, slots), F32)],
        compiler_params=params(),
        name="qkv_back",
    )(at, dqkv, w, x, dh, gain)


def body_any(
    tokens, cotangent, image_counts, patch_rows, patch_cols, ln1_gain, ln1_bias, qkv_weight, qkv_bias, rope_freqs,
    out_weight, out_bias, ln2_gain, ln2_bias, fc1_weight, fc1_bias, fc2_weight, fc2_bias,
):
    x = tokens[0]
    dy = cotangent[0]
    counts = image_counts[0]
    width = x.shape[1]
    small = (ln1_gain, ln1_bias, qkv_bias, rope_freqs, out_bias, ln2_gain, ln2_bias, fc1_bias, fc2_bias)
    sizes = [s.shape[0] for s in small]
    gather = partial(lax.all_gather, axis_name="fsdp", axis=0, tiled=True)
    packed = lax.all_gather(jnp.concatenate(small), "fsdp", axis=0)
    vectors = []
    at = 0
    for size in sizes:
        vectors.append(packed[:, at : at + size].reshape(-1).astype(F32))
        at += size
    gain1, shift1, b_qkv, freqs, b_out, gain2, shift2, b1, b2 = vectors
    w_qkv = gather(qkv_weight)
    w_out = gather(out_weight)
    w1 = gather(fc1_weight)
    w2 = gather(fc2_weight)

    row = lambda v: v[None, :]
    a, a_t = norm1(x, row(gain1), row(shift1))
    places = jnp.concatenate([patch_cols, patch_rows], axis=0).astype(F32)
    half = freqs.shape[0] // 2
    angle = freqs[:half, None] * places[0:1] + freqs[half:, None] * places[1:2]
    cos = jnp.cos(angle)
    sin = jnp.sin(angle)
    q, k, v = project(a, w_qkv, b_qkv[:, None], cos, sin)
    o, lse = attend(counts, q, k, v)
    h, c, c_t = out_project(o, x, w_out, row(b_out), row(gain2), row(shift2))
    y, dc, g_w1, g_w2, g_b1 = mlp(c, c_t, dy, h, w1, row(b1), w2, row(b2))
    dh, do, g_wout, sums2 = out_back(dc, h, dy, o, w_out, row(gain2))
    dq, dk, dv, s_bq, s_bk, s_bv, s_fc, s_fr = attend_back(counts, q, k, v, o, do, lse, cos, sin, places)
    dqkv = jnp.concatenate([dq, dk, dv], axis=0)
    g_wqkv, dx, sums1 = qkv_back(a_t, dqkv, w_qkv, x, dh, row(gain1))

    scatter = partial(lax.psum_scatter, axis_name="fsdp", scatter_dimension=0, tiled=True)
    both = lambda g: lax.psum(scatter(g), "rep").astype(F32)
    g_bqkv = jnp.sum(jnp.concatenate([s_bq, s_bk, s_bv], axis=0), axis=1)
    g_freq = jnp.sum(jnp.concatenate([s_fc, s_fr], axis=0), axis=1)
    small_grads = (sums1[0], sums1[1], g_bqkv, g_freq, sums2[2], sums2[0], sums2[1], g_b1[0], sums2[3])
    shards = mesh_size = packed.shape[0]
    block = jnp.concatenate([g.reshape(shards, -1) for g in small_grads], axis=1)
    total = lax.psum(block, ("rep", "fsdp"))
    mine = lax.dynamic_index_in_dim(total, lax.axis_index("fsdp"), 0, keepdims=False)
    outs = []
    at = 0
    for size in sizes:
        outs.append(mine[at : at + size])
        at += size
    s_gain1, s_shift1, s_bqkv, s_freq, s_bout, s_gain2, s_shift2, s_b1, s_b2 = outs
    return (
        y[None], dx[None], s_gain1, s_shift1, both(g_wqkv), s_bqkv, s_freq, both(g_wout), s_bout,
        s_gain2, s_shift2, both(g_w1), s_b1, both(g_w2), s_b2,
    )


SHARDS = 16
GROUPS = 2
LEAVING = (0, 8, 4, 12, 2, 10, 6, 14)


def swap(v, mask):
    return lax.ppermute(v, "fsdp", [(i, i ^ mask) for i in range(SHARDS)])


def tie(v, *after):
    return lax.optimization_barrier((v,) + after)[0]


class Gather:
    def __init__(self, mine):
        self.piece = {0: mine}

    def send(self, source, mask, after):
        v = self.piece[source]
        self.piece[source ^ mask] = swap(tie(v, *after) if after else v, mask)

    def hold(self, sources, after):
        for p in sources:
            self.piece[p] = tie(self.piece[p], after)

    def stage1(self, *after):
        for mask in (8, 4, 2):
            self.send(0, mask, after)

    def stage2(self, *after):
        self.send(8, 4, after)
        self.send(4, 2, after)
        self.send(8, 2, after)

    def stage3(self, *after):
        self.send(12, 2, after)

    def cores(self, *after):
        for p in (0, 8, 4, 2, 6, 10, 12, 14):
            self.send(p, 1, after)
        return [self.piece[p] for p in range(SHARDS)]


class Scatter:
    def __init__(self, near, far):
        self.got = [near, swap(far, 1)]
        self.size = 4

    def total(self, lo, hi):
        out = self.got[0][lo:hi].astype(F32)
        for g in self.got[1:]:
            out = out + g[lo:hi].astype(F32)
        return out.astype(BF)

    def hold(self, after):
        self.got[-1] = tie(self.got[-1], after)

    def step(self):
        lo = self.size
        sent = self.total(lo, 2 * lo)
        self.got.append(swap(sent, {4: 2, 2: 4, 1: 8}[lo]))
        self.size = lo // 2
        return sent

    def finish(self):
        mine = self.total(0, 1)[0]
        return mine, across(mine)


class SplitScatter(Scatter):
    def __init__(self, near, far):
        self.start = [near, swap(far, 1)]
        self.size = 4

    def split(self):
        sent = (self.start[0][1].astype(F32) + self.start[1][1].astype(F32)).astype(BF)
        got = across(sent)
        self.got = [self.start[0][0], self.start[1][0], got]
        return sent


def across(v):
    return lax.ppermute(v, "rep", [(0, 1), (1, 0)])


def start_all(copies):
    for copy in copies:
        copy.start()


def wait_all(copies):
    for copy in copies:
        copy.wait()


def fetch(refs, order_ref, moves, sem):
    copies = []
    for p, ref in enumerate(refs):
        for rows, place in moves:
            copies.append(pltpu.make_async_copy(ref.at[rows], place(order_ref[p]), sem.at[len(copies)]))
    return copies


ANY = pl.BlockSpec(memory_space=pl.ANY)
SMEM = pl.BlockSpec(memory_space=pltpu.SMEM)
VMEM = pl.BlockSpec(memory_space=pltpu.VMEM)


LINES = 16


def group_piece_kernel(w_ref, o_ref, v_ref, a_ref, b_ref):
    rows, cols = w_ref.shape[0], a_ref.shape[1]
    for i in range(3):
        for g, out in enumerate((a_ref, b_ref)):
            out[i * rows : (i + 1) * rows, :] = w_ref[:, (i * GROUPS + g) * cols : (i * GROUPS + g + 1) * cols]
    for i in range(2):
        b_ref[(3 + i) * rows : (4 + i) * rows, :] = o_ref[:, i * cols : (i + 1) * cols]
    a_ref[3 * rows :, :] = jnp.concatenate([v_ref[...], jnp.zeros((LINES - v_ref.shape[0], cols), BF)], axis=0)


def group_pieces(w, w_out, vectors):
    rows, cols = w.shape[0], w_out.shape[1] // 2
    return pl.pallas_call(
        group_piece_kernel,
        in_specs=[VMEM] * 3,
        out_specs=[VMEM, VMEM],
        out_shape=[jax.ShapeDtypeStruct((3 * rows + LINES, cols), BF), jax.ShapeDtypeStruct((5 * rows, cols), BF)],
        compiler_params=params(),
        cost_estimate=cost(2),
        name="group_pieces",
    )(w, w_out, vectors)


def mlp_piece_kernel(w1_ref, w2_ref, *outs):
    rows1 = w1_ref.shape[0]
    own = w2_ref.shape[0] // 2
    per = SHARDS // 2
    w1 = w1_ref[...].astype(F32)
    for i, out in enumerate(outs):
        for b in range(2):
            runs = [w1[:, (2 * (b * per + j) + i) * own :][:, :own] for j in range(per)]
            out[b * rows1 : (b + 1) * rows1, :] = jnp.concatenate(runs, axis=1).astype(BF)
        out[2 * rows1 :, :] = w2_ref[i * own : (i + 1) * own, :]


def mlp_pieces(w1, w2):
    rows = 2 * w1.shape[0] + w2.shape[0] // 2
    return pl.pallas_call(
        mlp_piece_kernel,
        in_specs=[VMEM, VMEM],
        out_specs=[VMEM, VMEM],
        out_shape=[jax.ShapeDtypeStruct((rows, w2.shape[1]), BF)] * 2,
        compiler_params=params(),
        cost_estimate=cost(2),
        name="mlp_pieces",
    )(w1, w2)


def mlp_join_kernel(order_ref, c_ref, c_other_ref, d_ref, d_other_ref, w1_ref, w2_ref):
    rows1 = w1_ref.shape[0]
    own = w2_ref.shape[0] // 2
    per = SHARDS // 2
    c = c_ref[...].astype(F32) + c_other_ref[...].astype(F32)
    mine = d_ref[...].astype(F32)
    other = d_other_ref[...].astype(F32)
    here = order_ref[SHARDS] == 0
    d = jnp.where(here, mine, other)
    runs = []
    for b in range(2):
        for j in range(per):
            runs += [m[b * rows1 : (b + 1) * rows1, j * own : (j + 1) * own] for m in (c, d)]
    w1_ref[...] = jnp.concatenate(runs, axis=1)
    w2_ref[:own, :] = c[2 * rows1 :]
    w2_ref[own:, :] = jnp.where(here, other, mine)


def mlp_join(rows1, order, parts):
    own = parts[0].shape[0] - 2 * rows1
    return pl.pallas_call(
        mlp_join_kernel,
        in_specs=[SMEM] + [VMEM] * 4,
        out_specs=[VMEM] * 2,
        out_shape=[
            jax.ShapeDtypeStruct((rows1, 2 * own * SHARDS), F32),
            jax.ShapeDtypeStruct((2 * own, parts[0].shape[1]), F32),
        ],
        compiler_params=params(),
        cost_estimate=cost(3),
        name="mlp_join",
    )(order, *parts)


def spread(packed, lo, size):
    return jnp.concatenate([packed[j : j + 1, lo : lo + size] for j in range(packed.shape[0])], axis=1)


def column(v):
    return jnp.broadcast_to(v, (8, v.shape[1])).T[:, 0:1]


def prepare_kernel(sizes, order_ref, x_ref, cols_ref, rows_ref, *rest):
    pieces = rest[:SHARDS]
    at_ref, cos_ref, sin_ref, vec_ref, b1_ref, bias_ref, sel_ref, line_scr, table_scr, sem = rest[SHARDS:]
    half = cos_ref.shape[0]

    @pl.when(pl.program_id(0) == 0)
    def _():
        last = pieces[0].shape[0]
        copies = fetch(pieces, order_ref, [(slice(last - LINES, last), lambda d: line_scr.at[d])], sem)
        start_all(copies)
        wait_all(copies)
        packed = jnp.concatenate([line_scr[:, i, :] for i in range(2)], axis=1).astype(F32)
        starts = [sum(sizes[:i]) for i in range(len(sizes))]
        gain1, shift1, b_qkv, freqs, b_out, gain2, shift2 = (spread(packed, starts[i], sizes[i]) for i in range(7))
        b2 = spread(packed, starts[8], sizes[8])
        for i, v in enumerate((b_out, gain1, gain2, shift2, b2, shift1)):
            vec_ref[i : i + 1, :] = v
        own = sizes[7] // 2
        for i in range(2):
            b1_ref[i : i + 1, :] = spread(packed, starts[7] + i * own, own)
        bias_ref[...] = column(b_qkv)
        freq = column(freqs)
        spots = lax.broadcasted_iota(jnp.int32, (1, 128), 1).astype(F32)
        for i in range(2):
            angle = freq[i * half : (i + 1) * half] * spots
            for k, table in enumerate((jnp.cos(angle), jnp.sin(angle))):
                for n in range(3):
                    term = table.astype(BF)
                    table_scr[i, k, n] = term
                    table = table - term.astype(F32)

    xhat, _ = norm_parts(x_ref[...].astype(F32))
    at_ref[...] = (xhat * vec_ref[1:2, :] + vec_ref[5:6, :]).astype(BF).T
    found = []
    for i, at in enumerate((cols_ref[...], rows_ref[...])):
        one_hot = jnp.where(lax.broadcasted_iota(jnp.int32, (128, at.shape[1]), 0) == at, 1.0, 0.0).astype(BF)
        found.append([sum(nn(table_scr[i, k, n], one_hot) for n in range(3)) for k in range(2)])
    (cos_c, sin_c), (cos_r, sin_r) = found
    cos_ref[...] = cos_c * cos_r - sin_c * sin_r
    sin_ref[...] = sin_c * cos_r + cos_c * sin_r
    line = lax.broadcasted_iota(jnp.int32, sel_ref.shape, 0)
    sel = jnp.where(line == 0, cols_ref[...].astype(F32), rows_ref[...].astype(F32))
    sel_ref[...] = jnp.where(line < 2, sel, jnp.where(line == 2, 1.0, 0.0)).astype(BF)


def prepare(sizes, order, x, patch_cols, patch_rows, pieces):
    slots, width = x.shape
    own = sizes[7] // 2
    blk = 256
    shape = jax.ShapeDtypeStruct
    tall = lambda n: pl.BlockSpec((n, blk), lambda i: (0, i))
    whole = lambda r, k: pl.BlockSpec((r, k), lambda i: (0, 0))
    return pl.pallas_call(
        partial(prepare_kernel, sizes),
        grid=(slots // blk,),
        in_specs=[SMEM, pl.BlockSpec((blk, width), lambda i: (i, 0)), tall(1), tall(1)] + [ANY] * SHARDS,
        out_specs=[
            tall(width), tall(width // 2), tall(width // 2),
            whole(8, width), whole(2, own * SHARDS), whole(3 * width, 1), tall(16),
        ],
        out_shape=[
            shape((width, slots), BF),
            shape((width // 2, slots), F32),
            shape((width // 2, slots), F32),
            shape((8, width), F32),
            shape((2, own * SHARDS), F32),
            shape((3 * width, 1), F32),
            shape((16, slots), BF),
        ],
        scratch_shapes=[
            pltpu.VMEM((SHARDS, LINES, width // GROUPS), BF),
            pltpu.VMEM((2, 2, 3, width // 2, 128), BF),
            pltpu.SemaphoreType.DMA((SHARDS,)),
        ],
        compiler_params=params(),
        cost_estimate=cost(8),
        name="prepare",
    )(order, x, patch_cols, patch_rows, *pieces)


def pack_kernel(sums1_ref, sums2_ref, b1a_ref, b1b_ref, *rest):
    heads, out_ref = rest[:-1], rest[-1]
    bias = [r[2:3, :] for r in heads[:GROUPS]]
    freq = [r[...] for r in heads[GROUPS:]]
    cols = bias[0].shape[1] // 3
    b_qkv = jnp.concatenate([b[:, i * cols : (i + 1) * cols] for i in range(3) for b in bias], axis=1)
    g_freq = jnp.concatenate([f[i : i + 1] for i in range(2) for f in freq], axis=1)
    vectors = (
        sums1_ref[0:1, :], sums1_ref[1:2, :], b_qkv, g_freq, sums2_ref[2:3, :], sums2_ref[0:1, :], sums2_ref[1:2, :],
        b1a_ref[...], b1b_ref[...], sums2_ref[3:4, :],
    )
    lines = []
    for j in range(SHARDS):
        runs = []
        for v in vectors:
            n = v.shape[1] // SHARDS
            runs.append(v[:, j * n : (j + 1) * n])
        lines.append(jnp.concatenate(runs, axis=1))
    out_ref[...] = jnp.concatenate(lines, axis=0)


def pack(size, *sums):
    return pl.pallas_call(
        pack_kernel,
        in_specs=[VMEM] * len(sums),
        out_specs=VMEM,
        out_shape=jax.ShapeDtypeStruct((SHARDS, size), F32),
        compiler_params=params(),
        cost_estimate=cost(3),
        name="pack",
    )(*sums)


def group_kernel(order_ref, at_ref, bq_ref, bk_ref, bv_ref, cos_ref, sin_ref, *rest):
    pieces, (q_ref, k_ref, v_ref, w_scr, wt_scr, sem) = rest[:SHARDS], rest[SHARDS:]
    cols = q_ref.shape[0]
    part = w_scr.shape[1] // 3

    @pl.when(pl.program_id(0) == 0)
    def _():
        copies = fetch(pieces, order_ref, [(slice(0, 3 * part), lambda d: w_scr.at[d])], sem)
        start_all(copies)
        wait_all(copies)
        for i in range(3):
            wt_scr[i] = w_scr[:, i * part : (i + 1) * part, :].reshape(SHARDS * part, cols).T

    a_t = at_ref[...]
    cos = cos_ref[...]
    sin = sin_ref[...]
    for i, b_ref, out_ref, scale in ((0, bq_ref, q_ref, HEAD_DIM**-0.5), (1, bk_ref, k_ref, 1.0)):
        u = nn(wt_scr[i], a_t) + b_ref[...]
        for h in range(cols // HEAD_DIM):
            u1 = u[h * HEAD_DIM : h * HEAD_DIM + HALF]
            u2 = u[h * HEAD_DIM + HALF : (h + 1) * HEAD_DIM]
            c = cos[h * HALF : (h + 1) * HALF]
            s = sin[h * HALF : (h + 1) * HALF]
            out_ref[h * HEAD_DIM : h * HEAD_DIM + HALF, :] = ((u1 * c - u2 * s) * scale).astype(BF)
            out_ref[h * HEAD_DIM + HALF : (h + 1) * HEAD_DIM, :] = ((u1 * s + u2 * c) * scale).astype(BF)
    v_ref[...] = (nn(wt_scr[2], a_t) + bv_ref[...]).astype(BF)


def project_group(group, order, a_t, bias, cos, sin, pieces):
    width, slots = a_t.shape
    cols = pieces[0].shape[1]
    blk = 512
    tall = lambda n, at: pl.BlockSpec((n, blk), lambda i: (at, i))
    return pl.pallas_call(
        group_kernel,
        grid=(slots // blk,),
        in_specs=[SMEM, tall(width, 0)]
        + [pl.BlockSpec((cols, 1), lambda i, n=n: (n * GROUPS + group, 0)) for n in range(3)]
        + [tall(cols // 2, group)] * 2
        + [ANY] * SHARDS,
        out_specs=[tall(cols, 0)] * 3,
        out_shape=[jax.ShapeDtypeStruct((cols, slots), BF)] * 3,
        scratch_shapes=[
            pltpu.VMEM((SHARDS, 3 * width // SHARDS, cols), BF),
            pltpu.VMEM((3, cols, width), BF),
            pltpu.SemaphoreType.DMA((SHARDS,)),
        ],
        compiler_params=params(),
        cost_estimate=cost(7),
        name="qkv_group",
    )(order, a_t, bias, bias, bias, cos, sin, *pieces)


def out_moves(w_scr, start):
    rows = w_scr.shape[1]
    half = w_scr.shape[2] // 2
    return [
        (slice(start + i * rows, start + (i + 1) * rows), lambda d, i=i: w_scr.at[d, :, pl.ds(i * half, half)])
        for i in range(2)
    ]


def out_group_kernel(start, order_ref, vec_ref, *rest):
    o_refs, x_ref, pieces = rest[:GROUPS], rest[GROUPS], rest[GROUPS + 1 : GROUPS + 1 + SHARDS]
    h_ref, c_ref, ct_ref, w_scr, sem = rest[GROUPS + 1 + SHARDS :]

    @pl.when(pl.program_id(0) == 0)
    def _():
        copies = fetch(pieces, order_ref, out_moves(w_scr, start), sem)
        start_all(copies)
        wait_all(copies)

    width = x_ref.shape[1]
    o = jnp.concatenate([r[...].T for r in o_refs], axis=1)
    h = x_ref[...].astype(F32) + (nn(o, w_scr[...].reshape(width, width)) + vec_ref[0:1, :])
    h_ref[...] = h
    xhat, _ = norm_parts(h)
    c = (xhat * vec_ref[2:3, :] + vec_ref[3:4, :]).astype(BF)
    c_ref[...] = c
    ct_ref[...] = c.T


def out_project_fast(order, o, x, vec, pieces, start):
    slots, width = x.shape
    blk = 256
    rows = pl.BlockSpec((blk, width), lambda i: (i, 0))
    cols = pl.BlockSpec((width, blk), lambda i: (0, i))
    return pl.pallas_call(
        partial(out_group_kernel, start),
        grid=(slots // blk,),
        in_specs=[SMEM, VMEM] + [pl.BlockSpec((width // GROUPS, blk), lambda i: (0, i))] * GROUPS + [rows] + [ANY] * SHARDS,
        out_specs=[rows, rows, cols],
        out_shape=[
            jax.ShapeDtypeStruct((slots, width), F32),
            jax.ShapeDtypeStruct((slots, width), BF),
            jax.ShapeDtypeStruct((width, slots), BF),
        ],
        scratch_shapes=[pltpu.VMEM((SHARDS, width // SHARDS, width), BF), pltpu.SemaphoreType.DMA((2 * SHARDS,))],
        compiler_params=params(),
        cost_estimate=cost(8),
        name="out_project",
    )(order, vec, *o, x, *pieces)


def mlp_half_kernel(part, first, split, n_in, order_ref, c_ref, ct_ref, dy_ref, b1_ref, vec_ref, *rest):
    acc_in, rest = (rest[:1], rest[1:]) if first else (rest[:2], rest[2:])
    pieces, rest = rest[:n_in], rest[n_in:]
    n_g = 2 if split else 1
    y_ref, dc_ref = rest[:2]
    g_refs = rest[2 : 2 + n_g]
    gb1_ref, w1_scr, w2_scr, g1_scr, g2_scr, hb_scr, dp_scr, y_acc, dc_acc, sem, load_sem = rest[2 + n_g : 13 + n_g]
    y_out = y_acc if first else rest[13 + n_g]
    slots, width = c_ref.shape
    rows1 = w1_scr.shape[2]
    rows2 = w2_scr.shape[1]
    blk = w1_scr.shape[3]
    steps = w1_scr.shape[0]
    per = blk // rows2
    tile = 512
    refs = [pieces[0].at[p] for p in range(SHARDS)] if n_in == 1 else pieces
    places = range(SHARDS) if n_in == 1 else order_ref
    loads = [
        fetch(refs, places, [(slice(j * rows1, (j + 1) * rows1), lambda d, j=j: w1_scr.at[j, d])], sem.at[j])
        for j in range(steps)
    ]
    loads.insert(1, fetch(refs, places, [(slice(steps * rows1, steps * rows1 + rows2), lambda d: w2_scr.at[d])], sem.at[steps]))
    sums = [pltpu.make_async_copy(src, dst, load_sem.at[i]) for i, (src, dst) in enumerate(zip(acc_in, (y_acc, dc_acc)))]
    for copies in loads[:2] + [sums] + loads[2:]:
        start_all(copies)
    sends = []
    for j in range(steps):
        cols = slice(j * blk, (j + 1) * blk)
        wait_all(loads[0] if j == 0 else loads[1 + j])
        w1 = w1_scr[j].reshape(width, blk)
        if j == 0:
            wait_all(loads[1] + sums)
        w2 = w2_scr[j * per : (j + 1) * per].reshape(blk, width)
        total = None
        for i in range(slots // tile):
            rows = slice(i * tile, (i + 1) * tile)
            pre = nn(c_ref[rows, :], w1) + b1_ref[part : part + 1, cols]
            square = pre * pre
            th = jnp.tanh(GELU_C * (pre + GELU_A * (pre * square)))
            cdf = 0.5 * (1.0 + th)
            hb = (pre * cdf).astype(BF)
            slope = cdf + 0.5 * pre * (1.0 - th * th) * (GELU_C * (1.0 + (3.0 * GELU_A) * square))
            hb_scr[rows, :] = hb
            y = y_acc[rows, :] + nn(hb, w2)
            if first and j == 0:
                y = y + vec_ref[4:5, :]
            dpre = (nt(dy_ref[rows, :], w2) * slope).astype(BF)
            dp_scr[rows, :] = dpre
            term = jnp.sum(dpre.astype(F32), axis=0, keepdims=True)
            total = term if total is None else total + term
            dc = nt(dpre, w1)
            if not (first and j == 0):
                dc = dc + dc_acc[rows, :]
            dc_acc[rows, :] = dc
            if j == steps - 1:
                y_out[rows, :] = y.astype(y_out.dtype)
                sends += [
                    pltpu.make_async_copy(y_out.at[rows], y_ref.at[rows], load_sem.at[2 + 2 * i]),
                    pltpu.make_async_copy(dc_acc.at[rows], dc_ref.at[rows], load_sem.at[3 + 2 * i]),
                ]
                start_all(sends[-2:])
            else:
                y_acc[rows, :] = y
        gb1_ref[:, cols] = total
        g1_scr[j] = nn(ct_ref[...], dp_scr[...]).astype(BF).reshape(SHARDS, rows1, blk)
        if split:
            mine = order_ref[SHARDS]
            dests = [(g_refs[b], i, order_ref[p + b]) for b in range(2) for i, p in enumerate(LEAVING)]
            place = lambda dst, i, lo, n: dst.at[lax.rem(lo // (steps * rows1) + mine, 2), i, pl.ds(lo % (steps * rows1), n)]
        else:
            dests = [(g_refs[0], p, p) for p in range(SHARDS)]
            place = lambda dst, i, lo, n: dst.at[i, pl.ds(lo, n)]
        copies = [
            pltpu.make_async_copy(g1_scr.at[j, d], place(dst, i, j * rows1, rows1), sem.at[j, n])
            for n, (dst, i, d) in enumerate(dests)
        ]
        start_all(copies)
        sends += copies
        g2_scr[j * per : (j + 1) * per] = tn(hb_scr[...], dy_ref[...]).astype(BF).reshape(per, rows2, width)
    copies = [
        pltpu.make_async_copy(g2_scr.at[d], place(dst, i, steps * rows1, rows2), sem.at[steps, n])
        for n, (dst, i, d) in enumerate(dests)
    ]
    start_all(copies)
    wait_all(sends + copies)


def mlp_half(part, order, c, ct, dy, b1, vec, sums, pieces, split):
    slots, width = c.shape
    rows1 = width // SHARDS
    rows2 = pieces[0].shape[-2] - 2 * rows1
    hidden = rows2 * SHARDS
    steps = 2
    blk = hidden // steps
    first = len(sums) == 1
    block = jax.ShapeDtypeStruct((SHARDS, 2 * rows1 + rows2, width), BF)
    if split:
        block = jax.ShapeDtypeStruct((2, SHARDS // 2, rows2, width), BF)
    return pl.pallas_call(
        partial(mlp_half_kernel, part, first, split, len(pieces)),
        in_specs=[SMEM] + [VMEM] * 5 + [ANY] * (len(sums) + len(pieces)),
        out_specs=[ANY, ANY] + [ANY] * (2 if split else 1) + [VMEM],
        out_shape=[jax.ShapeDtypeStruct((slots, width), F32 if first else BF), jax.ShapeDtypeStruct((slots, width), F32)]
        + [block] * (2 if split else 1)
        + [jax.ShapeDtypeStruct((1, hidden), F32)],
        scratch_shapes=[
            pltpu.VMEM((steps, SHARDS, rows1, blk), BF),
            pltpu.VMEM((SHARDS, rows2, width), BF),
            pltpu.VMEM((steps, SHARDS, rows1, blk), BF),
            pltpu.VMEM((SHARDS, rows2, width), BF),
            pltpu.VMEM((slots, blk), BF),
            pltpu.VMEM((slots, blk), BF),
            pltpu.VMEM((slots, width), F32),
            pltpu.VMEM((slots, width), F32),
            pltpu.SemaphoreType.DMA((steps + 1, SHARDS)),
            pltpu.SemaphoreType.DMA((8,)),
        ]
        + ([] if first else [pltpu.VMEM((slots, width), BF)]),
        compiler_params=params(),
        cost_estimate=cost(23),
        name="mlp_half",
    )(order, c, ct, dy, b1, vec, *sums, *pieces)


def out_back_fast_kernel(start, order_ref, dc_ref, h_ref, dy_ref, vec_ref, *rest):
    o_refs, pieces = rest[:GROUPS], rest[GROUPS : GROUPS + SHARDS]
    dh_ref, do_ref, near_ref, far_ref, sums_ref, acc_ref, g_scr, w_scr, sem = rest[GROUPS + SHARDS :]
    i = pl.program_id(0)
    width = h_ref.shape[1]
    each = width // SHARDS
    half = width // 2

    @pl.when(i == 0)
    def _():
        copies = fetch(pieces, order_ref, out_moves(w_scr, start), sem)
        start_all(copies)
        acc_ref[...] = jnp.zeros_like(acc_ref)
        sums_ref[...] = jnp.zeros_like(sums_ref)
        wait_all(copies)

    dy = dy_ref[...].astype(F32)
    part, dgain, dshift = norm_back(dc_ref[...], h_ref[...], vec_ref[2:3, :])
    dh = dy + part
    dh_ref[...] = dh
    dhb = dh.astype(BF)
    do_ref[...] = nt(w_scr[...].reshape(width, width), dhb).astype(BF)
    rows = width // GROUPS
    for g in range(GROUPS):
        acc_ref[g * rows : (g + 1) * rows, :] += nn(o_refs[g][...], dhb)
    sums_ref[0:1, :] += dgain
    sums_ref[1:2, :] += dshift
    sums_ref[2:3, :] += jnp.sum(dh, axis=0, keepdims=True)
    sums_ref[3:4, :] += jnp.sum(dy, axis=0, keepdims=True)

    @pl.when(i == pl.num_programs(0) - 1)
    def _():
        g_scr[...] = acc_ref[...].astype(BF).reshape(g_scr.shape)
        copies = []
        for b, out in enumerate((near_ref, far_ref)):
            for n, p in enumerate(LEAVING):
                for k in range(2):
                    src = g_scr.at[order_ref[p + b], :, pl.ds(k * half, half)]
                    dst = out.at[n, pl.ds(k * each, each)]
                    copies.append(pltpu.make_async_copy(src, dst, sem.at[len(copies)]))
        start_all(copies)
        wait_all(copies)


def out_back_fast(order, dc, h, dy, vec, o, pieces, start):
    slots, width = h.shape
    blk = 256
    rows = pl.BlockSpec((blk, width), lambda i: (i, 0))
    cols = pl.BlockSpec((width, blk), lambda i: (0, i))
    whole = lambda r, k: pl.BlockSpec((r, k), lambda i: (0, 0))
    block = jax.ShapeDtypeStruct((SHARDS // 2, 2 * width // SHARDS, width // 2), BF)
    return pl.pallas_call(
        partial(out_back_fast_kernel, start),
        grid=(slots // blk,),
        in_specs=[SMEM, rows, rows, rows, VMEM]
        + [pl.BlockSpec((width // GROUPS, blk), lambda i: (0, i))] * GROUPS
        + [ANY] * SHARDS,
        out_specs=[rows, cols, ANY, ANY, whole(8, width)],
        out_shape=[
            jax.ShapeDtypeStruct((slots, width), F32),
            jax.ShapeDtypeStruct((width, slots), BF),
            block,
            block,
            jax.ShapeDtypeStruct((8, width), F32),
        ],
        scratch_shapes=[
            pltpu.VMEM((width, width), F32),
            pltpu.VMEM((SHARDS, width // SHARDS, width), BF),
            pltpu.VMEM((SHARDS, width // SHARDS, width), BF),
            pltpu.SemaphoreType.DMA((2 * SHARDS,)),
        ],
        compiler_params=params(),
        cost_estimate=cost(12),
        name="out_back",
    )(order, dc, h, dy, vec, *o, *pieces)


def heads_back_kernel(
    counts_ref, q_ref, k_ref, v_ref, o_ref, do_ref, lse_ref, cos_ref, sin_ref,
    dq_ref, dk_ref, dv_ref, dangle_ref, bias_ref,
):
    slots = q_ref.shape[1]

    @pl.when(pl.program_id(0) == 0)
    def _():
        bias_ref[...] = second_bias(counts_ref, slots)

    lane1 = lax.broadcasted_iota(jnp.int32, (1, WIDE), 1)
    lane2 = lax.broadcasted_iota(jnp.int32, (1, slots - CUT), 1)
    scale = HEAD_DIM**-0.5

    def part(scores, grads, queries, outs, keys, delta_row, first):
        prob = jnp.exp(scores)
        ds = (prob * (grads - delta_row)).astype(BF)
        pb = prob.astype(BF)
        gap = jnp.zeros((keys.shape[1] - pb.shape[0], pb.shape[1]), BF)
        pb = jnp.concatenate([pb, gap] if first else [gap, pb], axis=0)
        ds = jnp.concatenate([ds, gap] if first else [gap, ds], axis=0)
        return nn(keys, ds), nt(queries, ds), nt(outs, pb)

    for h in range(q_ref.shape[0] // HEAD_DIM):
        top = h * HEAD_DIM
        rows = slice(top, top + HEAD_DIM)
        kt = k_ref[rows, :]
        k = kt.T
        v = v_ref[rows, :].T
        q = q_ref[rows, :]
        do = do_ref[rows, :]
        lse = lse_ref[h]
        delta = jnp.sum(do.astype(F32) * o_ref[rows, :].astype(F32), axis=0, keepdims=True)
        lse1 = jnp.where(lane1 < FIRST, lse[:, :WIDE], -NEG)
        lse2 = jnp.where(lane2 >= FIRST - CUT, lse[:, CUT:], -NEG)
        grads1 = part(
            nn(k[:FIRST], q[:, :WIDE]) - lse1, nn(v[:FIRST], do[:, :WIDE]),
            q[:, :WIDE], do[:, :WIDE], kt[:, :WIDE], delta[:, :WIDE], True,
        )
        grads2 = part(
            nn(k[FIRST:], q[:, CUT:]) + bias_ref[...] - lse2, nn(v[FIRST:], do[:, CUT:]),
            q[:, CUT:], do[:, CUT:], kt[:, CUT:], delta[:, CUT:], False,
        )
        dq, dk, dv = (
            jnp.concatenate([one[:, :CUT], one[:, CUT:] + two[:, : WIDE - CUT], two[:, WIDE - CUT :]], axis=1)
            for one, two in zip(grads1, grads2)
        )
        cos = cos_ref[h * HALF : (h + 1) * HALF, :]
        sin = sin_ref[h * HALF : (h + 1) * HALF, :]
        dangle = None
        for r, rot, out in ((dq * scale, q.astype(F32) * (1.0 / scale), dq_ref), (dk, kt.astype(F32), dk_ref)):
            r1, r2 = r[:HALF], r[HALF:]
            term = r2 * rot[:HALF] - r1 * rot[HALF:]
            dangle = term if dangle is None else dangle + term
            out[top : top + HALF, :] = (r1 * cos + r2 * sin).astype(BF)
            out[top + HALF : top + HEAD_DIM, :] = (r2 * cos - r1 * sin).astype(BF)
        dv_ref[rows, :] = dv.astype(BF)
        dangle_ref[h * HALF : (h + 1) * HALF, :] = dangle.astype(BF)


def heads_back(group, counts, q, k, v, o, do, lse, cos, sin):
    width, slots = q.shape
    heads = width // HEAD_DIM
    each = 2
    steps = heads // each
    head = pl.BlockSpec((each * HEAD_DIM, slots), lambda h: (h, 0))
    half = pl.BlockSpec((each * HALF, slots), lambda h: (h, 0))
    turn = pl.BlockSpec((each * HALF, slots), lambda h: (group * steps + h, 0))
    late = pl.BlockSpec((each * HEAD_DIM, slots), lambda h: (group * steps + h, 0))
    return pl.pallas_call(
        heads_back_kernel,
        grid=(steps,),
        in_specs=[SMEM] + [head] * 4 + [late, pl.BlockSpec((each, 1, slots), lambda h: (h, 0, 0)), turn, turn],
        out_specs=[head] * 3 + [half],
        out_shape=[jax.ShapeDtypeStruct((width, slots), BF)] * 3 + [jax.ShapeDtypeStruct((width // 2, slots), BF)],
        scratch_shapes=[pltpu.VMEM((slots - FIRST, slots - CUT), F32)],
        compiler_params=params(),
        cost_estimate=cost(13),
        name="heads_back",
    )(counts, q, k, v, o, do, lse, cos, sin)


def qkv_grad_kernel(order_ref, at_ref, sel_ref, dangle_ref, dq_ref, dk_ref, dv_ref, *rest):
    more, (near_ref, far_ref, bias_ref, freq_ref, g_scr, sem, more_sem) = rest[:-7], rest[-7:]
    part = g_scr.shape[1] // 3
    outs = (near_ref, far_ref)
    extra = [
        pltpu.make_async_copy(ref.at[n], out.at[n, pl.ds(3 * part, ref.shape[1])], more_sem.at[b, n])
        for b, (ref, out) in enumerate(zip(more, outs))
        for n in range(SHARDS // 2)
    ]
    start_all(extra)
    at = at_ref[...]
    for i, ref in enumerate((dq_ref, dk_ref, dv_ref)):
        g = nt(at, ref[...]).astype(BF)
        g_scr[:, i * part : (i + 1) * part, :] = g.reshape(SHARDS, part, g.shape[1])
        bias_ref[:, i * g.shape[1] : (i + 1) * g.shape[1]] = nt(sel_ref[...], ref[...])
    freq_ref[...] = nt(sel_ref[...], dangle_ref[...])
    copies = []
    for b, out in enumerate(outs):
        for n, p in enumerate(LEAVING):
            dst = out.at[n, pl.ds(0, 3 * part)]
            copies.append(pltpu.make_async_copy(g_scr.at[order_ref[p + b]], dst, sem.at[len(copies)]))
    start_all(copies)
    wait_all(copies + extra)


def qkv_grad(order, at, sel, dangle, dq, dk, dv, *more):
    width, slots = at.shape
    cols = dq.shape[0]
    rows = 3 * width // SHARDS
    total = rows + (more[0].shape[1] if more else 0)
    return pl.pallas_call(
        qkv_grad_kernel,
        in_specs=[SMEM] + [VMEM] * (6 + len(more)),
        out_specs=[ANY, ANY, VMEM, VMEM],
        out_shape=[jax.ShapeDtypeStruct((SHARDS // 2, total, cols), BF)] * 2
        + [jax.ShapeDtypeStruct((sel.shape[0], 3 * cols), F32), jax.ShapeDtypeStruct((sel.shape[0], cols // 2), F32)],
        scratch_shapes=[
            pltpu.VMEM((SHARDS, rows, cols), BF),
            pltpu.SemaphoreType.DMA((SHARDS,)),
            pltpu.SemaphoreType.DMA((2, SHARDS // 2)),
        ],
        compiler_params=params(),
        cost_estimate=cost(6),
        name="qkv_grad",
    )(order, at, sel, dangle, dq, dk, dv, *more)


def part_kernel(order_ref, *rest):
    grads, pieces, (da_ref, w_scr, sem) = rest[:3], rest[3 : 3 + SHARDS], rest[3 + SHARDS :]
    add_group(order_ref, grads, pieces, da_ref, w_scr, sem)


def group_weights(order_ref, pieces, w_scr, sem):
    rows = w_scr.shape[1]
    copies = fetch(pieces, order_ref, [(slice(0, rows), lambda d: w_scr.at[d])], sem)
    start_all(copies)
    wait_all(copies)


def group_product(grads, w_scr):
    rows = w_scr.shape[1] // 3
    total = None
    for n in range(3):
        w = w_scr[:, n * rows : (n + 1) * rows, :].reshape(SHARDS * rows, w_scr.shape[2])
        term = nn(w, grads[n][...])
        total = term if total is None else total + term
    return total


def add_group(order_ref, grads, pieces, da_ref, w_scr, sem):
    @pl.when(pl.program_id(0) == 0)
    def _():
        group_weights(order_ref, pieces, w_scr, sem)

    da_ref[...] = group_product(grads, w_scr)


def input_part(order, grads, pieces, width):
    cols, slots = grads[0].shape
    blk = 512
    return pl.pallas_call(
        part_kernel,
        grid=(slots // blk,),
        in_specs=[SMEM] + [pl.BlockSpec((cols, blk), lambda i: (0, i))] * 3 + [ANY] * SHARDS,
        out_specs=pl.BlockSpec((width, blk), lambda i: (0, i)),
        out_shape=jax.ShapeDtypeStruct((width, slots), F32),
        scratch_shapes=[pltpu.VMEM((SHARDS, 3 * width // SHARDS, cols), BF), pltpu.SemaphoreType.DMA((SHARDS,))],
        compiler_params=params(),
        cost_estimate=cost(6),
        name="input_part",
    )(order, *grads, *pieces)


def input_kernel(order_ref, x_ref, dh_ref, vec_ref, da_ref, *rest):
    grads, pieces, (dx_ref, sums_ref, w_scr, sem) = rest[:3], rest[3 : 3 + SHARDS], rest[3 + SHARDS :]

    @pl.when(pl.program_id(0) == 0)
    def _():
        group_weights(order_ref, pieces, w_scr, sem)
        sums_ref[...] = jnp.zeros_like(sums_ref)

    da = da_ref[...] + group_product(grads, w_scr)
    out, dgain, dshift = norm_back(da.T, x_ref[...].astype(F32), vec_ref[1:2, :])
    dx_ref[...] = (dh_ref[...] + out).astype(BF)
    sums_ref[0:1, :] += dgain
    sums_ref[1:2, :] += dshift


def input_back(order, x, dh, vec, da, grads, pieces):
    slots, width = x.shape
    cols = grads[0].shape[0]
    blk = 512
    rows = pl.BlockSpec((blk, width), lambda i: (i, 0))
    return pl.pallas_call(
        input_kernel,
        grid=(slots // blk,),
        in_specs=[SMEM, rows, rows, VMEM, pl.BlockSpec((width, blk), lambda i: (0, i))]
        + [pl.BlockSpec((cols, blk), lambda i: (0, i))] * 3
        + [ANY] * SHARDS,
        out_specs=[rows, pl.BlockSpec((8, width), lambda i: (0, 0))],
        out_shape=[jax.ShapeDtypeStruct((slots, width), BF), jax.ShapeDtypeStruct((8, width), F32)],
        scratch_shapes=[pltpu.VMEM((SHARDS, 3 * width // SHARDS, cols), BF), pltpu.SemaphoreType.DMA((SHARDS,))],
        compiler_params=params(),
        cost_estimate=cost(10),
        name="input_back",
    )(order, x, dh, vec, da, *grads, *pieces)


def body_fast(
    tokens, cotangent, image_counts, patch_rows, patch_cols, ln1_gain, ln1_bias, qkv_weight, qkv_bias, rope_freqs,
    out_weight, out_bias, ln2_gain, ln2_bias, fc1_weight, fc1_bias, fc2_weight, fc2_bias,
):
    x = tokens[0]
    dy = cotangent[0]
    counts = image_counts[0]
    slots, width = x.shape
    cols = width // GROUPS
    half = width // 2
    order = lax.axis_index("fsdp") ^ jnp.arange(SHARDS, dtype=jnp.int32)
    order = jnp.concatenate([order, lax.axis_index("rep")[None].astype(jnp.int32)])

    own = fc2_weight.shape[0] // 2
    small = (ln1_gain, ln1_bias, qkv_bias, rope_freqs, out_bias, ln2_gain, ln2_bias, fc1_bias, fc2_bias)
    sizes = [s.shape[0] for s in small]
    vectors = jnp.concatenate(small + (jnp.zeros((2 * cols - sum(sizes),), BF),)).reshape(2, cols)
    piece_c, piece_d = mlp_pieces(fc1_weight, fc2_weight)
    piece_a, piece_b = group_pieces(qkv_weight, out_weight, vectors)
    pieces_c = [lax.all_gather(piece_c, "fsdp", axis=0)]
    pieces_d = [lax.all_gather(piece_d, "fsdp", axis=0)]
    first = lambda g: (g.piece[8], g.piece[4], g.piece[2])
    second = lambda g: (g.piece[12], g.piece[6], g.piece[10])
    gather_a = Gather(piece_a)
    gather_a.stage1()
    gather_a.stage2(*first(gather_a))
    gather_a.stage3()
    pieces_a = gather_a.cores()
    gather_b = Gather(piece_b)
    gather_b.stage1(gather_a.piece[12])
    a_t, cos, sin, vec, b1, bias, sel = prepare(sizes, order, x, patch_cols, patch_rows, pieces_a)
    gather_b.stage2(sel)
    q, k, v = project_group(0, order, a_t, bias, cos, sin, pieces_a)
    gather_b.hold((12, 6, 10), q)
    gather_b.stage3()
    heads = [(q, k, v) + tuple(attend(counts, q, k, v))]
    gather_b.hold((14,), heads[0][3])
    pieces_b = gather_b.cores()
    q, k, v = project_group(1, order, a_t, bias, cos, sin, pieces_b)
    heads.append((q, k, v) + tuple(attend(counts, q, k, v)))
    o = [t[3] for t in heads]
    at_out = piece_b.shape[0] - 2 * out_weight.shape[0]
    h, c, c_t = out_project_fast(order, o, x, vec, pieces_b, at_out)
    y, dc, g_c, g_b1a = mlp_half(0, order, c, c_t, dy, b1, vec, (h,), pieces_c, False)
    mlp_c = lax.psum_scatter(tie(g_c, pieces_d[0]), "fsdp", scatter_dimension=0, tiled=True)[0]
    y, dc, near_d, far_d, g_b1b = mlp_half(1, order, c, c_t, dy, b1, vec, (y, dc), pieces_d, True)
    scatter_d = SplitScatter(near_d, far_d)
    dh, do, near_o, far_o, sums2 = out_back_fast(order, dc, h, dy, vec, o, pieces_b, at_out)

    def back(g, do):
        q, k, v, og, lse = heads[g]
        *three, dangle = heads_back(g, counts, q, k, v, og, do, lse, cos, sin)
        return three, dangle

    sent = scatter_d.split()
    grads_b, dangle_b = back(1, tie(do, sent))
    near_b, far_b, bias_b, freq_b = qkv_grad(order, a_t, sel, dangle_b, *grads_b, near_o, far_o)
    scatter_b = Scatter(near_b, far_b)
    scatter_d.hold(near_b)
    sent = scatter_d.step()
    grads_a, dangle_a = back(0, tie(do, sent, near_b))
    scatter_d.hold(dangle_a)
    scatter_b.hold(dangle_a)
    sent = (scatter_d.step(), scatter_b.step())
    near_a, far_a, bias_a, freq_a = qkv_grad(order, a_t, sel, tie(dangle_a, *sent), *grads_a)
    scatter_a = Scatter(near_a, far_a)
    scatter_d.hold(near_a)
    sent = scatter_d.step()
    da = input_part(order, lax.optimization_barrier((grads_b, near_a, sent))[0], pieces_b, width)
    scatter_a.hold(da)
    scatter_b.hold(da)
    scatter_d.hold(da)
    sent = (scatter_a.step(), scatter_b.step())
    mlp_d = scatter_d.finish()
    dx, sums1 = input_back(order, x, dh, vec, tie(da, mlp_d[0], *sent), grads_a, pieces_a)
    scatter_a.hold(sums1)
    scatter_b.hold(sums1)
    sent = (scatter_a.step(), scatter_b.step(), across(mlp_c))
    other_c = sent[2]
    block = pack(sum(sizes), tie(sums1, *sent), sums2, g_b1a, g_b1b, bias_a, bias_b, freq_a, freq_b)
    scatter_a.step()
    mine_b = scatter_b.finish()
    mine_a = scatter_a.finish()
    s_a = mine_a[0].astype(F32) + mine_a[1].astype(F32)
    s_b = mine_b[0].astype(F32) + mine_b[1].astype(F32)
    rows1 = width // SHARDS
    s_w1, s_w2 = mlp_join(rows1, order, (mlp_c, other_c) + mlp_d)
    s_wqkv = jnp.concatenate([s[i * rows1 : (i + 1) * rows1] for i in range(3) for s in (s_a, s_b)], axis=1)
    s_wout = jnp.concatenate([s_b[3 * rows1 : 4 * rows1], s_b[4 * rows1 :]], axis=1)

    mine = jnp.sum(lax.all_to_all(block, "fsdp", 0, 0, tiled=True), axis=0)
    mine = mine + lax.ppermute(mine, "rep", [(0, 1), (1, 0)])
    outs = []
    at = 0
    for size in sizes:
        outs.append(mine[at : at + size])
        at += size
    s_gain1, s_shift1, s_bqkv, s_freq, s_bout, s_gain2, s_shift2, s_b1, s_b2 = outs
    return (
        y[None], dx[None], s_gain1, s_shift1, s_wqkv, s_bqkv, s_freq, s_wout, s_bout,
        s_gain2, s_shift2, s_w1, s_b1, s_w2, s_b2,
    )


def solution(mesh):
    row = P(("rep", "fsdp"), None)
    rows = P(("rep", "fsdp"), None, None)
    vec = P("fsdp")
    mat = P("fsdp", None)
    in_specs = (rows, rows, row, row, row, vec, vec, mat, vec, vec, mat, vec, vec, vec, mat, vec, mat, vec)
    out_specs = (rows, rows, vec, vec, mat, vec, vec, mat, vec, vec, vec, mat, vec, mat, vec)
    fast = mesh.shape["fsdp"] == SHARDS and mesh.shape["rep"] == 2
    return jax.shard_map(
        body_fast if fast else body_any, mesh=mesh, in_specs=in_specs, out_specs=out_specs, check_vma=False
    )
```

```python
from functools import partial

import jax
import jax.numpy as jnp
from jax import lax
from jax.experimental import pallas as pl
from jax.experimental.pallas import tpu as pltpu
from jax.sharding import PartitionSpec as P

HEADS = 12
HEAD_DIM = 64
HALF = HEAD_DIM // 2
FIRST = 576
CUT = 512
WIDE = 640
NEG = -1e30
EPS = 1e-6
BF = jnp.bfloat16
F32 = jnp.float32
GELU_C = 0.7978845608028654
GELU_A = 0.044715


def nn(a, b):
    return lax.dot_general(a, b, (((1,), (0,)), ((), ())), preferred_element_type=F32)


def nt(a, b):
    return lax.dot_general(a, b, (((1,), (1,)), ((), ())), preferred_element_type=F32)


def tn(a, b):
    return lax.dot_general(a, b, (((0,), (0,)), ((), ())), preferred_element_type=F32)


def params(mib=56):
    return pltpu.CompilerParams(vmem_limit_bytes=mib << 20)


def cost(us):
    return pl.CostEstimate(flops=int(us * 1.1e9), bytes_accessed=1 << 16, transcendentals=0)


def norm_parts(v):
    mean = jnp.mean(v, axis=-1, keepdims=True)
    dev = v - mean
    var = jnp.mean(dev * dev, axis=-1, keepdims=True)
    inv = lax.rsqrt(var + EPS)
    return dev * inv, inv


def lane_partial(v):
    total = v[:, :128]
    for i in range(1, v.shape[1] // 128):
        total = total + v[:, i * 128 : (i + 1) * 128]
    return total


def norm1_kernel(x_ref, gain_ref, shift_ref, a_ref, at_ref):
    xhat, _ = norm_parts(x_ref[...].astype(F32))
    a = (xhat * gain_ref[...] + shift_ref[...]).astype(BF)
    a_ref[...] = a
    at_ref[...] = a.T


def norm1(x, gain, shift):
    slots, width = x.shape
    blk = 256
    return pl.pallas_call(
        norm1_kernel,
        grid=(slots // blk,),
        in_specs=[
            pl.BlockSpec((blk, width), lambda i: (i, 0)),
            pl.BlockSpec((1, width), lambda i: (0, 0)),
            pl.BlockSpec((1, width), lambda i: (0, 0)),
        ],
        out_specs=[
            pl.BlockSpec((blk, width), lambda i: (i, 0)),
            pl.BlockSpec((width, blk), lambda i: (0, i)),
        ],
        out_shape=[
            jax.ShapeDtypeStruct((slots, width), BF),
            jax.ShapeDtypeStruct((width, slots), BF),
        ],
        compiler_params=params(),
        cost_estimate=cost(5),
        name="norm1",
    )(x, gain, shift)


def qkv_kernel(a_ref, wq_ref, wk_ref, wv_ref, bq_ref, bk_ref, bv_ref, cos_ref, sin_ref, q_ref, k_ref, v_ref):
    heads = wq_ref.shape[1] // HEAD_DIM
    a = a_ref[...]
    cos = cos_ref[...]
    sin = sin_ref[...]
    for w_ref, b_ref, out_ref, scale in ((wq_ref, bq_ref, q_ref, HEAD_DIM**-0.5), (wk_ref, bk_ref, k_ref, 1.0)):
        u = nt(w_ref[...].T, a) + b_ref[...]
        for h in range(heads):
            u1 = u[h * HEAD_DIM : h * HEAD_DIM + HALF]
            u2 = u[h * HEAD_DIM + HALF : (h + 1) * HEAD_DIM]
            c = cos[h * HALF : (h + 1) * HALF]
            s = sin[h * HALF : (h + 1) * HALF]
            out_ref[h * HEAD_DIM : h * HEAD_DIM + HALF, :] = ((u1 * c - u2 * s) * scale).astype(BF)
            out_ref[h * HEAD_DIM + HALF : (h + 1) * HEAD_DIM, :] = ((u1 * s + u2 * c) * scale).astype(BF)
    v_ref[...] = (nt(wv_ref[...].T, a) + bv_ref[...]).astype(BF)


def project(a, w, bias, cos, sin):
    slots, width = a.shape
    cols = 256
    groups = width // cols
    wspec = lambda part: pl.BlockSpec((width, cols), lambda g: (0, part * groups + g))
    bspec = lambda part: pl.BlockSpec((cols, 1), lambda g: (part * groups + g, 0))
    out = pl.BlockSpec((cols, slots), lambda g: (g, 0))
    return pl.pallas_call(
        qkv_kernel,
        grid=(groups,),
        in_specs=[pl.BlockSpec((slots, width), lambda g: (0, 0))]
        + [wspec(i) for i in range(3)]
        + [bspec(i) for i in range(3)]
        + [pl.BlockSpec((cols // 2, slots), lambda g: (g, 0))] * 2,
        out_specs=[out] * 3,
        out_shape=[jax.ShapeDtypeStruct((width, slots), BF)] * 3,
        compiler_params=params(),
        name="qkv",
    )(a, w, w, w, bias, bias, bias, cos, sin)


def second_bias(counts_ref, slots):
    shape = (slots - FIRST, slots - CUT)
    key = lax.broadcasted_iota(jnp.int32, shape, 0) + FIRST
    query = lax.broadcasted_iota(jnp.int32, shape, 1) + CUT
    end0 = counts_ref[0]
    end1 = end0 + counts_ref[1]
    end2 = end1 + counts_ref[2]

    def seg(place):
        return (place >= end0).astype(jnp.int32) + (place >= end1).astype(jnp.int32)

    allowed = ((seg(key) == seg(query)) & (key < end2) & (query < end2)) | (key == query)
    return jnp.where(allowed, 0.0, NEG)


def attend_kernel(counts_ref, q_ref, k_ref, v_ref, o_ref, lse_ref, bias_ref):
    slots = q_ref.shape[1]

    @pl.when(pl.program_id(0) == 0)
    def _():
        bias_ref[...] = second_bias(counts_ref, slots)

    def part(scores, first, values):
        peak = jnp.max(scores, axis=0, keepdims=True)
        weights = jnp.exp(scores - peak)
        total = jnp.sum(weights, axis=0, keepdims=True)
        wb = weights.astype(BF)
        gap = jnp.zeros((values.shape[1] - wb.shape[0], wb.shape[1]), BF)
        wb = jnp.concatenate([wb, gap] if first else [gap, wb], axis=0)
        mixed = nn(values, wb) * (1.0 / total)
        return mixed, peak + jnp.log(total)

    edge = lax.broadcasted_iota(jnp.int32, (1, WIDE - CUT), 1) < FIRST - CUT
    for h in range(q_ref.shape[0] // HEAD_DIM):
        rows = slice(h * HEAD_DIM, (h + 1) * HEAD_DIM)
        k = k_ref[rows, :].T
        q = q_ref[rows, :]
        v = v_ref[rows, :]
        mixed1, lse1 = part(nn(k[:FIRST], q[:, :WIDE]), True, v[:, :WIDE])
        mixed2, lse2 = part(nn(k[FIRST:], q[:, CUT:]) + bias_ref[...], False, v[:, CUT:])
        for out, one, two in ((o_ref.at[rows], mixed1, mixed2), (lse_ref.at[h], lse1, lse2)):
            out[:, :CUT] = one[:, :CUT].astype(out.dtype)
            out[:, CUT:WIDE] = jnp.where(edge, one[:, CUT:], two[:, : WIDE - CUT]).astype(out.dtype)
            out[:, WIDE:] = two[:, WIDE - CUT :].astype(out.dtype)


def attend(counts, q, k, v):
    width, slots = q.shape
    heads = width // HEAD_DIM
    each = 2
    head = pl.BlockSpec((each * HEAD_DIM, slots), lambda h: (h, 0))
    return pl.pallas_call(
        attend_kernel,
        grid=(heads // each,),
        in_specs=[pl.BlockSpec(memory_space=pltpu.SMEM)] + [head] * 3,
        out_specs=[head, pl.BlockSpec((each, 1, slots), lambda h: (h, 0, 0))],
        out_shape=[jax.ShapeDtypeStruct((width, slots), BF), jax.ShapeDtypeStruct((heads, 1, slots), F32)],
        scratch_shapes=[pltpu.VMEM((slots - FIRST, slots - CUT), F32)],
        compiler_params=params(),
        cost_estimate=cost(8),
        name="attend",
    )(counts, q, k, v)


def attend_back_kernel(
    counts_ref, q_ref, k_ref, v_ref, o_ref, do_ref, lse_ref, cos_ref, sin_ref, place_ref,
    dq_ref, dk_ref, dv_ref, bq_ref, bk_ref, bv_ref, fc_ref, fr_ref, bias_ref,
):
    slots = q_ref.shape[1]

    @pl.when(pl.program_id(0) == 0)
    def _():
        bias_ref[...] = second_bias(counts_ref, slots)

    kt = k_ref[...]
    k = kt.T
    v = v_ref[...].T
    q = q_ref[...]
    do = do_ref[...]
    lse = lse_ref[0]
    delta = jnp.sum(do.astype(F32) * o_ref[...].astype(F32), axis=0, keepdims=True)
    lane1 = lax.broadcasted_iota(jnp.int32, (1, WIDE), 1)
    lane2 = lax.broadcasted_iota(jnp.int32, (1, slots - CUT), 1)
    lse1 = jnp.where(lane1 < FIRST, lse[:, :WIDE], -NEG)
    lse2 = jnp.where(lane2 >= FIRST - CUT, lse[:, CUT:], -NEG)

    def part(scores, grads, queries, outs, keys, delta_row, first):
        prob = jnp.exp(scores)
        ds = (prob * (grads - delta_row)).astype(BF)
        pb = prob.astype(BF)
        gap = jnp.zeros((keys.shape[1] - pb.shape[0], pb.shape[1]), BF)
        pb = jnp.concatenate([pb, gap] if first else [gap, pb], axis=0)
        ds = jnp.concatenate([ds, gap] if first else [gap, ds], axis=0)
        return nn(keys, ds), nt(queries, ds), nt(outs, pb)

    grads1 = part(
        nn(k[:FIRST], q[:, :WIDE]) - lse1, nn(v[:FIRST], do[:, :WIDE]),
        q[:, :WIDE], do[:, :WIDE], kt[:, :WIDE], delta[:, :WIDE], True,
    )
    grads2 = part(
        nn(k[FIRST:], q[:, CUT:]) + bias_ref[...] - lse2, nn(v[FIRST:], do[:, CUT:]),
        q[:, CUT:], do[:, CUT:], kt[:, CUT:], delta[:, CUT:], False,
    )
    dq, dk, dv = (
        jnp.concatenate([one[:, :CUT], one[:, CUT:] + two[:, : WIDE - CUT], two[:, WIDE - CUT :]], axis=1)
        for one, two in zip(grads1, grads2)
    )
    scale = HEAD_DIM**-0.5
    cos = cos_ref[...]
    sin = sin_ref[...]
    dangle = None
    for r, rot, out, bias_out in ((dq * scale, q.astype(F32) * (1.0 / scale), dq_ref, bq_ref), (dk, kt.astype(F32), dk_ref, bk_ref)):
        r1, r2 = r[:HALF], r[HALF:]
        term = r2 * rot[:HALF] - r1 * rot[HALF:]
        dangle = term if dangle is None else dangle + term
        g1 = (r1 * cos + r2 * sin).astype(BF)
        g2 = (r2 * cos - r1 * sin).astype(BF)
        out[:HALF, :] = g1
        out[HALF:, :] = g2
        bias_out[:HALF, :] = lane_partial(g1.astype(F32))
        bias_out[HALF:, :] = lane_partial(g2.astype(F32))
    dvb = dv.astype(BF)
    dv_ref[...] = dvb
    bv_ref[...] = lane_partial(dvb.astype(F32))
    fc_ref[...] = lane_partial(dangle * place_ref[0:1, :])
    fr_ref[...] = lane_partial(dangle * place_ref[1:2, :])


def attend_back(counts, q, k, v, o, do, lse, cos, sin, places):
    width, slots = q.shape
    heads = width // HEAD_DIM
    head = pl.BlockSpec((HEAD_DIM, slots), lambda h: (h, 0))
    half = pl.BlockSpec((HALF, slots), lambda h: (h, 0))
    return pl.pallas_call(
        attend_back_kernel,
        grid=(heads,),
        in_specs=[pl.BlockSpec(memory_space=pltpu.SMEM)]
        + [head] * 5
        + [pl.BlockSpec((1, 1, slots), lambda h: (h, 0, 0)), half, half]
        + [pl.BlockSpec((2, slots), lambda h: (0, 0))],
        out_specs=[head] * 3
        + [pl.BlockSpec((HEAD_DIM, 128), lambda h: (h, 0))] * 3
        + [pl.BlockSpec((HALF, 128), lambda h: (h, 0))] * 2,
        out_shape=[jax.ShapeDtypeStruct((width, slots), BF)] * 3
        + [jax.ShapeDtypeStruct((width, 128), F32)] * 3
        + [jax.ShapeDtypeStruct((width // 2, 128), F32)] * 2,
        scratch_shapes=[pltpu.VMEM((slots - FIRST, slots - CUT), F32)],
        compiler_params=params(),
        cost_estimate=cost(14),
        name="attend_back",
    )(counts, q, k, v, o, do, lse, cos, sin, places)


def out_kernel(o_ref, x_ref, w_ref, b_ref, gain_ref, shift_ref, h_ref, c_ref, ct_ref):
    h = x_ref[...].astype(F32) + (nn(o_ref[...].T, w_ref[...]) + b_ref[...])
    h_ref[...] = h
    xhat, _ = norm_parts(h)
    c = (xhat * gain_ref[...] + shift_ref[...]).astype(BF)
    c_ref[...] = c
    ct_ref[...] = c.T


def out_project(o, x, w, b, gain, shift):
    slots, width = x.shape
    blk = 256
    row = pl.BlockSpec((1, width), lambda i: (0, 0))
    rows = pl.BlockSpec((blk, width), lambda i: (i, 0))
    cols = pl.BlockSpec((width, blk), lambda i: (0, i))
    return pl.pallas_call(
        out_kernel,
        grid=(slots // blk,),
        in_specs=[cols, rows, pl.BlockSpec((width, width), lambda i: (0, 0)), row, row, row],
        out_specs=[rows, rows, cols],
        out_shape=[
            jax.ShapeDtypeStruct((slots, width), F32),
            jax.ShapeDtypeStruct((slots, width), BF),
            jax.ShapeDtypeStruct((width, slots), BF),
        ],
        compiler_params=params(),
        name="out_project",
    )(o, x, w, b, gain, shift)


def mlp_kernel(c_ref, ct_ref, dy_ref, h_ref, w1_ref, b1_ref, w2_ref, b2_ref, y_ref, dc_ref, g1_ref, g2_ref, gb1_ref, y_acc, hb_scr, dp_scr):
    slots = c_ref.shape[0]
    tile = 256

    @pl.when(pl.program_id(0) == 0)
    def _():
        y_acc[...] = h_ref[...] + b2_ref[...]
        dc_ref[...] = jnp.zeros_like(dc_ref)

    gb1_ref[...] = jnp.zeros_like(gb1_ref)

    def step(i, _):
        rows = pl.ds(pl.multiple_of(i * tile, tile), tile)
        pre = nn(c_ref[rows, :], w1_ref[...]) + b1_ref[...]
        square = pre * pre
        th = jnp.tanh(GELU_C * (pre + GELU_A * (pre * square)))
        cdf = 0.5 * (1.0 + th)
        hb = (pre * cdf).astype(BF)
        slope = cdf + 0.5 * pre * (1.0 - th * th) * (GELU_C * (1.0 + (3.0 * GELU_A) * square))
        hb_scr[rows, :] = hb
        y_acc[rows, :] += nn(hb, w2_ref[...])
        dpre = (nt(dy_ref[rows, :], w2_ref[...]) * slope).astype(BF)
        dp_scr[rows, :] = dpre
        dc_ref[rows, :] += nt(dpre, w1_ref[...])
        gb1_ref[...] += jnp.sum(dpre.astype(F32), axis=0, keepdims=True)
        return 0

    lax.fori_loop(0, slots // tile, step, 0)
    g1_ref[...] = nn(ct_ref[...], dp_scr[...]).astype(g1_ref.dtype)
    g2_ref[...] = tn(hb_scr[...], dy_ref[...]).astype(g2_ref.dtype)

    @pl.when(pl.program_id(0) == pl.num_programs(0) - 1)
    def _():
        y_ref[...] = y_acc[...].astype(BF)


def mlp(c, ct, dy, h, w1, b1, w2, b2):
    slots, width = c.shape
    hidden = w1.shape[1]
    blk = 512
    whole = lambda r, k: pl.BlockSpec((r, k), lambda j: (0, 0))
    return pl.pallas_call(
        mlp_kernel,
        grid=(hidden // blk,),
        in_specs=[
            whole(slots, width),
            whole(width, slots),
            whole(slots, width),
            whole(slots, width),
            pl.BlockSpec((width, blk), lambda j: (0, j)),
            pl.BlockSpec((1, blk), lambda j: (0, j)),
            pl.BlockSpec((blk, width), lambda j: (j, 0)),
            whole(1, width),
        ],
        out_specs=[
            whole(slots, width),
            whole(slots, width),
            pl.BlockSpec((width, blk), lambda j: (0, j)),
            pl.BlockSpec((blk, width), lambda j: (j, 0)),
            pl.BlockSpec((1, blk), lambda j: (0, j)),
        ],
        out_shape=[
            jax.ShapeDtypeStruct((slots, width), BF),
            jax.ShapeDtypeStruct((slots, width), F32),
            jax.ShapeDtypeStruct((width, hidden), BF),
            jax.ShapeDtypeStruct((hidden, width), BF),
            jax.ShapeDtypeStruct((1, hidden), F32),
        ],
        scratch_shapes=[
            pltpu.VMEM((slots, width), F32),
            pltpu.VMEM((slots, blk), BF),
            pltpu.VMEM((slots, blk), BF),
        ],
        compiler_params=params(),
        name="mlp",
    )(c, ct, dy, h, w1, b1, w2, b2)


def norm_back(grad, v, gain):
    xhat, inv = norm_parts(v)
    g = grad * gain
    lead = jnp.mean(g, axis=-1, keepdims=True)
    slope = jnp.mean(g * xhat, axis=-1, keepdims=True)
    return (g - lead - xhat * slope) * inv, jnp.sum(grad * xhat, axis=0, keepdims=True), jnp.sum(grad, axis=0, keepdims=True)


def out_back_kernel(dc_ref, h_ref, dy_ref, o_ref, w_ref, gain_ref, dh_ref, do_ref, gw_ref, sums_ref, acc_ref):
    i = pl.program_id(0)

    @pl.when(i == 0)
    def _():
        acc_ref[...] = jnp.zeros_like(acc_ref)
        sums_ref[...] = jnp.zeros_like(sums_ref)

    dy = dy_ref[...].astype(F32)
    part, dgain, dshift = norm_back(dc_ref[...], h_ref[...], gain_ref[...])
    dh = dy + part
    dh_ref[...] = dh
    dhb = dh.astype(BF)
    do_ref[...] = nt(w_ref[...], dhb).astype(BF)
    acc_ref[...] += nn(o_ref[...], dhb)
    sums_ref[0:1, :] += dgain
    sums_ref[1:2, :] += dshift
    sums_ref[2:3, :] += jnp.sum(dh, axis=0, keepdims=True)
    sums_ref[3:4, :] += jnp.sum(dy, axis=0, keepdims=True)

    @pl.when(i == pl.num_programs(0) - 1)
    def _():
        gw_ref[...] = acc_ref[...].astype(gw_ref.dtype)


def out_back(dc, h, dy, o, w, gain):
    slots, width = h.shape
    blk = 256
    rows = pl.BlockSpec((blk, width), lambda i: (i, 0))
    cols = pl.BlockSpec((width, blk), lambda i: (0, i))
    whole = lambda r, k: pl.BlockSpec((r, k), lambda i: (0, 0))
    return pl.pallas_call(
        out_back_kernel,
        grid=(slots // blk,),
        in_specs=[rows, rows, rows, cols, whole(width, width), whole(1, width)],
        out_specs=[rows, cols, whole(width, width), whole(8, width)],
        out_shape=[
            jax.ShapeDtypeStruct((slots, width), F32),
            jax.ShapeDtypeStruct((width, slots), BF),
            jax.ShapeDtypeStruct((width, width), BF),
            jax.ShapeDtypeStruct((8, width), F32),
        ],
        scratch_shapes=[pltpu.VMEM((width, width), F32)],
        compiler_params=params(),
        name="out_back",
    )(dc, h, dy, o, w, gain)


def qkv_back_kernel(at_ref, dqkv_ref, w_ref, x_ref, dh_ref, gain_ref, gw_ref, dx_ref, sums_ref, acc_ref):
    j = pl.program_id(0)

    @pl.when(j == 0)
    def _():
        acc_ref[...] = jnp.zeros_like(acc_ref)

    d = dqkv_ref[...]
    gw_ref[...] = nt(at_ref[...], d).astype(gw_ref.dtype)
    acc_ref[...] += nn(w_ref[...], d)

    @pl.when(j == pl.num_programs(0) - 1)
    def _():
        sums_ref[...] = jnp.zeros_like(sums_ref)
        tile = 256
        for i in range(x_ref.shape[0] // tile):
            rows = slice(i * tile, (i + 1) * tile)
            da = acc_ref[:, rows].T
            part, dgain, dshift = norm_back(da, x_ref[rows, :].astype(F32), gain_ref[...])
            dx_ref[rows, :] = (dh_ref[rows, :] + part).astype(BF)
            sums_ref[0:1, :] += dgain
            sums_ref[1:2, :] += dshift


def qkv_back(at, dqkv, w, x, dh, gain):
    slots, width = x.shape
    outs = w.shape[1]
    blk = 768
    whole = lambda r, k: pl.BlockSpec((r, k), lambda j: (0, 0))
    return pl.pallas_call(
        qkv_back_kernel,
        grid=(outs // blk,),
        in_specs=[
            whole(width, slots),
            pl.BlockSpec((blk, slots), lambda j: (j, 0)),
            pl.BlockSpec((width, blk), lambda j: (0, j)),
            whole(slots, width),
            whole(slots, width),
            whole(1, width),
        ],
        out_specs=[pl.BlockSpec((width, blk), lambda j: (0, j)), whole(slots, width), whole(8, width)],
        out_shape=[
            jax.ShapeDtypeStruct((width, outs), BF),
            jax.ShapeDtypeStruct((slots, width), BF),
            jax.ShapeDtypeStruct((8, width), F32),
        ],
        scratch_shapes=[pltpu.VMEM((width, slots), F32)],
        compiler_params=params(),
        name="qkv_back",
    )(at, dqkv, w, x, dh, gain)


def body_any(
    tokens, cotangent, image_counts, patch_rows, patch_cols, ln1_gain, ln1_bias, qkv_weight, qkv_bias, rope_freqs,
    out_weight, out_bias, ln2_gain, ln2_bias, fc1_weight, fc1_bias, fc2_weight, fc2_bias,
):
    x = tokens[0]
    dy = cotangent[0]
    counts = image_counts[0]
    width = x.shape[1]
    small = (ln1_gain, ln1_bias, qkv_bias, rope_freqs, out_bias, ln2_gain, ln2_bias, fc1_bias, fc2_bias)
    sizes = [s.shape[0] for s in small]
    gather = partial(lax.all_gather, axis_name="fsdp", axis=0, tiled=True)
    packed = lax.all_gather(jnp.concatenate(small), "fsdp", axis=0)
    vectors = []
    at = 0
    for size in sizes:
        vectors.append(packed[:, at : at + size].reshape(-1).astype(F32))
        at += size
    gain1, shift1, b_qkv, freqs, b_out, gain2, shift2, b1, b2 = vectors
    w_qkv = gather(qkv_weight)
    w_out = gather(out_weight)
    w1 = gather(fc1_weight)
    w2 = gather(fc2_weight)

    row = lambda v: v[None, :]
    a, a_t = norm1(x, row(gain1), row(shift1))
    places = jnp.concatenate([patch_cols, patch_rows], axis=0).astype(F32)
    half = freqs.shape[0] // 2
    angle = freqs[:half, None] * places[0:1] + freqs[half:, None] * places[1:2]
    cos = jnp.cos(angle)
    sin = jnp.sin(angle)
    q, k, v = project(a, w_qkv, b_qkv[:, None], cos, sin)
    o, lse = attend(counts, q, k, v)
    h, c, c_t = out_project(o, x, w_out, row(b_out), row(gain2), row(shift2))
    y, dc, g_w1, g_w2, g_b1 = mlp(c, c_t, dy, h, w1, row(b1), w2, row(b2))
    dh, do, g_wout, sums2 = out_back(dc, h, dy, o, w_out, row(gain2))
    dq, dk, dv, s_bq, s_bk, s_bv, s_fc, s_fr = attend_back(counts, q, k, v, o, do, lse, cos, sin, places)
    dqkv = jnp.concatenate([dq, dk, dv], axis=0)
    g_wqkv, dx, sums1 = qkv_back(a_t, dqkv, w_qkv, x, dh, row(gain1))

    scatter = partial(lax.psum_scatter, axis_name="fsdp", scatter_dimension=0, tiled=True)
    both = lambda g: lax.psum(scatter(g), "rep").astype(F32)
    g_bqkv = jnp.sum(jnp.concatenate([s_bq, s_bk, s_bv], axis=0), axis=1)
    g_freq = jnp.sum(jnp.concatenate([s_fc, s_fr], axis=0), axis=1)
    small_grads = (sums1[0], sums1[1], g_bqkv, g_freq, sums2[2], sums2[0], sums2[1], g_b1[0], sums2[3])
    shards = mesh_size = packed.shape[0]
    block = jnp.concatenate([g.reshape(shards, -1) for g in small_grads], axis=1)
    total = lax.psum(block, ("rep", "fsdp"))
    mine = lax.dynamic_index_in_dim(total, lax.axis_index("fsdp"), 0, keepdims=False)
    outs = []
    at = 0
    for size in sizes:
        outs.append(mine[at : at + size])
        at += size
    s_gain1, s_shift1, s_bqkv, s_freq, s_bout, s_gain2, s_shift2, s_b1, s_b2 = outs
    return (
        y[None], dx[None], s_gain1, s_shift1, both(g_wqkv), s_bqkv, s_freq, both(g_wout), s_bout,
        s_gain2, s_shift2, both(g_w1), s_b1, both(g_w2), s_b2,
    )


SHARDS = 16
GROUPS = 2
LEAVING = (0, 8, 4, 12, 2, 10, 6, 14)


def swap(v, mask):
    return lax.ppermute(v, "fsdp", [(i, i ^ mask) for i in range(SHARDS)])


def tie(v, *after):
    return lax.optimization_barrier((v,) + after)[0]


class Gather:
    def __init__(self, mine):
        self.piece = {0: mine}

    def send(self, source, mask, after):
        v = self.piece[source]
        self.piece[source ^ mask] = swap(tie(v, *after) if after else v, mask)

    def hold(self, sources, after):
        for p in sources:
            self.piece[p] = tie(self.piece[p], after)

    def stage1(self, *after):
        for mask in (8, 4, 2):
            self.send(0, mask, after)

    def stage2(self, *after):
        self.send(8, 4, after)
        self.send(4, 2, after)
        self.send(8, 2, after)

    def stage3(self, *after):
        self.send(12, 2, after)

    def cores(self, *after):
        for p in (0, 8, 4, 2, 6, 10, 12, 14):
            self.send(p, 1, after)
        return [self.piece[p] for p in range(SHARDS)]


class Scatter:
    def __init__(self, near, far):
        self.got = [near, swap(far, 1)]
        self.size = 4

    def total(self, lo, hi):
        out = self.got[0][lo:hi].astype(F32)
        for g in self.got[1:]:
            out = out + g[lo:hi].astype(F32)
        return out.astype(BF)

    def hold(self, *after):
        self.got[-1] = tie(self.got[-1], *after)

    def step(self):
        lo = self.size
        sent = self.total(lo, 2 * lo)
        self.got.append(swap(sent, {4: 2, 2: 4, 1: 8}[lo]))
        self.size = lo // 2
        return sent

    def finish(self):
        mine = self.total(0, 1)[0]
        return mine, across(mine)


class SplitScatter(Scatter):
    def __init__(self, near, far):
        self.start = [near, swap(far, 1)]
        self.size = 4

    def split(self):
        sent = (self.start[0][1].astype(F32) + self.start[1][1].astype(F32)).astype(BF)
        got = across(sent)
        self.got = [self.start[0][0], self.start[1][0], got]
        return sent


def across(v):
    return lax.ppermute(v, "rep", [(0, 1), (1, 0)])


def start_all(copies):
    for copy in copies:
        copy.start()


def wait_all(copies):
    for copy in copies:
        copy.wait()


def fetch(refs, order_ref, moves, sem):
    copies = []
    for p, ref in enumerate(refs):
        for rows, place in moves:
            copies.append(pltpu.make_async_copy(ref.at[rows], place(order_ref[p]), sem.at[len(copies)]))
    return copies


ANY = pl.BlockSpec(memory_space=pl.ANY)
HBM = pl.BlockSpec(memory_space=pltpu.HBM)
SMEM = pl.BlockSpec(memory_space=pltpu.SMEM)
VMEM = pl.BlockSpec(memory_space=pltpu.VMEM)


LINES = 16


def group_piece_kernel(w_ref, o_ref, v_ref, a_ref, b_ref):
    rows, cols = w_ref.shape[0], a_ref.shape[1]
    for i in range(3):
        for g, out in enumerate((a_ref, b_ref)):
            out[i * rows : (i + 1) * rows, :] = w_ref[:, (i * GROUPS + g) * cols : (i * GROUPS + g + 1) * cols]
    for i in range(2):
        b_ref[(3 + i) * rows : (4 + i) * rows, :] = o_ref[:, i * cols : (i + 1) * cols]
    a_ref[3 * rows :, :] = jnp.concatenate([v_ref[...], jnp.zeros((LINES - v_ref.shape[0], cols), BF)], axis=0)


def group_pieces(w, w_out, vectors):
    rows, cols = w.shape[0], w_out.shape[1] // 2
    return pl.pallas_call(
        group_piece_kernel,
        in_specs=[VMEM] * 3,
        out_specs=[VMEM, VMEM],
        out_shape=[jax.ShapeDtypeStruct((3 * rows + LINES, cols), BF), jax.ShapeDtypeStruct((5 * rows, cols), BF)],
        compiler_params=params(),
        cost_estimate=cost(2),
        name="group_pieces",
    )(w, w_out, vectors)


def mlp_piece_kernel(w1_ref, w2_ref, *outs):
    rows1 = w1_ref.shape[0]
    own = w2_ref.shape[0] // 2
    per = SHARDS // 2
    w1 = w1_ref[...].astype(F32)
    for i, out in enumerate(outs):
        for b in range(2):
            runs = [w1[:, (2 * (b * per + j) + i) * own :][:, :own] for j in range(per)]
            out[b * rows1 : (b + 1) * rows1, :] = jnp.concatenate(runs, axis=1).astype(BF)
        out[2 * rows1 :, :] = w2_ref[i * own : (i + 1) * own, :]


def mlp_pieces(w1, w2):
    rows = 2 * w1.shape[0] + w2.shape[0] // 2
    return pl.pallas_call(
        mlp_piece_kernel,
        in_specs=[VMEM, VMEM],
        out_specs=[VMEM, VMEM],
        out_shape=[jax.ShapeDtypeStruct((rows, w2.shape[1]), BF)] * 2,
        compiler_params=params(),
        cost_estimate=cost(2),
        name="mlp_pieces",
    )(w1, w2)


def mlp_join_kernel(order_ref, c_ref, c_other_ref, d_ref, d_other_ref, w1_ref, w2_ref):
    rows1 = w1_ref.shape[0]
    own = w2_ref.shape[0] // 2
    per = SHARDS // 2
    c = c_ref[...].astype(F32) + c_other_ref[...].astype(F32)
    mine = d_ref[...].astype(F32)
    other = d_other_ref[...].astype(F32)
    here = order_ref[SHARDS] == 0
    d = jnp.where(here, mine, other)
    runs = []
    for b in range(2):
        for j in range(per):
            runs += [m[b * rows1 : (b + 1) * rows1, j * own : (j + 1) * own] for m in (c, d)]
    w1_ref[...] = jnp.concatenate(runs, axis=1)
    w2_ref[:own, :] = c[2 * rows1 :]
    w2_ref[own:, :] = jnp.where(here, other, mine)


def mlp_join(rows1, order, parts):
    own = parts[0].shape[0] - 2 * rows1
    return pl.pallas_call(
        mlp_join_kernel,
        in_specs=[SMEM] + [VMEM] * 4,
        out_specs=[VMEM] * 2,
        out_shape=[
            jax.ShapeDtypeStruct((rows1, 2 * own * SHARDS), F32),
            jax.ShapeDtypeStruct((2 * own, parts[0].shape[1]), F32),
        ],
        compiler_params=params(8),
        cost_estimate=cost(3),
        name="mlp_join",
    )(order, *parts)


def spread(packed, lo, size):
    return jnp.concatenate([packed[j : j + 1, lo : lo + size] for j in range(packed.shape[0])], axis=1)


def column(v):
    return jnp.broadcast_to(v, (8, v.shape[1])).T[:, 0:1]


def prepare_kernel(sizes, order_ref, x_ref, cols_ref, rows_ref, *rest):
    pieces = rest[:SHARDS]
    at_ref, cos_ref, sin_ref, vec_ref, b1_ref, bias_ref, sel_ref, line_scr, table_scr, sem = rest[SHARDS:]
    half = cos_ref.shape[0]

    @pl.when(pl.program_id(0) == 0)
    def _():
        last = pieces[0].shape[0]
        copies = fetch(pieces, order_ref, [(slice(last - LINES, last), lambda d: line_scr.at[d])], sem)
        start_all(copies)
        wait_all(copies)
        packed = jnp.concatenate([line_scr[:, i, :] for i in range(2)], axis=1).astype(F32)
        starts = [sum(sizes[:i]) for i in range(len(sizes))]
        gain1, shift1, b_qkv, freqs, b_out, gain2, shift2 = (spread(packed, starts[i], sizes[i]) for i in range(7))
        b2 = spread(packed, starts[8], sizes[8])
        for i, v in enumerate((b_out, gain1, gain2, shift2, b2, shift1)):
            vec_ref[i : i + 1, :] = v
        own = sizes[7] // 2
        for i in range(2):
            b1_ref[i : i + 1, :] = spread(packed, starts[7] + i * own, own)
        bias_ref[...] = column(b_qkv)
        freq = column(freqs)
        spots = lax.broadcasted_iota(jnp.int32, (1, 128), 1).astype(F32)
        for i in range(2):
            angle = freq[i * half : (i + 1) * half] * spots
            for k, table in enumerate((jnp.cos(angle), jnp.sin(angle))):
                for n in range(3):
                    term = table.astype(BF)
                    table_scr[i, k, n] = term
                    table = table - term.astype(F32)

    xhat, _ = norm_parts(x_ref[...].astype(F32))
    at_ref[...] = (xhat * vec_ref[1:2, :] + vec_ref[5:6, :]).astype(BF).T
    found = []
    for i, at in enumerate((cols_ref[...], rows_ref[...])):
        one_hot = jnp.where(lax.broadcasted_iota(jnp.int32, (128, at.shape[1]), 0) == at, 1.0, 0.0).astype(BF)
        found.append([sum(nn(table_scr[i, k, n], one_hot) for n in range(3)) for k in range(2)])
    (cos_c, sin_c), (cos_r, sin_r) = found
    cos_ref[...] = cos_c * cos_r - sin_c * sin_r
    sin_ref[...] = sin_c * cos_r + cos_c * sin_r
    line = lax.broadcasted_iota(jnp.int32, sel_ref.shape, 0)
    sel = jnp.where(line == 0, cols_ref[...].astype(F32), rows_ref[...].astype(F32))
    sel_ref[...] = jnp.where(line < 2, sel, jnp.where(line == 2, 1.0, 0.0)).astype(BF)


def prepare(sizes, order, x, patch_cols, patch_rows, pieces):
    slots, width = x.shape
    own = sizes[7] // 2
    blk = 256
    shape = jax.ShapeDtypeStruct
    tall = lambda n: pl.BlockSpec((n, blk), lambda i: (0, i))
    whole = lambda r, k: pl.BlockSpec((r, k), lambda i: (0, 0))
    return pl.pallas_call(
        partial(prepare_kernel, sizes),
        grid=(slots // blk,),
        in_specs=[SMEM, pl.BlockSpec((blk, width), lambda i: (i, 0)), tall(1), tall(1)] + [HBM] * SHARDS,
        out_specs=[
            tall(width), tall(width // 2), tall(width // 2),
            whole(8, width), whole(2, own * SHARDS), whole(3 * width, 1), tall(16),
        ],
        out_shape=[
            shape((width, slots), BF),
            shape((width // 2, slots), F32),
            shape((width // 2, slots), F32),
            shape((8, width), F32),
            shape((2, own * SHARDS), F32),
            shape((3 * width, 1), F32),
            shape((16, slots), BF),
        ],
        scratch_shapes=[
            pltpu.VMEM((SHARDS, LINES, width // GROUPS), BF),
            pltpu.VMEM((2, 2, 3, width // 2, 128), BF),
            pltpu.SemaphoreType.DMA((SHARDS,)),
        ],
        compiler_params=params(),
        cost_estimate=cost(8),
        name="prepare",
    )(order, x, patch_cols, patch_rows, *pieces)


def pack_kernel(sums1_ref, sums2_ref, b1a_ref, b1b_ref, *rest):
    heads, out_ref = rest[:-1], rest[-1]
    bias = [r[2:3, :] for r in heads[:GROUPS]]
    freq = [r[...] for r in heads[GROUPS:]]
    cols = bias[0].shape[1] // 3
    b_qkv = jnp.concatenate([b[:, i * cols : (i + 1) * cols] for i in range(3) for b in bias], axis=1)
    g_freq = jnp.concatenate([f[i : i + 1] for i in range(2) for f in freq], axis=1)
    vectors = (
        sums1_ref[0:1, :], sums1_ref[1:2, :], b_qkv, g_freq, sums2_ref[2:3, :], sums2_ref[0:1, :], sums2_ref[1:2, :],
        b1a_ref[...], b1b_ref[...], sums2_ref[3:4, :],
    )
    lines = []
    for j in range(SHARDS):
        runs = []
        for v in vectors:
            n = v.shape[1] // SHARDS
            runs.append(v[:, j * n : (j + 1) * n])
        lines.append(jnp.concatenate(runs, axis=1))
    out_ref[...] = jnp.concatenate(lines, axis=0)


def pack(size, *sums):
    return pl.pallas_call(
        pack_kernel,
        in_specs=[VMEM] * len(sums),
        out_specs=VMEM,
        out_shape=jax.ShapeDtypeStruct((SHARDS, size), F32),
        compiler_params=params(4),
        cost_estimate=cost(3),
        name="pack",
    )(*sums)


def group_kernel(order_ref, at_ref, bq_ref, bk_ref, bv_ref, cos_ref, sin_ref, *rest):
    pieces, (q_ref, k_ref, v_ref, w_scr, wt_scr, sem) = rest[:SHARDS], rest[SHARDS:]
    cols = q_ref.shape[0]
    part = w_scr.shape[1] // 3

    @pl.when(pl.program_id(0) == 0)
    def _():
        copies = fetch(pieces, order_ref, [(slice(0, 3 * part), lambda d: w_scr.at[d])], sem)
        start_all(copies)
        wait_all(copies)
        for i in range(3):
            wt_scr[i] = w_scr[:, i * part : (i + 1) * part, :].reshape(SHARDS * part, cols).T

    a_t = at_ref[...]
    cos = cos_ref[...]
    sin = sin_ref[...]
    for i, b_ref, out_ref, scale in ((0, bq_ref, q_ref, HEAD_DIM**-0.5), (1, bk_ref, k_ref, 1.0)):
        u = nn(wt_scr[i], a_t) + b_ref[...]
        for h in range(cols // HEAD_DIM):
            u1 = u[h * HEAD_DIM : h * HEAD_DIM + HALF]
            u2 = u[h * HEAD_DIM + HALF : (h + 1) * HEAD_DIM]
            c = cos[h * HALF : (h + 1) * HALF]
            s = sin[h * HALF : (h + 1) * HALF]
            out_ref[h * HEAD_DIM : h * HEAD_DIM + HALF, :] = ((u1 * c - u2 * s) * scale).astype(BF)
            out_ref[h * HEAD_DIM + HALF : (h + 1) * HEAD_DIM, :] = ((u1 * s + u2 * c) * scale).astype(BF)
    v_ref[...] = (nn(wt_scr[2], a_t) + bv_ref[...]).astype(BF)


def project_group(group, order, a_t, bias, cos, sin, pieces):
    width, slots = a_t.shape
    cols = pieces[0].shape[1]
    blk = 512
    tall = lambda n, at: pl.BlockSpec((n, blk), lambda i: (at, i))
    return pl.pallas_call(
        group_kernel,
        grid=(slots // blk,),
        in_specs=[SMEM, tall(width, 0)]
        + [pl.BlockSpec((cols, 1), lambda i, n=n: (n * GROUPS + group, 0)) for n in range(3)]
        + [tall(cols // 2, group)] * 2
        + [HBM] * SHARDS,
        out_specs=[tall(cols, 0)] * 3,
        out_shape=[jax.ShapeDtypeStruct((cols, slots), BF)] * 3,
        scratch_shapes=[
            pltpu.VMEM((SHARDS, 3 * width // SHARDS, cols), BF),
            pltpu.VMEM((3, cols, width), BF),
            pltpu.SemaphoreType.DMA((SHARDS,)),
        ],
        compiler_params=params(),
        cost_estimate=cost(7),
        name="qkv_group",
    )(order, a_t, bias, bias, bias, cos, sin, *pieces)


def out_moves(w_scr, start):
    rows = w_scr.shape[1]
    half = w_scr.shape[2] // 2
    return [
        (slice(start + i * rows, start + (i + 1) * rows), lambda d, i=i: w_scr.at[d, :, pl.ds(i * half, half)])
        for i in range(2)
    ]


def out_group_kernel(start, order_ref, vec_ref, *rest):
    o_refs, x_ref, pieces = rest[:GROUPS], rest[GROUPS], rest[GROUPS + 1 : GROUPS + 1 + SHARDS]
    h_ref, c_ref, ct_ref, w_scr, sem = rest[GROUPS + 1 + SHARDS :]

    @pl.when(pl.program_id(0) == 0)
    def _():
        copies = fetch(pieces, order_ref, out_moves(w_scr, start), sem)
        start_all(copies)
        wait_all(copies)

    width = x_ref.shape[1]
    o = jnp.concatenate([r[...].T for r in o_refs], axis=1)
    h = x_ref[...].astype(F32) + (nn(o, w_scr[...].reshape(width, width)) + vec_ref[0:1, :])
    h_ref[...] = h
    xhat, _ = norm_parts(h)
    c = (xhat * vec_ref[2:3, :] + vec_ref[3:4, :]).astype(BF)
    c_ref[...] = c
    ct_ref[...] = c.T


def out_project_fast(order, o, x, vec, pieces, start):
    slots, width = x.shape
    blk = 256
    rows = pl.BlockSpec((blk, width), lambda i: (i, 0))
    cols = pl.BlockSpec((width, blk), lambda i: (0, i))
    return pl.pallas_call(
        partial(out_group_kernel, start),
        grid=(slots // blk,),
        in_specs=[SMEM, VMEM] + [pl.BlockSpec((width // GROUPS, blk), lambda i: (0, i))] * GROUPS + [rows] + [HBM] * SHARDS,
        out_specs=[rows, rows, cols],
        out_shape=[
            jax.ShapeDtypeStruct((slots, width), F32),
            jax.ShapeDtypeStruct((slots, width), BF),
            jax.ShapeDtypeStruct((width, slots), BF),
        ],
        scratch_shapes=[pltpu.VMEM((SHARDS, width // SHARDS, width), BF), pltpu.SemaphoreType.DMA((2 * SHARDS,))],
        compiler_params=params(),
        cost_estimate=cost(8),
        name="out_project",
    )(order, vec, *o, x, *pieces)


def mlp_half_kernel(part, first, split, n_in, order_ref, c_ref, ct_ref, dy_ref, b1_ref, vec_ref, *rest):
    acc_in, rest = (rest[:1], rest[1:]) if first else (rest[:2], rest[2:])
    pieces, rest = rest[:n_in], rest[n_in:]
    n_g = 2 if split else 1
    y_ref, dc_ref = rest[:2]
    g_refs = rest[2 : 2 + n_g]
    gb1_ref, w1_scr, w2_scr, g1_scr, g2_scr, hb_scr, dp_scr, y_acc, dc_acc, sem, load_sem = rest[2 + n_g : 13 + n_g]
    y_out = y_acc if first else rest[13 + n_g]
    slots, width = c_ref.shape
    rows1 = w1_scr.shape[2]
    rows2 = w2_scr.shape[1]
    blk = w1_scr.shape[3]
    steps = w1_scr.shape[0]
    per = blk // rows2
    tile = 512
    refs = [pieces[0].at[p] for p in range(SHARDS)] if n_in == 1 else pieces
    places = range(SHARDS) if n_in == 1 else order_ref
    loads = [
        fetch(refs, places, [(slice(j * rows1, (j + 1) * rows1), lambda d, j=j: w1_scr.at[j, d])], sem.at[j])
        for j in range(steps)
    ]
    loads.insert(1, fetch(refs, places, [(slice(steps * rows1, steps * rows1 + rows2), lambda d: w2_scr.at[d])], sem.at[steps]))
    sums = [pltpu.make_async_copy(src, dst, load_sem.at[i]) for i, (src, dst) in enumerate(zip(acc_in, (y_acc, dc_acc)))]
    for copies in loads[:2] + [sums] + loads[2:]:
        start_all(copies)
    sends = []
    for j in range(steps):
        cols = slice(j * blk, (j + 1) * blk)
        wait_all(loads[0] if j == 0 else loads[1 + j])
        w1 = w1_scr[j].reshape(width, blk)
        if j == 0:
            wait_all(loads[1] + sums)
        w2 = w2_scr[j * per : (j + 1) * per].reshape(blk, width)
        total = None
        for i in range(slots // tile):
            rows = slice(i * tile, (i + 1) * tile)
            pre = nn(c_ref[rows, :], w1) + b1_ref[part : part + 1, cols]
            square = pre * pre
            th = jnp.tanh(GELU_C * (pre + GELU_A * (pre * square)))
            cdf = 0.5 * (1.0 + th)
            hb = (pre * cdf).astype(BF)
            slope = cdf + 0.5 * pre * (1.0 - th * th) * (GELU_C * (1.0 + (3.0 * GELU_A) * square))
            hb_scr[rows, :] = hb
            y = y_acc[rows, :] + nn(hb, w2)
            if first and j == 0:
                y = y + vec_ref[4:5, :]
            dpre = (nt(dy_ref[rows, :], w2) * slope).astype(BF)
            dp_scr[rows, :] = dpre
            term = jnp.sum(dpre.astype(F32), axis=0, keepdims=True)
            total = term if total is None else total + term
            dc = nt(dpre, w1)
            if not (first and j == 0):
                dc = dc + dc_acc[rows, :]
            dc_acc[rows, :] = dc
            if j == steps - 1:
                y_out[rows, :] = y.astype(y_out.dtype)
                sends += [
                    pltpu.make_async_copy(y_out.at[rows], y_ref.at[rows], load_sem.at[2 + 2 * i]),
                    pltpu.make_async_copy(dc_acc.at[rows], dc_ref.at[rows], load_sem.at[3 + 2 * i]),
                ]
                start_all(sends[-2:])
            else:
                y_acc[rows, :] = y
        gb1_ref[:, cols] = total
        g1_scr[j] = nn(ct_ref[...], dp_scr[...]).astype(BF).reshape(SHARDS, rows1, blk)
        if split:
            mine = order_ref[SHARDS]
            dests = [(g_refs[b], i, order_ref[p + b]) for b in range(2) for i, p in enumerate(LEAVING)]
            place = lambda dst, i, lo, n: dst.at[lax.rem(lo // (steps * rows1) + mine, 2), i, pl.ds(lo % (steps * rows1), n)]
        else:
            dests = [(g_refs[0], p, p) for p in range(SHARDS)]
            place = lambda dst, i, lo, n: dst.at[i, pl.ds(lo, n)]
        copies = [
            pltpu.make_async_copy(g1_scr.at[j, d], place(dst, i, j * rows1, rows1), sem.at[j, n])
            for n, (dst, i, d) in enumerate(dests)
        ]
        start_all(copies)
        sends += copies
        g2_scr[j * per : (j + 1) * per] = tn(hb_scr[...], dy_ref[...]).astype(BF).reshape(per, rows2, width)
    copies = [
        pltpu.make_async_copy(g2_scr.at[d], place(dst, i, steps * rows1, rows2), sem.at[steps, n])
        for n, (dst, i, d) in enumerate(dests)
    ]
    start_all(copies)
    wait_all(sends + copies)


def mlp_half(part, order, c, ct, dy, b1, vec, sums, pieces, split):
    slots, width = c.shape
    rows1 = width // SHARDS
    rows2 = pieces[0].shape[-2] - 2 * rows1
    hidden = rows2 * SHARDS
    steps = 2
    blk = hidden // steps
    first = len(sums) == 1
    block = jax.ShapeDtypeStruct((SHARDS, 2 * rows1 + rows2, width), BF)
    if split:
        block = jax.ShapeDtypeStruct((2, SHARDS // 2, rows2, width), BF)
    return pl.pallas_call(
        partial(mlp_half_kernel, part, first, split, len(pieces)),
        in_specs=[SMEM] + [VMEM] * 5 + [ANY] * len(sums) + [HBM] * len(pieces),
        out_specs=[ANY, ANY] + [ANY] * (2 if split else 1) + [VMEM],
        out_shape=[jax.ShapeDtypeStruct((slots, width), F32 if first else BF), jax.ShapeDtypeStruct((slots, width), F32)]
        + [block] * (2 if split else 1)
        + [jax.ShapeDtypeStruct((1, hidden), F32)],
        scratch_shapes=[
            pltpu.VMEM((steps, SHARDS, rows1, blk), BF),
            pltpu.VMEM((SHARDS, rows2, width), BF),
            pltpu.VMEM((steps, SHARDS, rows1, blk), BF),
            pltpu.VMEM((SHARDS, rows2, width), BF),
            pltpu.VMEM((slots, blk), BF),
            pltpu.VMEM((slots, blk), BF),
            pltpu.VMEM((slots, width), F32),
            pltpu.VMEM((slots, width), F32),
            pltpu.SemaphoreType.DMA((steps + 1, SHARDS)),
            pltpu.SemaphoreType.DMA((8,)),
        ]
        + ([] if first else [pltpu.VMEM((slots, width), BF)]),
        compiler_params=params(),
        cost_estimate=cost(23),
        name="mlp_half",
    )(order, c, ct, dy, b1, vec, *sums, *pieces)


def out_back_fast_kernel(start, order_ref, dc_ref, h_ref, dy_ref, vec_ref, *rest):
    o_refs, pieces = rest[:GROUPS], rest[GROUPS : GROUPS + SHARDS]
    dh_ref, do_ref, near_ref, far_ref, sums_ref, acc_ref, g_scr, w_scr, sem = rest[GROUPS + SHARDS :]
    i = pl.program_id(0)
    width = h_ref.shape[1]
    each = width // SHARDS
    half = width // 2

    @pl.when(i == 0)
    def _():
        copies = fetch(pieces, order_ref, out_moves(w_scr, start), sem)
        start_all(copies)
        acc_ref[...] = jnp.zeros_like(acc_ref)
        sums_ref[...] = jnp.zeros_like(sums_ref)
        wait_all(copies)

    dy = dy_ref[...].astype(F32)
    part, dgain, dshift = norm_back(dc_ref[...], h_ref[...], vec_ref[2:3, :])
    dh = dy + part
    dh_ref[...] = dh
    dhb = dh.astype(BF)
    do_ref[...] = nt(w_scr[...].reshape(width, width), dhb).astype(BF)
    rows = width // GROUPS
    for g in range(GROUPS):
        acc_ref[g * rows : (g + 1) * rows, :] += nn(o_refs[g][...], dhb)
    sums_ref[0:1, :] += dgain
    sums_ref[1:2, :] += dshift
    sums_ref[2:3, :] += jnp.sum(dh, axis=0, keepdims=True)
    sums_ref[3:4, :] += jnp.sum(dy, axis=0, keepdims=True)

    @pl.when(i == pl.num_programs(0) - 1)
    def _():
        g_scr[...] = acc_ref[...].astype(BF).reshape(g_scr.shape)
        copies = []
        for b, out in enumerate((near_ref, far_ref)):
            for n, p in enumerate(LEAVING):
                for k in range(2):
                    src = g_scr.at[order_ref[p + b], :, pl.ds(k * half, half)]
                    dst = out.at[n, pl.ds(k * each, each)]
                    copies.append(pltpu.make_async_copy(src, dst, sem.at[len(copies)]))
        start_all(copies)
        wait_all(copies)


def out_back_fast(order, dc, h, dy, vec, o, pieces, start):
    slots, width = h.shape
    blk = 256
    rows = pl.BlockSpec((blk, width), lambda i: (i, 0))
    cols = pl.BlockSpec((width, blk), lambda i: (0, i))
    whole = lambda r, k: pl.BlockSpec((r, k), lambda i: (0, 0))
    block = jax.ShapeDtypeStruct((SHARDS // 2, 2 * width // SHARDS, width // 2), BF)
    return pl.pallas_call(
        partial(out_back_fast_kernel, start),
        grid=(slots // blk,),
        in_specs=[SMEM, rows, rows, rows, VMEM]
        + [pl.BlockSpec((width // GROUPS, blk), lambda i: (0, i))] * GROUPS
        + [HBM] * SHARDS,
        out_specs=[rows, cols, ANY, ANY, whole(8, width)],
        out_shape=[
            jax.ShapeDtypeStruct((slots, width), F32),
            jax.ShapeDtypeStruct((width, slots), BF),
            block,
            block,
            jax.ShapeDtypeStruct((8, width), F32),
        ],
        scratch_shapes=[
            pltpu.VMEM((width, width), F32),
            pltpu.VMEM((SHARDS, width // SHARDS, width), BF),
            pltpu.VMEM((SHARDS, width // SHARDS, width), BF),
            pltpu.SemaphoreType.DMA((2 * SHARDS,)),
        ],
        compiler_params=params(),
        cost_estimate=cost(12),
        name="out_back",
    )(order, dc, h, dy, vec, *o, *pieces)


def heads_back_kernel(
    counts_ref, q_ref, k_ref, v_ref, o_ref, do_ref, lse_ref, cos_ref, sin_ref,
    dq_ref, dk_ref, dv_ref, dangle_ref, bias_ref,
):
    slots = q_ref.shape[1]

    @pl.when(pl.program_id(0) == 0)
    def _():
        bias_ref[...] = second_bias(counts_ref, slots)

    lane1 = lax.broadcasted_iota(jnp.int32, (1, WIDE), 1)
    lane2 = lax.broadcasted_iota(jnp.int32, (1, slots - CUT), 1)
    scale = HEAD_DIM**-0.5

    def part(scores, grads, queries, outs, keys, delta_row, first):
        prob = jnp.exp(scores)
        ds = (prob * (grads - delta_row)).astype(BF)
        pb = prob.astype(BF)
        gap = jnp.zeros((keys.shape[1] - pb.shape[0], pb.shape[1]), BF)
        pb = jnp.concatenate([pb, gap] if first else [gap, pb], axis=0)
        ds = jnp.concatenate([ds, gap] if first else [gap, ds], axis=0)
        return nn(keys, ds), nt(queries, ds), nt(outs, pb)

    for h in range(q_ref.shape[0] // HEAD_DIM):
        top = h * HEAD_DIM
        rows = slice(top, top + HEAD_DIM)
        kt = k_ref[rows, :]
        k = kt.T
        v = v_ref[rows, :].T
        q = q_ref[rows, :]
        do = do_ref[rows, :]
        lse = lse_ref[h]
        delta = jnp.sum(do.astype(F32) * o_ref[rows, :].astype(F32), axis=0, keepdims=True)
        lse1 = jnp.where(lane1 < FIRST, lse[:, :WIDE], -NEG)
        lse2 = jnp.where(lane2 >= FIRST - CUT, lse[:, CUT:], -NEG)
        grads1 = part(
            nn(k[:FIRST], q[:, :WIDE]) - lse1, nn(v[:FIRST], do[:, :WIDE]),
            q[:, :WIDE], do[:, :WIDE], kt[:, :WIDE], delta[:, :WIDE], True,
        )
        grads2 = part(
            nn(k[FIRST:], q[:, CUT:]) + bias_ref[...] - lse2, nn(v[FIRST:], do[:, CUT:]),
            q[:, CUT:], do[:, CUT:], kt[:, CUT:], delta[:, CUT:], False,
        )
        dq, dk, dv = (
            jnp.concatenate([one[:, :CUT], one[:, CUT:] + two[:, : WIDE - CUT], two[:, WIDE - CUT :]], axis=1)
            for one, two in zip(grads1, grads2)
        )
        cos = cos_ref[h * HALF : (h + 1) * HALF, :]
        sin = sin_ref[h * HALF : (h + 1) * HALF, :]
        dangle = None
        for r, rot, out in ((dq * scale, q.astype(F32) * (1.0 / scale), dq_ref), (dk, kt.astype(F32), dk_ref)):
            r1, r2 = r[:HALF], r[HALF:]
            term = r2 * rot[:HALF] - r1 * rot[HALF:]
            dangle = term if dangle is None else dangle + term
            out[top : top + HALF, :] = (r1 * cos + r2 * sin).astype(BF)
            out[top + HALF : top + HEAD_DIM, :] = (r2 * cos - r1 * sin).astype(BF)
        dv_ref[rows, :] = dv.astype(BF)
        dangle_ref[h * HALF : (h + 1) * HALF, :] = dangle.astype(BF)


def heads_back(group, counts, q, k, v, o, do, lse, cos, sin):
    width, slots = q.shape
    heads = width // HEAD_DIM
    each = 2
    steps = heads // each
    head = pl.BlockSpec((each * HEAD_DIM, slots), lambda h: (h, 0))
    half = pl.BlockSpec((each * HALF, slots), lambda h: (h, 0))
    turn = pl.BlockSpec((each * HALF, slots), lambda h: (group * steps + h, 0))
    late = pl.BlockSpec((each * HEAD_DIM, slots), lambda h: (group * steps + h, 0))
    return pl.pallas_call(
        heads_back_kernel,
        grid=(steps,),
        in_specs=[SMEM] + [head] * 4 + [late, pl.BlockSpec((each, 1, slots), lambda h: (h, 0, 0)), turn, turn],
        out_specs=[head] * 3 + [half],
        out_shape=[jax.ShapeDtypeStruct((width, slots), BF)] * 3 + [jax.ShapeDtypeStruct((width // 2, slots), BF)],
        scratch_shapes=[pltpu.VMEM((slots - FIRST, slots - CUT), F32)],
        compiler_params=params(20),
        cost_estimate=cost(13),
        name="heads_back",
    )(counts, q, k, v, o, do, lse, cos, sin)


def qkv_grad_kernel(order_ref, at_ref, sel_ref, dangle_ref, dq_ref, dk_ref, dv_ref, *rest):
    more, (near_ref, far_ref, bias_ref, freq_ref, g_scr, sem, more_sem) = rest[:-7], rest[-7:]
    part = g_scr.shape[1] // 3
    outs = (near_ref, far_ref)
    extra = [
        pltpu.make_async_copy(ref.at[n], out.at[n, pl.ds(3 * part, ref.shape[1])], more_sem.at[b, n])
        for b, (ref, out) in enumerate(zip(more, outs))
        for n in range(SHARDS // 2)
    ]
    start_all(extra)
    at = at_ref[...]
    for i, ref in enumerate((dq_ref, dk_ref, dv_ref)):
        g = nt(at, ref[...]).astype(BF)
        g_scr[:, i * part : (i + 1) * part, :] = g.reshape(SHARDS, part, g.shape[1])
        bias_ref[:, i * g.shape[1] : (i + 1) * g.shape[1]] = nt(sel_ref[...], ref[...])
    freq_ref[...] = nt(sel_ref[...], dangle_ref[...])
    copies = []
    for b, out in enumerate(outs):
        for n, p in enumerate(LEAVING):
            dst = out.at[n, pl.ds(0, 3 * part)]
            copies.append(pltpu.make_async_copy(g_scr.at[order_ref[p + b]], dst, sem.at[len(copies)]))
    start_all(copies)
    wait_all(copies + extra)


def qkv_grad(order, at, sel, dangle, dq, dk, dv, *more):
    width, slots = at.shape
    cols = dq.shape[0]
    rows = 3 * width // SHARDS
    total = rows + (more[0].shape[1] if more else 0)
    return pl.pallas_call(
        qkv_grad_kernel,
        in_specs=[SMEM] + [VMEM] * (6 + len(more)),
        out_specs=[ANY, ANY, VMEM, VMEM],
        out_shape=[jax.ShapeDtypeStruct((SHARDS // 2, total, cols), BF)] * 2
        + [jax.ShapeDtypeStruct((sel.shape[0], 3 * cols), F32), jax.ShapeDtypeStruct((sel.shape[0], cols // 2), F32)],
        scratch_shapes=[
            pltpu.VMEM((SHARDS, rows, cols), BF),
            pltpu.SemaphoreType.DMA((SHARDS,)),
            pltpu.SemaphoreType.DMA((2, SHARDS // 2)),
        ],
        compiler_params=params(16),
        cost_estimate=cost(6),
        name="qkv_grad",
    )(order, at, sel, dangle, dq, dk, dv, *more)


def part_kernel(order_ref, *rest):
    grads, pieces, (da_ref, w_scr, sem) = rest[:3], rest[3 : 3 + SHARDS], rest[3 + SHARDS :]
    add_group(order_ref, grads, pieces, da_ref, w_scr, sem)


def group_weights(order_ref, pieces, w_scr, sem):
    rows = w_scr.shape[1]
    copies = fetch(pieces, order_ref, [(slice(0, rows), lambda d: w_scr.at[d])], sem)
    start_all(copies)
    wait_all(copies)


def group_product(grads, w_scr):
    rows = w_scr.shape[1] // 3
    total = None
    for n in range(3):
        w = w_scr[:, n * rows : (n + 1) * rows, :].reshape(SHARDS * rows, w_scr.shape[2])
        term = nn(w, grads[n][...])
        total = term if total is None else total + term
    return total


def add_group(order_ref, grads, pieces, da_ref, w_scr, sem):
    @pl.when(pl.program_id(0) == 0)
    def _():
        group_weights(order_ref, pieces, w_scr, sem)

    da_ref[...] = group_product(grads, w_scr)


def input_part(order, grads, pieces, width):
    cols, slots = grads[0].shape
    blk = 512
    return pl.pallas_call(
        part_kernel,
        grid=(slots // blk,),
        in_specs=[SMEM] + [pl.BlockSpec((cols, blk), lambda i: (0, i))] * 3 + [HBM] * SHARDS,
        out_specs=pl.BlockSpec((width, blk), lambda i: (0, i)),
        out_shape=jax.ShapeDtypeStruct((width, slots), F32),
        scratch_shapes=[pltpu.VMEM((SHARDS, 3 * width // SHARDS, cols), BF), pltpu.SemaphoreType.DMA((SHARDS,))],
        compiler_params=params(16),
        cost_estimate=cost(6),
        name="input_part",
    )(order, *grads, *pieces)


def input_kernel(order_ref, x_ref, dh_ref, vec_ref, da_ref, *rest):
    grads, pieces, (dx_ref, sums_ref, w_scr, sem) = rest[:3], rest[3 : 3 + SHARDS], rest[3 + SHARDS :]

    @pl.when(pl.program_id(0) == 0)
    def _():
        group_weights(order_ref, pieces, w_scr, sem)
        sums_ref[...] = jnp.zeros_like(sums_ref)

    da = da_ref[...] + group_product(grads, w_scr)
    out, dgain, dshift = norm_back(da.T, x_ref[...].astype(F32), vec_ref[1:2, :])
    dx_ref[...] = (dh_ref[...] + out).astype(BF)
    sums_ref[0:1, :] += dgain
    sums_ref[1:2, :] += dshift


def input_back(order, x, dh, vec, da, grads, pieces):
    slots, width = x.shape
    cols = grads[0].shape[0]
    blk = 512
    rows = pl.BlockSpec((blk, width), lambda i: (i, 0))
    return pl.pallas_call(
        input_kernel,
        grid=(slots // blk,),
        in_specs=[SMEM, rows, rows, VMEM, pl.BlockSpec((width, blk), lambda i: (0, i))]
        + [pl.BlockSpec((cols, blk), lambda i: (0, i))] * 3
        + [HBM] * SHARDS,
        out_specs=[rows, pl.BlockSpec((8, width), lambda i: (0, 0))],
        out_shape=[jax.ShapeDtypeStruct((slots, width), BF), jax.ShapeDtypeStruct((8, width), F32)],
        scratch_shapes=[pltpu.VMEM((SHARDS, 3 * width // SHARDS, cols), BF), pltpu.SemaphoreType.DMA((SHARDS,))],
        compiler_params=params(20),
        cost_estimate=cost(10),
        name="input_back",
    )(order, x, dh, vec, da, *grads, *pieces)


def body_fast(
    tokens, cotangent, image_counts, patch_rows, patch_cols, ln1_gain, ln1_bias, qkv_weight, qkv_bias, rope_freqs,
    out_weight, out_bias, ln2_gain, ln2_bias, fc1_weight, fc1_bias, fc2_weight, fc2_bias,
):
    x = tokens[0]
    dy = cotangent[0]
    counts = image_counts[0]
    slots, width = x.shape
    cols = width // GROUPS
    half = width // 2
    order = lax.axis_index("fsdp") ^ jnp.arange(SHARDS, dtype=jnp.int32)
    order = jnp.concatenate([order, lax.axis_index("rep")[None].astype(jnp.int32)])

    own = fc2_weight.shape[0] // 2
    small = (ln1_gain, ln1_bias, qkv_bias, rope_freqs, out_bias, ln2_gain, ln2_bias, fc1_bias, fc2_bias)
    sizes = [s.shape[0] for s in small]
    vectors = jnp.concatenate(small + (jnp.zeros((2 * cols - sum(sizes),), BF),)).reshape(2, cols)
    piece_c, piece_d = mlp_pieces(fc1_weight, fc2_weight)
    piece_a, piece_b = group_pieces(qkv_weight, out_weight, vectors)
    pieces_c = [lax.all_gather(piece_c, "fsdp", axis=0)]
    pieces_d = [lax.all_gather(piece_d, "fsdp", axis=0)]
    first = lambda g: (g.piece[8], g.piece[4], g.piece[2])
    second = lambda g: (g.piece[12], g.piece[6], g.piece[10])
    gather_a = Gather(piece_a)
    gather_a.stage1()
    gather_a.stage2(*first(gather_a))
    gather_a.stage3()
    pieces_a = gather_a.cores()
    gather_b = Gather(piece_b)
    gather_b.stage1(gather_a.piece[12])
    a_t, cos, sin, vec, b1, bias, sel = prepare(sizes, order, x, patch_cols, patch_rows, pieces_a)
    gather_b.stage2(sel)
    q, k, v = project_group(0, order, a_t, bias, cos, sin, pieces_a)
    gather_b.hold((12, 6, 10), q)
    gather_b.stage3()
    heads = [(q, k, v) + tuple(attend(counts, q, k, v))]
    gather_b.hold((14,), heads[0][3])
    pieces_b = gather_b.cores()
    q, k, v = project_group(1, order, a_t, bias, cos, sin, pieces_b)
    heads.append((q, k, v) + tuple(attend(counts, q, k, v)))
    o = [t[3] for t in heads]
    at_out = piece_b.shape[0] - 2 * out_weight.shape[0]
    h, c, c_t = out_project_fast(order, o, x, vec, pieces_b, at_out)
    y, dc, g_c, g_b1a = mlp_half(0, order, c, c_t, dy, b1, vec, (h,), pieces_c, False)
    mlp_c = lax.psum_scatter(tie(g_c, pieces_d[0]), "fsdp", scatter_dimension=0, tiled=True)[0]
    y, dc, near_d, far_d, g_b1b = mlp_half(1, order, c, c_t, dy, b1, vec, (y, dc), pieces_d, True)
    scatter_d = SplitScatter(near_d, far_d)
    dh, do, near_o, far_o, sums2 = out_back_fast(order, dc, h, dy, vec, o, pieces_b, at_out)

    def back(g, do):
        q, k, v, og, lse = heads[g]
        *three, dangle = heads_back(g, counts, q, k, v, og, do, lse, cos, sin)
        return three, dangle

    sent = scatter_d.split()
    grads_b, dangle_b = back(1, tie(do, sent))
    near_b, far_b, bias_b, freq_b = qkv_grad(order, a_t, sel, dangle_b, *grads_b, near_o, far_o)
    scatter_b = Scatter(near_b, far_b)
    scatter_d.hold(near_b)
    sent = scatter_d.step()
    grads_a, dangle_a = back(0, tie(do, sent, near_b))
    scatter_d.hold(dangle_a)
    scatter_b.hold(dangle_a)
    sent = (scatter_d.step(), scatter_b.step())
    near_a, far_a, bias_a, freq_a = qkv_grad(order, a_t, sel, tie(dangle_a, *sent), *grads_a)
    scatter_a = Scatter(near_a, far_a)
    da = input_part(order, lax.optimization_barrier((grads_b, near_a))[0], pieces_b, width)
    for scatter in (scatter_d, scatter_b, scatter_a):
        scatter.hold(da)
    sent = (scatter_a.step(), scatter_b.step(), scatter_d.step())
    dx, sums1 = input_back(order, x, dh, vec, tie(da, *sent), grads_a, pieces_a)
    scatter_a.hold(sums1, scatter_b.got[-1], scatter_d.got[-1])
    sent = scatter_a.step()
    scatter_b.hold(sent)
    scatter_d.hold(sent)
    other_c = across(tie(mlp_c, sent))
    sent = (sent, scatter_b.step())
    block = pack(sum(sizes), tie(sums1, *sent), sums2, g_b1a, g_b1b, bias_a, bias_b, freq_a, freq_b)
    mlp_d = scatter_d.finish()
    scatter_a.hold(block)
    sent = scatter_a.step()
    mine_b = scatter_b.finish()
    mine = jnp.sum(lax.all_to_all(block, "fsdp", 0, 0, tiled=True), axis=0)
    rows1 = width // SHARDS
    s_w1, s_w2 = mlp_join(rows1, order, (mlp_c, other_c) + mlp_d)
    scatter_a.hold(mine, other_c)
    mine_a = scatter_a.finish()
    mine_a = (mine_a[0], tie(mine_a[1], s_w1))
    mine = mine + across(mine)
    s_a = mine_a[0].astype(F32) + mine_a[1].astype(F32)
    s_b = mine_b[0].astype(F32) + mine_b[1].astype(F32)
    s_wqkv = jnp.concatenate([s[i * rows1 : (i + 1) * rows1] for i in range(3) for s in (s_a, s_b)], axis=1)
    s_wout = jnp.concatenate([s_b[3 * rows1 : 4 * rows1], s_b[4 * rows1 :]], axis=1)

    outs = []
    at = 0
    for size in sizes:
        outs.append(mine[at : at + size])
        at += size
    s_gain1, s_shift1, s_bqkv, s_freq, s_bout, s_gain2, s_shift2, s_b1, s_b2 = outs
    return (
        y[None], dx[None], s_gain1, s_shift1, s_wqkv, s_bqkv, s_freq, s_wout, s_bout,
        s_gain2, s_shift2, s_w1, s_b1, s_w2, s_b2,
    )


def solution(mesh):
    row = P(("rep", "fsdp"), None)
    rows = P(("rep", "fsdp"), None, None)
    vec = P("fsdp")
    mat = P("fsdp", None)
    in_specs = (rows, rows, row, row, row, vec, vec, mat, vec, vec, mat, vec, vec, vec, mat, vec, mat, vec)
    out_specs = (rows, rows, vec, vec, mat, vec, vec, mat, vec, vec, vec, mat, vec, mat, vec)
    fast = mesh.shape["fsdp"] == SHARDS and mesh.shape["rep"] == 2
    return jax.shard_map(
        body_fast if fast else body_any, mesh=mesh, in_specs=in_specs, out_specs=out_specs, check_vma=False
    )
```

```python
from functools import partial

import jax
import jax.numpy as jnp
from jax import lax
from jax.experimental import pallas as pl
from jax.experimental.pallas import tpu as pltpu
from jax.sharding import PartitionSpec as P

HEADS = 12
HEAD_DIM = 64
HALF = HEAD_DIM // 2
FIRST = 576
CUT = 512
WIDE = 640
NEG = -1e30
EPS = 1e-6
BF = jnp.bfloat16
F32 = jnp.float32
GELU_C = 0.7978845608028654
GELU_A = 0.044715


def nn(a, b):
    return lax.dot_general(a, b, (((1,), (0,)), ((), ())), preferred_element_type=F32)


def nt(a, b):
    return lax.dot_general(a, b, (((1,), (1,)), ((), ())), preferred_element_type=F32)


def tn(a, b):
    return lax.dot_general(a, b, (((0,), (0,)), ((), ())), preferred_element_type=F32)


def params(mib=56):
    return pltpu.CompilerParams(vmem_limit_bytes=mib << 20)


def cost(us):
    return pl.CostEstimate(flops=int(us * 1.1e9), bytes_accessed=1 << 16, transcendentals=0)


def norm_parts(v):
    mean = jnp.mean(v, axis=-1, keepdims=True)
    dev = v - mean
    var = jnp.mean(dev * dev, axis=-1, keepdims=True)
    inv = lax.rsqrt(var + EPS)
    return dev * inv, inv


def lane_partial(v):
    total = v[:, :128]
    for i in range(1, v.shape[1] // 128):
        total = total + v[:, i * 128 : (i + 1) * 128]
    return total


def norm1_kernel(x_ref, gain_ref, shift_ref, a_ref, at_ref):
    xhat, _ = norm_parts(x_ref[...].astype(F32))
    a = (xhat * gain_ref[...] + shift_ref[...]).astype(BF)
    a_ref[...] = a
    at_ref[...] = a.T


def norm1(x, gain, shift):
    slots, width = x.shape
    blk = 256
    return pl.pallas_call(
        norm1_kernel,
        grid=(slots // blk,),
        in_specs=[
            pl.BlockSpec((blk, width), lambda i: (i, 0)),
            pl.BlockSpec((1, width), lambda i: (0, 0)),
            pl.BlockSpec((1, width), lambda i: (0, 0)),
        ],
        out_specs=[
            pl.BlockSpec((blk, width), lambda i: (i, 0)),
            pl.BlockSpec((width, blk), lambda i: (0, i)),
        ],
        out_shape=[
            jax.ShapeDtypeStruct((slots, width), BF),
            jax.ShapeDtypeStruct((width, slots), BF),
        ],
        compiler_params=params(),
        cost_estimate=cost(5),
        name="norm1",
    )(x, gain, shift)


def qkv_kernel(a_ref, wq_ref, wk_ref, wv_ref, bq_ref, bk_ref, bv_ref, cos_ref, sin_ref, q_ref, k_ref, v_ref):
    heads = wq_ref.shape[1] // HEAD_DIM
    a = a_ref[...]
    cos = cos_ref[...]
    sin = sin_ref[...]
    for w_ref, b_ref, out_ref, scale in ((wq_ref, bq_ref, q_ref, HEAD_DIM**-0.5), (wk_ref, bk_ref, k_ref, 1.0)):
        u = nt(w_ref[...].T, a) + b_ref[...]
        for h in range(heads):
            u1 = u[h * HEAD_DIM : h * HEAD_DIM + HALF]
            u2 = u[h * HEAD_DIM + HALF : (h + 1) * HEAD_DIM]
            c = cos[h * HALF : (h + 1) * HALF]
            s = sin[h * HALF : (h + 1) * HALF]
            out_ref[h * HEAD_DIM : h * HEAD_DIM + HALF, :] = ((u1 * c - u2 * s) * scale).astype(BF)
            out_ref[h * HEAD_DIM + HALF : (h + 1) * HEAD_DIM, :] = ((u1 * s + u2 * c) * scale).astype(BF)
    v_ref[...] = (nt(wv_ref[...].T, a) + bv_ref[...]).astype(BF)


def project(a, w, bias, cos, sin):
    slots, width = a.shape
    cols = 256
    groups = width // cols
    wspec = lambda part: pl.BlockSpec((width, cols), lambda g: (0, part * groups + g))
    bspec = lambda part: pl.BlockSpec((cols, 1), lambda g: (part * groups + g, 0))
    out = pl.BlockSpec((cols, slots), lambda g: (g, 0))
    return pl.pallas_call(
        qkv_kernel,
        grid=(groups,),
        in_specs=[pl.BlockSpec((slots, width), lambda g: (0, 0))]
        + [wspec(i) for i in range(3)]
        + [bspec(i) for i in range(3)]
        + [pl.BlockSpec((cols // 2, slots), lambda g: (g, 0))] * 2,
        out_specs=[out] * 3,
        out_shape=[jax.ShapeDtypeStruct((width, slots), BF)] * 3,
        compiler_params=params(),
        name="qkv",
    )(a, w, w, w, bias, bias, bias, cos, sin)


def second_bias(counts_ref, slots):
    shape = (slots - FIRST, slots - CUT)
    key = lax.broadcasted_iota(jnp.int32, shape, 0) + FIRST
    query = lax.broadcasted_iota(jnp.int32, shape, 1) + CUT
    end0 = counts_ref[0]
    end1 = end0 + counts_ref[1]
    end2 = end1 + counts_ref[2]

    def seg(place):
        return (place >= end0).astype(jnp.int32) + (place >= end1).astype(jnp.int32)

    allowed = ((seg(key) == seg(query)) & (key < end2) & (query < end2)) | (key == query)
    return jnp.where(allowed, 0.0, NEG)


def attend_kernel(counts_ref, q_ref, k_ref, v_ref, o_ref, lse_ref, bias_ref):
    slots = q_ref.shape[1]

    @pl.when(pl.program_id(0) == 0)
    def _():
        bias_ref[...] = second_bias(counts_ref, slots)

    def part(scores, first, values):
        peak = jnp.max(scores, axis=0, keepdims=True)
        wb = jnp.exp(scores - peak).astype(BF)
        gap = jnp.zeros((values.shape[1] - wb.shape[0], wb.shape[1]), BF)
        wb = jnp.concatenate([wb, gap] if first else [gap, wb], axis=0)
        lines = jnp.concatenate([values, jnp.ones((16, values.shape[1]), BF)], axis=0)
        mixed = nn(lines, wb)
        total = mixed[HEAD_DIM : HEAD_DIM + 1]
        return mixed[:HEAD_DIM] * (1.0 / total), peak + jnp.log(total)

    edge = lax.broadcasted_iota(jnp.int32, (1, WIDE - CUT), 1) < FIRST - CUT
    for h in range(q_ref.shape[0] // HEAD_DIM):
        rows = slice(h * HEAD_DIM, (h + 1) * HEAD_DIM)
        k = k_ref[rows, :].T
        q = q_ref[rows, :]
        v = v_ref[rows, :]
        mixed1, lse1 = part(nn(k[:FIRST], q[:, :WIDE]), True, v[:, :WIDE])
        mixed2, lse2 = part(nn(k[FIRST:], q[:, CUT:]) + bias_ref[...], False, v[:, CUT:])
        for out, one, two in ((o_ref.at[rows], mixed1, mixed2), (lse_ref.at[h], lse1, lse2)):
            out[:, :CUT] = one[:, :CUT].astype(out.dtype)
            out[:, CUT:WIDE] = jnp.where(edge, one[:, CUT:], two[:, : WIDE - CUT]).astype(out.dtype)
            out[:, WIDE:] = two[:, WIDE - CUT :].astype(out.dtype)


def attend(counts, q, k, v):
    width, slots = q.shape
    heads = width // HEAD_DIM
    each = 2
    head = pl.BlockSpec((each * HEAD_DIM, slots), lambda h: (h, 0))
    return pl.pallas_call(
        attend_kernel,
        grid=(heads // each,),
        in_specs=[pl.BlockSpec(memory_space=pltpu.SMEM)] + [head] * 3,
        out_specs=[head, pl.BlockSpec((each, 1, slots), lambda h: (h, 0, 0))],
        out_shape=[jax.ShapeDtypeStruct((width, slots), BF), jax.ShapeDtypeStruct((heads, 1, slots), F32)],
        scratch_shapes=[pltpu.VMEM((slots - FIRST, slots - CUT), F32)],
        compiler_params=params(),
        cost_estimate=cost(8),
        name="attend",
    )(counts, q, k, v)


def attend_back_kernel(
    counts_ref, q_ref, k_ref, v_ref, o_ref, do_ref, lse_ref, cos_ref, sin_ref, place_ref,
    dq_ref, dk_ref, dv_ref, bq_ref, bk_ref, bv_ref, fc_ref, fr_ref, bias_ref,
):
    slots = q_ref.shape[1]

    @pl.when(pl.program_id(0) == 0)
    def _():
        bias_ref[...] = second_bias(counts_ref, slots)

    kt = k_ref[...]
    k = kt.T
    v = v_ref[...].T
    q = q_ref[...]
    do = do_ref[...]
    lse = lse_ref[0]
    delta = jnp.sum(do.astype(F32) * o_ref[...].astype(F32), axis=0, keepdims=True)
    lane1 = lax.broadcasted_iota(jnp.int32, (1, WIDE), 1)
    lane2 = lax.broadcasted_iota(jnp.int32, (1, slots - CUT), 1)
    lse1 = jnp.where(lane1 < FIRST, lse[:, :WIDE], -NEG)
    lse2 = jnp.where(lane2 >= FIRST - CUT, lse[:, CUT:], -NEG)

    def part(scores, grads, queries, outs, keys, delta_row, first):
        prob = jnp.exp(scores)
        ds = (prob * (grads - delta_row)).astype(BF)
        pb = prob.astype(BF)
        gap = jnp.zeros((keys.shape[1] - pb.shape[0], pb.shape[1]), BF)
        pb = jnp.concatenate([pb, gap] if first else [gap, pb], axis=0)
        ds = jnp.concatenate([ds, gap] if first else [gap, ds], axis=0)
        return nn(keys, ds), nt(queries, ds), nt(outs, pb)

    grads1 = part(
        nn(k[:FIRST], q[:, :WIDE]) - lse1, nn(v[:FIRST], do[:, :WIDE]),
        q[:, :WIDE], do[:, :WIDE], kt[:, :WIDE], delta[:, :WIDE], True,
    )
    grads2 = part(
        nn(k[FIRST:], q[:, CUT:]) + bias_ref[...] - lse2, nn(v[FIRST:], do[:, CUT:]),
        q[:, CUT:], do[:, CUT:], kt[:, CUT:], delta[:, CUT:], False,
    )
    dq, dk, dv = (
        jnp.concatenate([one[:, :CUT], one[:, CUT:] + two[:, : WIDE - CUT], two[:, WIDE - CUT :]], axis=1)
        for one, two in zip(grads1, grads2)
    )
    scale = HEAD_DIM**-0.5
    cos = cos_ref[...]
    sin = sin_ref[...]
    dangle = None
    for r, rot, out, bias_out in ((dq * scale, q.astype(F32) * (1.0 / scale), dq_ref, bq_ref), (dk, kt.astype(F32), dk_ref, bk_ref)):
        r1, r2 = r[:HALF], r[HALF:]
        term = r2 * rot[:HALF] - r1 * rot[HALF:]
        dangle = term if dangle is None else dangle + term
        g1 = (r1 * cos + r2 * sin).astype(BF)
        g2 = (r2 * cos - r1 * sin).astype(BF)
        out[:HALF, :] = g1
        out[HALF:, :] = g2
        bias_out[:HALF, :] = lane_partial(g1.astype(F32))
        bias_out[HALF:, :] = lane_partial(g2.astype(F32))
    dvb = dv.astype(BF)
    dv_ref[...] = dvb
    bv_ref[...] = lane_partial(dvb.astype(F32))
    fc_ref[...] = lane_partial(dangle * place_ref[0:1, :])
    fr_ref[...] = lane_partial(dangle * place_ref[1:2, :])


def attend_back(counts, q, k, v, o, do, lse, cos, sin, places):
    width, slots = q.shape
    heads = width // HEAD_DIM
    head = pl.BlockSpec((HEAD_DIM, slots), lambda h: (h, 0))
    half = pl.BlockSpec((HALF, slots), lambda h: (h, 0))
    return pl.pallas_call(
        attend_back_kernel,
        grid=(heads,),
        in_specs=[pl.BlockSpec(memory_space=pltpu.SMEM)]
        + [head] * 5
        + [pl.BlockSpec((1, 1, slots), lambda h: (h, 0, 0)), half, half]
        + [pl.BlockSpec((2, slots), lambda h: (0, 0))],
        out_specs=[head] * 3
        + [pl.BlockSpec((HEAD_DIM, 128), lambda h: (h, 0))] * 3
        + [pl.BlockSpec((HALF, 128), lambda h: (h, 0))] * 2,
        out_shape=[jax.ShapeDtypeStruct((width, slots), BF)] * 3
        + [jax.ShapeDtypeStruct((width, 128), F32)] * 3
        + [jax.ShapeDtypeStruct((width // 2, 128), F32)] * 2,
        scratch_shapes=[pltpu.VMEM((slots - FIRST, slots - CUT), F32)],
        compiler_params=params(),
        cost_estimate=cost(14),
        name="attend_back",
    )(counts, q, k, v, o, do, lse, cos, sin, places)


def out_kernel(o_ref, x_ref, w_ref, b_ref, gain_ref, shift_ref, h_ref, c_ref, ct_ref):
    h = x_ref[...].astype(F32) + (nn(o_ref[...].T, w_ref[...]) + b_ref[...])
    h_ref[...] = h
    xhat, _ = norm_parts(h)
    c = (xhat * gain_ref[...] + shift_ref[...]).astype(BF)
    c_ref[...] = c
    ct_ref[...] = c.T


def out_project(o, x, w, b, gain, shift):
    slots, width = x.shape
    blk = 256
    row = pl.BlockSpec((1, width), lambda i: (0, 0))
    rows = pl.BlockSpec((blk, width), lambda i: (i, 0))
    cols = pl.BlockSpec((width, blk), lambda i: (0, i))
    return pl.pallas_call(
        out_kernel,
        grid=(slots // blk,),
        in_specs=[cols, rows, pl.BlockSpec((width, width), lambda i: (0, 0)), row, row, row],
        out_specs=[rows, rows, cols],
        out_shape=[
            jax.ShapeDtypeStruct((slots, width), F32),
            jax.ShapeDtypeStruct((slots, width), BF),
            jax.ShapeDtypeStruct((width, slots), BF),
        ],
        compiler_params=params(),
        name="out_project",
    )(o, x, w, b, gain, shift)


def mlp_kernel(c_ref, ct_ref, dy_ref, h_ref, w1_ref, b1_ref, w2_ref, b2_ref, y_ref, dc_ref, g1_ref, g2_ref, gb1_ref, y_acc, hb_scr, dp_scr):
    slots = c_ref.shape[0]
    tile = 256

    @pl.when(pl.program_id(0) == 0)
    def _():
        y_acc[...] = h_ref[...] + b2_ref[...]
        dc_ref[...] = jnp.zeros_like(dc_ref)

    gb1_ref[...] = jnp.zeros_like(gb1_ref)

    def step(i, _):
        rows = pl.ds(pl.multiple_of(i * tile, tile), tile)
        pre = nn(c_ref[rows, :], w1_ref[...]) + b1_ref[...]
        square = pre * pre
        th = jnp.tanh(GELU_C * (pre + GELU_A * (pre * square)))
        cdf = 0.5 * (1.0 + th)
        hb = (pre * cdf).astype(BF)
        slope = cdf + 0.5 * pre * (1.0 - th * th) * (GELU_C * (1.0 + (3.0 * GELU_A) * square))
        hb_scr[rows, :] = hb
        y_acc[rows, :] += nn(hb, w2_ref[...])
        dpre = (nt(dy_ref[rows, :], w2_ref[...]) * slope).astype(BF)
        dp_scr[rows, :] = dpre
        dc_ref[rows, :] += nt(dpre, w1_ref[...])
        gb1_ref[...] += jnp.sum(dpre.astype(F32), axis=0, keepdims=True)
        return 0

    lax.fori_loop(0, slots // tile, step, 0)
    g1_ref[...] = nn(ct_ref[...], dp_scr[...]).astype(g1_ref.dtype)
    g2_ref[...] = tn(hb_scr[...], dy_ref[...]).astype(g2_ref.dtype)

    @pl.when(pl.program_id(0) == pl.num_programs(0) - 1)
    def _():
        y_ref[...] = y_acc[...].astype(BF)


def mlp(c, ct, dy, h, w1, b1, w2, b2):
    slots, width = c.shape
    hidden = w1.shape[1]
    blk = 512
    whole = lambda r, k: pl.BlockSpec((r, k), lambda j: (0, 0))
    return pl.pallas_call(
        mlp_kernel,
        grid=(hidden // blk,),
        in_specs=[
            whole(slots, width),
            whole(width, slots),
            whole(slots, width),
            whole(slots, width),
            pl.BlockSpec((width, blk), lambda j: (0, j)),
            pl.BlockSpec((1, blk), lambda j: (0, j)),
            pl.BlockSpec((blk, width), lambda j: (j, 0)),
            whole(1, width),
        ],
        out_specs=[
            whole(slots, width),
            whole(slots, width),
            pl.BlockSpec((width, blk), lambda j: (0, j)),
            pl.BlockSpec((blk, width), lambda j: (j, 0)),
            pl.BlockSpec((1, blk), lambda j: (0, j)),
        ],
        out_shape=[
            jax.ShapeDtypeStruct((slots, width), BF),
            jax.ShapeDtypeStruct((slots, width), F32),
            jax.ShapeDtypeStruct((width, hidden), BF),
            jax.ShapeDtypeStruct((hidden, width), BF),
            jax.ShapeDtypeStruct((1, hidden), F32),
        ],
        scratch_shapes=[
            pltpu.VMEM((slots, width), F32),
            pltpu.VMEM((slots, blk), BF),
            pltpu.VMEM((slots, blk), BF),
        ],
        compiler_params=params(),
        name="mlp",
    )(c, ct, dy, h, w1, b1, w2, b2)


def norm_back(grad, v, gain):
    xhat, inv = norm_parts(v)
    g = grad * gain
    lead = jnp.mean(g, axis=-1, keepdims=True)
    slope = jnp.mean(g * xhat, axis=-1, keepdims=True)
    return (g - lead - xhat * slope) * inv, jnp.sum(grad * xhat, axis=0, keepdims=True), jnp.sum(grad, axis=0, keepdims=True)


def out_back_kernel(dc_ref, h_ref, dy_ref, o_ref, w_ref, gain_ref, dh_ref, do_ref, gw_ref, sums_ref, acc_ref):
    i = pl.program_id(0)

    @pl.when(i == 0)
    def _():
        acc_ref[...] = jnp.zeros_like(acc_ref)
        sums_ref[...] = jnp.zeros_like(sums_ref)

    dy = dy_ref[...].astype(F32)
    part, dgain, dshift = norm_back(dc_ref[...], h_ref[...], gain_ref[...])
    dh = dy + part
    dh_ref[...] = dh
    dhb = dh.astype(BF)
    do_ref[...] = nt(w_ref[...], dhb).astype(BF)
    acc_ref[...] += nn(o_ref[...], dhb)
    sums_ref[0:1, :] += dgain
    sums_ref[1:2, :] += dshift
    sums_ref[2:3, :] += jnp.sum(dh, axis=0, keepdims=True)
    sums_ref[3:4, :] += jnp.sum(dy, axis=0, keepdims=True)

    @pl.when(i == pl.num_programs(0) - 1)
    def _():
        gw_ref[...] = acc_ref[...].astype(gw_ref.dtype)


def out_back(dc, h, dy, o, w, gain):
    slots, width = h.shape
    blk = 256
    rows = pl.BlockSpec((blk, width), lambda i: (i, 0))
    cols = pl.BlockSpec((width, blk), lambda i: (0, i))
    whole = lambda r, k: pl.BlockSpec((r, k), lambda i: (0, 0))
    return pl.pallas_call(
        out_back_kernel,
        grid=(slots // blk,),
        in_specs=[rows, rows, rows, cols, whole(width, width), whole(1, width)],
        out_specs=[rows, cols, whole(width, width), whole(8, width)],
        out_shape=[
            jax.ShapeDtypeStruct((slots, width), F32),
            jax.ShapeDtypeStruct((width, slots), BF),
            jax.ShapeDtypeStruct((width, width), BF),
            jax.ShapeDtypeStruct((8, width), F32),
        ],
        scratch_shapes=[pltpu.VMEM((width, width), F32)],
        compiler_params=params(),
        name="out_back",
    )(dc, h, dy, o, w, gain)


def qkv_back_kernel(at_ref, dqkv_ref, w_ref, x_ref, dh_ref, gain_ref, gw_ref, dx_ref, sums_ref, acc_ref):
    j = pl.program_id(0)

    @pl.when(j == 0)
    def _():
        acc_ref[...] = jnp.zeros_like(acc_ref)

    d = dqkv_ref[...]
    gw_ref[...] = nt(at_ref[...], d).astype(gw_ref.dtype)
    acc_ref[...] += nn(w_ref[...], d)

    @pl.when(j == pl.num_programs(0) - 1)
    def _():
        sums_ref[...] = jnp.zeros_like(sums_ref)
        tile = 256
        for i in range(x_ref.shape[0] // tile):
            rows = slice(i * tile, (i + 1) * tile)
            da = acc_ref[:, rows].T
            part, dgain, dshift = norm_back(da, x_ref[rows, :].astype(F32), gain_ref[...])
            dx_ref[rows, :] = (dh_ref[rows, :] + part).astype(BF)
            sums_ref[0:1, :] += dgain
            sums_ref[1:2, :] += dshift


def qkv_back(at, dqkv, w, x, dh, gain):
    slots, width = x.shape
    outs = w.shape[1]
    blk = 768
    whole = lambda r, k: pl.BlockSpec((r, k), lambda j: (0, 0))
    return pl.pallas_call(
        qkv_back_kernel,
        grid=(outs // blk,),
        in_specs=[
            whole(width, slots),
            pl.BlockSpec((blk, slots), lambda j: (j, 0)),
            pl.BlockSpec((width, blk), lambda j: (0, j)),
            whole(slots, width),
            whole(slots, width),
            whole(1, width),
        ],
        out_specs=[pl.BlockSpec((width, blk), lambda j: (0, j)), whole(slots, width), whole(8, width)],
        out_shape=[
            jax.ShapeDtypeStruct((width, outs), BF),
            jax.ShapeDtypeStruct((slots, width), BF),
            jax.ShapeDtypeStruct((8, width), F32),
        ],
        scratch_shapes=[pltpu.VMEM((width, slots), F32)],
        compiler_params=params(),
        name="qkv_back",
    )(at, dqkv, w, x, dh, gain)


def body_any(
    tokens, cotangent, image_counts, patch_rows, patch_cols, ln1_gain, ln1_bias, qkv_weight, qkv_bias, rope_freqs,
    out_weight, out_bias, ln2_gain, ln2_bias, fc1_weight, fc1_bias, fc2_weight, fc2_bias,
):
    x = tokens[0]
    dy = cotangent[0]
    counts = image_counts[0]
    width = x.shape[1]
    small = (ln1_gain, ln1_bias, qkv_bias, rope_freqs, out_bias, ln2_gain, ln2_bias, fc1_bias, fc2_bias)
    sizes = [s.shape[0] for s in small]
    gather = partial(lax.all_gather, axis_name="fsdp", axis=0, tiled=True)
    packed = lax.all_gather(jnp.concatenate(small), "fsdp", axis=0)
    vectors = []
    at = 0
    for size in sizes:
        vectors.append(packed[:, at : at + size].reshape(-1).astype(F32))
        at += size
    gain1, shift1, b_qkv, freqs, b_out, gain2, shift2, b1, b2 = vectors
    w_qkv = gather(qkv_weight)
    w_out = gather(out_weight)
    w1 = gather(fc1_weight)
    w2 = gather(fc2_weight)

    row = lambda v: v[None, :]
    a, a_t = norm1(x, row(gain1), row(shift1))
    places = jnp.concatenate([patch_cols, patch_rows], axis=0).astype(F32)
    half = freqs.shape[0] // 2
    angle = freqs[:half, None] * places[0:1] + freqs[half:, None] * places[1:2]
    cos = jnp.cos(angle)
    sin = jnp.sin(angle)
    q, k, v = project(a, w_qkv, b_qkv[:, None], cos, sin)
    o, lse = attend(counts, q, k, v)
    h, c, c_t = out_project(o, x, w_out, row(b_out), row(gain2), row(shift2))
    y, dc, g_w1, g_w2, g_b1 = mlp(c, c_t, dy, h, w1, row(b1), w2, row(b2))
    dh, do, g_wout, sums2 = out_back(dc, h, dy, o, w_out, row(gain2))
    dq, dk, dv, s_bq, s_bk, s_bv, s_fc, s_fr = attend_back(counts, q, k, v, o, do, lse, cos, sin, places)
    dqkv = jnp.concatenate([dq, dk, dv], axis=0)
    g_wqkv, dx, sums1 = qkv_back(a_t, dqkv, w_qkv, x, dh, row(gain1))

    scatter = partial(lax.psum_scatter, axis_name="fsdp", scatter_dimension=0, tiled=True)
    both = lambda g: lax.psum(scatter(g), "rep").astype(F32)
    g_bqkv = jnp.sum(jnp.concatenate([s_bq, s_bk, s_bv], axis=0), axis=1)
    g_freq = jnp.sum(jnp.concatenate([s_fc, s_fr], axis=0), axis=1)
    small_grads = (sums1[0], sums1[1], g_bqkv, g_freq, sums2[2], sums2[0], sums2[1], g_b1[0], sums2[3])
    shards = mesh_size = packed.shape[0]
    block = jnp.concatenate([g.reshape(shards, -1) for g in small_grads], axis=1)
    total = lax.psum(block, ("rep", "fsdp"))
    mine = lax.dynamic_index_in_dim(total, lax.axis_index("fsdp"), 0, keepdims=False)
    outs = []
    at = 0
    for size in sizes:
        outs.append(mine[at : at + size])
        at += size
    s_gain1, s_shift1, s_bqkv, s_freq, s_bout, s_gain2, s_shift2, s_b1, s_b2 = outs
    return (
        y[None], dx[None], s_gain1, s_shift1, both(g_wqkv), s_bqkv, s_freq, both(g_wout), s_bout,
        s_gain2, s_shift2, both(g_w1), s_b1, both(g_w2), s_b2,
    )


SHARDS = 16
GROUPS = 2
LEAVING = (0, 8, 4, 12, 2, 10, 6, 14)


def swap(v, mask):
    return lax.ppermute(v, "fsdp", [(i, i ^ mask) for i in range(SHARDS)])


def tie(v, *after):
    return lax.optimization_barrier((v,) + after)[0]


class Gather:
    def __init__(self, mine):
        self.piece = {0: mine}

    def send(self, source, mask, after):
        v = self.piece[source]
        self.piece[source ^ mask] = swap(tie(v, *after) if after else v, mask)

    def hold(self, sources, after):
        for p in sources:
            self.piece[p] = tie(self.piece[p], after)

    def stage1(self, *after):
        for mask in (8, 4, 2):
            self.send(0, mask, after)

    def stage2(self, *after):
        self.send(8, 4, after)
        self.send(4, 2, after)
        self.send(8, 2, after)

    def stage3(self, *after):
        self.send(12, 2, after)

    def cores(self, *after):
        for p in (0, 8, 4, 2, 6, 10, 12, 14):
            self.send(p, 1, after)
        return [self.piece[p] for p in range(SHARDS)]


class Scatter:
    def __init__(self, near, far):
        self.got = [near, swap(far, 1)]
        self.size = 4

    def total(self, lo, hi):
        out = self.got[0][lo:hi].astype(F32)
        for g in self.got[1:]:
            out = out + g[lo:hi].astype(F32)
        return out.astype(BF)

    def hold(self, *after):
        self.got[-1] = tie(self.got[-1], *after)

    def step(self):
        lo = self.size
        sent = self.total(lo, 2 * lo)
        self.got.append(swap(sent, {4: 2, 2: 4, 1: 8}[lo]))
        self.size = lo // 2
        return sent

    def finish(self):
        mine = self.total(0, 1)[0]
        return mine, across(mine)


class SplitScatter(Scatter):
    def __init__(self, near, far):
        self.start = [near, swap(far, 1)]
        self.size = 4

    def split(self):
        sent = (self.start[0][1].astype(F32) + self.start[1][1].astype(F32)).astype(BF)
        got = across(sent)
        self.got = [self.start[0][0], self.start[1][0], got]
        return sent


def across(v):
    return lax.ppermute(v, "rep", [(0, 1), (1, 0)])


def start_all(copies):
    for copy in copies:
        copy.start()


def wait_all(copies):
    for copy in copies:
        copy.wait()


def fetch(refs, order_ref, moves, sem):
    copies = []
    for p, ref in enumerate(refs):
        for rows, place in moves:
            copies.append(pltpu.make_async_copy(ref.at[rows], place(order_ref[p]), sem.at[len(copies)]))
    return copies


ANY = pl.BlockSpec(memory_space=pl.ANY)
HBM = pl.BlockSpec(memory_space=pltpu.HBM)
SMEM = pl.BlockSpec(memory_space=pltpu.SMEM)
VMEM = pl.BlockSpec(memory_space=pltpu.VMEM)


LINES = 16


def group_piece_kernel(w_ref, o_ref, v_ref, a_ref, b_ref):
    rows, cols = w_ref.shape[0], a_ref.shape[1]
    for i in range(3):
        for g, out in enumerate((a_ref, b_ref)):
            out[i * rows : (i + 1) * rows, :] = w_ref[:, (i * GROUPS + g) * cols : (i * GROUPS + g + 1) * cols]
    for i in range(2):
        b_ref[(3 + i) * rows : (4 + i) * rows, :] = o_ref[:, i * cols : (i + 1) * cols]
    a_ref[3 * rows :, :] = jnp.concatenate([v_ref[...], jnp.zeros((LINES - v_ref.shape[0], cols), BF)], axis=0)


def group_pieces(w, w_out, vectors):
    rows, cols = w.shape[0], w_out.shape[1] // 2
    return pl.pallas_call(
        group_piece_kernel,
        in_specs=[VMEM] * 3,
        out_specs=[VMEM, VMEM],
        out_shape=[jax.ShapeDtypeStruct((3 * rows + LINES, cols), BF), jax.ShapeDtypeStruct((5 * rows, cols), BF)],
        compiler_params=params(),
        cost_estimate=cost(2),
        name="group_pieces",
    )(w, w_out, vectors)


def mlp_piece_kernel(w1_ref, w2_ref, *outs):
    rows1 = w1_ref.shape[0]
    own = w2_ref.shape[0] // 2
    per = SHARDS // 2
    w1 = w1_ref[...].astype(F32)
    for i, out in enumerate(outs):
        for b in range(2):
            runs = [w1[:, (2 * (b * per + j) + i) * own :][:, :own] for j in range(per)]
            out[b * rows1 : (b + 1) * rows1, :] = jnp.concatenate(runs, axis=1).astype(BF)
        out[2 * rows1 :, :] = w2_ref[i * own : (i + 1) * own, :]


def mlp_pieces(w1, w2):
    rows = 2 * w1.shape[0] + w2.shape[0] // 2
    return pl.pallas_call(
        mlp_piece_kernel,
        in_specs=[VMEM, VMEM],
        out_specs=[VMEM, VMEM],
        out_shape=[jax.ShapeDtypeStruct((rows, w2.shape[1]), BF)] * 2,
        compiler_params=params(),
        cost_estimate=cost(2),
        name="mlp_pieces",
    )(w1, w2)


def mlp_join_kernel(order_ref, c_ref, c_other_ref, d_ref, d_other_ref, w1_ref, w2_ref):
    rows1 = w1_ref.shape[0]
    own = w2_ref.shape[0] // 2
    per = SHARDS // 2
    c = c_ref[...].astype(F32) + c_other_ref[...].astype(F32)
    mine = d_ref[...].astype(F32)
    other = d_other_ref[...].astype(F32)
    here = order_ref[SHARDS] == 0
    d = jnp.where(here, mine, other)
    runs = []
    for b in range(2):
        for j in range(per):
            runs += [m[b * rows1 : (b + 1) * rows1, j * own : (j + 1) * own] for m in (c, d)]
    w1_ref[...] = jnp.concatenate(runs, axis=1)
    w2_ref[:own, :] = c[2 * rows1 :]
    w2_ref[own:, :] = jnp.where(here, other, mine)


def mlp_join(rows1, order, parts):
    own = parts[0].shape[0] - 2 * rows1
    return pl.pallas_call(
        mlp_join_kernel,
        in_specs=[SMEM] + [VMEM] * 4,
        out_specs=[VMEM] * 2,
        out_shape=[
            jax.ShapeDtypeStruct((rows1, 2 * own * SHARDS), F32),
            jax.ShapeDtypeStruct((2 * own, parts[0].shape[1]), F32),
        ],
        compiler_params=params(8),
        cost_estimate=cost(3),
        name="mlp_join",
    )(order, *parts)


def spread(packed, lo, size):
    return jnp.concatenate([packed[j : j + 1, lo : lo + size] for j in range(packed.shape[0])], axis=1)


def column(v):
    return jnp.broadcast_to(v, (8, v.shape[1])).T[:, 0:1]


def prepare_kernel(sizes, order_ref, x_ref, cols_ref, rows_ref, *rest):
    pieces = rest[:SHARDS]
    at_ref, cos_ref, sin_ref, vec_ref, b1_ref, bias_ref, sel_ref, line_scr, table_scr, sem = rest[SHARDS:]
    half = cos_ref.shape[0]

    @pl.when(pl.program_id(0) == 0)
    def _():
        last = pieces[0].shape[0]
        copies = fetch(pieces, order_ref, [(slice(last - LINES, last), lambda d: line_scr.at[d])], sem)
        start_all(copies)
        wait_all(copies)
        packed = jnp.concatenate([line_scr[:, i, :] for i in range(2)], axis=1).astype(F32)
        starts = [sum(sizes[:i]) for i in range(len(sizes))]
        gain1, shift1, b_qkv, freqs, b_out, gain2, shift2 = (spread(packed, starts[i], sizes[i]) for i in range(7))
        b2 = spread(packed, starts[8], sizes[8])
        for i, v in enumerate((b_out, gain1, gain2, shift2, b2, shift1)):
            vec_ref[i : i + 1, :] = v
        own = sizes[7] // 2
        for i in range(2):
            b1_ref[i : i + 1, :] = spread(packed, starts[7] + i * own, own)
        bias_ref[...] = column(b_qkv)
        freq = column(freqs)
        spots = lax.broadcasted_iota(jnp.int32, (1, 128), 1).astype(F32)
        for i in range(2):
            angle = freq[i * half : (i + 1) * half] * spots
            for k, table in enumerate((jnp.cos(angle), jnp.sin(angle))):
                for n in range(3):
                    term = table.astype(BF)
                    table_scr[i, k, n] = term
                    table = table - term.astype(F32)

    xhat, _ = norm_parts(x_ref[...].astype(F32))
    at_ref[...] = (xhat * vec_ref[1:2, :] + vec_ref[5:6, :]).astype(BF).T
    found = []
    for i, at in enumerate((cols_ref[...], rows_ref[...])):
        one_hot = jnp.where(lax.broadcasted_iota(jnp.int32, (128, at.shape[1]), 0) == at, 1.0, 0.0).astype(BF)
        found.append([sum(nn(table_scr[i, k, n], one_hot) for n in range(3)) for k in range(2)])
    (cos_c, sin_c), (cos_r, sin_r) = found
    cos_ref[...] = cos_c * cos_r - sin_c * sin_r
    sin_ref[...] = sin_c * cos_r + cos_c * sin_r
    line = lax.broadcasted_iota(jnp.int32, sel_ref.shape, 0)
    sel = jnp.where(line == 0, cols_ref[...].astype(F32), rows_ref[...].astype(F32))
    sel_ref[...] = jnp.where(line < 2, sel, jnp.where(line == 2, 1.0, 0.0)).astype(BF)


def prepare(sizes, order, x, patch_cols, patch_rows, pieces):
    slots, width = x.shape
    own = sizes[7] // 2
    blk = 256
    shape = jax.ShapeDtypeStruct
    tall = lambda n: pl.BlockSpec((n, blk), lambda i: (0, i))
    whole = lambda r, k: pl.BlockSpec((r, k), lambda i: (0, 0))
    return pl.pallas_call(
        partial(prepare_kernel, sizes),
        grid=(slots // blk,),
        in_specs=[SMEM, pl.BlockSpec((blk, width), lambda i: (i, 0)), tall(1), tall(1)] + [HBM] * SHARDS,
        out_specs=[
            tall(width), tall(width // 2), tall(width // 2),
            whole(8, width), whole(2, own * SHARDS), whole(3 * width, 1), tall(16),
        ],
        out_shape=[
            shape((width, slots), BF),
            shape((width // 2, slots), F32),
            shape((width // 2, slots), F32),
            shape((8, width), F32),
            shape((2, own * SHARDS), F32),
            shape((3 * width, 1), F32),
            shape((16, slots), BF),
        ],
        scratch_shapes=[
            pltpu.VMEM((SHARDS, LINES, width // GROUPS), BF),
            pltpu.VMEM((2, 2, 3, width // 2, 128), BF),
            pltpu.SemaphoreType.DMA((SHARDS,)),
        ],
        compiler_params=params(),
        cost_estimate=cost(8),
        name="prepare",
    )(order, x, patch_cols, patch_rows, *pieces)


def pack_kernel(sums1_ref, sums2_ref, b1a_ref, b1b_ref, *rest):
    heads, out_ref = rest[:-1], rest[-1]
    bias = [r[2:3, :] for r in heads[:GROUPS]]
    freq = [r[...] for r in heads[GROUPS:]]
    cols = bias[0].shape[1] // 3
    b_qkv = jnp.concatenate([b[:, i * cols : (i + 1) * cols] for i in range(3) for b in bias], axis=1)
    g_freq = jnp.concatenate([f[i : i + 1] for i in range(2) for f in freq], axis=1)
    vectors = (
        sums1_ref[0:1, :], sums1_ref[1:2, :], b_qkv, g_freq, sums2_ref[2:3, :], sums2_ref[0:1, :], sums2_ref[1:2, :],
        b1a_ref[...], b1b_ref[...], sums2_ref[3:4, :],
    )
    lines = []
    for j in range(SHARDS):
        runs = []
        for v in vectors:
            n = v.shape[1] // SHARDS
            runs.append(v[:, j * n : (j + 1) * n])
        lines.append(jnp.concatenate(runs, axis=1))
    out_ref[...] = jnp.concatenate(lines, axis=0)


def pack(size, *sums):
    return pl.pallas_call(
        pack_kernel,
        in_specs=[VMEM] * len(sums),
        out_specs=VMEM,
        out_shape=jax.ShapeDtypeStruct((SHARDS, size), F32),
        compiler_params=params(4),
        cost_estimate=cost(3),
        name="pack",
    )(*sums)


def group_kernel(order_ref, at_ref, bq_ref, bk_ref, bv_ref, cos_ref, sin_ref, *rest):
    pieces, (q_ref, k_ref, v_ref, w_scr, wt_scr, sem) = rest[:SHARDS], rest[SHARDS:]
    cols = q_ref.shape[0]
    part = w_scr.shape[1] // 3

    @pl.when(pl.program_id(0) == 0)
    def _():
        copies = fetch(pieces, order_ref, [(slice(0, 3 * part), lambda d: w_scr.at[d])], sem)
        start_all(copies)
        wait_all(copies)
        for i in range(3):
            wt_scr[i] = w_scr[:, i * part : (i + 1) * part, :].reshape(SHARDS * part, cols).T

    a_t = at_ref[...]
    cos = cos_ref[...]
    sin = sin_ref[...]
    for i, b_ref, out_ref, scale in ((0, bq_ref, q_ref, HEAD_DIM**-0.5), (1, bk_ref, k_ref, 1.0)):
        u = nn(wt_scr[i], a_t) + b_ref[...]
        for h in range(cols // HEAD_DIM):
            u1 = u[h * HEAD_DIM : h * HEAD_DIM + HALF]
            u2 = u[h * HEAD_DIM + HALF : (h + 1) * HEAD_DIM]
            c = cos[h * HALF : (h + 1) * HALF]
            s = sin[h * HALF : (h + 1) * HALF]
            out_ref[h * HEAD_DIM : h * HEAD_DIM + HALF, :] = ((u1 * c - u2 * s) * scale).astype(BF)
            out_ref[h * HEAD_DIM + HALF : (h + 1) * HEAD_DIM, :] = ((u1 * s + u2 * c) * scale).astype(BF)
    v_ref[...] = (nn(wt_scr[2], a_t) + bv_ref[...]).astype(BF)


def project_group(group, order, a_t, bias, cos, sin, pieces):
    width, slots = a_t.shape
    cols = pieces[0].shape[1]
    blk = 512
    tall = lambda n, at: pl.BlockSpec((n, blk), lambda i: (at, i))
    return pl.pallas_call(
        group_kernel,
        grid=(slots // blk,),
        in_specs=[SMEM, tall(width, 0)]
        + [pl.BlockSpec((cols, 1), lambda i, n=n: (n * GROUPS + group, 0)) for n in range(3)]
        + [tall(cols // 2, group)] * 2
        + [HBM] * SHARDS,
        out_specs=[tall(cols, 0)] * 3,
        out_shape=[jax.ShapeDtypeStruct((cols, slots), BF)] * 3,
        scratch_shapes=[
            pltpu.VMEM((SHARDS, 3 * width // SHARDS, cols), BF),
            pltpu.VMEM((3, cols, width), BF),
            pltpu.SemaphoreType.DMA((SHARDS,)),
        ],
        compiler_params=params(),
        cost_estimate=cost(7),
        name="qkv_group",
    )(order, a_t, bias, bias, bias, cos, sin, *pieces)


def out_moves(w_scr, start):
    rows = w_scr.shape[1]
    half = w_scr.shape[2] // 2
    return [
        (slice(start + i * rows, start + (i + 1) * rows), lambda d, i=i: w_scr.at[d, :, pl.ds(i * half, half)])
        for i in range(2)
    ]


def out_group_kernel(start, order_ref, vec_ref, *rest):
    o_refs, x_ref, pieces = rest[:GROUPS], rest[GROUPS], rest[GROUPS + 1 : GROUPS + 1 + SHARDS]
    h_ref, c_ref, ct_ref, w_scr, sem = rest[GROUPS + 1 + SHARDS :]

    @pl.when(pl.program_id(0) == 0)
    def _():
        copies = fetch(pieces, order_ref, out_moves(w_scr, start), sem)
        start_all(copies)
        wait_all(copies)

    width = x_ref.shape[1]
    o = jnp.concatenate([r[...].T for r in o_refs], axis=1)
    h = x_ref[...].astype(F32) + (nn(o, w_scr[...].reshape(width, width)) + vec_ref[0:1, :])
    h_ref[...] = h
    xhat, _ = norm_parts(h)
    c = (xhat * vec_ref[2:3, :] + vec_ref[3:4, :]).astype(BF)
    c_ref[...] = c
    ct_ref[...] = c.T


def out_project_fast(order, o, x, vec, pieces, start):
    slots, width = x.shape
    blk = 256
    rows = pl.BlockSpec((blk, width), lambda i: (i, 0))
    cols = pl.BlockSpec((width, blk), lambda i: (0, i))
    return pl.pallas_call(
        partial(out_group_kernel, start),
        grid=(slots // blk,),
        in_specs=[SMEM, VMEM] + [pl.BlockSpec((width // GROUPS, blk), lambda i: (0, i))] * GROUPS + [rows] + [HBM] * SHARDS,
        out_specs=[rows, rows, cols],
        out_shape=[
            jax.ShapeDtypeStruct((slots, width), F32),
            jax.ShapeDtypeStruct((slots, width), BF),
            jax.ShapeDtypeStruct((width, slots), BF),
        ],
        scratch_shapes=[pltpu.VMEM((SHARDS, width // SHARDS, width), BF), pltpu.SemaphoreType.DMA((2 * SHARDS,))],
        compiler_params=params(),
        cost_estimate=cost(8),
        name="out_project",
    )(order, vec, *o, x, *pieces)


def mlp_half_kernel(part, first, split, n_in, order_ref, c_in, ct_in, dy_in, b1_ref, vec_ref, *rest):
    acc_in, rest = (rest[:1], rest[1:]) if first else (rest[:2], rest[2:])
    pieces, rest = rest[:n_in], rest[n_in:]
    n_g = 2 if split else 1
    y_ref, dc_ref = rest[:2]
    g_refs = rest[2 : 2 + n_g]
    gb1_ref, w1_scr, w2_scr, g1_scr, g2_scr, hb_scr, dp_scr, y_acc, dc_acc = rest[2 + n_g : 11 + n_g]
    c_ref, ct_ref, dy_ref, y_out, dc_out, sem, load_sem = rest[11 + n_g :]
    slots, width = c_ref.shape
    rows1 = w1_scr.shape[2]
    rows2 = w2_scr.shape[1]
    blk = w1_scr.shape[3]
    steps = w1_scr.shape[0]
    per = blk // rows2
    tile = 512
    refs = [pieces[0].at[p] for p in range(SHARDS)] if n_in == 1 else pieces
    places = range(SHARDS) if n_in == 1 else order_ref
    loads = [
        fetch(refs, places, [(slice(j * rows1, (j + 1) * rows1), lambda d, j=j: w1_scr.at[j, d])], sem.at[j])
        for j in range(steps)
    ]
    loads.insert(1, fetch(refs, places, [(slice(steps * rows1, steps * rows1 + rows2), lambda d: w2_scr.at[d])], sem.at[steps]))
    sums = list(zip(acc_in, (y_acc,) if first else (y_out, dc_out)))
    rows_in = [(c_in, c_ref), (dy_in, dy_ref), (ct_in, ct_ref)]
    whole = [pltpu.make_async_copy(src, dst, load_sem.at[i]) for i, (src, dst) in enumerate(rows_in + sums)]
    (c_load, dy_load, ct_load), sums = whole[:3], whole[3:]
    for copies in [[c_load], loads[0], [dy_load], loads[1], sums, [ct_load]] + loads[2:]:
        start_all(copies)
    sends = []
    for j in range(steps):
        cols = slice(j * blk, (j + 1) * blk)
        wait_all([c_load] + loads[0] if j == 0 else loads[1 + j])
        w1 = w1_scr[j].reshape(width, blk)
        w2 = None
        total = None
        for i in range(slots // tile):
            rows = slice(i * tile, (i + 1) * tile)
            pre = nn(c_ref[rows, :], w1) + b1_ref[part : part + 1, cols]
            square = pre * pre
            th = jnp.tanh(GELU_C * (pre + GELU_A * (pre * square)))
            cdf = 0.5 * (1.0 + th)
            hb = (pre * cdf).astype(BF)
            slope = cdf + 0.5 * pre * (1.0 - th * th) * (GELU_C * (1.0 + (3.0 * GELU_A) * square))
            hb_scr[rows, :] = hb
            if w2 is None:
                if j == 0:
                    wait_all(loads[1] + [dy_load] + sums)
                w2 = w2_scr[j * per : (j + 1) * per].reshape(blk, width)
            before = y_acc if first or j else y_out
            y = before[rows, :].astype(F32) + nn(hb, w2)
            if first and j == 0:
                y = y + vec_ref[4:5, :]
            dpre = (nt(dy_ref[rows, :], w2) * slope).astype(BF)
            dp_scr[rows, :] = dpre
            term = jnp.sum(dpre.astype(F32), axis=0, keepdims=True)
            total = term if total is None else total + term
            dc = nt(dpre, w1)
            if j or not first:
                dc = dc + (dc_acc if j else dc_out)[rows, :].astype(F32)
            if j == steps - 1:
                y_out[rows, :] = y.astype(BF)
                dc_out[rows, :] = dc.astype(BF)
                sends += [
                    pltpu.make_async_copy(y_out.at[rows], y_ref.at[rows], load_sem.at[5 + 2 * i]),
                    pltpu.make_async_copy(dc_out.at[rows], dc_ref.at[rows], load_sem.at[6 + 2 * i]),
                ]
                start_all(sends[-2:])
            else:
                y_acc[rows, :] = y
                dc_acc[rows, :] = dc
        gb1_ref[:, cols] = total
        if j == 0:
            wait_all([ct_load])
        g1_scr[j] = nn(ct_ref[...], dp_scr[...]).astype(BF).reshape(SHARDS, rows1, blk)
        if split:
            mine = order_ref[SHARDS]
            dests = [(g_refs[b], i, order_ref[p + b]) for b in range(2) for i, p in enumerate(LEAVING)]
            place = lambda dst, i, lo, n: dst.at[lax.rem(lo // (steps * rows1) + mine, 2), i, pl.ds(lo % (steps * rows1), n)]
        else:
            dests = [(g_refs[0], p, p) for p in range(SHARDS)]
            place = lambda dst, i, lo, n: dst.at[i, pl.ds(lo, n)]
        copies = [
            pltpu.make_async_copy(g1_scr.at[j, d], place(dst, i, j * rows1, rows1), sem.at[j, n])
            for n, (dst, i, d) in enumerate(dests)
        ]
        start_all(copies)
        sends += copies
        g2_scr[j * per : (j + 1) * per] = tn(hb_scr[...], dy_ref[...]).astype(BF).reshape(per, rows2, width)
    copies = [
        pltpu.make_async_copy(g2_scr.at[d], place(dst, i, steps * rows1, rows2), sem.at[steps, n])
        for n, (dst, i, d) in enumerate(dests)
    ]
    start_all(copies)
    wait_all(sends + copies)


def mlp_half(part, order, c, ct, dy, b1, vec, sums, pieces, split):
    slots, width = c.shape
    rows1 = width // SHARDS
    rows2 = pieces[0].shape[-2] - 2 * rows1
    hidden = rows2 * SHARDS
    steps = 2
    blk = hidden // steps
    first = len(sums) == 1
    block = jax.ShapeDtypeStruct((SHARDS, 2 * rows1 + rows2, width), BF)
    if split:
        block = jax.ShapeDtypeStruct((2, SHARDS // 2, rows2, width), BF)
    return pl.pallas_call(
        partial(mlp_half_kernel, part, first, split, len(pieces)),
        in_specs=[SMEM] + [ANY] * 3 + [VMEM] * 2 + [ANY] * len(sums) + [HBM] * len(pieces),
        out_specs=[ANY, ANY] + [ANY] * (2 if split else 1) + [VMEM],
        out_shape=[jax.ShapeDtypeStruct((slots, width), BF)] * 2
        + [block] * (2 if split else 1)
        + [jax.ShapeDtypeStruct((1, hidden), F32)],
        scratch_shapes=[
            pltpu.VMEM((steps, SHARDS, rows1, blk), BF),
            pltpu.VMEM((SHARDS, rows2, width), BF),
            pltpu.VMEM((steps, SHARDS, rows1, blk), BF),
            pltpu.VMEM((SHARDS, rows2, width), BF),
            pltpu.VMEM((slots, blk), BF),
            pltpu.VMEM((slots, blk), BF),
            pltpu.VMEM((slots, width), F32),
            pltpu.VMEM((slots, width), F32),
            pltpu.VMEM((slots, width), BF),
            pltpu.VMEM((width, slots), BF),
            pltpu.VMEM((slots, width), BF),
            pltpu.VMEM((slots, width), BF),
            pltpu.VMEM((slots, width), BF),
            pltpu.SemaphoreType.DMA((steps + 1, SHARDS)),
            pltpu.SemaphoreType.DMA((9,)),
        ],
        compiler_params=params(),
        cost_estimate=cost(23),
        name="mlp_half",
    )(order, c, ct, dy, b1, vec, *sums, *pieces)


def out_back_fast_kernel(start, order_ref, dc_ref, h_ref, dy_ref, vec_ref, *rest):
    o_refs, pieces = rest[:GROUPS], rest[GROUPS : GROUPS + SHARDS]
    dh_ref, do_ref, near_ref, far_ref, sums_ref, acc_ref, g_scr, w_scr, sem = rest[GROUPS + SHARDS :]
    i = pl.program_id(0)
    width = h_ref.shape[1]
    each = width // SHARDS
    half = width // 2

    @pl.when(i == 0)
    def _():
        copies = fetch(pieces, order_ref, out_moves(w_scr, start), sem)
        start_all(copies)
        acc_ref[...] = jnp.zeros_like(acc_ref)
        sums_ref[...] = jnp.zeros_like(sums_ref)
        wait_all(copies)

    dy = dy_ref[...].astype(F32)
    part, dgain, dshift = norm_back(dc_ref[...].astype(F32), h_ref[...], vec_ref[2:3, :])
    dh = dy + part
    dhb = dh.astype(BF)
    dh_ref[...] = dhb
    do_ref[...] = nt(w_scr[...].reshape(width, width), dhb).astype(BF)
    rows = width // GROUPS
    for g in range(GROUPS):
        acc_ref[g * rows : (g + 1) * rows, :] += nn(o_refs[g][...], dhb)
    sums_ref[0:1, :] += dgain
    sums_ref[1:2, :] += dshift
    sums_ref[2:3, :] += jnp.sum(dh, axis=0, keepdims=True)
    sums_ref[3:4, :] += jnp.sum(dy, axis=0, keepdims=True)

    @pl.when(i == pl.num_programs(0) - 1)
    def _():
        g_scr[...] = acc_ref[...].astype(BF).reshape(g_scr.shape)
        copies = []
        for b, out in enumerate((near_ref, far_ref)):
            for n, p in enumerate(LEAVING):
                for k in range(2):
                    src = g_scr.at[order_ref[p + b], :, pl.ds(k * half, half)]
                    dst = out.at[n, pl.ds(k * each, each)]
                    copies.append(pltpu.make_async_copy(src, dst, sem.at[len(copies)]))
        start_all(copies)
        wait_all(copies)


def out_back_fast(order, dc, h, dy, vec, o, pieces, start):
    slots, width = h.shape
    blk = 256
    rows = pl.BlockSpec((blk, width), lambda i: (i, 0))
    cols = pl.BlockSpec((width, blk), lambda i: (0, i))
    whole = lambda r, k: pl.BlockSpec((r, k), lambda i: (0, 0))
    block = jax.ShapeDtypeStruct((SHARDS // 2, 2 * width // SHARDS, width // 2), BF)
    return pl.pallas_call(
        partial(out_back_fast_kernel, start),
        grid=(slots // blk,),
        in_specs=[SMEM, rows, rows, rows, VMEM]
        + [pl.BlockSpec((width // GROUPS, blk), lambda i: (0, i))] * GROUPS
        + [HBM] * SHARDS,
        out_specs=[rows, cols, ANY, ANY, whole(8, width)],
        out_shape=[
            jax.ShapeDtypeStruct((slots, width), BF),
            jax.ShapeDtypeStruct((width, slots), BF),
            block,
            block,
            jax.ShapeDtypeStruct((8, width), F32),
        ],
        scratch_shapes=[
            pltpu.VMEM((width, width), F32),
            pltpu.VMEM((SHARDS, width // SHARDS, width), BF),
            pltpu.VMEM((SHARDS, width // SHARDS, width), BF),
            pltpu.SemaphoreType.DMA((2 * SHARDS,)),
        ],
        compiler_params=params(),
        cost_estimate=cost(12),
        name="out_back",
    )(order, dc, h, dy, vec, *o, *pieces)


def heads_back_kernel(
    counts_ref, q_ref, k_ref, v_ref, o_ref, do_ref, lse_ref, cos_ref, sin_ref,
    dq_ref, dk_ref, dv_ref, dangle_ref, bias_ref,
):
    slots = q_ref.shape[1]

    @pl.when(pl.program_id(0) == 0)
    def _():
        bias_ref[...] = second_bias(counts_ref, slots)

    lane1 = lax.broadcasted_iota(jnp.int32, (1, WIDE), 1)
    lane2 = lax.broadcasted_iota(jnp.int32, (1, slots - CUT), 1)
    scale = HEAD_DIM**-0.5

    def part(scores, grads, queries, outs, keys, delta_row, first):
        prob = jnp.exp(scores)
        ds = (prob * (grads - delta_row)).astype(BF)
        pb = prob.astype(BF)
        gap = jnp.zeros((keys.shape[1] - pb.shape[0], pb.shape[1]), BF)
        pb = jnp.concatenate([pb, gap] if first else [gap, pb], axis=0)
        ds = jnp.concatenate([ds, gap] if first else [gap, ds], axis=0)
        return nn(keys, ds), nt(queries, ds), nt(outs, pb)

    for h in range(q_ref.shape[0] // HEAD_DIM):
        top = h * HEAD_DIM
        rows = slice(top, top + HEAD_DIM)
        kt = k_ref[rows, :]
        k = kt.T
        v = v_ref[rows, :].T
        q = q_ref[rows, :]
        do = do_ref[rows, :]
        lse = lse_ref[h]
        delta = jnp.sum(do.astype(F32) * o_ref[rows, :].astype(F32), axis=0, keepdims=True)
        lse1 = jnp.where(lane1 < FIRST, lse[:, :WIDE], -NEG)
        lse2 = jnp.where(lane2 >= FIRST - CUT, lse[:, CUT:], -NEG)
        grads1 = part(
            nn(k[:FIRST], q[:, :WIDE]) - lse1, nn(v[:FIRST], do[:, :WIDE]),
            q[:, :WIDE], do[:, :WIDE], kt[:, :WIDE], delta[:, :WIDE], True,
        )
        grads2 = part(
            nn(k[FIRST:], q[:, CUT:]) + bias_ref[...] - lse2, nn(v[FIRST:], do[:, CUT:]),
            q[:, CUT:], do[:, CUT:], kt[:, CUT:], delta[:, CUT:], False,
        )
        dq, dk, dv = (
            jnp.concatenate([one[:, :CUT], one[:, CUT:] + two[:, : WIDE - CUT], two[:, WIDE - CUT :]], axis=1)
            for one, two in zip(grads1, grads2)
        )
        cos = cos_ref[h * HALF : (h + 1) * HALF, :]
        sin = sin_ref[h * HALF : (h + 1) * HALF, :]
        dangle = None
        for r, rot, out in ((dq * scale, q.astype(F32) * (1.0 / scale), dq_ref), (dk, kt.astype(F32), dk_ref)):
            r1, r2 = r[:HALF], r[HALF:]
            term = r2 * rot[:HALF] - r1 * rot[HALF:]
            dangle = term if dangle is None else dangle + term
            out[top : top + HALF, :] = (r1 * cos + r2 * sin).astype(BF)
            out[top + HALF : top + HEAD_DIM, :] = (r2 * cos - r1 * sin).astype(BF)
        dv_ref[rows, :] = dv.astype(BF)
        dangle_ref[h * HALF : (h + 1) * HALF, :] = dangle.astype(BF)


def heads_back(group, counts, q, k, v, o, do, lse, cos, sin):
    width, slots = q.shape
    heads = width // HEAD_DIM
    each = 2
    steps = heads // each
    head = pl.BlockSpec((each * HEAD_DIM, slots), lambda h: (h, 0))
    half = pl.BlockSpec((each * HALF, slots), lambda h: (h, 0))
    turn = pl.BlockSpec((each * HALF, slots), lambda h: (group * steps + h, 0))
    late = pl.BlockSpec((each * HEAD_DIM, slots), lambda h: (group * steps + h, 0))
    return pl.pallas_call(
        heads_back_kernel,
        grid=(steps,),
        in_specs=[SMEM] + [head] * 4 + [late, pl.BlockSpec((each, 1, slots), lambda h: (h, 0, 0)), turn, turn],
        out_specs=[head] * 3 + [half],
        out_shape=[jax.ShapeDtypeStruct((width, slots), BF)] * 3 + [jax.ShapeDtypeStruct((width // 2, slots), BF)],
        scratch_shapes=[pltpu.VMEM((slots - FIRST, slots - CUT), F32)],
        compiler_params=params(20),
        cost_estimate=cost(13),
        name="heads_back",
    )(counts, q, k, v, o, do, lse, cos, sin)


def qkv_grad_kernel(order_ref, at_ref, sel_ref, dangle_ref, dq_ref, dk_ref, dv_ref, *rest):
    more, (near_ref, far_ref, bias_ref, freq_ref, g_scr, sem, more_sem) = rest[:-7], rest[-7:]
    part = g_scr.shape[1] // 3
    outs = (near_ref, far_ref)
    extra = [
        pltpu.make_async_copy(ref.at[n], out.at[n, pl.ds(3 * part, ref.shape[1])], more_sem.at[b, n])
        for b, (ref, out) in enumerate(zip(more, outs))
        for n in range(SHARDS // 2)
    ]
    start_all(extra)
    at = at_ref[...]
    for i, ref in enumerate((dq_ref, dk_ref, dv_ref)):
        g = nt(at, ref[...]).astype(BF)
        g_scr[:, i * part : (i + 1) * part, :] = g.reshape(SHARDS, part, g.shape[1])
        bias_ref[:, i * g.shape[1] : (i + 1) * g.shape[1]] = nt(sel_ref[...], ref[...])
    freq_ref[...] = nt(sel_ref[...], dangle_ref[...])
    copies = []
    for b, out in enumerate(outs):
        for n, p in enumerate(LEAVING):
            dst = out.at[n, pl.ds(0, 3 * part)]
            copies.append(pltpu.make_async_copy(g_scr.at[order_ref[p + b]], dst, sem.at[len(copies)]))
    start_all(copies)
    wait_all(copies + extra)


def qkv_grad(order, at, sel, dangle, dq, dk, dv, *more):
    width, slots = at.shape
    cols = dq.shape[0]
    rows = 3 * width // SHARDS
    total = rows + (more[0].shape[1] if more else 0)
    return pl.pallas_call(
        qkv_grad_kernel,
        in_specs=[SMEM] + [VMEM] * (6 + len(more)),
        out_specs=[ANY, ANY, VMEM, VMEM],
        out_shape=[jax.ShapeDtypeStruct((SHARDS // 2, total, cols), BF)] * 2
        + [jax.ShapeDtypeStruct((sel.shape[0], 3 * cols), F32), jax.ShapeDtypeStruct((sel.shape[0], cols // 2), F32)],
        scratch_shapes=[
            pltpu.VMEM((SHARDS, rows, cols), BF),
            pltpu.SemaphoreType.DMA((SHARDS,)),
            pltpu.SemaphoreType.DMA((2, SHARDS // 2)),
        ],
        compiler_params=params(16),
        cost_estimate=cost(6),
        name="qkv_grad",
    )(order, at, sel, dangle, dq, dk, dv, *more)


def part_kernel(order_ref, *rest):
    grads, pieces, (da_ref, w_scr, sem) = rest[:3], rest[3 : 3 + SHARDS], rest[3 + SHARDS :]
    add_group(order_ref, grads, pieces, da_ref, w_scr, sem)


def group_weights(order_ref, pieces, w_scr, sem):
    rows = w_scr.shape[1]
    copies = fetch(pieces, order_ref, [(slice(0, rows), lambda d: w_scr.at[d])], sem)
    start_all(copies)
    wait_all(copies)


def group_product(grads, w_scr):
    rows = w_scr.shape[1] // 3
    total = None
    for n in range(3):
        w = w_scr[:, n * rows : (n + 1) * rows, :].reshape(SHARDS * rows, w_scr.shape[2])
        term = nn(w, grads[n][...])
        total = term if total is None else total + term
    return total


def add_group(order_ref, grads, pieces, da_ref, w_scr, sem):
    @pl.when(pl.program_id(0) == 0)
    def _():
        group_weights(order_ref, pieces, w_scr, sem)

    da_ref[...] = group_product(grads, w_scr)


def input_part(order, grads, pieces, width):
    cols, slots = grads[0].shape
    blk = 512
    return pl.pallas_call(
        part_kernel,
        grid=(slots // blk,),
        in_specs=[SMEM] + [pl.BlockSpec((cols, blk), lambda i: (0, i))] * 3 + [HBM] * SHARDS,
        out_specs=pl.BlockSpec((width, blk), lambda i: (0, i)),
        out_shape=jax.ShapeDtypeStruct((width, slots), F32),
        scratch_shapes=[pltpu.VMEM((SHARDS, 3 * width // SHARDS, cols), BF), pltpu.SemaphoreType.DMA((SHARDS,))],
        compiler_params=params(16),
        cost_estimate=cost(6),
        name="input_part",
    )(order, *grads, *pieces)


def input_kernel(order_ref, x_ref, dh_ref, vec_ref, da_ref, *rest):
    grads, pieces, (dx_ref, sums_ref, w_scr, sem) = rest[:3], rest[3 : 3 + SHARDS], rest[3 + SHARDS :]

    @pl.when(pl.program_id(0) == 0)
    def _():
        group_weights(order_ref, pieces, w_scr, sem)
        sums_ref[...] = jnp.zeros_like(sums_ref)

    da = da_ref[...] + group_product(grads, w_scr)
    out, dgain, dshift = norm_back(da.T, x_ref[...].astype(F32), vec_ref[1:2, :])
    dx_ref[...] = (dh_ref[...].astype(F32) + out).astype(BF)
    sums_ref[0:1, :] += dgain
    sums_ref[1:2, :] += dshift


def input_back(order, x, dh, vec, da, grads, pieces):
    slots, width = x.shape
    cols = grads[0].shape[0]
    blk = 512
    rows = pl.BlockSpec((blk, width), lambda i: (i, 0))
    return pl.pallas_call(
        input_kernel,
        grid=(slots // blk,),
        in_specs=[SMEM, rows, rows, VMEM, pl.BlockSpec((width, blk), lambda i: (0, i))]
        + [pl.BlockSpec((cols, blk), lambda i: (0, i))] * 3
        + [HBM] * SHARDS,
        out_specs=[rows, pl.BlockSpec((8, width), lambda i: (0, 0))],
        out_shape=[jax.ShapeDtypeStruct((slots, width), BF), jax.ShapeDtypeStruct((8, width), F32)],
        scratch_shapes=[pltpu.VMEM((SHARDS, 3 * width // SHARDS, cols), BF), pltpu.SemaphoreType.DMA((SHARDS,))],
        compiler_params=params(20),
        cost_estimate=cost(10),
        name="input_back",
    )(order, x, dh, vec, da, *grads, *pieces)


def body_fast(
    tokens, cotangent, image_counts, patch_rows, patch_cols, ln1_gain, ln1_bias, qkv_weight, qkv_bias, rope_freqs,
    out_weight, out_bias, ln2_gain, ln2_bias, fc1_weight, fc1_bias, fc2_weight, fc2_bias,
):
    x = tokens[0]
    dy = cotangent[0]
    counts = image_counts[0]
    slots, width = x.shape
    cols = width // GROUPS
    half = width // 2
    order = lax.axis_index("fsdp") ^ jnp.arange(SHARDS, dtype=jnp.int32)
    order = jnp.concatenate([order, lax.axis_index("rep")[None].astype(jnp.int32)])

    own = fc2_weight.shape[0] // 2
    small = (ln1_gain, ln1_bias, qkv_bias, rope_freqs, out_bias, ln2_gain, ln2_bias, fc1_bias, fc2_bias)
    sizes = [s.shape[0] for s in small]
    vectors = jnp.concatenate(small + (jnp.zeros((2 * cols - sum(sizes),), BF),)).reshape(2, cols)
    piece_c, piece_d = mlp_pieces(fc1_weight, fc2_weight)
    piece_a, piece_b = group_pieces(qkv_weight, out_weight, vectors)
    pieces_c = [lax.all_gather(piece_c, "fsdp", axis=0)]
    pieces_d = [lax.all_gather(piece_d, "fsdp", axis=0)]
    first = lambda g: (g.piece[8], g.piece[4], g.piece[2])
    second = lambda g: (g.piece[12], g.piece[6], g.piece[10])
    gather_a = Gather(piece_a)
    gather_a.stage1()
    gather_a.stage2(*first(gather_a))
    gather_a.stage3()
    pieces_a = gather_a.cores()
    gather_b = Gather(piece_b)
    gather_b.stage1(gather_a.piece[12])
    a_t, cos, sin, vec, b1, bias, sel = prepare(sizes, order, x, patch_cols, patch_rows, pieces_a)
    gather_b.stage2(sel)
    q, k, v = project_group(0, order, a_t, bias, cos, sin, pieces_a)
    gather_b.hold((12, 6, 10), q)
    gather_b.stage3()
    heads = [(q, k, v) + tuple(attend(counts, q, k, v))]
    gather_b.hold((14,), heads[0][3])
    pieces_b = gather_b.cores()
    q, k, v = project_group(1, order, a_t, bias, cos, sin, pieces_b)
    heads.append((q, k, v) + tuple(attend(counts, q, k, v)))
    o = [t[3] for t in heads]
    at_out = piece_b.shape[0] - 2 * out_weight.shape[0]
    h, c, c_t = out_project_fast(order, o, x, vec, pieces_b, at_out)
    y, dc, g_c, g_b1a = mlp_half(0, order, c, c_t, dy, b1, vec, (h,), pieces_c, False)
    mlp_c = lax.psum_scatter(tie(g_c, pieces_d[0]), "fsdp", scatter_dimension=0, tiled=True)[0]
    y, dc, near_d, far_d, g_b1b = mlp_half(1, order, c, c_t, dy, b1, vec, (y, dc), pieces_d, True)
    scatter_d = SplitScatter(near_d, far_d)
    dh, do, near_o, far_o, sums2 = out_back_fast(order, dc, h, dy, vec, o, pieces_b, at_out)

    def back(g, do):
        q, k, v, og, lse = heads[g]
        *three, dangle = heads_back(g, counts, q, k, v, og, do, lse, cos, sin)
        return three, dangle

    sent = scatter_d.split()
    grads_b, dangle_b = back(1, tie(do, sent))
    near_b, far_b, bias_b, freq_b = qkv_grad(order, a_t, sel, dangle_b, *grads_b, near_o, far_o)
    scatter_b = Scatter(near_b, far_b)
    scatter_d.hold(near_b)
    sent = scatter_d.step()
    grads_a, dangle_a = back(0, tie(do, sent, near_b))
    scatter_d.hold(dangle_a)
    scatter_b.hold(dangle_a)
    sent = (scatter_d.step(), scatter_b.step())
    near_a, far_a, bias_a, freq_a = qkv_grad(order, a_t, sel, tie(dangle_a, *sent), *grads_a)
    scatter_a = Scatter(near_a, far_a)
    da = input_part(order, lax.optimization_barrier((grads_b, near_a))[0], pieces_b, width)
    for scatter in (scatter_d, scatter_b, scatter_a):
        scatter.hold(da)
    sent = (scatter_a.step(), scatter_b.step(), scatter_d.step())
    dx, sums1 = input_back(order, x, dh, vec, tie(da, *sent), grads_a, pieces_a)
    scatter_a.hold(sums1, scatter_b.got[-1], scatter_d.got[-1])
    sent = scatter_a.step()
    other_c = across(tie(mlp_c, sent))
    scatter_b.hold(sent)
    scatter_d.hold(sent)
    block = pack(sum(sizes), tie(sums1, sent), sums2, g_b1a, g_b1b, bias_a, bias_b, freq_a, freq_b)
    scatter_a.hold(block)
    sent = scatter_a.step()
    scatter_b.step()
    mlp_d = scatter_d.finish()
    scatter_b.hold(other_c, sent)
    mine_b = scatter_b.finish()
    mine = jnp.sum(tie(lax.all_to_all(block, "fsdp", 0, 0, tiled=True), sent), axis=0)
    mine = tie(mine, scatter_a.got[-1])
    rows1 = width // SHARDS
    s_w1, s_w2 = mlp_join(rows1, order, (mlp_c, other_c) + mlp_d)
    scatter_a.hold(mine)
    mine_a = scatter_a.finish()
    mine_a = (mine_a[0], tie(mine_a[1], s_w1))
    mine = mine + across(mine)
    s_a = mine_a[0].astype(F32) + mine_a[1].astype(F32)
    s_b = mine_b[0].astype(F32) + mine_b[1].astype(F32)
    s_wqkv = jnp.concatenate([s[i * rows1 : (i + 1) * rows1] for i in range(3) for s in (s_a, s_b)], axis=1)
    s_wout = jnp.concatenate([s_b[3 * rows1 : 4 * rows1], s_b[4 * rows1 :]], axis=1)

    outs = []
    at = 0
    for size in sizes:
        outs.append(mine[at : at + size])
        at += size
    s_gain1, s_shift1, s_bqkv, s_freq, s_bout, s_gain2, s_shift2, s_b1, s_b2 = outs
    return (
        y[None], dx[None], s_gain1, s_shift1, s_wqkv, s_bqkv, s_freq, s_wout, s_bout,
        s_gain2, s_shift2, s_w1, s_b1, s_w2, s_b2,
    )


def solution(mesh):
    row = P(("rep", "fsdp"), None)
    rows = P(("rep", "fsdp"), None, None)
    vec = P("fsdp")
    mat = P("fsdp", None)
    in_specs = (rows, rows, row, row, row, vec, vec, mat, vec, vec, mat, vec, vec, vec, mat, vec, mat, vec)
    out_specs = (rows, rows, vec, vec, mat, vec, vec, mat, vec, vec, vec, mat, vec, mat, vec)
    fast = mesh.shape["fsdp"] == SHARDS and mesh.shape["rep"] == 2
    return jax.shard_map(
        body_fast if fast else body_any, mesh=mesh, in_specs=in_specs, out_specs=out_specs, check_vma=False
    )
```

```python
from functools import partial

import jax
import jax.numpy as jnp
from jax import lax
from jax.experimental import pallas as pl
from jax.experimental.pallas import tpu as pltpu
from jax.sharding import PartitionSpec as P

HEADS = 12
HEAD_DIM = 64
HALF = HEAD_DIM // 2
FIRST = 576
CUT = 512
WIDE = 640
NEG = -1e30
EPS = 1e-6
BF = jnp.bfloat16
F32 = jnp.float32
GELU_C = 0.7978845608028654
GELU_A = 0.044715


def nn(a, b):
    return lax.dot_general(a, b, (((1,), (0,)), ((), ())), preferred_element_type=F32)


def nt(a, b):
    return lax.dot_general(a, b, (((1,), (1,)), ((), ())), preferred_element_type=F32)


def tn(a, b):
    return lax.dot_general(a, b, (((0,), (0,)), ((), ())), preferred_element_type=F32)


def params(mib=56):
    return pltpu.CompilerParams(vmem_limit_bytes=mib << 20)


def cost(us):
    return pl.CostEstimate(flops=int(us * 1.1e9), bytes_accessed=1 << 16, transcendentals=0)


def norm_parts(v):
    mean = jnp.mean(v, axis=-1, keepdims=True)
    dev = v - mean
    var = jnp.mean(dev * dev, axis=-1, keepdims=True)
    inv = lax.rsqrt(var + EPS)
    return dev * inv, inv


def lane_partial(v):
    total = v[:, :128]
    for i in range(1, v.shape[1] // 128):
        total = total + v[:, i * 128 : (i + 1) * 128]
    return total


def norm1_kernel(x_ref, gain_ref, shift_ref, a_ref, at_ref):
    xhat, _ = norm_parts(x_ref[...].astype(F32))
    a = (xhat * gain_ref[...] + shift_ref[...]).astype(BF)
    a_ref[...] = a
    at_ref[...] = a.T


def norm1(x, gain, shift):
    slots, width = x.shape
    blk = 256
    return pl.pallas_call(
        norm1_kernel,
        grid=(slots // blk,),
        in_specs=[
            pl.BlockSpec((blk, width), lambda i: (i, 0)),
            pl.BlockSpec((1, width), lambda i: (0, 0)),
            pl.BlockSpec((1, width), lambda i: (0, 0)),
        ],
        out_specs=[
            pl.BlockSpec((blk, width), lambda i: (i, 0)),
            pl.BlockSpec((width, blk), lambda i: (0, i)),
        ],
        out_shape=[
            jax.ShapeDtypeStruct((slots, width), BF),
            jax.ShapeDtypeStruct((width, slots), BF),
        ],
        compiler_params=params(),
        cost_estimate=cost(5),
        name="norm1",
    )(x, gain, shift)


def qkv_kernel(a_ref, wq_ref, wk_ref, wv_ref, bq_ref, bk_ref, bv_ref, cos_ref, sin_ref, q_ref, k_ref, v_ref):
    heads = wq_ref.shape[1] // HEAD_DIM
    a = a_ref[...]
    cos = cos_ref[...]
    sin = sin_ref[...]
    for w_ref, b_ref, out_ref, scale in ((wq_ref, bq_ref, q_ref, HEAD_DIM**-0.5), (wk_ref, bk_ref, k_ref, 1.0)):
        u = nt(w_ref[...].T, a) + b_ref[...]
        for h in range(heads):
            u1 = u[h * HEAD_DIM : h * HEAD_DIM + HALF]
            u2 = u[h * HEAD_DIM + HALF : (h + 1) * HEAD_DIM]
            c = cos[h * HALF : (h + 1) * HALF]
            s = sin[h * HALF : (h + 1) * HALF]
            out_ref[h * HEAD_DIM : h * HEAD_DIM + HALF, :] = ((u1 * c - u2 * s) * scale).astype(BF)
            out_ref[h * HEAD_DIM + HALF : (h + 1) * HEAD_DIM, :] = ((u1 * s + u2 * c) * scale).astype(BF)
    v_ref[...] = (nt(wv_ref[...].T, a) + bv_ref[...]).astype(BF)


def project(a, w, bias, cos, sin):
    slots, width = a.shape
    cols = 256
    groups = width // cols
    wspec = lambda part: pl.BlockSpec((width, cols), lambda g: (0, part * groups + g))
    bspec = lambda part: pl.BlockSpec((cols, 1), lambda g: (part * groups + g, 0))
    out = pl.BlockSpec((cols, slots), lambda g: (g, 0))
    return pl.pallas_call(
        qkv_kernel,
        grid=(groups,),
        in_specs=[pl.BlockSpec((slots, width), lambda g: (0, 0))]
        + [wspec(i) for i in range(3)]
        + [bspec(i) for i in range(3)]
        + [pl.BlockSpec((cols // 2, slots), lambda g: (g, 0))] * 2,
        out_specs=[out] * 3,
        out_shape=[jax.ShapeDtypeStruct((width, slots), BF)] * 3,
        compiler_params=params(),
        name="qkv",
    )(a, w, w, w, bias, bias, bias, cos, sin)


def second_bias(counts_ref, slots):
    shape = (slots - FIRST, slots - CUT)
    key = lax.broadcasted_iota(jnp.int32, shape, 0) + FIRST
    query = lax.broadcasted_iota(jnp.int32, shape, 1) + CUT
    end0 = counts_ref[0]
    end1 = end0 + counts_ref[1]
    end2 = end1 + counts_ref[2]

    def seg(place):
        return (place >= end0).astype(jnp.int32) + (place >= end1).astype(jnp.int32)

    allowed = ((seg(key) == seg(query)) & (key < end2) & (query < end2)) | (key == query)
    return jnp.where(allowed, 0.0, NEG)


def attend_kernel(counts_ref, q_ref, k_ref, v_ref, o_ref, lse_ref, bias_ref):
    slots = q_ref.shape[1]

    @pl.when(pl.program_id(0) == 0)
    def _():
        bias_ref[...] = second_bias(counts_ref, slots)

    def part(scores, first, values):
        peak = jnp.max(scores, axis=0, keepdims=True)
        wb = jnp.exp(scores - peak).astype(BF)
        gap = jnp.zeros((values.shape[1] - wb.shape[0], wb.shape[1]), BF)
        wb = jnp.concatenate([wb, gap] if first else [gap, wb], axis=0)
        lines = jnp.concatenate([values, jnp.ones((16, values.shape[1]), BF)], axis=0)
        mixed = nn(lines, wb)
        total = mixed[HEAD_DIM : HEAD_DIM + 1]
        return mixed[:HEAD_DIM] * (1.0 / total), peak + jnp.log(total)

    edge = lax.broadcasted_iota(jnp.int32, (1, WIDE - CUT), 1) < FIRST - CUT
    for h in range(q_ref.shape[0] // HEAD_DIM):
        rows = slice(h * HEAD_DIM, (h + 1) * HEAD_DIM)
        k = k_ref[rows, :].T
        q = q_ref[rows, :]
        v = v_ref[rows, :]
        mixed1, lse1 = part(nn(k[:FIRST], q[:, :WIDE]), True, v[:, :WIDE])
        mixed2, lse2 = part(nn(k[FIRST:], q[:, CUT:]) + bias_ref[...], False, v[:, CUT:])
        for out, one, two in ((o_ref.at[rows], mixed1, mixed2), (lse_ref.at[h], lse1, lse2)):
            out[:, :CUT] = one[:, :CUT].astype(out.dtype)
            out[:, CUT:WIDE] = jnp.where(edge, one[:, CUT:], two[:, : WIDE - CUT]).astype(out.dtype)
            out[:, WIDE:] = two[:, WIDE - CUT :].astype(out.dtype)


def attend(counts, q, k, v):
    width, slots = q.shape
    heads = width // HEAD_DIM
    each = 2
    head = pl.BlockSpec((each * HEAD_DIM, slots), lambda h: (h, 0))
    return pl.pallas_call(
        attend_kernel,
        grid=(heads // each,),
        in_specs=[pl.BlockSpec(memory_space=pltpu.SMEM)] + [head] * 3,
        out_specs=[head, pl.BlockSpec((each, 1, slots), lambda h: (h, 0, 0))],
        out_shape=[jax.ShapeDtypeStruct((width, slots), BF), jax.ShapeDtypeStruct((heads, 1, slots), F32)],
        scratch_shapes=[pltpu.VMEM((slots - FIRST, slots - CUT), F32)],
        compiler_params=params(),
        cost_estimate=cost(8),
        name="attend",
    )(counts, q, k, v)


def attend_back_kernel(
    counts_ref, q_ref, k_ref, v_ref, o_ref, do_ref, lse_ref, cos_ref, sin_ref, place_ref,
    dq_ref, dk_ref, dv_ref, bq_ref, bk_ref, bv_ref, fc_ref, fr_ref, bias_ref,
):
    slots = q_ref.shape[1]

    @pl.when(pl.program_id(0) == 0)
    def _():
        bias_ref[...] = second_bias(counts_ref, slots)

    kt = k_ref[...]
    k = kt.T
    v = v_ref[...].T
    q = q_ref[...]
    do = do_ref[...]
    lse = lse_ref[0]
    delta = jnp.sum(do.astype(F32) * o_ref[...].astype(F32), axis=0, keepdims=True)
    lane1 = lax.broadcasted_iota(jnp.int32, (1, WIDE), 1)
    lane2 = lax.broadcasted_iota(jnp.int32, (1, slots - CUT), 1)
    lse1 = jnp.where(lane1 < FIRST, lse[:, :WIDE], -NEG)
    lse2 = jnp.where(lane2 >= FIRST - CUT, lse[:, CUT:], -NEG)

    def part(scores, grads, queries, outs, keys, delta_row, first):
        prob = jnp.exp(scores)
        ds = (prob * (grads - delta_row)).astype(BF)
        pb = prob.astype(BF)
        gap = jnp.zeros((keys.shape[1] - pb.shape[0], pb.shape[1]), BF)
        pb = jnp.concatenate([pb, gap] if first else [gap, pb], axis=0)
        ds = jnp.concatenate([ds, gap] if first else [gap, ds], axis=0)
        return nn(keys, ds), nt(queries, ds), nt(outs, pb)

    grads1 = part(
        nn(k[:FIRST], q[:, :WIDE]) - lse1, nn(v[:FIRST], do[:, :WIDE]),
        q[:, :WIDE], do[:, :WIDE], kt[:, :WIDE], delta[:, :WIDE], True,
    )
    grads2 = part(
        nn(k[FIRST:], q[:, CUT:]) + bias_ref[...] - lse2, nn(v[FIRST:], do[:, CUT:]),
        q[:, CUT:], do[:, CUT:], kt[:, CUT:], delta[:, CUT:], False,
    )
    dq, dk, dv = (
        jnp.concatenate([one[:, :CUT], one[:, CUT:] + two[:, : WIDE - CUT], two[:, WIDE - CUT :]], axis=1)
        for one, two in zip(grads1, grads2)
    )
    scale = HEAD_DIM**-0.5
    cos = cos_ref[...]
    sin = sin_ref[...]
    dangle = None
    for r, rot, out, bias_out in ((dq * scale, q.astype(F32) * (1.0 / scale), dq_ref, bq_ref), (dk, kt.astype(F32), dk_ref, bk_ref)):
        r1, r2 = r[:HALF], r[HALF:]
        term = r2 * rot[:HALF] - r1 * rot[HALF:]
        dangle = term if dangle is None else dangle + term
        g1 = (r1 * cos + r2 * sin).astype(BF)
        g2 = (r2 * cos - r1 * sin).astype(BF)
        out[:HALF, :] = g1
        out[HALF:, :] = g2
        bias_out[:HALF, :] = lane_partial(g1.astype(F32))
        bias_out[HALF:, :] = lane_partial(g2.astype(F32))
    dvb = dv.astype(BF)
    dv_ref[...] = dvb
    bv_ref[...] = lane_partial(dvb.astype(F32))
    fc_ref[...] = lane_partial(dangle * place_ref[0:1, :])
    fr_ref[...] = lane_partial(dangle * place_ref[1:2, :])


def attend_back(counts, q, k, v, o, do, lse, cos, sin, places):
    width, slots = q.shape
    heads = width // HEAD_DIM
    head = pl.BlockSpec((HEAD_DIM, slots), lambda h: (h, 0))
    half = pl.BlockSpec((HALF, slots), lambda h: (h, 0))
    return pl.pallas_call(
        attend_back_kernel,
        grid=(heads,),
        in_specs=[pl.BlockSpec(memory_space=pltpu.SMEM)]
        + [head] * 5
        + [pl.BlockSpec((1, 1, slots), lambda h: (h, 0, 0)), half, half]
        + [pl.BlockSpec((2, slots), lambda h: (0, 0))],
        out_specs=[head] * 3
        + [pl.BlockSpec((HEAD_DIM, 128), lambda h: (h, 0))] * 3
        + [pl.BlockSpec((HALF, 128), lambda h: (h, 0))] * 2,
        out_shape=[jax.ShapeDtypeStruct((width, slots), BF)] * 3
        + [jax.ShapeDtypeStruct((width, 128), F32)] * 3
        + [jax.ShapeDtypeStruct((width // 2, 128), F32)] * 2,
        scratch_shapes=[pltpu.VMEM((slots - FIRST, slots - CUT), F32)],
        compiler_params=params(),
        cost_estimate=cost(14),
        name="attend_back",
    )(counts, q, k, v, o, do, lse, cos, sin, places)


def out_kernel(o_ref, x_ref, w_ref, b_ref, gain_ref, shift_ref, h_ref, c_ref, ct_ref):
    h = x_ref[...].astype(F32) + (nn(o_ref[...].T, w_ref[...]) + b_ref[...])
    h_ref[...] = h
    xhat, _ = norm_parts(h)
    c = (xhat * gain_ref[...] + shift_ref[...]).astype(BF)
    c_ref[...] = c
    ct_ref[...] = c.T


def out_project(o, x, w, b, gain, shift):
    slots, width = x.shape
    blk = 256
    row = pl.BlockSpec((1, width), lambda i: (0, 0))
    rows = pl.BlockSpec((blk, width), lambda i: (i, 0))
    cols = pl.BlockSpec((width, blk), lambda i: (0, i))
    return pl.pallas_call(
        out_kernel,
        grid=(slots // blk,),
        in_specs=[cols, rows, pl.BlockSpec((width, width), lambda i: (0, 0)), row, row, row],
        out_specs=[rows, rows, cols],
        out_shape=[
            jax.ShapeDtypeStruct((slots, width), F32),
            jax.ShapeDtypeStruct((slots, width), BF),
            jax.ShapeDtypeStruct((width, slots), BF),
        ],
        compiler_params=params(),
        name="out_project",
    )(o, x, w, b, gain, shift)


def mlp_kernel(c_ref, ct_ref, dy_ref, h_ref, w1_ref, b1_ref, w2_ref, b2_ref, y_ref, dc_ref, g1_ref, g2_ref, gb1_ref, y_acc, hb_scr, dp_scr):
    slots = c_ref.shape[0]
    tile = 256

    @pl.when(pl.program_id(0) == 0)
    def _():
        y_acc[...] = h_ref[...] + b2_ref[...]
        dc_ref[...] = jnp.zeros_like(dc_ref)

    gb1_ref[...] = jnp.zeros_like(gb1_ref)

    def step(i, _):
        rows = pl.ds(pl.multiple_of(i * tile, tile), tile)
        pre = nn(c_ref[rows, :], w1_ref[...]) + b1_ref[...]
        square = pre * pre
        th = jnp.tanh(GELU_C * (pre + GELU_A * (pre * square)))
        cdf = 0.5 * (1.0 + th)
        hb = (pre * cdf).astype(BF)
        slope = cdf + 0.5 * pre * (1.0 - th * th) * (GELU_C * (1.0 + (3.0 * GELU_A) * square))
        hb_scr[rows, :] = hb
        y_acc[rows, :] += nn(hb, w2_ref[...])
        dpre = (nt(dy_ref[rows, :], w2_ref[...]) * slope).astype(BF)
        dp_scr[rows, :] = dpre
        dc_ref[rows, :] += nt(dpre, w1_ref[...])
        gb1_ref[...] += jnp.sum(dpre.astype(F32), axis=0, keepdims=True)
        return 0

    lax.fori_loop(0, slots // tile, step, 0)
    g1_ref[...] = nn(ct_ref[...], dp_scr[...]).astype(g1_ref.dtype)
    g2_ref[...] = tn(hb_scr[...], dy_ref[...]).astype(g2_ref.dtype)

    @pl.when(pl.program_id(0) == pl.num_programs(0) - 1)
    def _():
        y_ref[...] = y_acc[...].astype(BF)


def mlp(c, ct, dy, h, w1, b1, w2, b2):
    slots, width = c.shape
    hidden = w1.shape[1]
    blk = 512
    whole = lambda r, k: pl.BlockSpec((r, k), lambda j: (0, 0))
    return pl.pallas_call(
        mlp_kernel,
        grid=(hidden // blk,),
        in_specs=[
            whole(slots, width),
            whole(width, slots),
            whole(slots, width),
            whole(slots, width),
            pl.BlockSpec((width, blk), lambda j: (0, j)),
            pl.BlockSpec((1, blk), lambda j: (0, j)),
            pl.BlockSpec((blk, width), lambda j: (j, 0)),
            whole(1, width),
        ],
        out_specs=[
            whole(slots, width),
            whole(slots, width),
            pl.BlockSpec((width, blk), lambda j: (0, j)),
            pl.BlockSpec((blk, width), lambda j: (j, 0)),
            pl.BlockSpec((1, blk), lambda j: (0, j)),
        ],
        out_shape=[
            jax.ShapeDtypeStruct((slots, width), BF),
            jax.ShapeDtypeStruct((slots, width), F32),
            jax.ShapeDtypeStruct((width, hidden), BF),
            jax.ShapeDtypeStruct((hidden, width), BF),
            jax.ShapeDtypeStruct((1, hidden), F32),
        ],
        scratch_shapes=[
            pltpu.VMEM((slots, width), F32),
            pltpu.VMEM((slots, blk), BF),
            pltpu.VMEM((slots, blk), BF),
        ],
        compiler_params=params(),
        name="mlp",
    )(c, ct, dy, h, w1, b1, w2, b2)


def norm_back(grad, v, gain):
    xhat, inv = norm_parts(v)
    g = grad * gain
    lead = jnp.mean(g, axis=-1, keepdims=True)
    slope = jnp.mean(g * xhat, axis=-1, keepdims=True)
    return (g - lead - xhat * slope) * inv, jnp.sum(grad * xhat, axis=0, keepdims=True), jnp.sum(grad, axis=0, keepdims=True)


def out_back_kernel(dc_ref, h_ref, dy_ref, o_ref, w_ref, gain_ref, dh_ref, do_ref, gw_ref, sums_ref, acc_ref):
    i = pl.program_id(0)

    @pl.when(i == 0)
    def _():
        acc_ref[...] = jnp.zeros_like(acc_ref)
        sums_ref[...] = jnp.zeros_like(sums_ref)

    dy = dy_ref[...].astype(F32)
    part, dgain, dshift = norm_back(dc_ref[...], h_ref[...], gain_ref[...])
    dh = dy + part
    dh_ref[...] = dh
    dhb = dh.astype(BF)
    do_ref[...] = nt(w_ref[...], dhb).astype(BF)
    acc_ref[...] += nn(o_ref[...], dhb)
    sums_ref[0:1, :] += dgain
    sums_ref[1:2, :] += dshift
    sums_ref[2:3, :] += jnp.sum(dh, axis=0, keepdims=True)
    sums_ref[3:4, :] += jnp.sum(dy, axis=0, keepdims=True)

    @pl.when(i == pl.num_programs(0) - 1)
    def _():
        gw_ref[...] = acc_ref[...].astype(gw_ref.dtype)


def out_back(dc, h, dy, o, w, gain):
    slots, width = h.shape
    blk = 256
    rows = pl.BlockSpec((blk, width), lambda i: (i, 0))
    cols = pl.BlockSpec((width, blk), lambda i: (0, i))
    whole = lambda r, k: pl.BlockSpec((r, k), lambda i: (0, 0))
    return pl.pallas_call(
        out_back_kernel,
        grid=(slots // blk,),
        in_specs=[rows, rows, rows, cols, whole(width, width), whole(1, width)],
        out_specs=[rows, cols, whole(width, width), whole(8, width)],
        out_shape=[
            jax.ShapeDtypeStruct((slots, width), F32),
            jax.ShapeDtypeStruct((width, slots), BF),
            jax.ShapeDtypeStruct((width, width), BF),
            jax.ShapeDtypeStruct((8, width), F32),
        ],
        scratch_shapes=[pltpu.VMEM((width, width), F32)],
        compiler_params=params(),
        name="out_back",
    )(dc, h, dy, o, w, gain)


def qkv_back_kernel(at_ref, dqkv_ref, w_ref, x_ref, dh_ref, gain_ref, gw_ref, dx_ref, sums_ref, acc_ref):
    j = pl.program_id(0)

    @pl.when(j == 0)
    def _():
        acc_ref[...] = jnp.zeros_like(acc_ref)

    d = dqkv_ref[...]
    gw_ref[...] = nt(at_ref[...], d).astype(gw_ref.dtype)
    acc_ref[...] += nn(w_ref[...], d)

    @pl.when(j == pl.num_programs(0) - 1)
    def _():
        sums_ref[...] = jnp.zeros_like(sums_ref)
        tile = 256
        for i in range(x_ref.shape[0] // tile):
            rows = slice(i * tile, (i + 1) * tile)
            da = acc_ref[:, rows].T
            part, dgain, dshift = norm_back(da, x_ref[rows, :].astype(F32), gain_ref[...])
            dx_ref[rows, :] = (dh_ref[rows, :] + part).astype(BF)
            sums_ref[0:1, :] += dgain
            sums_ref[1:2, :] += dshift


def qkv_back(at, dqkv, w, x, dh, gain):
    slots, width = x.shape
    outs = w.shape[1]
    blk = 768
    whole = lambda r, k: pl.BlockSpec((r, k), lambda j: (0, 0))
    return pl.pallas_call(
        qkv_back_kernel,
        grid=(outs // blk,),
        in_specs=[
            whole(width, slots),
            pl.BlockSpec((blk, slots), lambda j: (j, 0)),
            pl.BlockSpec((width, blk), lambda j: (0, j)),
            whole(slots, width),
            whole(slots, width),
            whole(1, width),
        ],
        out_specs=[pl.BlockSpec((width, blk), lambda j: (0, j)), whole(slots, width), whole(8, width)],
        out_shape=[
            jax.ShapeDtypeStruct((width, outs), BF),
            jax.ShapeDtypeStruct((slots, width), BF),
            jax.ShapeDtypeStruct((8, width), F32),
        ],
        scratch_shapes=[pltpu.VMEM((width, slots), F32)],
        compiler_params=params(),
        name="qkv_back",
    )(at, dqkv, w, x, dh, gain)


def body_any(
    tokens, cotangent, image_counts, patch_rows, patch_cols, ln1_gain, ln1_bias, qkv_weight, qkv_bias, rope_freqs,
    out_weight, out_bias, ln2_gain, ln2_bias, fc1_weight, fc1_bias, fc2_weight, fc2_bias,
):
    x = tokens[0]
    dy = cotangent[0]
    counts = image_counts[0]
    width = x.shape[1]
    small = (ln1_gain, ln1_bias, qkv_bias, rope_freqs, out_bias, ln2_gain, ln2_bias, fc1_bias, fc2_bias)
    sizes = [s.shape[0] for s in small]
    gather = partial(lax.all_gather, axis_name="fsdp", axis=0, tiled=True)
    packed = lax.all_gather(jnp.concatenate(small), "fsdp", axis=0)
    vectors = []
    at = 0
    for size in sizes:
        vectors.append(packed[:, at : at + size].reshape(-1).astype(F32))
        at += size
    gain1, shift1, b_qkv, freqs, b_out, gain2, shift2, b1, b2 = vectors
    w_qkv = gather(qkv_weight)
    w_out = gather(out_weight)
    w1 = gather(fc1_weight)
    w2 = gather(fc2_weight)

    row = lambda v: v[None, :]
    a, a_t = norm1(x, row(gain1), row(shift1))
    places = jnp.concatenate([patch_cols, patch_rows], axis=0).astype(F32)
    half = freqs.shape[0] // 2
    angle = freqs[:half, None] * places[0:1] + freqs[half:, None] * places[1:2]
    cos = jnp.cos(angle)
    sin = jnp.sin(angle)
    q, k, v = project(a, w_qkv, b_qkv[:, None], cos, sin)
    o, lse = attend(counts, q, k, v)
    h, c, c_t = out_project(o, x, w_out, row(b_out), row(gain2), row(shift2))
    y, dc, g_w1, g_w2, g_b1 = mlp(c, c_t, dy, h, w1, row(b1), w2, row(b2))
    dh, do, g_wout, sums2 = out_back(dc, h, dy, o, w_out, row(gain2))
    dq, dk, dv, s_bq, s_bk, s_bv, s_fc, s_fr = attend_back(counts, q, k, v, o, do, lse, cos, sin, places)
    dqkv = jnp.concatenate([dq, dk, dv], axis=0)
    g_wqkv, dx, sums1 = qkv_back(a_t, dqkv, w_qkv, x, dh, row(gain1))

    scatter = partial(lax.psum_scatter, axis_name="fsdp", scatter_dimension=0, tiled=True)
    both = lambda g: lax.psum(scatter(g), "rep").astype(F32)
    g_bqkv = jnp.sum(jnp.concatenate([s_bq, s_bk, s_bv], axis=0), axis=1)
    g_freq = jnp.sum(jnp.concatenate([s_fc, s_fr], axis=0), axis=1)
    small_grads = (sums1[0], sums1[1], g_bqkv, g_freq, sums2[2], sums2[0], sums2[1], g_b1[0], sums2[3])
    shards = mesh_size = packed.shape[0]
    block = jnp.concatenate([g.reshape(shards, -1) for g in small_grads], axis=1)
    total = lax.psum(block, ("rep", "fsdp"))
    mine = lax.dynamic_index_in_dim(total, lax.axis_index("fsdp"), 0, keepdims=False)
    outs = []
    at = 0
    for size in sizes:
        outs.append(mine[at : at + size])
        at += size
    s_gain1, s_shift1, s_bqkv, s_freq, s_bout, s_gain2, s_shift2, s_b1, s_b2 = outs
    return (
        y[None], dx[None], s_gain1, s_shift1, both(g_wqkv), s_bqkv, s_freq, both(g_wout), s_bout,
        s_gain2, s_shift2, both(g_w1), s_b1, both(g_w2), s_b2,
    )


SHARDS = 16
GROUPS = 2
LEAVING = (0, 8, 4, 12, 2, 10, 6, 14)


def swap(v, mask):
    return lax.ppermute(v, "fsdp", [(i, i ^ mask) for i in range(SHARDS)])


def tie(v, *after):
    return lax.optimization_barrier((v,) + after)[0]


class Gather:
    def __init__(self, mine):
        self.piece = {0: mine}

    def send(self, source, mask, after):
        v = self.piece[source]
        self.piece[source ^ mask] = swap(tie(v, *after) if after else v, mask)

    def hold(self, sources, after):
        for p in sources:
            self.piece[p] = tie(self.piece[p], after)

    def stage1(self, *after):
        for mask in (8, 4, 2):
            self.send(0, mask, after)

    def stage2(self, *after):
        self.send(8, 4, after)
        self.send(4, 2, after)
        self.send(8, 2, after)

    def stage3(self, *after):
        self.send(12, 2, after)

    def cores(self, *after):
        for p in (0, 8, 4, 2, 6, 10, 12, 14):
            self.send(p, 1, after)
        return [self.piece[p] for p in range(SHARDS)]


class Scatter:
    def __init__(self, near, far):
        self.got = [near, swap(far, 1)]
        self.size = 4

    def total(self, lo, hi):
        out = self.got[0][lo:hi].astype(F32)
        for g in self.got[1:]:
            out = out + g[lo:hi].astype(F32)
        return out.astype(BF)

    def hold(self, *after):
        self.got[-1] = tie(self.got[-1], *after)

    def step(self):
        lo = self.size
        sent = self.total(lo, 2 * lo)
        self.got.append(swap(sent, {4: 2, 2: 4, 1: 8}[lo]))
        self.size = lo // 2
        return sent

    def finish(self):
        mine = self.total(0, 1)[0]
        return mine, across(mine)


class SplitScatter(Scatter):
    def __init__(self, near, far):
        self.start = [near, swap(far, 1)]
        self.size = 4

    def split(self):
        sent = (self.start[0][1].astype(F32) + self.start[1][1].astype(F32)).astype(BF)
        got = across(sent)
        self.got = [self.start[0][0], self.start[1][0], got]
        return sent


def across(v):
    return lax.ppermute(v, "rep", [(0, 1), (1, 0)])


def start_all(copies):
    for copy in copies:
        copy.start()


def wait_all(copies):
    for copy in copies:
        copy.wait()


def fetch(refs, order_ref, moves, sem):
    copies = []
    for p, ref in enumerate(refs):
        for rows, place in moves:
            copies.append(pltpu.make_async_copy(ref.at[rows], place(order_ref[p]), sem.at[len(copies)]))
    return copies


ANY = pl.BlockSpec(memory_space=pl.ANY)
HBM = pl.BlockSpec(memory_space=pltpu.HBM)
SMEM = pl.BlockSpec(memory_space=pltpu.SMEM)
VMEM = pl.BlockSpec(memory_space=pltpu.VMEM)


LINES = 16


def group_piece_kernel(w_ref, o_ref, v_ref, a_ref, b_ref):
    rows, cols = w_ref.shape[0], a_ref.shape[1]
    for i in range(3):
        for g, out in enumerate((a_ref, b_ref)):
            out[i * rows : (i + 1) * rows, :] = w_ref[:, (i * GROUPS + g) * cols : (i * GROUPS + g + 1) * cols]
    for i in range(2):
        b_ref[(3 + i) * rows : (4 + i) * rows, :] = o_ref[:, i * cols : (i + 1) * cols]
    a_ref[3 * rows :, :] = jnp.concatenate([v_ref[...], jnp.zeros((LINES - v_ref.shape[0], cols), BF)], axis=0)


def group_pieces(w, w_out, vectors):
    rows, cols = w.shape[0], w_out.shape[1] // 2
    return pl.pallas_call(
        group_piece_kernel,
        in_specs=[VMEM] * 3,
        out_specs=[VMEM, VMEM],
        out_shape=[jax.ShapeDtypeStruct((3 * rows + LINES, cols), BF), jax.ShapeDtypeStruct((5 * rows, cols), BF)],
        compiler_params=params(),
        cost_estimate=cost(2),
        name="group_pieces",
    )(w, w_out, vectors)


def mlp_piece_kernel(w1_ref, w2_ref, *outs):
    rows1 = w1_ref.shape[0]
    own = w2_ref.shape[0] // 2
    per = SHARDS // 2
    w1 = w1_ref[...].astype(F32)
    for i, out in enumerate(outs):
        for b in range(2):
            runs = [w1[:, (2 * (b * per + j) + i) * own :][:, :own] for j in range(per)]
            out[b * rows1 : (b + 1) * rows1, :] = jnp.concatenate(runs, axis=1).astype(BF)
        out[2 * rows1 :, :] = w2_ref[i * own : (i + 1) * own, :]


def mlp_pieces(w1, w2):
    rows = 2 * w1.shape[0] + w2.shape[0] // 2
    return pl.pallas_call(
        mlp_piece_kernel,
        in_specs=[VMEM, VMEM],
        out_specs=[VMEM, VMEM],
        out_shape=[jax.ShapeDtypeStruct((rows, w2.shape[1]), BF)] * 2,
        compiler_params=params(),
        cost_estimate=cost(2),
        name="mlp_pieces",
    )(w1, w2)


def mlp_join_kernel(order_ref, c_ref, c_other_ref, d_ref, d_other_ref, w1_ref, w2_ref):
    rows1 = w1_ref.shape[0]
    own = w2_ref.shape[0] // 2
    per = SHARDS // 2
    c = c_ref[...].astype(F32) + c_other_ref[...].astype(F32)
    mine = d_ref[...].astype(F32)
    other = d_other_ref[...].astype(F32)
    here = order_ref[SHARDS] == 0
    d = jnp.where(here, mine, other)
    runs = []
    for b in range(2):
        for j in range(per):
            runs += [m[b * rows1 : (b + 1) * rows1, j * own : (j + 1) * own] for m in (c, d)]
    w1_ref[...] = jnp.concatenate(runs, axis=1)
    w2_ref[:own, :] = c[2 * rows1 :]
    w2_ref[own:, :] = jnp.where(here, other, mine)


def mlp_join(rows1, order, parts):
    own = parts[0].shape[0] - 2 * rows1
    return pl.pallas_call(
        mlp_join_kernel,
        in_specs=[SMEM] + [VMEM] * 4,
        out_specs=[VMEM] * 2,
        out_shape=[
            jax.ShapeDtypeStruct((rows1, 2 * own * SHARDS), F32),
            jax.ShapeDtypeStruct((2 * own, parts[0].shape[1]), F32),
        ],
        compiler_params=params(8),
        cost_estimate=cost(3),
        name="mlp_join",
    )(order, *parts)


def spread(packed, lo, size):
    return jnp.concatenate([packed[j : j + 1, lo : lo + size] for j in range(packed.shape[0])], axis=1)


def column(v):
    return jnp.broadcast_to(v, (8, v.shape[1])).T[:, 0:1]


def prepare_kernel(sizes, order_ref, x_ref, cols_ref, rows_ref, *rest):
    pieces = rest[:SHARDS]
    at_ref, cos_ref, sin_ref, vec_ref, b1_ref, bias_ref, sel_ref, line_scr, table_scr, sem = rest[SHARDS:]
    half = cos_ref.shape[0]

    @pl.when(pl.program_id(0) == 0)
    def _():
        last = pieces[0].shape[0]
        copies = fetch(pieces, order_ref, [(slice(last - LINES, last), lambda d: line_scr.at[d])], sem)
        start_all(copies)
        wait_all(copies)
        packed = jnp.concatenate([line_scr[:, i, :] for i in range(2)], axis=1).astype(F32)
        starts = [sum(sizes[:i]) for i in range(len(sizes))]
        gain1, shift1, b_qkv, freqs, b_out, gain2, shift2 = (spread(packed, starts[i], sizes[i]) for i in range(7))
        b2 = spread(packed, starts[8], sizes[8])
        for i, v in enumerate((b_out, gain1, gain2, shift2, b2, shift1)):
            vec_ref[i : i + 1, :] = v
        own = sizes[7] // 2
        for i in range(2):
            b1_ref[i : i + 1, :] = spread(packed, starts[7] + i * own, own)
        bias_ref[...] = column(b_qkv)
        freq = column(freqs)
        spots = lax.broadcasted_iota(jnp.int32, (1, 128), 1).astype(F32)
        for i in range(2):
            angle = freq[i * half : (i + 1) * half] * spots
            for k, table in enumerate((jnp.cos(angle), jnp.sin(angle))):
                for n in range(3):
                    term = table.astype(BF)
                    table_scr[i, k, n] = term
                    table = table - term.astype(F32)

    xhat, _ = norm_parts(x_ref[...].astype(F32))
    at_ref[...] = (xhat * vec_ref[1:2, :] + vec_ref[5:6, :]).astype(BF).T
    found = []
    for i, at in enumerate((cols_ref[...], rows_ref[...])):
        one_hot = jnp.where(lax.broadcasted_iota(jnp.int32, (128, at.shape[1]), 0) == at, 1.0, 0.0).astype(BF)
        found.append([sum(nn(table_scr[i, k, n], one_hot) for n in range(3)) for k in range(2)])
    (cos_c, sin_c), (cos_r, sin_r) = found
    cos_ref[...] = cos_c * cos_r - sin_c * sin_r
    sin_ref[...] = sin_c * cos_r + cos_c * sin_r
    line = lax.broadcasted_iota(jnp.int32, sel_ref.shape, 0)
    sel = jnp.where(line == 0, cols_ref[...].astype(F32), rows_ref[...].astype(F32))
    sel_ref[...] = jnp.where(line < 2, sel, jnp.where(line == 2, 1.0, 0.0)).astype(BF)


def prepare(sizes, order, x, patch_cols, patch_rows, pieces):
    slots, width = x.shape
    own = sizes[7] // 2
    blk = 256
    shape = jax.ShapeDtypeStruct
    tall = lambda n: pl.BlockSpec((n, blk), lambda i: (0, i))
    whole = lambda r, k: pl.BlockSpec((r, k), lambda i: (0, 0))
    return pl.pallas_call(
        partial(prepare_kernel, sizes),
        grid=(slots // blk,),
        in_specs=[SMEM, pl.BlockSpec((blk, width), lambda i: (i, 0)), tall(1), tall(1)] + [HBM] * SHARDS,
        out_specs=[
            tall(width), tall(width // 2), tall(width // 2),
            whole(8, width), whole(2, own * SHARDS), whole(3 * width, 1), tall(16),
        ],
        out_shape=[
            shape((width, slots), BF),
            shape((width // 2, slots), F32),
            shape((width // 2, slots), F32),
            shape((8, width), F32),
            shape((2, own * SHARDS), F32),
            shape((3 * width, 1), F32),
            shape((16, slots), BF),
        ],
        scratch_shapes=[
            pltpu.VMEM((SHARDS, LINES, width // GROUPS), BF),
            pltpu.VMEM((2, 2, 3, width // 2, 128), BF),
            pltpu.SemaphoreType.DMA((SHARDS,)),
        ],
        compiler_params=params(),
        cost_estimate=cost(8),
        name="prepare",
    )(order, x, patch_cols, patch_rows, *pieces)


def pack_kernel(sums1_ref, sums2_ref, b1a_ref, b1b_ref, *rest):
    heads, out_ref = rest[:-1], rest[-1]
    bias = [r[2:3, :] for r in heads[:GROUPS]]
    freq = [r[...] for r in heads[GROUPS:]]
    cols = bias[0].shape[1] // 3
    b_qkv = jnp.concatenate([b[:, i * cols : (i + 1) * cols] for i in range(3) for b in bias], axis=1)
    g_freq = jnp.concatenate([f[i : i + 1] for i in range(2) for f in freq], axis=1)
    vectors = (
        sums1_ref[0:1, :], sums1_ref[1:2, :], b_qkv, g_freq, sums2_ref[2:3, :], sums2_ref[0:1, :], sums2_ref[1:2, :],
        b1a_ref[...], b1b_ref[...], sums2_ref[3:4, :],
    )
    for j in range(SHARDS):
        runs = []
        for v in vectors:
            n = v.shape[1] // SHARDS
            runs.append(v[:, j * n : (j + 1) * n])
        out_ref[j] = jnp.concatenate(runs, axis=1)


def pack(size, *sums):
    return pl.pallas_call(
        pack_kernel,
        in_specs=[VMEM] * len(sums),
        out_specs=VMEM,
        out_shape=jax.ShapeDtypeStruct((SHARDS, 1, size), F32),
        compiler_params=params(4),
        cost_estimate=cost(3),
        name="pack",
    )(*sums)


def group_kernel(order_ref, at_ref, bq_ref, bk_ref, bv_ref, cos_ref, sin_ref, *rest):
    pieces, (q_ref, k_ref, v_ref, w_scr, wt_scr, sem) = rest[:SHARDS], rest[SHARDS:]
    cols = q_ref.shape[0]
    part = w_scr.shape[1] // 3

    @pl.when(pl.program_id(0) == 0)
    def _():
        copies = fetch(pieces, order_ref, [(slice(0, 3 * part), lambda d: w_scr.at[d])], sem)
        start_all(copies)
        wait_all(copies)
        for i in range(3):
            wt_scr[i] = w_scr[:, i * part : (i + 1) * part, :].reshape(SHARDS * part, cols).T

    a_t = at_ref[...]
    cos = cos_ref[...]
    sin = sin_ref[...]
    for i, b_ref, out_ref, scale in ((0, bq_ref, q_ref, HEAD_DIM**-0.5), (1, bk_ref, k_ref, 1.0)):
        u = nn(wt_scr[i], a_t) + b_ref[...]
        for h in range(cols // HEAD_DIM):
            u1 = u[h * HEAD_DIM : h * HEAD_DIM + HALF]
            u2 = u[h * HEAD_DIM + HALF : (h + 1) * HEAD_DIM]
            c = cos[h * HALF : (h + 1) * HALF]
            s = sin[h * HALF : (h + 1) * HALF]
            out_ref[h * HEAD_DIM : h * HEAD_DIM + HALF, :] = ((u1 * c - u2 * s) * scale).astype(BF)
            out_ref[h * HEAD_DIM + HALF : (h + 1) * HEAD_DIM, :] = ((u1 * s + u2 * c) * scale).astype(BF)
    v_ref[...] = (nn(wt_scr[2], a_t) + bv_ref[...]).astype(BF)


def project_group(group, order, a_t, bias, cos, sin, pieces):
    width, slots = a_t.shape
    cols = pieces[0].shape[1]
    blk = 512
    tall = lambda n, at: pl.BlockSpec((n, blk), lambda i: (at, i))
    return pl.pallas_call(
        group_kernel,
        grid=(slots // blk,),
        in_specs=[SMEM, tall(width, 0)]
        + [pl.BlockSpec((cols, 1), lambda i, n=n: (n * GROUPS + group, 0)) for n in range(3)]
        + [tall(cols // 2, group)] * 2
        + [HBM] * SHARDS,
        out_specs=[tall(cols, 0)] * 3,
        out_shape=[jax.ShapeDtypeStruct((cols, slots), BF)] * 3,
        scratch_shapes=[
            pltpu.VMEM((SHARDS, 3 * width // SHARDS, cols), BF),
            pltpu.VMEM((3, cols, width), BF),
            pltpu.SemaphoreType.DMA((SHARDS,)),
        ],
        compiler_params=params(),
        cost_estimate=cost(7),
        name="qkv_group",
    )(order, a_t, bias, bias, bias, cos, sin, *pieces)


def out_moves(w_scr, start):
    rows = w_scr.shape[1]
    half = w_scr.shape[2] // 2
    return [
        (slice(start + i * rows, start + (i + 1) * rows), lambda d, i=i: w_scr.at[d, :, pl.ds(i * half, half)])
        for i in range(2)
    ]


def out_group_kernel(start, order_ref, vec_ref, *rest):
    o_refs, x_ref, pieces = rest[:GROUPS], rest[GROUPS], rest[GROUPS + 1 : GROUPS + 1 + SHARDS]
    h_ref, c_ref, ct_ref, w_scr, sem = rest[GROUPS + 1 + SHARDS :]

    @pl.when(pl.program_id(0) == 0)
    def _():
        copies = fetch(pieces, order_ref, out_moves(w_scr, start), sem)
        start_all(copies)
        wait_all(copies)

    width = x_ref.shape[1]
    o = jnp.concatenate([r[...].T for r in o_refs], axis=1)
    h = x_ref[...].astype(F32) + (nn(o, w_scr[...].reshape(width, width)) + vec_ref[0:1, :])
    h_ref[...] = h.astype(BF)
    xhat, _ = norm_parts(h)
    c = (xhat * vec_ref[2:3, :] + vec_ref[3:4, :]).astype(BF)
    c_ref[...] = c
    ct_ref[...] = c.T


def out_project_fast(order, o, x, vec, pieces, start):
    slots, width = x.shape
    blk = 256
    rows = pl.BlockSpec((blk, width), lambda i: (i, 0))
    cols = pl.BlockSpec((width, blk), lambda i: (0, i))
    return pl.pallas_call(
        partial(out_group_kernel, start),
        grid=(slots // blk,),
        in_specs=[SMEM, VMEM] + [pl.BlockSpec((width // GROUPS, blk), lambda i: (0, i))] * GROUPS + [rows] + [HBM] * SHARDS,
        out_specs=[rows, rows, cols],
        out_shape=[
            jax.ShapeDtypeStruct((slots, width), BF),
            jax.ShapeDtypeStruct((slots, width), BF),
            jax.ShapeDtypeStruct((width, slots), BF),
        ],
        scratch_shapes=[pltpu.VMEM((SHARDS, width // SHARDS, width), BF), pltpu.SemaphoreType.DMA((2 * SHARDS,))],
        compiler_params=params(),
        cost_estimate=cost(8),
        name="out_project",
    )(order, vec, *o, x, *pieces)


def mlp_half_kernel(part, first, split, n_in, order_ref, c_in, ct_in, dy_in, b1_ref, vec_ref, *rest):
    acc_in, rest = (rest[:1], rest[1:]) if first else (rest[:2], rest[2:])
    pieces, rest = rest[:n_in], rest[n_in:]
    n_g = 2 if split else 1
    y_ref, dc_ref = rest[:2]
    g_refs = rest[2 : 2 + n_g]
    gb1_ref, w1_scr, w2_scr, g1_scr, g2_scr, hb_scr, dp_scr, y_acc, dc_acc = rest[2 + n_g : 11 + n_g]
    c_ref, ct_ref, dy_ref, y_out, dc_out, sem, load_sem = rest[11 + n_g :]
    slots, width = c_ref.shape
    rows1 = w1_scr.shape[2]
    rows2 = w2_scr.shape[1]
    blk = w1_scr.shape[3]
    steps = w1_scr.shape[0]
    per = blk // rows2
    tile = 512
    refs = [pieces[0].at[p] for p in range(SHARDS)] if n_in == 1 else pieces
    places = range(SHARDS) if n_in == 1 else order_ref
    loads = [
        fetch(refs, places, [(slice(j * rows1, (j + 1) * rows1), lambda d, j=j: w1_scr.at[j, d])], sem.at[j])
        for j in range(steps)
    ]
    loads.insert(1, fetch(refs, places, [(slice(steps * rows1, steps * rows1 + rows2), lambda d: w2_scr.at[d])], sem.at[steps]))
    sums = list(zip(acc_in, (y_out, dc_out)))
    rows_in = [(c_in, c_ref), (dy_in, dy_ref), (ct_in, ct_ref)]
    whole = [pltpu.make_async_copy(src, dst, load_sem.at[i]) for i, (src, dst) in enumerate(rows_in + sums)]
    (c_load, dy_load, ct_load), sums = whole[:3], whole[3:]
    for copies in [[c_load], loads[0], [dy_load], loads[1], sums, [ct_load]] + loads[2:]:
        start_all(copies)
    sends = []
    for j in range(steps):
        cols = slice(j * blk, (j + 1) * blk)
        wait_all([c_load] + loads[0] if j == 0 else loads[1 + j])
        w1 = w1_scr[j].reshape(width, blk)
        w2 = None
        total = None
        for i in range(slots // tile):
            rows = slice(i * tile, (i + 1) * tile)
            pre = nn(c_ref[rows, :], w1) + b1_ref[part : part + 1, cols]
            square = pre * pre
            th = jnp.tanh(GELU_C * (pre + GELU_A * (pre * square)))
            cdf = 0.5 * (1.0 + th)
            hb = (pre * cdf).astype(BF)
            slope = cdf + 0.5 * pre * (1.0 - th * th) * (GELU_C * (1.0 + (3.0 * GELU_A) * square))
            hb_scr[rows, :] = hb
            if w2 is None:
                if j == 0:
                    wait_all(loads[1] + [dy_load] + sums)
                w2 = w2_scr[j * per : (j + 1) * per].reshape(blk, width)
            before = y_acc if j else y_out
            y = before[rows, :].astype(F32) + nn(hb, w2)
            if first and j == 0:
                y = y + vec_ref[4:5, :]
            dpre = (nt(dy_ref[rows, :], w2) * slope).astype(BF)
            dp_scr[rows, :] = dpre
            term = jnp.sum(dpre.astype(F32), axis=0, keepdims=True)
            total = term if total is None else total + term
            dc = nt(dpre, w1)
            if j or not first:
                dc = dc + (dc_acc if j else dc_out)[rows, :].astype(F32)
            if j == steps - 1:
                y_out[rows, :] = y.astype(BF)
                dc_out[rows, :] = dc.astype(BF)
                sends += [
                    pltpu.make_async_copy(y_out.at[rows], y_ref.at[rows], load_sem.at[5 + 2 * i]),
                    pltpu.make_async_copy(dc_out.at[rows], dc_ref.at[rows], load_sem.at[6 + 2 * i]),
                ]
                start_all(sends[-2:])
            else:
                y_acc[rows, :] = y
                dc_acc[rows, :] = dc
        gb1_ref[:, cols] = total
        if j == 0:
            wait_all([ct_load])
        g1_scr[j] = nn(ct_ref[...], dp_scr[...]).astype(BF).reshape(SHARDS, rows1, blk)
        if split:
            mine = order_ref[SHARDS]
            dests = [(g_refs[b], i, order_ref[p + b]) for b in range(2) for i, p in enumerate(LEAVING)]
            place = lambda dst, i, lo, n: dst.at[lax.rem(lo // (steps * rows1) + mine, 2), i, pl.ds(lo % (steps * rows1), n)]
        else:
            dests = [(g_refs[0], p, p) for p in range(SHARDS)]
            place = lambda dst, i, lo, n: dst.at[i, pl.ds(lo, n)]
        copies = [
            pltpu.make_async_copy(g1_scr.at[j, d], place(dst, i, j * rows1, rows1), sem.at[j, n])
            for n, (dst, i, d) in enumerate(dests)
        ]
        start_all(copies)
        sends += copies
        g2_scr[j * per : (j + 1) * per] = tn(hb_scr[...], dy_ref[...]).astype(BF).reshape(per, rows2, width)
    copies = [
        pltpu.make_async_copy(g2_scr.at[d], place(dst, i, steps * rows1, rows2), sem.at[steps, n])
        for n, (dst, i, d) in enumerate(dests)
    ]
    start_all(copies)
    wait_all(sends + copies)


def mlp_half(part, order, c, ct, dy, b1, vec, sums, pieces, split):
    slots, width = c.shape
    rows1 = width // SHARDS
    rows2 = pieces[0].shape[-2] - 2 * rows1
    hidden = rows2 * SHARDS
    steps = 2
    blk = hidden // steps
    first = len(sums) == 1
    block = jax.ShapeDtypeStruct((SHARDS, 2 * rows1 + rows2, width), BF)
    if split:
        block = jax.ShapeDtypeStruct((2, SHARDS // 2, rows2, width), BF)
    return pl.pallas_call(
        partial(mlp_half_kernel, part, first, split, len(pieces)),
        in_specs=[SMEM] + [ANY] * 3 + [VMEM] * 2 + [ANY] * len(sums) + [HBM] * len(pieces),
        out_specs=[ANY, ANY] + [ANY] * (2 if split else 1) + [VMEM],
        out_shape=[jax.ShapeDtypeStruct((slots, width), BF)] * 2
        + [block] * (2 if split else 1)
        + [jax.ShapeDtypeStruct((1, hidden), F32)],
        scratch_shapes=[
            pltpu.VMEM((steps, SHARDS, rows1, blk), BF),
            pltpu.VMEM((SHARDS, rows2, width), BF),
            pltpu.VMEM((steps, SHARDS, rows1, blk), BF),
            pltpu.VMEM((SHARDS, rows2, width), BF),
            pltpu.VMEM((slots, blk), BF),
            pltpu.VMEM((slots, blk), BF),
            pltpu.VMEM((slots, width), F32),
            pltpu.VMEM((slots, width), F32),
            pltpu.VMEM((slots, width), BF),
            pltpu.VMEM((width, slots), BF),
            pltpu.VMEM((slots, width), BF),
            pltpu.VMEM((slots, width), BF),
            pltpu.VMEM((slots, width), BF),
            pltpu.SemaphoreType.DMA((steps + 1, SHARDS)),
            pltpu.SemaphoreType.DMA((9,)),
        ],
        compiler_params=params(),
        cost_estimate=cost(23),
        name="mlp_half",
    )(order, c, ct, dy, b1, vec, *sums, *pieces)


def out_back_fast_kernel(start, order_ref, dc_ref, h_ref, dy_ref, vec_ref, *rest):
    o_refs, pieces = rest[:GROUPS], rest[GROUPS : GROUPS + SHARDS]
    dh_ref, do_ref, near_ref, far_ref, sums_ref, acc_ref, g_scr, w_scr, sem = rest[GROUPS + SHARDS :]
    i = pl.program_id(0)
    width = h_ref.shape[1]
    each = width // SHARDS
    half = width // 2

    @pl.when(i == 0)
    def _():
        copies = fetch(pieces, order_ref, out_moves(w_scr, start), sem)
        start_all(copies)
        acc_ref[...] = jnp.zeros_like(acc_ref)
        sums_ref[...] = jnp.zeros_like(sums_ref)
        wait_all(copies)

    dy = dy_ref[...].astype(F32)
    part, dgain, dshift = norm_back(dc_ref[...].astype(F32), h_ref[...].astype(F32), vec_ref[2:3, :])
    dh = dy + part
    dhb = dh.astype(BF)
    dh_ref[...] = dhb
    do_ref[...] = nt(w_scr[...].reshape(width, width), dhb).astype(BF)
    rows = width // GROUPS
    for g in range(GROUPS):
        acc_ref[g * rows : (g + 1) * rows, :] += nn(o_refs[g][...], dhb)
    sums_ref[0:1, :] += dgain
    sums_ref[1:2, :] += dshift
    sums_ref[2:3, :] += jnp.sum(dh, axis=0, keepdims=True)
    sums_ref[3:4, :] += jnp.sum(dy, axis=0, keepdims=True)

    @pl.when(i == pl.num_programs(0) - 1)
    def _():
        g_scr[...] = acc_ref[...].astype(BF).reshape(g_scr.shape)
        copies = []
        for b, out in enumerate((near_ref, far_ref)):
            for n, p in enumerate(LEAVING):
                for k in range(2):
                    src = g_scr.at[order_ref[p + b], :, pl.ds(k * half, half)]
                    dst = out.at[n, pl.ds((3 + k) * each, each)]
                    copies.append(pltpu.make_async_copy(src, dst, sem.at[len(copies)]))
        start_all(copies)
        wait_all(copies)


def out_back_fast(order, dc, h, dy, vec, o, pieces, start):
    slots, width = h.shape
    blk = 256
    rows = pl.BlockSpec((blk, width), lambda i: (i, 0))
    cols = pl.BlockSpec((width, blk), lambda i: (0, i))
    whole = lambda r, k: pl.BlockSpec((r, k), lambda i: (0, 0))
    block = jax.ShapeDtypeStruct((SHARDS // 2, 5 * width // SHARDS, width // 2), BF)
    return pl.pallas_call(
        partial(out_back_fast_kernel, start),
        grid=(slots // blk,),
        in_specs=[SMEM, rows, rows, rows, VMEM]
        + [pl.BlockSpec((width // GROUPS, blk), lambda i: (0, i))] * GROUPS
        + [HBM] * SHARDS,
        out_specs=[rows, cols, ANY, ANY, whole(8, width)],
        out_shape=[
            jax.ShapeDtypeStruct((slots, width), BF),
            jax.ShapeDtypeStruct((width, slots), BF),
            block,
            block,
            jax.ShapeDtypeStruct((8, width), F32),
        ],
        scratch_shapes=[
            pltpu.VMEM((width, width), F32),
            pltpu.VMEM((SHARDS, width // SHARDS, width), BF),
            pltpu.VMEM((SHARDS, width // SHARDS, width), BF),
            pltpu.SemaphoreType.DMA((2 * SHARDS,)),
        ],
        compiler_params=params(),
        cost_estimate=cost(12),
        name="out_back",
    )(order, dc, h, dy, vec, *o, *pieces)


def heads_back_kernel(
    counts_ref, q_ref, k_ref, v_ref, o_ref, do_ref, lse_ref, cos_ref, sin_ref,
    dq_ref, dk_ref, dv_ref, dangle_ref, bias_ref,
):
    slots = q_ref.shape[1]

    @pl.when(pl.program_id(0) == 0)
    def _():
        bias_ref[...] = second_bias(counts_ref, slots)

    lane1 = lax.broadcasted_iota(jnp.int32, (1, WIDE), 1)
    lane2 = lax.broadcasted_iota(jnp.int32, (1, slots - CUT), 1)
    scale = HEAD_DIM**-0.5

    def part(scores, grads, queries, outs, keys, delta_row, first):
        prob = jnp.exp(scores)
        ds = (prob * (grads - delta_row)).astype(BF)
        pb = prob.astype(BF)
        gap = jnp.zeros((keys.shape[1] - pb.shape[0], pb.shape[1]), BF)
        pb = jnp.concatenate([pb, gap] if first else [gap, pb], axis=0)
        ds = jnp.concatenate([ds, gap] if first else [gap, ds], axis=0)
        return nn(keys, ds), nt(queries, ds), nt(outs, pb)

    for h in range(q_ref.shape[0] // HEAD_DIM):
        top = h * HEAD_DIM
        rows = slice(top, top + HEAD_DIM)
        kt = k_ref[rows, :]
        k = kt.T
        v = v_ref[rows, :].T
        q = q_ref[rows, :]
        do = do_ref[rows, :]
        lse = lse_ref[h]
        delta = jnp.sum(do.astype(F32) * o_ref[rows, :].astype(F32), axis=0, keepdims=True)
        lse1 = jnp.where(lane1 < FIRST, lse[:, :WIDE], -NEG)
        lse2 = jnp.where(lane2 >= FIRST - CUT, lse[:, CUT:], -NEG)
        grads1 = part(
            nn(k[:FIRST], q[:, :WIDE]) - lse1, nn(v[:FIRST], do[:, :WIDE]),
            q[:, :WIDE], do[:, :WIDE], kt[:, :WIDE], delta[:, :WIDE], True,
        )
        grads2 = part(
            nn(k[FIRST:], q[:, CUT:]) + bias_ref[...] - lse2, nn(v[FIRST:], do[:, CUT:]),
            q[:, CUT:], do[:, CUT:], kt[:, CUT:], delta[:, CUT:], False,
        )
        dq, dk, dv = (
            jnp.concatenate([one[:, :CUT], one[:, CUT:] + two[:, : WIDE - CUT], two[:, WIDE - CUT :]], axis=1)
            for one, two in zip(grads1, grads2)
        )
        cos = cos_ref[h * HALF : (h + 1) * HALF, :]
        sin = sin_ref[h * HALF : (h + 1) * HALF, :]
        dangle = None
        for r, rot, out in ((dq * scale, q.astype(F32) * (1.0 / scale), dq_ref), (dk, kt.astype(F32), dk_ref)):
            r1, r2 = r[:HALF], r[HALF:]
            term = r2 * rot[:HALF] - r1 * rot[HALF:]
            dangle = term if dangle is None else dangle + term
            out[top : top + HALF, :] = (r1 * cos + r2 * sin).astype(BF)
            out[top + HALF : top + HEAD_DIM, :] = (r2 * cos - r1 * sin).astype(BF)
        dv_ref[rows, :] = dv.astype(BF)
        dangle_ref[h * HALF : (h + 1) * HALF, :] = dangle.astype(BF)


def heads_back(group, counts, q, k, v, o, do, lse, cos, sin):
    width, slots = q.shape
    heads = width // HEAD_DIM
    each = 2
    steps = heads // each
    head = pl.BlockSpec((each * HEAD_DIM, slots), lambda h: (h, 0))
    half = pl.BlockSpec((each * HALF, slots), lambda h: (h, 0))
    turn = pl.BlockSpec((each * HALF, slots), lambda h: (group * steps + h, 0))
    late = pl.BlockSpec((each * HEAD_DIM, slots), lambda h: (group * steps + h, 0))
    return pl.pallas_call(
        heads_back_kernel,
        grid=(steps,),
        in_specs=[SMEM] + [head] * 4 + [late, pl.BlockSpec((each, 1, slots), lambda h: (h, 0, 0)), turn, turn],
        out_specs=[head] * 3 + [half],
        out_shape=[jax.ShapeDtypeStruct((width, slots), BF)] * 3 + [jax.ShapeDtypeStruct((width // 2, slots), BF)],
        scratch_shapes=[pltpu.VMEM((slots - FIRST, slots - CUT), F32)],
        compiler_params=params(20),
        cost_estimate=cost(13),
        name="heads_back",
    )(counts, q, k, v, o, do, lse, cos, sin)


def qkv_grad_kernel(order_ref, at_ref, sel_ref, dangle_ref, dq_ref, dk_ref, dv_ref, *rest):
    near_ref, far_ref, bias_ref, freq_ref, g_scr, sem = rest[-6:]
    part = g_scr.shape[1] // 3
    outs = (near_ref, far_ref)
    at = at_ref[...]
    for i, ref in enumerate((dq_ref, dk_ref, dv_ref)):
        g = nt(at, ref[...]).astype(BF)
        g_scr[:, i * part : (i + 1) * part, :] = g.reshape(SHARDS, part, g.shape[1])
        bias_ref[:, i * g.shape[1] : (i + 1) * g.shape[1]] = nt(sel_ref[...], ref[...])
    freq_ref[...] = nt(sel_ref[...], dangle_ref[...])
    copies = []
    for b, out in enumerate(outs):
        for n, p in enumerate(LEAVING):
            dst = out.at[n, pl.ds(0, 3 * part)]
            copies.append(pltpu.make_async_copy(g_scr.at[order_ref[p + b]], dst, sem.at[len(copies)]))
    start_all(copies)
    wait_all(copies)


def qkv_grad(order, at, sel, dangle, dq, dk, dv, *more):
    width, slots = at.shape
    cols = dq.shape[0]
    rows = 3 * width // SHARDS
    total = more[0].shape[1] if more else rows
    return pl.pallas_call(
        qkv_grad_kernel,
        in_specs=[SMEM] + [VMEM] * 6 + [ANY] * len(more),
        out_specs=[ANY, ANY, VMEM, VMEM],
        out_shape=[jax.ShapeDtypeStruct((SHARDS // 2, total, cols), BF)] * 2
        + [jax.ShapeDtypeStruct((sel.shape[0], 3 * cols), F32), jax.ShapeDtypeStruct((sel.shape[0], cols // 2), F32)],
        scratch_shapes=[
            pltpu.VMEM((SHARDS, rows, cols), BF),
            pltpu.SemaphoreType.DMA((SHARDS,)),
        ],
        input_output_aliases={7: 0, 8: 1} if more else {},
        compiler_params=params(16),
        cost_estimate=cost(6),
        name="qkv_grad",
    )(order, at, sel, dangle, dq, dk, dv, *more)


def part_kernel(order_ref, *rest):
    grads, pieces, (da_ref, w_scr, sem) = rest[:3], rest[3 : 3 + SHARDS], rest[3 + SHARDS :]
    add_group(order_ref, grads, pieces, da_ref, w_scr, sem)


def group_weights(order_ref, pieces, w_scr, sem):
    rows = w_scr.shape[1]
    copies = fetch(pieces, order_ref, [(slice(0, rows), lambda d: w_scr.at[d])], sem)
    start_all(copies)
    wait_all(copies)


def group_product(grads, w_scr):
    rows = w_scr.shape[1] // 3
    total = None
    for n in range(3):
        w = w_scr[:, n * rows : (n + 1) * rows, :].reshape(SHARDS * rows, w_scr.shape[2])
        term = nn(w, grads[n][...])
        total = term if total is None else total + term
    return total


def add_group(order_ref, grads, pieces, da_ref, w_scr, sem):
    @pl.when(pl.program_id(0) == 0)
    def _():
        group_weights(order_ref, pieces, w_scr, sem)

    da_ref[...] = group_product(grads, w_scr)


def input_part(order, grads, pieces, width):
    cols, slots = grads[0].shape
    blk = 512
    return pl.pallas_call(
        part_kernel,
        grid=(slots // blk,),
        in_specs=[SMEM] + [pl.BlockSpec((cols, blk), lambda i: (0, i))] * 3 + [HBM] * SHARDS,
        out_specs=pl.BlockSpec((width, blk), lambda i: (0, i)),
        out_shape=jax.ShapeDtypeStruct((width, slots), F32),
        scratch_shapes=[pltpu.VMEM((SHARDS, 3 * width // SHARDS, cols), BF), pltpu.SemaphoreType.DMA((SHARDS,))],
        compiler_params=params(16),
        cost_estimate=cost(6),
        name="input_part",
    )(order, *grads, *pieces)


def input_kernel(order_ref, x_ref, dh_ref, vec_ref, da_ref, *rest):
    grads, pieces, (dx_ref, sums_ref, w_scr, sem) = rest[:3], rest[3 : 3 + SHARDS], rest[3 + SHARDS :]

    @pl.when(pl.program_id(0) == 0)
    def _():
        group_weights(order_ref, pieces, w_scr, sem)
        sums_ref[...] = jnp.zeros_like(sums_ref)

    da = da_ref[...] + group_product(grads, w_scr)
    out, dgain, dshift = norm_back(da.T, x_ref[...].astype(F32), vec_ref[1:2, :])
    dx_ref[...] = (dh_ref[...].astype(F32) + out).astype(BF)
    sums_ref[0:1, :] += dgain
    sums_ref[1:2, :] += dshift


def input_back(order, x, dh, vec, da, grads, pieces):
    slots, width = x.shape
    cols = grads[0].shape[0]
    blk = 512
    rows = pl.BlockSpec((blk, width), lambda i: (i, 0))
    return pl.pallas_call(
        input_kernel,
        grid=(slots // blk,),
        in_specs=[SMEM, rows, rows, VMEM, pl.BlockSpec((width, blk), lambda i: (0, i))]
        + [pl.BlockSpec((cols, blk), lambda i: (0, i))] * 3
        + [HBM] * SHARDS,
        out_specs=[rows, pl.BlockSpec((8, width), lambda i: (0, 0))],
        out_shape=[jax.ShapeDtypeStruct((slots, width), BF), jax.ShapeDtypeStruct((8, width), F32)],
        scratch_shapes=[pltpu.VMEM((SHARDS, 3 * width // SHARDS, cols), BF), pltpu.SemaphoreType.DMA((SHARDS,))],
        compiler_params=params(20),
        cost_estimate=cost(10),
        name="input_back",
    )(order, x, dh, vec, da, *grads, *pieces)


def body_fast(
    tokens, cotangent, image_counts, patch_rows, patch_cols, ln1_gain, ln1_bias, qkv_weight, qkv_bias, rope_freqs,
    out_weight, out_bias, ln2_gain, ln2_bias, fc1_weight, fc1_bias, fc2_weight, fc2_bias,
):
    x = tokens[0]
    dy = cotangent[0]
    counts = image_counts[0]
    slots, width = x.shape
    cols = width // GROUPS
    half = width // 2
    order = lax.axis_index("fsdp") ^ jnp.arange(SHARDS, dtype=jnp.int32)
    order = jnp.concatenate([order, lax.axis_index("rep")[None].astype(jnp.int32)])

    own = fc2_weight.shape[0] // 2
    small = (ln1_gain, ln1_bias, qkv_bias, rope_freqs, out_bias, ln2_gain, ln2_bias, fc1_bias, fc2_bias)
    sizes = [s.shape[0] for s in small]
    vectors = jnp.concatenate(small + (jnp.zeros((2 * cols - sum(sizes),), BF),)).reshape(2, cols)
    piece_c, piece_d = mlp_pieces(fc1_weight, fc2_weight)
    piece_a, piece_b = group_pieces(qkv_weight, out_weight, vectors)
    pieces_c = [lax.all_gather(piece_c, "fsdp", axis=0)]
    pieces_d = [lax.all_gather(piece_d, "fsdp", axis=0)]
    first = lambda g: (g.piece[8], g.piece[4], g.piece[2])
    second = lambda g: (g.piece[12], g.piece[6], g.piece[10])
    gather_a = Gather(piece_a)
    gather_a.stage1()
    gather_a.stage2(*first(gather_a))
    gather_a.stage3()
    pieces_a = gather_a.cores()
    gather_b = Gather(piece_b)
    gather_b.stage1(gather_a.piece[12])
    a_t, cos, sin, vec, b1, bias, sel = prepare(sizes, order, x, patch_cols, patch_rows, pieces_a)
    gather_b.stage2(sel)
    q, k, v = project_group(0, order, a_t, bias, cos, sin, pieces_a)
    gather_b.hold((12, 6, 10), q)
    gather_b.stage3()
    heads = [(q, k, v) + tuple(attend(counts, q, k, v))]
    gather_b.hold((14,), heads[0][3])
    pieces_b = gather_b.cores()
    q, k, v = project_group(1, order, a_t, bias, cos, sin, pieces_b)
    heads.append((q, k, v) + tuple(attend(counts, q, k, v)))
    o = [t[3] for t in heads]
    at_out = piece_b.shape[0] - 2 * out_weight.shape[0]
    h, c, c_t = out_project_fast(order, o, x, vec, pieces_b, at_out)
    y, dc, g_c, g_b1a = mlp_half(0, order, c, c_t, dy, b1, vec, (h,), pieces_c, False)
    mlp_c = lax.psum_scatter(tie(g_c, pieces_d[0]), "fsdp", scatter_dimension=0, tiled=True)[0]
    y, dc, near_d, far_d, g_b1b = mlp_half(1, order, c, c_t, dy, b1, vec, (y, dc), pieces_d, True)
    scatter_d = SplitScatter(near_d, far_d)
    dh, do, near_o, far_o, sums2 = out_back_fast(order, dc, h, dy, vec, o, pieces_b, at_out)

    def back(g, do):
        q, k, v, og, lse = heads[g]
        *three, dangle = heads_back(g, counts, q, k, v, og, do, lse, cos, sin)
        return three, dangle

    sent = scatter_d.split()
    grads_b, dangle_b = back(1, tie(do, sent))
    near_b, far_b, bias_b, freq_b = qkv_grad(order, a_t, sel, dangle_b, *grads_b, near_o, far_o)
    scatter_b = Scatter(near_b, far_b)
    scatter_d.hold(near_b)
    sent = scatter_d.step()
    grads_a, dangle_a = back(0, tie(do, sent, near_b))
    scatter_d.hold(dangle_a)
    scatter_b.hold(dangle_a)
    sent = (scatter_d.step(), scatter_b.step())
    near_a, far_a, bias_a, freq_a = qkv_grad(order, a_t, sel, tie(dangle_a, *sent), *grads_a)
    scatter_a = Scatter(near_a, far_a)
    da = input_part(order, lax.optimization_barrier((grads_b, near_a))[0], pieces_b, width)
    for scatter in (scatter_d, scatter_b, scatter_a):
        scatter.hold(da)
    sent = (scatter_a.step(), scatter_b.step(), scatter_d.step())
    dx, sums1 = input_back(order, x, dh, vec, tie(da, *sent), grads_a, pieces_a)
    scatter_a.hold(sums1, scatter_b.got[-1], scatter_d.got[-1])
    sent = scatter_a.step()
    other_c = across(tie(mlp_c, sent))
    scatter_b.hold(sent)
    scatter_d.hold(sent)
    sent = (sent, scatter_b.step())
    block = pack(sum(sizes), tie(sums1, *sent), sums2, g_b1a, g_b1b, bias_a, bias_b, freq_a, freq_b)
    scatter_a.hold(block)
    sent = scatter_a.step()
    mlp_d = scatter_d.finish()
    scatter_b.hold(other_c, sent)
    mine_b = scatter_b.finish()
    mine = jnp.sum(tie(lax.all_to_all(block, "fsdp", 0, 0, tiled=True), sent), axis=0)
    mine = tie(mine[0], scatter_a.got[-1])
    rows1 = width // SHARDS
    s_w1, s_w2 = mlp_join(rows1, order, (mlp_c, other_c) + mlp_d)
    scatter_a.hold(mine)
    mine_a = scatter_a.finish()
    mine_a = (mine_a[0], tie(mine_a[1], s_w1))
    mine = mine + across(mine)
    s_a = mine_a[0].astype(F32) + mine_a[1].astype(F32)
    s_b = mine_b[0].astype(F32) + mine_b[1].astype(F32)
    s_wqkv = jnp.concatenate([s[i * rows1 : (i + 1) * rows1] for i in range(3) for s in (s_a, s_b)], axis=1)
    s_wout = jnp.concatenate([s_b[3 * rows1 : 4 * rows1], s_b[4 * rows1 :]], axis=1)

    outs = []
    at = 0
    for size in sizes:
        outs.append(mine[at : at + size])
        at += size
    s_gain1, s_shift1, s_bqkv, s_freq, s_bout, s_gain2, s_shift2, s_b1, s_b2 = outs
    return (
        y[None], dx[None], s_gain1, s_shift1, s_wqkv, s_bqkv, s_freq, s_wout, s_bout,
        s_gain2, s_shift2, s_w1, s_b1, s_w2, s_b2,
    )


def solution(mesh):
    row = P(("rep", "fsdp"), None)
    rows = P(("rep", "fsdp"), None, None)
    vec = P("fsdp")
    mat = P("fsdp", None)
    in_specs = (rows, rows, row, row, row, vec, vec, mat, vec, vec, mat, vec, vec, vec, mat, vec, mat, vec)
    out_specs = (rows, rows, vec, vec, mat, vec, vec, mat, vec, vec, vec, mat, vec, mat, vec)
    fast = mesh.shape["fsdp"] == SHARDS and mesh.shape["rep"] == 2
    return jax.shard_map(
        body_fast if fast else body_any, mesh=mesh, in_specs=in_specs, out_specs=out_specs, check_vma=False
    )
```

```python
from functools import partial

import jax
import jax.numpy as jnp
from jax import lax
from jax.experimental import pallas as pl
from jax.experimental.pallas import tpu as pltpu
from jax.sharding import PartitionSpec as P

HEADS = 12
HEAD_DIM = 64
HALF = HEAD_DIM // 2
FIRST = 576
CUT = 512
WIDE = 640
NEG = -1e30
EPS = 1e-6
BF = jnp.bfloat16
F32 = jnp.float32
GELU_C = 0.7978845608028654
GELU_A = 0.044715


def nn(a, b):
    return lax.dot_general(a, b, (((1,), (0,)), ((), ())), preferred_element_type=F32)


def nt(a, b):
    return lax.dot_general(a, b, (((1,), (1,)), ((), ())), preferred_element_type=F32)


def tn(a, b):
    return lax.dot_general(a, b, (((0,), (0,)), ((), ())), preferred_element_type=F32)


def params(mib=56):
    return pltpu.CompilerParams(vmem_limit_bytes=mib << 20)


def cost(us):
    return pl.CostEstimate(flops=int(us * 1.1e9), bytes_accessed=1 << 16, transcendentals=0)


def norm_parts(v):
    mean = jnp.mean(v, axis=-1, keepdims=True)
    dev = v - mean
    var = jnp.mean(dev * dev, axis=-1, keepdims=True)
    inv = lax.rsqrt(var + EPS)
    return dev * inv, inv


def lane_partial(v):
    total = v[:, :128]
    for i in range(1, v.shape[1] // 128):
        total = total + v[:, i * 128 : (i + 1) * 128]
    return total


def norm1_kernel(x_ref, gain_ref, shift_ref, a_ref, at_ref):
    xhat, _ = norm_parts(x_ref[...].astype(F32))
    a = (xhat * gain_ref[...] + shift_ref[...]).astype(BF)
    a_ref[...] = a
    at_ref[...] = a.T


def norm1(x, gain, shift):
    slots, width = x.shape
    blk = 256
    return pl.pallas_call(
        norm1_kernel,
        grid=(slots // blk,),
        in_specs=[
            pl.BlockSpec((blk, width), lambda i: (i, 0)),
            pl.BlockSpec((1, width), lambda i: (0, 0)),
            pl.BlockSpec((1, width), lambda i: (0, 0)),
        ],
        out_specs=[
            pl.BlockSpec((blk, width), lambda i: (i, 0)),
            pl.BlockSpec((width, blk), lambda i: (0, i)),
        ],
        out_shape=[
            jax.ShapeDtypeStruct((slots, width), BF),
            jax.ShapeDtypeStruct((width, slots), BF),
        ],
        compiler_params=params(),
        cost_estimate=cost(5),
        name="norm1",
    )(x, gain, shift)


def qkv_kernel(a_ref, wq_ref, wk_ref, wv_ref, bq_ref, bk_ref, bv_ref, cos_ref, sin_ref, q_ref, k_ref, v_ref):
    heads = wq_ref.shape[1] // HEAD_DIM
    a = a_ref[...]
    cos = cos_ref[...]
    sin = sin_ref[...]
    for w_ref, b_ref, out_ref, scale in ((wq_ref, bq_ref, q_ref, HEAD_DIM**-0.5), (wk_ref, bk_ref, k_ref, 1.0)):
        u = nt(w_ref[...].T, a) + b_ref[...]
        for h in range(heads):
            u1 = u[h * HEAD_DIM : h * HEAD_DIM + HALF]
            u2 = u[h * HEAD_DIM + HALF : (h + 1) * HEAD_DIM]
            c = cos[h * HALF : (h + 1) * HALF]
            s = sin[h * HALF : (h + 1) * HALF]
            out_ref[h * HEAD_DIM : h * HEAD_DIM + HALF, :] = ((u1 * c - u2 * s) * scale).astype(BF)
            out_ref[h * HEAD_DIM + HALF : (h + 1) * HEAD_DIM, :] = ((u1 * s + u2 * c) * scale).astype(BF)
    v_ref[...] = (nt(wv_ref[...].T, a) + bv_ref[...]).astype(BF)


def project(a, w, bias, cos, sin):
    slots, width = a.shape
    cols = 256
    groups = width // cols
    wspec = lambda part: pl.BlockSpec((width, cols), lambda g: (0, part * groups + g))
    bspec = lambda part: pl.BlockSpec((cols, 1), lambda g: (part * groups + g, 0))
    out = pl.BlockSpec((cols, slots), lambda g: (g, 0))
    return pl.pallas_call(
        qkv_kernel,
        grid=(groups,),
        in_specs=[pl.BlockSpec((slots, width), lambda g: (0, 0))]
        + [wspec(i) for i in range(3)]
        + [bspec(i) for i in range(3)]
        + [pl.BlockSpec((cols // 2, slots), lambda g: (g, 0))] * 2,
        out_specs=[out] * 3,
        out_shape=[jax.ShapeDtypeStruct((width, slots), BF)] * 3,
        compiler_params=params(),
        name="qkv",
    )(a, w, w, w, bias, bias, bias, cos, sin)


def second_bias(counts_ref, slots):
    shape = (slots - FIRST, slots - CUT)
    key = lax.broadcasted_iota(jnp.int32, shape, 0) + FIRST
    query = lax.broadcasted_iota(jnp.int32, shape, 1) + CUT
    end0 = counts_ref[0]
    end1 = end0 + counts_ref[1]
    end2 = end1 + counts_ref[2]

    def seg(place):
        return (place >= end0).astype(jnp.int32) + (place >= end1).astype(jnp.int32)

    allowed = ((seg(key) == seg(query)) & (key < end2) & (query < end2)) | (key == query)
    return jnp.where(allowed, 0.0, NEG)


def attend_kernel(counts_ref, q_ref, k_ref, v_ref, o_ref, lse_ref, bias_ref):
    slots = q_ref.shape[1]

    @pl.when(pl.program_id(0) == 0)
    def _():
        bias_ref[...] = second_bias(counts_ref, slots)

    def part(scores, first, values):
        peak = jnp.max(scores, axis=0, keepdims=True)
        wb = jnp.exp(scores - peak).astype(BF)
        gap = jnp.zeros((values.shape[1] - wb.shape[0], wb.shape[1]), BF)
        wb = jnp.concatenate([wb, gap] if first else [gap, wb], axis=0)
        lines = jnp.concatenate([values, jnp.ones((16, values.shape[1]), BF)], axis=0)
        mixed = nn(lines, wb)
        total = mixed[HEAD_DIM : HEAD_DIM + 1]
        return mixed[:HEAD_DIM] * (1.0 / total), peak + jnp.log(total)

    edge = lax.broadcasted_iota(jnp.int32, (1, WIDE - CUT), 1) < FIRST - CUT
    for h in range(q_ref.shape[0] // HEAD_DIM):
        rows = slice(h * HEAD_DIM, (h + 1) * HEAD_DIM)
        k = k_ref[rows, :].T
        q = q_ref[rows, :]
        v = v_ref[rows, :]
        mixed1, lse1 = part(nn(k[:FIRST], q[:, :WIDE]), True, v[:, :WIDE])
        mixed2, lse2 = part(nn(k[FIRST:], q[:, CUT:]) + bias_ref[...], False, v[:, CUT:])
        for out, one, two in ((o_ref.at[rows], mixed1, mixed2), (lse_ref.at[h], lse1, lse2)):
            out[:, :CUT] = one[:, :CUT].astype(out.dtype)
            out[:, CUT:WIDE] = jnp.where(edge, one[:, CUT:], two[:, : WIDE - CUT]).astype(out.dtype)
            out[:, WIDE:] = two[:, WIDE - CUT :].astype(out.dtype)


def attend(counts, q, k, v):
    width, slots = q.shape
    heads = width // HEAD_DIM
    each = 2
    head = pl.BlockSpec((each * HEAD_DIM, slots), lambda h: (h, 0))
    return pl.pallas_call(
        attend_kernel,
        grid=(heads // each,),
        in_specs=[pl.BlockSpec(memory_space=pltpu.SMEM)] + [head] * 3,
        out_specs=[head, pl.BlockSpec((each, 1, slots), lambda h: (h, 0, 0))],
        out_shape=[jax.ShapeDtypeStruct((width, slots), BF), jax.ShapeDtypeStruct((heads, 1, slots), F32)],
        scratch_shapes=[pltpu.VMEM((slots - FIRST, slots - CUT), F32)],
        compiler_params=params(),
        cost_estimate=cost(8),
        name="attend",
    )(counts, q, k, v)


def attend_back_kernel(
    counts_ref, q_ref, k_ref, v_ref, o_ref, do_ref, lse_ref, cos_ref, sin_ref, place_ref,
    dq_ref, dk_ref, dv_ref, bq_ref, bk_ref, bv_ref, fc_ref, fr_ref, bias_ref,
):
    slots = q_ref.shape[1]

    @pl.when(pl.program_id(0) == 0)
    def _():
        bias_ref[...] = second_bias(counts_ref, slots)

    kt = k_ref[...]
    k = kt.T
    v = v_ref[...].T
    q = q_ref[...]
    do = do_ref[...]
    lse = lse_ref[0]
    delta = jnp.sum(do.astype(F32) * o_ref[...].astype(F32), axis=0, keepdims=True)
    lane1 = lax.broadcasted_iota(jnp.int32, (1, WIDE), 1)
    lane2 = lax.broadcasted_iota(jnp.int32, (1, slots - CUT), 1)
    lse1 = jnp.where(lane1 < FIRST, lse[:, :WIDE], -NEG)
    lse2 = jnp.where(lane2 >= FIRST - CUT, lse[:, CUT:], -NEG)

    def part(scores, grads, queries, outs, keys, delta_row, first):
        prob = jnp.exp(scores)
        ds = (prob * (grads - delta_row)).astype(BF)
        pb = prob.astype(BF)
        gap = jnp.zeros((keys.shape[1] - pb.shape[0], pb.shape[1]), BF)
        pb = jnp.concatenate([pb, gap] if first else [gap, pb], axis=0)
        ds = jnp.concatenate([ds, gap] if first else [gap, ds], axis=0)
        return nn(keys, ds), nt(queries, ds), nt(outs, pb)

    grads1 = part(
        nn(k[:FIRST], q[:, :WIDE]) - lse1, nn(v[:FIRST], do[:, :WIDE]),
        q[:, :WIDE], do[:, :WIDE], kt[:, :WIDE], delta[:, :WIDE], True,
    )
    grads2 = part(
        nn(k[FIRST:], q[:, CUT:]) + bias_ref[...] - lse2, nn(v[FIRST:], do[:, CUT:]),
        q[:, CUT:], do[:, CUT:], kt[:, CUT:], delta[:, CUT:], False,
    )
    dq, dk, dv = (
        jnp.concatenate([one[:, :CUT], one[:, CUT:] + two[:, : WIDE - CUT], two[:, WIDE - CUT :]], axis=1)
        for one, two in zip(grads1, grads2)
    )
    scale = HEAD_DIM**-0.5
    cos = cos_ref[...]
    sin = sin_ref[...]
    dangle = None
    for r, rot, out, bias_out in ((dq * scale, q.astype(F32) * (1.0 / scale), dq_ref, bq_ref), (dk, kt.astype(F32), dk_ref, bk_ref)):
        r1, r2 = r[:HALF], r[HALF:]
        term = r2 * rot[:HALF] - r1 * rot[HALF:]
        dangle = term if dangle is None else dangle + term
        g1 = (r1 * cos + r2 * sin).astype(BF)
        g2 = (r2 * cos - r1 * sin).astype(BF)
        out[:HALF, :] = g1
        out[HALF:, :] = g2
        bias_out[:HALF, :] = lane_partial(g1.astype(F32))
        bias_out[HALF:, :] = lane_partial(g2.astype(F32))
    dvb = dv.astype(BF)
    dv_ref[...] = dvb
    bv_ref[...] = lane_partial(dvb.astype(F32))
    fc_ref[...] = lane_partial(dangle * place_ref[0:1, :])
    fr_ref[...] = lane_partial(dangle * place_ref[1:2, :])


def attend_back(counts, q, k, v, o, do, lse, cos, sin, places):
    width, slots = q.shape
    heads = width // HEAD_DIM
    head = pl.BlockSpec((HEAD_DIM, slots), lambda h: (h, 0))
    half = pl.BlockSpec((HALF, slots), lambda h: (h, 0))
    return pl.pallas_call(
        attend_back_kernel,
        grid=(heads,),
        in_specs=[pl.BlockSpec(memory_space=pltpu.SMEM)]
        + [head] * 5
        + [pl.BlockSpec((1, 1, slots), lambda h: (h, 0, 0)), half, half]
        + [pl.BlockSpec((2, slots), lambda h: (0, 0))],
        out_specs=[head] * 3
        + [pl.BlockSpec((HEAD_DIM, 128), lambda h: (h, 0))] * 3
        + [pl.BlockSpec((HALF, 128), lambda h: (h, 0))] * 2,
        out_shape=[jax.ShapeDtypeStruct((width, slots), BF)] * 3
        + [jax.ShapeDtypeStruct((width, 128), F32)] * 3
        + [jax.ShapeDtypeStruct((width // 2, 128), F32)] * 2,
        scratch_shapes=[pltpu.VMEM((slots - FIRST, slots - CUT), F32)],
        compiler_params=params(),
        cost_estimate=cost(14),
        name="attend_back",
    )(counts, q, k, v, o, do, lse, cos, sin, places)


def out_kernel(o_ref, x_ref, w_ref, b_ref, gain_ref, shift_ref, h_ref, c_ref, ct_ref):
    h = x_ref[...].astype(F32) + (nn(o_ref[...].T, w_ref[...]) + b_ref[...])
    h_ref[...] = h
    xhat, _ = norm_parts(h)
    c = (xhat * gain_ref[...] + shift_ref[...]).astype(BF)
    c_ref[...] = c
    ct_ref[...] = c.T


def out_project(o, x, w, b, gain, shift):
    slots, width = x.shape
    blk = 256
    row = pl.BlockSpec((1, width), lambda i: (0, 0))
    rows = pl.BlockSpec((blk, width), lambda i: (i, 0))
    cols = pl.BlockSpec((width, blk), lambda i: (0, i))
    return pl.pallas_call(
        out_kernel,
        grid=(slots // blk,),
        in_specs=[cols, rows, pl.BlockSpec((width, width), lambda i: (0, 0)), row, row, row],
        out_specs=[rows, rows, cols],
        out_shape=[
            jax.ShapeDtypeStruct((slots, width), F32),
            jax.ShapeDtypeStruct((slots, width), BF),
            jax.ShapeDtypeStruct((width, slots), BF),
        ],
        compiler_params=params(),
        name="out_project",
    )(o, x, w, b, gain, shift)


def mlp_kernel(c_ref, ct_ref, dy_ref, h_ref, w1_ref, b1_ref, w2_ref, b2_ref, y_ref, dc_ref, g1_ref, g2_ref, gb1_ref, y_acc, hb_scr, dp_scr):
    slots = c_ref.shape[0]
    tile = 256

    @pl.when(pl.program_id(0) == 0)
    def _():
        y_acc[...] = h_ref[...] + b2_ref[...]
        dc_ref[...] = jnp.zeros_like(dc_ref)

    gb1_ref[...] = jnp.zeros_like(gb1_ref)

    def step(i, _):
        rows = pl.ds(pl.multiple_of(i * tile, tile), tile)
        pre = nn(c_ref[rows, :], w1_ref[...]) + b1_ref[...]
        square = pre * pre
        th = jnp.tanh(GELU_C * (pre + GELU_A * (pre * square)))
        cdf = 0.5 * (1.0 + th)
        hb = (pre * cdf).astype(BF)
        slope = cdf + 0.5 * pre * (1.0 - th * th) * (GELU_C * (1.0 + (3.0 * GELU_A) * square))
        hb_scr[rows, :] = hb
        y_acc[rows, :] += nn(hb, w2_ref[...])
        dpre = (nt(dy_ref[rows, :], w2_ref[...]) * slope).astype(BF)
        dp_scr[rows, :] = dpre
        dc_ref[rows, :] += nt(dpre, w1_ref[...])
        gb1_ref[...] += jnp.sum(dpre.astype(F32), axis=0, keepdims=True)
        return 0

    lax.fori_loop(0, slots // tile, step, 0)
    g1_ref[...] = nn(ct_ref[...], dp_scr[...]).astype(g1_ref.dtype)
    g2_ref[...] = tn(hb_scr[...], dy_ref[...]).astype(g2_ref.dtype)

    @pl.when(pl.program_id(0) == pl.num_programs(0) - 1)
    def _():
        y_ref[...] = y_acc[...].astype(BF)


def mlp(c, ct, dy, h, w1, b1, w2, b2):
    slots, width = c.shape
    hidden = w1.shape[1]
    blk = 512
    whole = lambda r, k: pl.BlockSpec((r, k), lambda j: (0, 0))
    return pl.pallas_call(
        mlp_kernel,
        grid=(hidden // blk,),
        in_specs=[
            whole(slots, width),
            whole(width, slots),
            whole(slots, width),
            whole(slots, width),
            pl.BlockSpec((width, blk), lambda j: (0, j)),
            pl.BlockSpec((1, blk), lambda j: (0, j)),
            pl.BlockSpec((blk, width), lambda j: (j, 0)),
            whole(1, width),
        ],
        out_specs=[
            whole(slots, width),
            whole(slots, width),
            pl.BlockSpec((width, blk), lambda j: (0, j)),
            pl.BlockSpec((blk, width), lambda j: (j, 0)),
            pl.BlockSpec((1, blk), lambda j: (0, j)),
        ],
        out_shape=[
            jax.ShapeDtypeStruct((slots, width), BF),
            jax.ShapeDtypeStruct((slots, width), F32),
            jax.ShapeDtypeStruct((width, hidden), BF),
            jax.ShapeDtypeStruct((hidden, width), BF),
            jax.ShapeDtypeStruct((1, hidden), F32),
        ],
        scratch_shapes=[
            pltpu.VMEM((slots, width), F32),
            pltpu.VMEM((slots, blk), BF),
            pltpu.VMEM((slots, blk), BF),
        ],
        compiler_params=params(),
        name="mlp",
    )(c, ct, dy, h, w1, b1, w2, b2)


def norm_back(grad, v, gain):
    xhat, inv = norm_parts(v)
    g = grad * gain
    lead = jnp.mean(g, axis=-1, keepdims=True)
    slope = jnp.mean(g * xhat, axis=-1, keepdims=True)
    return (g - lead - xhat * slope) * inv, jnp.sum(grad * xhat, axis=0, keepdims=True), jnp.sum(grad, axis=0, keepdims=True)


def out_back_kernel(dc_ref, h_ref, dy_ref, o_ref, w_ref, gain_ref, dh_ref, do_ref, gw_ref, sums_ref, acc_ref):
    i = pl.program_id(0)

    @pl.when(i == 0)
    def _():
        acc_ref[...] = jnp.zeros_like(acc_ref)
        sums_ref[...] = jnp.zeros_like(sums_ref)

    dy = dy_ref[...].astype(F32)
    part, dgain, dshift = norm_back(dc_ref[...], h_ref[...], gain_ref[...])
    dh = dy + part
    dh_ref[...] = dh
    dhb = dh.astype(BF)
    do_ref[...] = nt(w_ref[...], dhb).astype(BF)
    acc_ref[...] += nn(o_ref[...], dhb)
    sums_ref[0:1, :] += dgain
    sums_ref[1:2, :] += dshift
    sums_ref[2:3, :] += jnp.sum(dh, axis=0, keepdims=True)
    sums_ref[3:4, :] += jnp.sum(dy, axis=0, keepdims=True)

    @pl.when(i == pl.num_programs(0) - 1)
    def _():
        gw_ref[...] = acc_ref[...].astype(gw_ref.dtype)


def out_back(dc, h, dy, o, w, gain):
    slots, width = h.shape
    blk = 256
    rows = pl.BlockSpec((blk, width), lambda i: (i, 0))
    cols = pl.BlockSpec((width, blk), lambda i: (0, i))
    whole = lambda r, k: pl.BlockSpec((r, k), lambda i: (0, 0))
    return pl.pallas_call(
        out_back_kernel,
        grid=(slots // blk,),
        in_specs=[rows, rows, rows, cols, whole(width, width), whole(1, width)],
        out_specs=[rows, cols, whole(width, width), whole(8, width)],
        out_shape=[
            jax.ShapeDtypeStruct((slots, width), F32),
            jax.ShapeDtypeStruct((width, slots), BF),
            jax.ShapeDtypeStruct((width, width), BF),
            jax.ShapeDtypeStruct((8, width), F32),
        ],
        scratch_shapes=[pltpu.VMEM((width, width), F32)],
        compiler_params=params(),
        name="out_back",
    )(dc, h, dy, o, w, gain)


def qkv_back_kernel(at_ref, dqkv_ref, w_ref, x_ref, dh_ref, gain_ref, gw_ref, dx_ref, sums_ref, acc_ref):
    j = pl.program_id(0)

    @pl.when(j == 0)
    def _():
        acc_ref[...] = jnp.zeros_like(acc_ref)

    d = dqkv_ref[...]
    gw_ref[...] = nt(at_ref[...], d).astype(gw_ref.dtype)
    acc_ref[...] += nn(w_ref[...], d)

    @pl.when(j == pl.num_programs(0) - 1)
    def _():
        sums_ref[...] = jnp.zeros_like(sums_ref)
        tile = 256
        for i in range(x_ref.shape[0] // tile):
            rows = slice(i * tile, (i + 1) * tile)
            da = acc_ref[:, rows].T
            part, dgain, dshift = norm_back(da, x_ref[rows, :].astype(F32), gain_ref[...])
            dx_ref[rows, :] = (dh_ref[rows, :] + part).astype(BF)
            sums_ref[0:1, :] += dgain
            sums_ref[1:2, :] += dshift


def qkv_back(at, dqkv, w, x, dh, gain):
    slots, width = x.shape
    outs = w.shape[1]
    blk = 768
    whole = lambda r, k: pl.BlockSpec((r, k), lambda j: (0, 0))
    return pl.pallas_call(
        qkv_back_kernel,
        grid=(outs // blk,),
        in_specs=[
            whole(width, slots),
            pl.BlockSpec((blk, slots), lambda j: (j, 0)),
            pl.BlockSpec((width, blk), lambda j: (0, j)),
            whole(slots, width),
            whole(slots, width),
            whole(1, width),
        ],
        out_specs=[pl.BlockSpec((width, blk), lambda j: (0, j)), whole(slots, width), whole(8, width)],
        out_shape=[
            jax.ShapeDtypeStruct((width, outs), BF),
            jax.ShapeDtypeStruct((slots, width), BF),
            jax.ShapeDtypeStruct((8, width), F32),
        ],
        scratch_shapes=[pltpu.VMEM((width, slots), F32)],
        compiler_params=params(),
        name="qkv_back",
    )(at, dqkv, w, x, dh, gain)


def body_any(
    tokens, cotangent, image_counts, patch_rows, patch_cols, ln1_gain, ln1_bias, qkv_weight, qkv_bias, rope_freqs,
    out_weight, out_bias, ln2_gain, ln2_bias, fc1_weight, fc1_bias, fc2_weight, fc2_bias,
):
    x = tokens[0]
    dy = cotangent[0]
    counts = image_counts[0]
    width = x.shape[1]
    small = (ln1_gain, ln1_bias, qkv_bias, rope_freqs, out_bias, ln2_gain, ln2_bias, fc1_bias, fc2_bias)
    sizes = [s.shape[0] for s in small]
    gather = partial(lax.all_gather, axis_name="fsdp", axis=0, tiled=True)
    packed = lax.all_gather(jnp.concatenate(small), "fsdp", axis=0)
    vectors = []
    at = 0
    for size in sizes:
        vectors.append(packed[:, at : at + size].reshape(-1).astype(F32))
        at += size
    gain1, shift1, b_qkv, freqs, b_out, gain2, shift2, b1, b2 = vectors
    w_qkv = gather(qkv_weight)
    w_out = gather(out_weight)
    w1 = gather(fc1_weight)
    w2 = gather(fc2_weight)

    row = lambda v: v[None, :]
    a, a_t = norm1(x, row(gain1), row(shift1))
    places = jnp.concatenate([patch_cols, patch_rows], axis=0).astype(F32)
    half = freqs.shape[0] // 2
    angle = freqs[:half, None] * places[0:1] + freqs[half:, None] * places[1:2]
    cos = jnp.cos(angle)
    sin = jnp.sin(angle)
    q, k, v = project(a, w_qkv, b_qkv[:, None], cos, sin)
    o, lse = attend(counts, q, k, v)
    h, c, c_t = out_project(o, x, w_out, row(b_out), row(gain2), row(shift2))
    y, dc, g_w1, g_w2, g_b1 = mlp(c, c_t, dy, h, w1, row(b1), w2, row(b2))
    dh, do, g_wout, sums2 = out_back(dc, h, dy, o, w_out, row(gain2))
    dq, dk, dv, s_bq, s_bk, s_bv, s_fc, s_fr = attend_back(counts, q, k, v, o, do, lse, cos, sin, places)
    dqkv = jnp.concatenate([dq, dk, dv], axis=0)
    g_wqkv, dx, sums1 = qkv_back(a_t, dqkv, w_qkv, x, dh, row(gain1))

    scatter = partial(lax.psum_scatter, axis_name="fsdp", scatter_dimension=0, tiled=True)
    both = lambda g: lax.psum(scatter(g), "rep").astype(F32)
    g_bqkv = jnp.sum(jnp.concatenate([s_bq, s_bk, s_bv], axis=0), axis=1)
    g_freq = jnp.sum(jnp.concatenate([s_fc, s_fr], axis=0), axis=1)
    small_grads = (sums1[0], sums1[1], g_bqkv, g_freq, sums2[2], sums2[0], sums2[1], g_b1[0], sums2[3])
    shards = mesh_size = packed.shape[0]
    block = jnp.concatenate([g.reshape(shards, -1) for g in small_grads], axis=1)
    total = lax.psum(block, ("rep", "fsdp"))
    mine = lax.dynamic_index_in_dim(total, lax.axis_index("fsdp"), 0, keepdims=False)
    outs = []
    at = 0
    for size in sizes:
        outs.append(mine[at : at + size])
        at += size
    s_gain1, s_shift1, s_bqkv, s_freq, s_bout, s_gain2, s_shift2, s_b1, s_b2 = outs
    return (
        y[None], dx[None], s_gain1, s_shift1, both(g_wqkv), s_bqkv, s_freq, both(g_wout), s_bout,
        s_gain2, s_shift2, both(g_w1), s_b1, both(g_w2), s_b2,
    )


SHARDS = 16
GROUPS = 2
LEAVING = (0, 8, 4, 12, 2, 10, 6, 14)


def swap(v, mask):
    return lax.ppermute(v, "fsdp", [(i, i ^ mask) for i in range(SHARDS)])


def tie(v, *after):
    return lax.optimization_barrier((v,) + after)[0]


class Gather:
    def __init__(self, mine):
        self.piece = {0: mine}

    def send(self, source, mask, after):
        v = self.piece[source]
        self.piece[source ^ mask] = swap(tie(v, *after) if after else v, mask)

    def hold(self, sources, after):
        for p in sources:
            self.piece[p] = tie(self.piece[p], after)

    def stage1(self, *after):
        for mask in (8, 4, 2):
            self.send(0, mask, after)

    def stage2(self, *after):
        self.send(8, 4, after)
        self.send(4, 2, after)
        self.send(8, 2, after)

    def stage3(self, *after):
        self.send(12, 2, after)

    def cores(self, *after):
        for p in (0, 8, 4, 2, 6, 10, 12, 14):
            self.send(p, 1, after)
        return [self.piece[p] for p in range(SHARDS)]


class Scatter:
    def __init__(self, near, far):
        self.got = [near, swap(far, 1)]
        self.size = 4

    def total(self, lo, hi):
        out = self.got[0][lo:hi].astype(F32)
        for g in self.got[1:]:
            out = out + g[lo:hi].astype(F32)
        return out.astype(BF)

    def hold(self, *after):
        self.got[-1] = tie(self.got[-1], *after)

    def step(self):
        lo = self.size
        sent = self.total(lo, 2 * lo)
        self.got.append(swap(sent, {4: 2, 2: 4, 1: 8}[lo]))
        self.size = lo // 2
        return sent

    def finish(self):
        mine = self.total(0, 1)[0]
        return mine, across(mine)


class SplitScatter(Scatter):
    def __init__(self, near, far):
        self.start = [near, swap(far, 1)]
        self.size = 4

    def split(self):
        sent = (self.start[0][1].astype(F32) + self.start[1][1].astype(F32)).astype(BF)
        got = across(sent)
        self.got = [self.start[0][0], self.start[1][0], got]
        return sent


def across(v):
    return lax.ppermute(v, "rep", [(0, 1), (1, 0)])


def start_all(copies):
    for copy in copies:
        copy.start()


def wait_all(copies):
    for copy in copies:
        copy.wait()


def fetch(refs, order_ref, moves, sem):
    copies = []
    for p, ref in enumerate(refs):
        for rows, place in moves:
            copies.append(pltpu.make_async_copy(ref.at[rows], place(order_ref[p]), sem.at[len(copies)]))
    return copies


ANY = pl.BlockSpec(memory_space=pl.ANY)
HBM = pl.BlockSpec(memory_space=pltpu.HBM)
SMEM = pl.BlockSpec(memory_space=pltpu.SMEM)
VMEM = pl.BlockSpec(memory_space=pltpu.VMEM)


LINES = 16


def group_piece_kernel(w_ref, o_ref, v_ref, a_ref, b_ref):
    rows, cols = w_ref.shape[0], a_ref.shape[1]
    for i in range(3):
        for g, out in enumerate((a_ref, b_ref)):
            out[i * rows : (i + 1) * rows, :] = w_ref[:, (i * GROUPS + g) * cols : (i * GROUPS + g + 1) * cols]
    for i in range(2):
        b_ref[(3 + i) * rows : (4 + i) * rows, :] = o_ref[:, i * cols : (i + 1) * cols]
    a_ref[3 * rows :, :] = jnp.concatenate([v_ref[...], jnp.zeros((LINES - v_ref.shape[0], cols), BF)], axis=0)


def group_pieces(w, w_out, vectors):
    rows, cols = w.shape[0], w_out.shape[1] // 2
    return pl.pallas_call(
        group_piece_kernel,
        in_specs=[VMEM] * 3,
        out_specs=[VMEM, VMEM],
        out_shape=[jax.ShapeDtypeStruct((3 * rows + LINES, cols), BF), jax.ShapeDtypeStruct((5 * rows, cols), BF)],
        compiler_params=params(),
        cost_estimate=cost(2),
        name="group_pieces",
    )(w, w_out, vectors)


def mlp_piece_kernel(w1_ref, w2_ref, *outs):
    rows1 = w1_ref.shape[0]
    own = w2_ref.shape[0] // 2
    per = SHARDS // 2
    w1 = w1_ref[...].astype(F32)
    for i, out in enumerate(outs):
        for b in range(2):
            runs = [w1[:, (2 * (b * per + j) + i) * own :][:, :own] for j in range(per)]
            out[b * rows1 : (b + 1) * rows1, :] = jnp.concatenate(runs, axis=1).astype(BF)
        out[2 * rows1 :, :] = w2_ref[i * own : (i + 1) * own, :]


def mlp_pieces(w1, w2):
    rows = 2 * w1.shape[0] + w2.shape[0] // 2
    return pl.pallas_call(
        mlp_piece_kernel,
        in_specs=[VMEM, VMEM],
        out_specs=[VMEM, VMEM],
        out_shape=[jax.ShapeDtypeStruct((rows, w2.shape[1]), BF)] * 2,
        compiler_params=params(),
        cost_estimate=cost(2),
        name="mlp_pieces",
    )(w1, w2)


def mlp_join_kernel(order_ref, c_ref, c_other_ref, d_ref, d_other_ref, w1_ref, w2_ref):
    rows1 = w1_ref.shape[0]
    own = w2_ref.shape[0] // 2
    per = SHARDS // 2
    c = c_ref[...].astype(F32) + c_other_ref[...].astype(F32)
    mine = d_ref[...].astype(F32)
    other = d_other_ref[...].astype(F32)
    here = order_ref[SHARDS] == 0
    d = jnp.where(here, mine, other)
    runs = []
    for b in range(2):
        for j in range(per):
            runs += [m[b * rows1 : (b + 1) * rows1, j * own : (j + 1) * own] for m in (c, d)]
    w1_ref[...] = jnp.concatenate(runs, axis=1)
    w2_ref[:own, :] = c[2 * rows1 :]
    w2_ref[own:, :] = jnp.where(here, other, mine)


def mlp_join(rows1, order, parts):
    own = parts[0].shape[0] - 2 * rows1
    return pl.pallas_call(
        mlp_join_kernel,
        in_specs=[SMEM] + [VMEM] * 4,
        out_specs=[VMEM] * 2,
        out_shape=[
            jax.ShapeDtypeStruct((rows1, 2 * own * SHARDS), F32),
            jax.ShapeDtypeStruct((2 * own, parts[0].shape[1]), F32),
        ],
        compiler_params=params(8),
        cost_estimate=cost(3),
        name="mlp_join",
    )(order, *parts)


def spread(packed, lo, size):
    return jnp.concatenate([packed[j : j + 1, lo : lo + size] for j in range(packed.shape[0])], axis=1)


def column(v):
    return jnp.broadcast_to(v, (8, v.shape[1])).T[:, 0:1]


def prepare_kernel(sizes, order_ref, x_ref, cols_ref, rows_ref, *rest):
    pieces = rest[:SHARDS]
    at_ref, cos_ref, sin_ref, vec_ref, b1_ref, bias_ref, sel_ref, line_scr, table_scr, sem = rest[SHARDS:]
    half = cos_ref.shape[0]

    @pl.when(pl.program_id(0) == 0)
    def _():
        last = pieces[0].shape[0]
        copies = fetch(pieces, order_ref, [(slice(last - LINES, last), lambda d: line_scr.at[d])], sem)
        start_all(copies)
        wait_all(copies)
        packed = jnp.concatenate([line_scr[:, i, :] for i in range(2)], axis=1).astype(F32)
        starts = [sum(sizes[:i]) for i in range(len(sizes))]
        gain1, shift1, b_qkv, freqs, b_out, gain2, shift2 = (spread(packed, starts[i], sizes[i]) for i in range(7))
        b2 = spread(packed, starts[8], sizes[8])
        for i, v in enumerate((b_out, gain1, gain2, shift2, b2, shift1)):
            vec_ref[i : i + 1, :] = v
        own = sizes[7] // 2
        for i in range(2):
            b1_ref[i : i + 1, :] = spread(packed, starts[7] + i * own, own)
        bias_ref[...] = b_qkv
        freq = column(freqs)
        spots = lax.broadcasted_iota(jnp.int32, (1, 128), 1).astype(F32)
        for i in range(2):
            angle = freq[i * half : (i + 1) * half] * spots
            for k, table in enumerate((jnp.cos(angle), jnp.sin(angle))):
                for n in range(3):
                    term = table.astype(BF)
                    table_scr[i, k, n] = term
                    table = table - term.astype(F32)

    xhat, _ = norm_parts(x_ref[...].astype(F32))
    at_ref[...] = (xhat * vec_ref[1:2, :] + vec_ref[5:6, :]).astype(BF).T
    found = []
    for i, at in enumerate((cols_ref[...], rows_ref[...])):
        one_hot = jnp.where(lax.broadcasted_iota(jnp.int32, (128, at.shape[1]), 0) == at, 1.0, 0.0).astype(BF)
        found.append([sum(nn(table_scr[i, k, n], one_hot) for n in range(3)) for k in range(2)])
    (cos_c, sin_c), (cos_r, sin_r) = found
    cos_ref[...] = cos_c * cos_r - sin_c * sin_r
    sin_ref[...] = sin_c * cos_r + cos_c * sin_r
    line = lax.broadcasted_iota(jnp.int32, sel_ref.shape, 0)
    sel = jnp.where(line == 0, cols_ref[...].astype(F32), rows_ref[...].astype(F32))
    sel_ref[...] = jnp.where(line < 2, sel, jnp.where(line == 2, 1.0, 0.0)).astype(BF)


def prepare(sizes, order, x, patch_cols, patch_rows, pieces):
    slots, width = x.shape
    own = sizes[7] // 2
    blk = 256
    shape = jax.ShapeDtypeStruct
    tall = lambda n: pl.BlockSpec((n, blk), lambda i: (0, i))
    whole = lambda r, k: pl.BlockSpec((r, k), lambda i: (0, 0))
    return pl.pallas_call(
        partial(prepare_kernel, sizes),
        grid=(slots // blk,),
        in_specs=[SMEM, pl.BlockSpec((blk, width), lambda i: (i, 0)), tall(1), tall(1)] + [HBM] * SHARDS,
        out_specs=[
            tall(width), tall(width // 2), tall(width // 2),
            whole(8, width), whole(2, own * SHARDS), whole(1, 3 * width), tall(16),
        ],
        out_shape=[
            shape((width, slots), BF),
            shape((width // 2, slots), F32),
            shape((width // 2, slots), F32),
            shape((8, width), F32),
            shape((2, own * SHARDS), F32),
            shape((1, 3 * width), F32),
            shape((16, slots), BF),
        ],
        scratch_shapes=[
            pltpu.VMEM((SHARDS, LINES, width // GROUPS), BF),
            pltpu.VMEM((2, 2, 3, width // 2, 128), BF),
            pltpu.SemaphoreType.DMA((SHARDS,)),
        ],
        compiler_params=params(),
        cost_estimate=cost(8),
        name="prepare",
    )(order, x, patch_cols, patch_rows, *pieces)


def pack_kernel(sums1_ref, sums2_ref, b1a_ref, b1b_ref, *rest):
    heads, out_ref = rest[:-1], rest[-1]
    bias = [r[2:3, :] for r in heads[:GROUPS]]
    freq = [r[...] for r in heads[GROUPS:]]
    cols = bias[0].shape[1] // 3
    b_qkv = jnp.concatenate([b[:, i * cols : (i + 1) * cols] for i in range(3) for b in bias], axis=1)
    g_freq = jnp.concatenate([f[i : i + 1] for i in range(2) for f in freq], axis=1)
    vectors = (
        sums1_ref[0:1, :], sums1_ref[1:2, :], b_qkv, g_freq, sums2_ref[2:3, :], sums2_ref[0:1, :], sums2_ref[1:2, :],
        b1a_ref[...], b1b_ref[...], sums2_ref[3:4, :],
    )
    for j in range(SHARDS):
        runs = []
        for v in vectors:
            n = v.shape[1] // SHARDS
            runs.append(v[:, j * n : (j + 1) * n])
        out_ref[j] = jnp.concatenate(runs, axis=1)


def pack(size, *sums):
    return pl.pallas_call(
        pack_kernel,
        in_specs=[VMEM] * len(sums),
        out_specs=VMEM,
        out_shape=jax.ShapeDtypeStruct((SHARDS, 1, size), F32),
        compiler_params=params(4),
        cost_estimate=cost(3),
        name="pack",
    )(*sums)


def group_kernel(order_ref, at_ref, bq_ref, bk_ref, bv_ref, cos_ref, sin_ref, *rest):
    pieces, (q_ref, k_ref, v_ref, w_scr, wt_scr, bias_scr, sem) = rest[:SHARDS], rest[SHARDS:]
    cols = q_ref.shape[0]
    part = w_scr.shape[1] // 3

    @pl.when(pl.program_id(0) == 0)
    def _():
        copies = fetch(pieces, order_ref, [(slice(0, 3 * part), lambda d: w_scr.at[d])], sem)
        start_all(copies)
        wait_all(copies)
        for i in range(3):
            wt_scr[i] = w_scr[:, i * part : (i + 1) * part, :].reshape(SHARDS * part, cols).T
            bias_scr[i] = column((bq_ref, bk_ref, bv_ref)[i][...])

    a_t = at_ref[...]
    cos = cos_ref[...]
    sin = sin_ref[...]
    for i, out_ref, scale in ((0, q_ref, HEAD_DIM**-0.5), (1, k_ref, 1.0)):
        u = nn(wt_scr[i], a_t) + bias_scr[i]
        for h in range(cols // HEAD_DIM):
            u1 = u[h * HEAD_DIM : h * HEAD_DIM + HALF]
            u2 = u[h * HEAD_DIM + HALF : (h + 1) * HEAD_DIM]
            c = cos[h * HALF : (h + 1) * HALF]
            s = sin[h * HALF : (h + 1) * HALF]
            out_ref[h * HEAD_DIM : h * HEAD_DIM + HALF, :] = ((u1 * c - u2 * s) * scale).astype(BF)
            out_ref[h * HEAD_DIM + HALF : (h + 1) * HEAD_DIM, :] = ((u1 * s + u2 * c) * scale).astype(BF)
    v_ref[...] = (nn(wt_scr[2], a_t) + bias_scr[2]).astype(BF)


def project_group(group, order, a_t, bias, cos, sin, pieces):
    width, slots = a_t.shape
    cols = pieces[0].shape[1]
    blk = 512
    tall = lambda n, at: pl.BlockSpec((n, blk), lambda i: (at, i))
    return pl.pallas_call(
        group_kernel,
        grid=(slots // blk,),
        in_specs=[SMEM, tall(width, 0)]
        + [pl.BlockSpec((1, cols), lambda i, n=n: (0, n * GROUPS + group)) for n in range(3)]
        + [tall(cols // 2, group)] * 2
        + [HBM] * SHARDS,
        out_specs=[tall(cols, 0)] * 3,
        out_shape=[jax.ShapeDtypeStruct((cols, slots), BF)] * 3,
        scratch_shapes=[
            pltpu.VMEM((SHARDS, 3 * width // SHARDS, cols), BF),
            pltpu.VMEM((3, cols, width), BF),
            pltpu.VMEM((3, cols, 1), F32),
            pltpu.SemaphoreType.DMA((SHARDS,)),
        ],
        compiler_params=params(),
        cost_estimate=cost(7),
        name="qkv_group",
    )(order, a_t, bias, bias, bias, cos, sin, *pieces)


def out_moves(w_scr, start):
    rows = w_scr.shape[1]
    half = w_scr.shape[2] // 2
    return [
        (slice(start + i * rows, start + (i + 1) * rows), lambda d, i=i: w_scr.at[d, :, pl.ds(i * half, half)])
        for i in range(2)
    ]


def out_group_kernel(start, order_ref, vec_ref, *rest):
    o_refs, x_ref, pieces = rest[:GROUPS], rest[GROUPS], rest[GROUPS + 1 : GROUPS + 1 + SHARDS]
    h_ref, c_ref, ct_ref, w_scr, sem = rest[GROUPS + 1 + SHARDS :]

    @pl.when(pl.program_id(0) == 0)
    def _():
        copies = fetch(pieces, order_ref, out_moves(w_scr, start), sem)
        start_all(copies)
        wait_all(copies)

    width = x_ref.shape[1]
    o = jnp.concatenate([r[...].T for r in o_refs], axis=1)
    h = x_ref[...].astype(F32) + (nn(o, w_scr[...].reshape(width, width)) + vec_ref[0:1, :])
    h_ref[...] = h.astype(BF)
    xhat, _ = norm_parts(h)
    c = (xhat * vec_ref[2:3, :] + vec_ref[3:4, :]).astype(BF)
    c_ref[...] = c
    ct_ref[...] = c.T


def out_project_fast(order, o, x, vec, pieces, start):
    slots, width = x.shape
    blk = 256
    rows = pl.BlockSpec((blk, width), lambda i: (i, 0))
    cols = pl.BlockSpec((width, blk), lambda i: (0, i))
    return pl.pallas_call(
        partial(out_group_kernel, start),
        grid=(slots // blk,),
        in_specs=[SMEM, VMEM] + [pl.BlockSpec((width // GROUPS, blk), lambda i: (0, i))] * GROUPS + [rows] + [HBM] * SHARDS,
        out_specs=[rows, rows, cols],
        out_shape=[
            jax.ShapeDtypeStruct((slots, width), BF),
            jax.ShapeDtypeStruct((slots, width), BF),
            jax.ShapeDtypeStruct((width, slots), BF),
        ],
        scratch_shapes=[pltpu.VMEM((SHARDS, width // SHARDS, width), BF), pltpu.SemaphoreType.DMA((2 * SHARDS,))],
        compiler_params=params(),
        cost_estimate=cost(8),
        name="out_project",
    )(order, vec, *o, x, *pieces)


def mlp_half_kernel(part, first, split, n_in, order_ref, c_in, ct_in, dy_in, b1_ref, vec_ref, *rest):
    acc_in, rest = (rest[:1], rest[1:]) if first else (rest[:2], rest[2:])
    pieces, rest = rest[:n_in], rest[n_in:]
    n_g = 2 if split else 1
    y_ref, dc_ref = rest[:2]
    g_refs = rest[2 : 2 + n_g]
    gb1_ref, w1_scr, w2_scr, g1_scr, g2_scr, hb_scr, dp_scr, y_acc, dc_acc = rest[2 + n_g : 11 + n_g]
    c_ref, ct_ref, dy_ref, y_out, dc_out, sem, load_sem = rest[11 + n_g :]
    slots, width = c_ref.shape
    rows1 = w1_scr.shape[2]
    rows2 = w2_scr.shape[1]
    blk = w1_scr.shape[3]
    steps = w1_scr.shape[0]
    per = blk // rows2
    tile = 512
    refs = [pieces[0].at[p] for p in range(SHARDS)] if n_in == 1 else pieces
    places = range(SHARDS) if n_in == 1 else order_ref
    loads = [
        fetch(refs, places, [(slice(j * rows1, (j + 1) * rows1), lambda d, j=j: w1_scr.at[j, d])], sem.at[j])
        for j in range(steps)
    ]
    loads.insert(1, fetch(refs, places, [(slice(steps * rows1, steps * rows1 + rows2), lambda d: w2_scr.at[d])], sem.at[steps]))
    sums = list(zip(acc_in, (y_out, dc_out)))
    rows_in = [(c_in, c_ref), (dy_in, dy_ref), (ct_in, ct_ref)]
    whole = [pltpu.make_async_copy(src, dst, load_sem.at[i]) for i, (src, dst) in enumerate(rows_in + sums)]
    (c_load, dy_load, ct_load), sums = whole[:3], whole[3:]
    for copies in [[c_load], loads[0], [dy_load], loads[1], sums, [ct_load]] + loads[2:]:
        start_all(copies)
    sends = []
    for j in range(steps):
        cols = slice(j * blk, (j + 1) * blk)
        wait_all([c_load] + loads[0] if j == 0 else loads[1 + j])
        w1 = w1_scr[j].reshape(width, blk)
        w2 = None
        total = None
        for i in range(slots // tile):
            rows = slice(i * tile, (i + 1) * tile)
            pre = nn(c_ref[rows, :], w1) + b1_ref[part : part + 1, cols]
            square = pre * pre
            th = jnp.tanh(GELU_C * (pre + GELU_A * (pre * square)))
            cdf = 0.5 * (1.0 + th)
            hb = (pre * cdf).astype(BF)
            slope = cdf + 0.5 * pre * (1.0 - th * th) * (GELU_C * (1.0 + (3.0 * GELU_A) * square))
            hb_scr[rows, :] = hb
            if w2 is None:
                if j == 0:
                    wait_all(loads[1] + [dy_load] + sums)
                w2 = w2_scr[j * per : (j + 1) * per].reshape(blk, width)
            before = y_acc if j else y_out
            y = before[rows, :].astype(F32) + nn(hb, w2)
            if first and j == 0:
                y = y + vec_ref[4:5, :]
            dpre = (nt(dy_ref[rows, :], w2) * slope).astype(BF)
            dp_scr[rows, :] = dpre
            term = jnp.sum(dpre.astype(F32), axis=0, keepdims=True)
            total = term if total is None else total + term
            dc = nt(dpre, w1)
            if j or not first:
                dc = dc + (dc_acc if j else dc_out)[rows, :].astype(F32)
            if j == steps - 1:
                y_out[rows, :] = y.astype(BF)
                dc_out[rows, :] = dc.astype(BF)
                sends += [
                    pltpu.make_async_copy(y_out.at[rows], y_ref.at[rows], load_sem.at[5 + 2 * i]),
                    pltpu.make_async_copy(dc_out.at[rows], dc_ref.at[rows], load_sem.at[6 + 2 * i]),
                ]
                start_all(sends[-2:])
            else:
                y_acc[rows, :] = y
                dc_acc[rows, :] = dc
        gb1_ref[:, cols] = total
        if j == 0:
            wait_all([ct_load])
        g1_scr[j] = nn(ct_ref[...], dp_scr[...]).astype(BF).reshape(SHARDS, rows1, blk)
        if split:
            mine = order_ref[SHARDS]
            dests = [(g_refs[b], i, order_ref[p + b]) for b in range(2) for i, p in enumerate(LEAVING)]
            place = lambda dst, i, lo, n: dst.at[lax.rem(lo // (steps * rows1) + mine, 2), i, pl.ds(lo % (steps * rows1), n)]
        else:
            dests = [(g_refs[0], p, p) for p in range(SHARDS)]
            place = lambda dst, i, lo, n: dst.at[i, pl.ds(lo, n)]
        copies = [
            pltpu.make_async_copy(g1_scr.at[j, d], place(dst, i, j * rows1, rows1), sem.at[j, n])
            for n, (dst, i, d) in enumerate(dests)
        ]
        start_all(copies)
        sends += copies
        g2_scr[j * per : (j + 1) * per] = tn(hb_scr[...], dy_ref[...]).astype(BF).reshape(per, rows2, width)
    copies = [
        pltpu.make_async_copy(g2_scr.at[d], place(dst, i, steps * rows1, rows2), sem.at[steps, n])
        for n, (dst, i, d) in enumerate(dests)
    ]
    start_all(copies)
    wait_all(sends + copies)


def mlp_half(part, order, c, ct, dy, b1, vec, sums, pieces, split):
    slots, width = c.shape
    rows1 = width // SHARDS
    rows2 = pieces[0].shape[-2] - 2 * rows1
    hidden = rows2 * SHARDS
    steps = 2
    blk = hidden // steps
    first = len(sums) == 1
    block = jax.ShapeDtypeStruct((SHARDS, 2 * rows1 + rows2, width), BF)
    if split:
        block = jax.ShapeDtypeStruct((2, SHARDS // 2, rows2, width), BF)
    return pl.pallas_call(
        partial(mlp_half_kernel, part, first, split, len(pieces)),
        in_specs=[SMEM] + [ANY] * 3 + [VMEM] * 2 + [ANY] * len(sums) + [HBM] * len(pieces),
        out_specs=[ANY, ANY] + [ANY] * (2 if split else 1) + [VMEM],
        out_shape=[jax.ShapeDtypeStruct((slots, width), BF)] * 2
        + [block] * (2 if split else 1)
        + [jax.ShapeDtypeStruct((1, hidden), F32)],
        scratch_shapes=[
            pltpu.VMEM((steps, SHARDS, rows1, blk), BF),
            pltpu.VMEM((SHARDS, rows2, width), BF),
            pltpu.VMEM((steps, SHARDS, rows1, blk), BF),
            pltpu.VMEM((SHARDS, rows2, width), BF),
            pltpu.VMEM((slots, blk), BF),
            pltpu.VMEM((slots, blk), BF),
            pltpu.VMEM((slots, width), F32),
            pltpu.VMEM((slots, width), F32),
            pltpu.VMEM((slots, width), BF),
            pltpu.VMEM((width, slots), BF),
            pltpu.VMEM((slots, width), BF),
            pltpu.VMEM((slots, width), BF),
            pltpu.VMEM((slots, width), BF),
            pltpu.SemaphoreType.DMA((steps + 1, SHARDS)),
            pltpu.SemaphoreType.DMA((9,)),
        ],
        compiler_params=params(),
        cost_estimate=cost(23),
        name="mlp_half",
    )(order, c, ct, dy, b1, vec, *sums, *pieces)


def out_back_fast_kernel(start, order_ref, dc_ref, h_ref, dy_ref, vec_ref, *rest):
    o_refs, pieces = rest[:GROUPS], rest[GROUPS : GROUPS + SHARDS]
    dh_ref, do_ref, near_ref, far_ref, sums_ref, acc_ref, g_scr, w_scr, sem = rest[GROUPS + SHARDS :]
    i = pl.program_id(0)
    width = h_ref.shape[1]
    each = width // SHARDS
    half = width // 2

    @pl.when(i == 0)
    def _():
        copies = fetch(pieces, order_ref, out_moves(w_scr, start), sem)
        start_all(copies)
        acc_ref[...] = jnp.zeros_like(acc_ref)
        sums_ref[...] = jnp.zeros_like(sums_ref)
        wait_all(copies)

    dy = dy_ref[...].astype(F32)
    part, dgain, dshift = norm_back(dc_ref[...].astype(F32), h_ref[...].astype(F32), vec_ref[2:3, :])
    dh = dy + part
    dhb = dh.astype(BF)
    dh_ref[...] = dhb
    do_ref[...] = nt(w_scr[...].reshape(width, width), dhb).astype(BF)
    rows = width // GROUPS
    for g in range(GROUPS):
        acc_ref[g * rows : (g + 1) * rows, :] += nn(o_refs[g][...], dhb)
    sums_ref[0:1, :] += dgain
    sums_ref[1:2, :] += dshift
    sums_ref[2:3, :] += jnp.sum(dh, axis=0, keepdims=True)
    sums_ref[3:4, :] += jnp.sum(dy, axis=0, keepdims=True)

    @pl.when(i == pl.num_programs(0) - 1)
    def _():
        g_scr[...] = acc_ref[...].astype(BF).reshape(g_scr.shape)
        copies = []
        for b, out in enumerate((near_ref, far_ref)):
            for n, p in enumerate(LEAVING):
                for k in range(2):
                    src = g_scr.at[order_ref[p + b], :, pl.ds(k * half, half)]
                    dst = out.at[n, pl.ds((3 + k) * each, each)]
                    copies.append(pltpu.make_async_copy(src, dst, sem.at[len(copies)]))
        start_all(copies)
        wait_all(copies)


def out_back_fast(order, dc, h, dy, vec, o, pieces, start):
    slots, width = h.shape
    blk = 256
    rows = pl.BlockSpec((blk, width), lambda i: (i, 0))
    cols = pl.BlockSpec((width, blk), lambda i: (0, i))
    whole = lambda r, k: pl.BlockSpec((r, k), lambda i: (0, 0))
    block = jax.ShapeDtypeStruct((SHARDS // 2, 5 * width // SHARDS, width // 2), BF)
    return pl.pallas_call(
        partial(out_back_fast_kernel, start),
        grid=(slots // blk,),
        in_specs=[SMEM, rows, rows, rows, VMEM]
        + [pl.BlockSpec((width // GROUPS, blk), lambda i: (0, i))] * GROUPS
        + [HBM] * SHARDS,
        out_specs=[rows, cols, ANY, ANY, whole(8, width)],
        out_shape=[
            jax.ShapeDtypeStruct((slots, width), BF),
            jax.ShapeDtypeStruct((width, slots), BF),
            block,
            block,
            jax.ShapeDtypeStruct((8, width), F32),
        ],
        scratch_shapes=[
            pltpu.VMEM((width, width), F32),
            pltpu.VMEM((SHARDS, width // SHARDS, width), BF),
            pltpu.VMEM((SHARDS, width // SHARDS, width), BF),
            pltpu.SemaphoreType.DMA((2 * SHARDS,)),
        ],
        compiler_params=params(),
        cost_estimate=cost(12),
        name="out_back",
    )(order, dc, h, dy, vec, *o, *pieces)


def heads_back_kernel(
    counts_ref, q_ref, k_ref, v_ref, o_ref, do_ref, lse_ref, cos_ref, sin_ref,
    dq_ref, dk_ref, dv_ref, dangle_ref, bias_ref,
):
    slots = q_ref.shape[1]

    @pl.when(pl.program_id(0) == 0)
    def _():
        bias_ref[...] = second_bias(counts_ref, slots)

    lane1 = lax.broadcasted_iota(jnp.int32, (1, WIDE), 1)
    lane2 = lax.broadcasted_iota(jnp.int32, (1, slots - CUT), 1)
    scale = HEAD_DIM**-0.5

    def part(scores, grads, queries, outs, keys, delta_row, first):
        prob = jnp.exp(scores)
        ds = (prob * (grads - delta_row)).astype(BF)
        pb = prob.astype(BF)
        gap = jnp.zeros((keys.shape[1] - pb.shape[0], pb.shape[1]), BF)
        pb = jnp.concatenate([pb, gap] if first else [gap, pb], axis=0)
        ds = jnp.concatenate([ds, gap] if first else [gap, ds], axis=0)
        return nn(keys, ds), nt(queries, ds), nt(outs, pb)

    for h in range(q_ref.shape[0] // HEAD_DIM):
        top = h * HEAD_DIM
        rows = slice(top, top + HEAD_DIM)
        kt = k_ref[rows, :]
        k = kt.T
        v = v_ref[rows, :].T
        q = q_ref[rows, :]
        do = do_ref[rows, :]
        lse = lse_ref[h]
        delta = jnp.sum(do.astype(F32) * o_ref[rows, :].astype(F32), axis=0, keepdims=True)
        lse1 = jnp.where(lane1 < FIRST, lse[:, :WIDE], -NEG)
        lse2 = jnp.where(lane2 >= FIRST - CUT, lse[:, CUT:], -NEG)
        grads1 = part(
            nn(k[:FIRST], q[:, :WIDE]) - lse1, nn(v[:FIRST], do[:, :WIDE]),
            q[:, :WIDE], do[:, :WIDE], kt[:, :WIDE], delta[:, :WIDE], True,
        )
        grads2 = part(
            nn(k[FIRST:], q[:, CUT:]) + bias_ref[...] - lse2, nn(v[FIRST:], do[:, CUT:]),
            q[:, CUT:], do[:, CUT:], kt[:, CUT:], delta[:, CUT:], False,
        )
        dq, dk, dv = (
            jnp.concatenate([one[:, :CUT], one[:, CUT:] + two[:, : WIDE - CUT], two[:, WIDE - CUT :]], axis=1)
            for one, two in zip(grads1, grads2)
        )
        cos = cos_ref[h * HALF : (h + 1) * HALF, :]
        sin = sin_ref[h * HALF : (h + 1) * HALF, :]
        dangle = None
        for r, rot, out in ((dq * scale, q.astype(F32) * (1.0 / scale), dq_ref), (dk, kt.astype(F32), dk_ref)):
            r1, r2 = r[:HALF], r[HALF:]
            term = r2 * rot[:HALF] - r1 * rot[HALF:]
            dangle = term if dangle is None else dangle + term
            out[top : top + HALF, :] = (r1 * cos + r2 * sin).astype(BF)
            out[top + HALF : top + HEAD_DIM, :] = (r2 * cos - r1 * sin).astype(BF)
        dv_ref[rows, :] = dv.astype(BF)
        dangle_ref[h * HALF : (h + 1) * HALF, :] = dangle.astype(BF)


def heads_back(group, counts, q, k, v, o, do, lse, cos, sin):
    width, slots = q.shape
    heads = width // HEAD_DIM
    each = 2
    steps = heads // each
    head = pl.BlockSpec((each * HEAD_DIM, slots), lambda h: (h, 0))
    half = pl.BlockSpec((each * HALF, slots), lambda h: (h, 0))
    turn = pl.BlockSpec((each * HALF, slots), lambda h: (group * steps + h, 0))
    late = pl.BlockSpec((each * HEAD_DIM, slots), lambda h: (group * steps + h, 0))
    return pl.pallas_call(
        heads_back_kernel,
        grid=(steps,),
        in_specs=[SMEM] + [head] * 4 + [late, pl.BlockSpec((each, 1, slots), lambda h: (h, 0, 0)), turn, turn],
        out_specs=[head] * 3 + [half],
        out_shape=[jax.ShapeDtypeStruct((width, slots), BF)] * 3 + [jax.ShapeDtypeStruct((width // 2, slots), BF)],
        scratch_shapes=[pltpu.VMEM((slots - FIRST, slots - CUT), F32)],
        compiler_params=params(20),
        cost_estimate=cost(13),
        name="heads_back",
    )(counts, q, k, v, o, do, lse, cos, sin)


def qkv_grad_kernel(order_ref, at_ref, sel_ref, dangle_ref, dq_ref, dk_ref, dv_ref, *rest):
    near_ref, far_ref, bias_ref, freq_ref, g_scr, sem = rest[-6:]
    part = g_scr.shape[1] // 3
    outs = (near_ref, far_ref)
    at = at_ref[...]
    for i, ref in enumerate((dq_ref, dk_ref, dv_ref)):
        g = nt(at, ref[...]).astype(BF)
        g_scr[:, i * part : (i + 1) * part, :] = g.reshape(SHARDS, part, g.shape[1])
        bias_ref[:, i * g.shape[1] : (i + 1) * g.shape[1]] = nt(sel_ref[...], ref[...])
    freq_ref[...] = nt(sel_ref[...], dangle_ref[...])
    copies = []
    for b, out in enumerate(outs):
        for n, p in enumerate(LEAVING):
            dst = out.at[n, pl.ds(0, 3 * part)]
            copies.append(pltpu.make_async_copy(g_scr.at[order_ref[p + b]], dst, sem.at[len(copies)]))
    start_all(copies)
    wait_all(copies)


def qkv_grad(order, at, sel, dangle, dq, dk, dv, *more):
    width, slots = at.shape
    cols = dq.shape[0]
    rows = 3 * width // SHARDS
    total = more[0].shape[1] if more else rows
    return pl.pallas_call(
        qkv_grad_kernel,
        in_specs=[SMEM] + [VMEM] * 6 + [ANY] * len(more),
        out_specs=[ANY, ANY, VMEM, VMEM],
        out_shape=[jax.ShapeDtypeStruct((SHARDS // 2, total, cols), BF)] * 2
        + [jax.ShapeDtypeStruct((sel.shape[0], 3 * cols), F32), jax.ShapeDtypeStruct((sel.shape[0], cols // 2), F32)],
        scratch_shapes=[
            pltpu.VMEM((SHARDS, rows, cols), BF),
            pltpu.SemaphoreType.DMA((SHARDS,)),
        ],
        input_output_aliases={7: 0, 8: 1} if more else {},
        compiler_params=params(16),
        cost_estimate=cost(6),
        name="qkv_grad",
    )(order, at, sel, dangle, dq, dk, dv, *more)


def part_kernel(order_ref, *rest):
    grads, pieces, (da_ref, w_scr, sem) = rest[:3], rest[3 : 3 + SHARDS], rest[3 + SHARDS :]
    add_group(order_ref, grads, pieces, da_ref, w_scr, sem)


def group_weights(order_ref, pieces, w_scr, sem):
    rows = w_scr.shape[1]
    copies = fetch(pieces, order_ref, [(slice(0, rows), lambda d: w_scr.at[d])], sem)
    start_all(copies)
    wait_all(copies)


def group_product(grads, w_scr):
    rows = w_scr.shape[1] // 3
    total = None
    for n in range(3):
        w = w_scr[:, n * rows : (n + 1) * rows, :].reshape(SHARDS * rows, w_scr.shape[2])
        term = nn(w, grads[n][...])
        total = term if total is None else total + term
    return total


def add_group(order_ref, grads, pieces, da_ref, w_scr, sem):
    @pl.when(pl.program_id(0) == 0)
    def _():
        group_weights(order_ref, pieces, w_scr, sem)

    da_ref[...] = group_product(grads, w_scr)


def input_part(order, grads, pieces, width):
    cols, slots = grads[0].shape
    blk = 512
    return pl.pallas_call(
        part_kernel,
        grid=(slots // blk,),
        in_specs=[SMEM] + [pl.BlockSpec((cols, blk), lambda i: (0, i))] * 3 + [HBM] * SHARDS,
        out_specs=pl.BlockSpec((width, blk), lambda i: (0, i)),
        out_shape=jax.ShapeDtypeStruct((width, slots), F32),
        scratch_shapes=[pltpu.VMEM((SHARDS, 3 * width // SHARDS, cols), BF), pltpu.SemaphoreType.DMA((SHARDS,))],
        compiler_params=params(16),
        cost_estimate=cost(6),
        name="input_part",
    )(order, *grads, *pieces)


def input_kernel(order_ref, x_ref, dh_ref, vec_ref, da_ref, *rest):
    grads, pieces, (dx_ref, sums_ref, w_scr, sem) = rest[:3], rest[3 : 3 + SHARDS], rest[3 + SHARDS :]

    @pl.when(pl.program_id(0) == 0)
    def _():
        group_weights(order_ref, pieces, w_scr, sem)
        sums_ref[...] = jnp.zeros_like(sums_ref)

    da = da_ref[...] + group_product(grads, w_scr)
    out, dgain, dshift = norm_back(da.T, x_ref[...].astype(F32), vec_ref[1:2, :])
    dx_ref[...] = (dh_ref[...].astype(F32) + out).astype(BF)
    sums_ref[0:1, :] += dgain
    sums_ref[1:2, :] += dshift


def input_back(order, x, dh, vec, da, grads, pieces):
    slots, width = x.shape
    cols = grads[0].shape[0]
    blk = 512
    rows = pl.BlockSpec((blk, width), lambda i: (i, 0))
    return pl.pallas_call(
        input_kernel,
        grid=(slots // blk,),
        in_specs=[SMEM, rows, rows, VMEM, pl.BlockSpec((width, blk), lambda i: (0, i))]
        + [pl.BlockSpec((cols, blk), lambda i: (0, i))] * 3
        + [HBM] * SHARDS,
        out_specs=[rows, pl.BlockSpec((8, width), lambda i: (0, 0))],
        out_shape=[jax.ShapeDtypeStruct((slots, width), BF), jax.ShapeDtypeStruct((8, width), F32)],
        scratch_shapes=[pltpu.VMEM((SHARDS, 3 * width // SHARDS, cols), BF), pltpu.SemaphoreType.DMA((SHARDS,))],
        compiler_params=params(20),
        cost_estimate=cost(10),
        name="input_back",
    )(order, x, dh, vec, da, *grads, *pieces)


def body_fast(
    tokens, cotangent, image_counts, patch_rows, patch_cols, ln1_gain, ln1_bias, qkv_weight, qkv_bias, rope_freqs,
    out_weight, out_bias, ln2_gain, ln2_bias, fc1_weight, fc1_bias, fc2_weight, fc2_bias,
):
    x = tokens[0]
    dy = cotangent[0]
    counts = image_counts[0]
    slots, width = x.shape
    cols = width // GROUPS
    half = width // 2
    order = lax.axis_index("fsdp") ^ jnp.arange(SHARDS, dtype=jnp.int32)
    order = jnp.concatenate([order, lax.axis_index("rep")[None].astype(jnp.int32)])

    own = fc2_weight.shape[0] // 2
    small = (ln1_gain, ln1_bias, qkv_bias, rope_freqs, out_bias, ln2_gain, ln2_bias, fc1_bias, fc2_bias)
    sizes = [s.shape[0] for s in small]
    vectors = jnp.concatenate(small + (jnp.zeros((2 * cols - sum(sizes),), BF),)).reshape(2, cols)
    piece_c, piece_d = mlp_pieces(fc1_weight, fc2_weight)
    piece_a, piece_b = group_pieces(qkv_weight, out_weight, vectors)
    pieces_c = [lax.all_gather(piece_c, "fsdp", axis=0)]
    pieces_d = [lax.all_gather(piece_d, "fsdp", axis=0)]
    first = lambda g: (g.piece[8], g.piece[4], g.piece[2])
    second = lambda g: (g.piece[12], g.piece[6], g.piece[10])
    gather_a = Gather(piece_a)
    gather_a.stage1()
    gather_a.stage2(*first(gather_a))
    gather_a.stage3()
    pieces_a = gather_a.cores()
    gather_b = Gather(piece_b)
    gather_b.stage1(gather_a.piece[12])
    a_t, cos, sin, vec, b1, bias, sel = prepare(sizes, order, x, patch_cols, patch_rows, pieces_a)
    gather_b.stage2(sel)
    q, k, v = project_group(0, order, a_t, bias, cos, sin, pieces_a)
    gather_b.hold((12, 6, 10), q)
    gather_b.stage3()
    heads = [(q, k, v) + tuple(attend(counts, q, k, v))]
    gather_b.hold((14,), heads[0][3])
    pieces_b = gather_b.cores()
    q, k, v = project_group(1, order, a_t, bias, cos, sin, pieces_b)
    heads.append((q, k, v) + tuple(attend(counts, q, k, v)))
    o = [t[3] for t in heads]
    at_out = piece_b.shape[0] - 2 * out_weight.shape[0]
    h, c, c_t = out_project_fast(order, o, x, vec, pieces_b, at_out)
    y, dc, g_c, g_b1a = mlp_half(0, order, c, c_t, dy, b1, vec, (h,), pieces_c, False)
    mlp_c = lax.psum_scatter(tie(g_c, pieces_d[0]), "fsdp", scatter_dimension=0, tiled=True)[0]
    y, dc, near_d, far_d, g_b1b = mlp_half(1, order, c, c_t, dy, b1, vec, (y, dc), pieces_d, True)
    scatter_d = SplitScatter(near_d, far_d)
    dh, do, near_o, far_o, sums2 = out_back_fast(order, dc, h, dy, vec, o, pieces_b, at_out)

    def back(g, do):
        q, k, v, og, lse = heads[g]
        *three, dangle = heads_back(g, counts, q, k, v, og, do, lse, cos, sin)
        return three, dangle

    sent = scatter_d.split()
    grads_b, dangle_b = back(1, tie(do, sent))
    near_b, far_b, bias_b, freq_b = qkv_grad(order, a_t, sel, dangle_b, *grads_b, near_o, far_o)
    scatter_b = Scatter(near_b, far_b)
    scatter_d.hold(near_b)
    sent = scatter_d.step()
    grads_a, dangle_a = back(0, tie(do, sent, near_b))
    scatter_d.hold(dangle_a)
    scatter_b.hold(dangle_a)
    sent = (scatter_d.step(), scatter_b.step())
    near_a, far_a, bias_a, freq_a = qkv_grad(order, a_t, sel, tie(dangle_a, *sent), *grads_a)
    scatter_a = Scatter(near_a, far_a)
    da = input_part(order, lax.optimization_barrier((grads_b, near_a))[0], pieces_b, width)
    for scatter in (scatter_d, scatter_b, scatter_a):
        scatter.hold(da)
    sent = (scatter_a.step(), scatter_b.step(), scatter_d.step())
    dx, sums1 = input_back(order, x, dh, vec, tie(da, *sent), grads_a, pieces_a)
    scatter_a.hold(sums1, scatter_b.got[-1], scatter_d.got[-1])
    sent = scatter_a.step()
    other_c = across(tie(mlp_c, sent))
    scatter_b.hold(sent)
    scatter_d.hold(sent)
    sent = (sent, scatter_b.step())
    block = pack(sum(sizes), tie(sums1, *sent), sums2, g_b1a, g_b1b, bias_a, bias_b, freq_a, freq_b)
    scatter_a.hold(block)
    sent = scatter_a.step()
    mlp_d = scatter_d.finish()
    scatter_b.hold(sent)
    mine_b = scatter_b.finish()
    mine = jnp.sum(tie(lax.all_to_all(block, "fsdp", 0, 0, tiled=True), sent), axis=0)
    mine = tie(mine[0], scatter_a.got[-1])
    rows1 = width // SHARDS
    s_w1, s_w2 = mlp_join(rows1, order, (mlp_c, other_c) + mlp_d)
    scatter_a.hold(mine)
    mine_a = scatter_a.finish()
    mine_a = (mine_a[0], tie(mine_a[1], s_w1))
    mine = mine + across(mine)
    s_a = mine_a[0].astype(F32) + mine_a[1].astype(F32)
    s_b = mine_b[0].astype(F32) + mine_b[1].astype(F32)
    s_wqkv = jnp.concatenate([s[i * rows1 : (i + 1) * rows1] for i in range(3) for s in (s_a, s_b)], axis=1)
    s_wout = jnp.concatenate([s_b[3 * rows1 : 4 * rows1], s_b[4 * rows1 :]], axis=1)

    outs = []
    at = 0
    for size in sizes:
        outs.append(mine[at : at + size])
        at += size
    s_gain1, s_shift1, s_bqkv, s_freq, s_bout, s_gain2, s_shift2, s_b1, s_b2 = outs
    return (
        y[None], dx[None], s_gain1, s_shift1, s_wqkv, s_bqkv, s_freq, s_wout, s_bout,
        s_gain2, s_shift2, s_w1, s_b1, s_w2, s_b2,
    )


def solution(mesh):
    row = P(("rep", "fsdp"), None)
    rows = P(("rep", "fsdp"), None, None)
    vec = P("fsdp")
    mat = P("fsdp", None)
    in_specs = (rows, rows, row, row, row, vec, vec, mat, vec, vec, mat, vec, vec, vec, mat, vec, mat, vec)
    out_specs = (rows, rows, vec, vec, mat, vec, vec, mat, vec, vec, vec, mat, vec, mat, vec)
    fast = mesh.shape["fsdp"] == SHARDS and mesh.shape["rep"] == 2
    return jax.shard_map(
        body_fast if fast else body_any, mesh=mesh, in_specs=in_specs, out_specs=out_specs, check_vma=False
    )
```
